32 devices in a mesh: dp: 8 (over z, x), expert: 4 (over y, core).
Axes of the slice: x: 2, y: 2, z: 4, core: 2. Of those that a mesh axis runs over, the one named last changes fastest.
Arguments:
- inputs: bfloat16 [32768, 512], P(('dp', 'expert')), may hold values from -12 to 12
- embedding: bfloat16 [32768, 512], P(('dp', 'expert')), may hold values from -6 to 6
- cotangent: bfloat16 [32768, 512], P(('dp', 'expert')), may hold values from -6 to 6
- first_routes: int32 [32768, 1], P(('dp', 'expert')), may hold values from 0 to 3; in each aligned block of 1024 rows (0 to 1023, 1024 to 2047, ...) at most 272 rows name the same one
- second_routes: int32 [32768, 1], P(('dp', 'expert')), may hold values from 0 to 3; in each aligned block of 1024 rows (0 to 1023, 1024 to 2047, ...) at most 272 rows name the same one
- segment_starts: int32 [32, 5], P(('dp', 'expert')), may hold values from 0 to 1024, as said below
- norm_gains: bfloat16 [5, 512], P(None, ('dp', 'expert')), may hold values from 0.099609375 to 1.8984375
- first_router: bfloat16 [1024, 4], P(('dp', 'expert')), may hold values from -0.119628906 to 0.119628906
- second_router: bfloat16 [1024, 4], P(('dp', 'expert')), may hold values from -0.119628906 to 0.119628906
- first_in: bfloat16 [4, 512, 2048], P('expert', 'dp'), may hold values from -0.25 to 0.25
- first_out: bfloat16 [4, 2048, 512], P('expert', 'dp'), may hold values from -2 to 2
- second_in: bfloat16 [4, 512, 2048], P('expert', 'dp'), may hold values from -0.25 to 0.25
- second_out: bfloat16 [4, 2048, 512], P('expert', 'dp'), may hold values from -2 to 2
- attention_in: bfloat16 [512, 1536], P(('dp', 'expert')), may hold values from -0.25 to 0.25
- position_weight: bfloat16 [512, 512], P(('dp', 'expert')), may hold values from -0.25 to 0.25
- position_bias: bfloat16 [2, 512], P(None, ('dp', 'expert')), may hold values from -3 to 3
- attention_out: bfloat16 [512, 512], P(('dp', 'expert')), may hold values from -0.75 to 0.75
- pointwise_in: bfloat16 [512, 1024], P(('dp', 'expert')), may hold values from -0.25 to 0.25
- depthwise_kernel: bfloat16 [15, 512], P(None, ('dp', 'expert')), may hold values from -1.5 to 1.5
- batch_gain: bfloat16 [512], P(('dp', 'expert')), may hold values from 0.099609375 to 1.8984375
- batch_bias: bfloat16 [512], P(('dp', 'expert')), may hold values from -1.796875 to 1.796875
- pointwise_out: bfloat16 [512, 512], P(('dp', 'expert')), may hold values from -0.25 to 0.25
Outputs:
- output: bfloat16 [32768, 512], P(('dp', 'expert'))
- inputs_gradient: float32 [32768, 512], P(('dp', 'expert'))
- embedding_gradient: float32 [32768, 512], P(('dp', 'expert'))
- norm_gains_gradient: float32 [5, 512], P(None, ('dp', 'expert'))
- first_router_gradient: float32 [1024, 4], P(('dp', 'expert'))
- second_router_gradient: float32 [1024, 4], P(('dp', 'expert'))
- first_in_gradient: float32 [4, 512, 2048], P('expert', 'dp')
- first_out_gradient: float32 [4, 2048, 512], P('expert', 'dp')
- second_in_gradient: float32 [4, 512, 2048], P('expert', 'dp')
- second_out_gradient: float32 [4, 2048, 512], P('expert', 'dp')
- attention_in_gradient: float32 [512, 1536], P(('dp', 'expert'))
- position_weight_gradient: float32 [512, 512], P(('dp', 'expert'))
- position_bias_gradient: float32 [2, 512], P(None, ('dp', 'expert'))
- attention_out_gradient: float32 [512, 512], P(('dp', 'expert'))
- pointwise_in_gradient: float32 [512, 1024], P(('dp', 'expert'))
- depthwise_kernel_gradient: float32 [15, 512], P(None, ('dp', 'expert'))
- batch_gain_gradient: float32 [512], P(('dp', 'expert'))
- batch_bias_gradient: float32 [512], P(('dp', 'expert'))
- pointwise_out_gradient: float32 [512, 512], P(('dp', 'expert'))
The draws below stay inside these ranges and needn't reach their ends.
Inputs may be any that keep to these rules, and one draw needn't show every extreme that they name: `first_routes`: at most 272 frames of one row name the same expert. `second_routes`: at most 272 frames of one row name the same expert. `segment_starts`: each row starts with 0 and rises; consecutive entries differ by 128 to 256; the last entry is the row's count of valid frames, and some row has 1024.
All inputs are finite; a program needn't handle non-finite values.
Results may differ from the reference program's by a relative error of at most 0.025.
Values may be sent and summed in bfloat16 or wider, within the bound.
No kernel may reach another device: no remote copies, remote signals or barrier semaphores. Data moves between devices by JAX's collectives and lax.ppermute only.
A program may use at most 384 MiB of HBM per device.

```python
import math
import jax
import jax.numpy as jnp
import numpy as np
from jax import lax

D = 512
DE = 512
FF = 2048
H = 8
KERNEL = 15
ROW_LEN = 1024
NSEG = 4
EXPERTS = 4
CAP = 272
ROWS = 32
TOKENS = 32768


def draw_segment_starts(key, part):
    key = jax.random.fold_in(key, 11)
    lengths = jax.random.randint(jax.random.fold_in(key, 1), (ROWS, NSEG), ROW_LEN // 8, ROW_LEN // 4 + 1)
    chosen = jax.random.randint(jax.random.fold_in(key, 2), (), 0, ROWS)
    lengths = jnp.where((jnp.arange(ROWS) == chosen)[:, None], ROW_LEN // 4, lengths)
    starts = jnp.cumsum(lengths, axis=1)
    return jnp.concatenate([jnp.zeros((ROWS, 1), jnp.int32), starts.astype(jnp.int32)], axis=1).astype(jnp.int32)


def shared_frames(base, key, low_end, high_end):
    common = jnp.clip(jax.random.normal(jax.random.fold_in(key, 2), (D,), jnp.float32), -3.0, 3.0)
    row_index = (jnp.arange(TOKENS, dtype=jnp.int32) // ROW_LEN).astype(jnp.float32)
    fraction = row_index / max(ROWS - 1, 1)
    scales = low_end * jnp.exp(fraction * math.log(high_end / low_end))
    return base + scales[:, None] * common[None, :]


def draw_inputs(key, part):
    key = jax.random.fold_in(key, 23)
    base = jnp.clip(jax.random.normal(jax.random.fold_in(key, 1), (TOKENS, D), jnp.float32), -6.0, 6.0)
    values = shared_frames(base, key, 0.2, 1.5)
    return values.astype(jnp.bfloat16)


def steps_of(key, dims, cuts, least, largest):
    def one(axis_at, parts):
        draws = jax.random.uniform(jax.random.fold_in(jax.random.fold_in(key, 6), axis_at), (parts,), jnp.float32, least / len(cuts), largest / len(cuts))
        return jnp.repeat(jnp.exp(draws), dims[axis_at] // parts).reshape((-1,) + (1,) * (len(dims) - axis_at - 1))

    factor_of = one(*cuts[0])
    for cut in cuts[1:]:
        factor_of = factor_of * one(*cut)
    return factor_of


def shared_out(stream_key, own, number, rows, count, top, most, slope):
    ranking = jax.random.permutation(stream_key, count)
    packed, ordinary = portions_of(count, rows * top, most, slope, True), portions_of(count, rows * top, most, slope, False)
    places = jnp.arange(count)

    def named(tallies, offset_by):
        used = int((tallies > 0).sum())
        fixed = max(1, used // 4)
        moved = fixed + (places - fixed + offset_by * (used - fixed)) % max(1, count - fixed)
        return jnp.zeros((count,), jnp.int32).at[ranking[jnp.where(places < fixed, places, moved)]].set(jnp.asarray(tallies, jnp.int32))

    tallies = jnp.where(number % 4 == 0, named(packed, number // 4), named(ordinary, number - number // 4 - 1))
    mixed = jax.random.permutation(jax.random.fold_in(own, 3), count)
    giver, receiver = mixed[0:count // 2 * 2:2], mixed[1:count // 2 * 2:2]
    margin = jnp.minimum(tallies[giver] - 1, most - tallies[receiver]) // 2
    margin = jnp.where((giver == ranking[0]) | (receiver == ranking[0]) | (tallies[receiver] == 0), 0, jnp.maximum(margin, 0))
    moved = jax.random.randint(jax.random.fold_in(own, 4), (count // 2,), 0, 1 << 20) % (margin + 1)
    tallies = tallies.at[giver].add(-moved).at[receiver].add(moved)
    items = jnp.searchsorted(jnp.cumsum(tallies), jnp.arange(rows * top), side="right").astype(jnp.int32)
    listing = items.reshape(top, rows).T
    listing = listing[jax.random.permutation(jax.random.fold_in(own, 1), rows)]
    offset_by = jax.random.randint(jax.random.fold_in(own, 2), (rows, 1), 0, top)
    return jnp.take_along_axis(listing, (jnp.arange(top)[None, :] + offset_by) % top, axis=1)


def portions_of(amount, total, limit, skew, full):
    portions = [(1 << 20) // math.isqrt(standing ** skew) + 1 for standing in range(1, amount + 1)]
    largest = limit if full else min(limit, max(-(-total // amount), total * portions[0] // sum(portions)))
    least = 1 if total - largest >= amount - 1 else 0
    given, surplus = [largest] + [least] * (amount - 1), total - largest - least * (amount - 1)
    while surplus > 0:
        candidates = [i for i in range(1, amount) if given[i] < largest] or [i for i in range(1, amount) if given[i] < limit]
        pool, budget = sum([portions[i] for i in candidates]), surplus
        for i in candidates:
            extra = min(limit - given[i], max(1, budget * portions[i] // pool), surplus)
            given[i] = given[i] + extra
            surplus = surplus - extra
    return np.array(given)


def normal_values(key, dims, scale, most, pieces=(), held_as=jnp.bfloat16):
    values = jax.random.normal(key, dims, jnp.float32) * scale
    if len(pieces) > 0:
        values = steps_of(key, dims, pieces, -0.22, 0.18) * values
    return jnp.clip(values, min=-most, max=most).astype(held_as)


def setup_inputs(seed: int = 0) -> dict:
    streams_of = jax.random.split(jax.random.key(seed), 23)
    inputs = draw_inputs(jax.random.fold_in(streams_of[22], 71), 0)
    embedding = normal_values(streams_of[1], (TOKENS, DE), 1.0, 6.0, ((0, 32),))
    cotangent = normal_values(streams_of[2], (TOKENS, D), 1.0, 6.0, ((0, 32),))
    first_routes_keys = jax.random.split(jax.random.fold_in(streams_of[3], 1), TOKENS // ROW_LEN)
    first_routes_turns = jax.random.permutation(jax.random.fold_in(streams_of[3], 3), TOKENS // ROW_LEN)
    first_routes = jax.vmap(lambda own, number: shared_out(jax.random.fold_in(streams_of[3], 2), own, number, ROW_LEN, EXPERTS, 1, CAP, 2))(first_routes_keys, first_routes_turns).reshape((TOKENS, 1))
    second_routes_keys = jax.random.split(jax.random.fold_in(streams_of[4], 1), TOKENS // ROW_LEN)
    second_routes_turns = jax.random.permutation(jax.random.fold_in(streams_of[4], 3), TOKENS // ROW_LEN)
    second_routes = jax.vmap(lambda own, number: shared_out(jax.random.fold_in(streams_of[4], 2), own, number, ROW_LEN, EXPERTS, 1, CAP, 2))(second_routes_keys, second_routes_turns).reshape((TOKENS, 1))
    segment_starts = draw_segment_starts(jax.random.fold_in(streams_of[22], 71), 0)
    norm_gains = jnp.clip(1.0 + 0.18 * jax.random.normal(streams_of[6], (5, D), jnp.float32), 0.099609375, 1.8984375).astype(jnp.bfloat16)
    first_router = normal_values(streams_of[7], (D + DE, EXPERTS), 0.02, 0.119628906, ((0, 32),))
    second_router = normal_values(streams_of[8], (D + DE, EXPERTS), 0.02, 0.119628906, ((0, 32),))
    first_in = normal_values(streams_of[9], (EXPERTS, D, FF), D ** -0.5, 0.25, ((0, 4), (1, 8)))
    first_out = normal_values(streams_of[10], (EXPERTS, FF, D), ((FF + 255) // 256) ** -0.5, 2.0, ((0, 4), (1, 8)))
    second_in = normal_values(streams_of[11], (EXPERTS, D, FF), D ** -0.5, 0.25, ((0, 4), (1, 8)))
    second_out = normal_values(streams_of[12], (EXPERTS, FF, D), ((FF + 255) // 256) ** -0.5, 2.0, ((0, 4), (1, 8)))
    attention_in = normal_values(streams_of[13], (D, 3 * D), D ** -0.5, 0.25, ((0, 32),))
    position_weight = normal_values(streams_of[14], (D, D), D ** -0.5, 0.25, ((0, 32),))
    position_bias = normal_values(streams_of[15], (2, D), 0.5, 3.0, ((1, 32),))
    attention_out = normal_values(streams_of[16], (D, D), (D // 8) ** -0.5, 0.75, ((0, 32),))
    pointwise_in = normal_values(streams_of[17], (D, 2 * D), D ** -0.5, 0.25, ((0, 32),))
    depthwise_kernel = normal_values(streams_of[18], (KERNEL, D), KERNEL ** -0.5, 1.5, ((1, 32),))
    batch_gain = jnp.clip(1.0 + 0.18 * jax.random.normal(streams_of[19], (D,), jnp.float32), 0.099609375, 1.8984375).astype(jnp.bfloat16)
    batch_bias = normal_values(streams_of[20], (D,), 0.3, 1.796875, ((0, 32),))
    pointwise_out = normal_values(streams_of[21], (D, D), D ** -0.5, 0.25, ((0, 32),))
    return dict(inputs=inputs, embedding=embedding, cotangent=cotangent, first_routes=first_routes, second_routes=second_routes, segment_starts=segment_starts, norm_gains=norm_gains, first_router=first_router, second_router=second_router, first_in=first_in, first_out=first_out, second_in=second_in, second_out=second_out, attention_in=attention_in, position_weight=position_weight, position_bias=position_bias, attention_out=attention_out, pointwise_in=pointwise_in, depthwise_kernel=depthwise_kernel, batch_gain=batch_gain, batch_bias=batch_bias, pointwise_out=pointwise_out)


@jax.custom_vjp
def low(v):
    return lax.optimization_barrier(v.astype(jnp.bfloat16)).astype(jnp.float32)

@jax.custom_vjp
def low_back(v):
    return v

def low_keep(v):
    return (low(v), None)

def low_pass(kept, grad):
    return (grad,)

def back_keep(v):
    return (v, None)

def back_low(kept, grad):
    return (low(grad),)
low.defvjp(low_keep, low_pass)
low_back.defvjp(back_keep, back_low)
epsilon = 1e-05
masked_score = -1e+30
highest = lax.Precision.HIGHEST

def product(left, right):
    return jnp.dot(left, right, precision=highest)

def norm_scale(values, gain):
    center = values - lax.optimization_barrier(jnp.mean(values, axis=-1, keepdims=True))
    spread = lax.optimization_barrier(jnp.mean(center * center, axis=-1, keepdims=True))
    return center * lax.rsqrt(spread + epsilon) * gain

def segment_numbers(starts, length):
    frames = jnp.arange(length, dtype=jnp.int32)
    numbers = lax.optimization_barrier(jnp.sum((starts[1:][None, :] <= frames[:, None]).astype(jnp.int32), axis=1))
    return (numbers, frames < starts[-1])

def sinus_table(length, width):
    distance = (length - 1 - jnp.arange(2 * length - 1, dtype=jnp.int32)).astype(jnp.float32)
    rates = jnp.exp(jnp.arange(width // 2, dtype=jnp.int32).astype(jnp.float32) * (-2.0 * math.log(10000.0) / width))
    angles = distance[:, None] * rates[None, :]
    return jnp.concatenate([jnp.sin(angles), jnp.cos(angles)], axis=1)

def relative_shift(flipped, length):
    heads, rows, span = flipped.shape
    flat = flipped.reshape(heads, rows * span)
    flat = flat[:, rows - 1:rows - 1 + rows * (span - 1)]
    return flat.reshape(heads, rows, span - 1)[:, :, :length]

def depthwise(gates_in, kernel, numbers):
    length, double = gates_in.shape
    width = double // 2
    linear = gates_in[:, :width] * jax.nn.sigmoid(gates_in[:, width:])
    reach = kernel.shape[0] // 2
    padded = jnp.pad(linear, ((reach, reach), (0, 0)))
    padded_numbers = jnp.pad(numbers, (reach, reach), constant_values=-1)
    total = jnp.zeros_like(linear)
    for offset in range(kernel.shape[0]):
        same = (padded_numbers[offset:offset + length] == numbers)[:, None]
        total = total + jnp.where(same, padded[offset:offset + length], 0.0) * kernel[offset]
    return total

def expert_step(hidden_in, embed, gain, router, weight_in, weight_out, routes):
    length, width = hidden_in.shape
    experts = router.shape[1]
    normed = low(norm_scale(hidden_in, gain))
    logits = product(jnp.concatenate([normed, embed], axis=1), router)
    probs = jax.nn.softmax(logits, axis=-1)
    chosen = routes[:, 0]
    onehot = chosen[:, None] == jnp.arange(experts, dtype=jnp.int32)[None, :]
    gate = lax.optimization_barrier(jnp.sum(jnp.where(onehot, probs, 0.0), axis=1))
    counts = jnp.cumsum(onehot.astype(jnp.int32), axis=0) - 1
    rank = lax.optimization_barrier(jnp.sum(jnp.where(onehot, counts, 0), axis=1))
    slot = (chosen * CAP + rank).astype(jnp.int32)
    owner = jnp.full((experts * CAP,), length, jnp.int32).at[slot].set(jnp.arange(length, dtype=jnp.int32))
    padded = jnp.concatenate([normed, jnp.zeros((1, width), normed.dtype)], axis=0)
    outgoing = low_back(padded[owner]).reshape(experts, CAP, width)
    inner = low_back(jnp.einsum('ecd,edf->ecf', outgoing, weight_in, precision=highest))
    activated = low(jax.nn.silu(inner))
    returned = low_back(low(jnp.einsum('ecf,efd->ecd', activated, weight_out, precision=highest)))
    picked = returned.reshape(experts * CAP, width)[slot]
    return hidden_in + 0.5 * gate[:, None] * picked

def attention(normed, mixing_in, table_weight, bias_pair, mixing_out, numbers, sinus):
    length, width = normed.shape
    size = width // H
    mixed = low_back(product(normed, mixing_in))
    queries = mixed[:, :width]
    query_u = low(queries + bias_pair[0]).reshape(length, H, size)
    query_v = low(queries + bias_pair[1]).reshape(length, H, size)
    keys = low(mixed[:, width:2 * width]).reshape(length, H, size)
    values = low(mixed[:, 2 * width:]).reshape(length, H, size)
    table = low_back(low(product(sinus, table_weight))).reshape(2 * length - 1, H, size)
    block = min(512, length)
    span = length + block - 1
    scale = 1.0 / math.sqrt(size)

    def one_block(index):
        start_row = index * block
        block_u = lax.dynamic_slice_in_dim(query_u, start_row, block, 0)
        block_v = lax.dynamic_slice_in_dim(query_v, start_row, block, 0)
        block_numbers = lax.dynamic_slice_in_dim(numbers, start_row, block, 0)
        window = lax.dynamic_slice_in_dim(table, length - start_row - block, span, 0)
        content = jnp.einsum('qhd,khd->hqk', block_u, keys, precision=highest)
        flipped = jnp.einsum('qhd,whd->hqw', block_v, window, precision=highest)
        scores = (content + relative_shift(flipped, length)) * scale
        same = block_numbers[:, None] == numbers[None, :]
        scores = low_back(jnp.where(same[None], scores, masked_score))
        probs = low(jax.nn.softmax(scores, axis=-1))
        return jnp.einsum('hqk,khd->qhd', probs, values, precision=highest)
    context = lax.map(jax.checkpoint(one_block), jnp.arange(length // block, dtype=jnp.int32))
    context = low_back(low(context.reshape(length, width)))
    return low_back(product(context, mixing_out))

def forward(inputs, embedding, norm_gains, first_router, second_router, first_in, first_out, second_in, second_out, attention_in, position_weight, position_bias, attention_out, pointwise_in, depthwise_kernel, batch_gain, batch_bias, pointwise_out, first_routes, second_routes, segment_starts):
    rows = segment_starts.shape[0]
    length = inputs.shape[0] // rows
    width = inputs.shape[1]
    sinus = low(sinus_table(length, width))
    frames = inputs.reshape(rows, length, width)
    embeds = embedding.reshape(rows, length, -1)
    routes_one = first_routes.reshape(rows, length, 1)
    routes_two = second_routes.reshape(rows, length, 1)

    def front(pack):
        row_frames, row_embed, row_routes, starts = pack
        numbers, valid = segment_numbers(starts, length)
        mixed_one = expert_step(row_frames, row_embed, norm_gains[0], first_router, first_in, first_out, row_routes)
        normed_two = low(norm_scale(mixed_one, norm_gains[1]))
        mixed_two = mixed_one + attention(normed_two, attention_in, position_weight, position_bias, attention_out, numbers, sinus)
        normed_three = low(norm_scale(mixed_two, norm_gains[2]))
        gates_in = low_back(product(normed_three, pointwise_in))
        return (mixed_two, depthwise(gates_in, depthwise_kernel, numbers))
    mixed_two, convolved = lax.map(jax.checkpoint(front), (frames, embeds, routes_one, segment_starts))

    def valid_frames(starts):
        return segment_numbers(starts, length)[1]
    mask = jax.vmap(valid_frames)(segment_starts).astype(jnp.float32)[:, :, None]
    count = jnp.sum(mask)
    mean = lax.optimization_barrier(jnp.sum(mask * convolved, axis=(0, 1))) / count
    variance = lax.optimization_barrier(jnp.sum(mask * convolved * convolved, axis=(0, 1))) / count - mean * mean
    inverse = lax.rsqrt(variance + epsilon)

    def back_half(pack):
        row_mixed, row_conv, row_embed, row_routes = pack
        batched = (row_conv - mean) * inverse * batch_gain + batch_bias
        active = low(jax.nn.silu(batched))
        mixed_three = row_mixed + low_back(product(active, pointwise_out))
        mixed_four = expert_step(mixed_three, row_embed, norm_gains[3], second_router, second_in, second_out, row_routes)
        return norm_scale(mixed_four, norm_gains[4])
    result = lax.map(jax.checkpoint(back_half), (mixed_two, convolved, embeds, routes_two))
    return result.reshape(rows * length, width)

def reference(inputs, embedding, cotangent, first_routes, second_routes, segment_starts, norm_gains, first_router, second_router, first_in, first_out, second_in, second_out, attention_in, position_weight, position_bias, attention_out, pointwise_in, depthwise_kernel, batch_gain, batch_bias, pointwise_out):
    floats = (inputs, embedding, norm_gains, first_router, second_router, first_in, first_out, second_in, second_out, attention_in, position_weight, position_bias, attention_out, pointwise_in, depthwise_kernel, batch_gain, batch_bias, pointwise_out)
    floats = tuple((item.astype(jnp.float32) for item in floats))

    def wrapped(*values):
        return forward(*values, first_routes, second_routes, segment_starts)
    result, pullback = jax.vjp(wrapped, *floats)
    grads = pullback(cotangent.astype(jnp.float32))
    return (result.astype(jnp.bfloat16), grads[0], grads[1], grads[2], grads[3], grads[4], grads[5], grads[6], grads[7], grads[8], grads[9], grads[10], grads[11], grads[12], grads[13], grads[14], grads[15], grads[16], grads[17])
```

```python
import functools
import math

import jax
import jax.numpy as jnp
import numpy as np
from jax import lax
from jax.experimental import pallas as pl
from jax.experimental.pallas import tpu as pltpu
from jax.sharding import PartitionSpec as P

H = 8
TILE = 128
epsilon = 1e-05
masked_score = -1e30
BOTH = ("dp", "expert")
f32 = jnp.float32
bf16 = jnp.bfloat16

VMEM = pl.BlockSpec(memory_space=pltpu.VMEM)
SMEM = pl.BlockSpec(memory_space=pltpu.SMEM)


def shape_of(dims, kind):
    return jax.ShapeDtypeStruct(dims, kind)


def run(kernel, args, in_specs, outs, scratch=(), flops=0, name=None):
    moved = sum(math.prod(a.shape) * a.dtype.itemsize for a in list(args) + list(outs))
    return pl.pallas_call(
        kernel,
        out_shape=outs,
        in_specs=in_specs,
        out_specs=[VMEM] * len(outs),
        scratch_shapes=list(scratch),
        compiler_params=pltpu.CompilerParams(vmem_limit_bytes=56 * 2**20),
        cost_estimate=pl.CostEstimate(flops=flops, bytes_accessed=moved, transcendentals=0),
        name=name,
    )(*args)


def dot(left, right):
    return lax.dot_general(left, right, (((1,), (0,)), ((), ())), preferred_element_type=f32)


def dot_t(left, right):
    return lax.dot_general(left, right, (((1,), (1,)), ((), ())), preferred_element_type=f32)


def t_dot(left, right):
    return lax.dot_general(left, right, (((0,), (0,)), ((), ())), preferred_element_type=f32)


def iota(dims, axis):
    return lax.broadcasted_iota(jnp.int32, dims, axis)


def normalize(values):
    center = values - jnp.mean(values, axis=-1, keepdims=True)
    spread = jnp.mean(center * center, axis=-1, keepdims=True)
    inverse = lax.rsqrt(spread + epsilon)
    return center * inverse, inverse


def normalize_back(standard, inverse, gain, upstream):
    scaled = upstream * gain
    first = jnp.mean(scaled, axis=-1, keepdims=True)
    second = jnp.mean(scaled * standard, axis=-1, keepdims=True)
    return inverse * (scaled - first - standard * second)


def column_sum(values):
    return jnp.sum(values, axis=0, keepdims=True)


def sigmoid(values):
    return 1.0 / (1.0 + jnp.exp(-values))


def loop(count, body):
    def step(index, carry):
        body(index)
        return carry

    lax.fori_loop(0, count, step, 0)


def rows_at(index, size):
    return pl.ds(pl.multiple_of(index * size, size), size)


def slots_kernel(experts, capacity, rows_ref, cols_ref, slot_row_ref, slot_one_ref, slot_two_ref):
    length = rows_ref.shape[1]
    block = 256
    slot_row_ref[...] = jnp.zeros_like(slot_row_ref)
    for half, out_ref in enumerate((slot_one_ref, slot_two_ref)):
        chosen = rows_ref[half : half + 1, :]
        onehot = jnp.where(iota((8, length), 0) == chosen, 1.0, 0.0)
        onehot_low = onehot.astype(bf16)
        for index in range(length // block):
            earlier = iota((length, block), 0) < iota((length, block), 1) + index * block
            counts = dot(onehot_low, jnp.where(earlier, 1.0, 0.0).astype(bf16))
            span = slice(index * block, (index + 1) * block)
            rank = column_sum(onehot[:, span] * counts).astype(jnp.int32)
            slot_row_ref[half : half + 1, span] = chosen[:, span] * capacity + rank
        picks = cols_ref[:, half : half + 1]
        wide = jnp.where(iota((length, TILE), 1) == picks, 1.0, 0.0)
        wide_low = wide.astype(bf16)
        for index in range(length // block):
            earlier = iota((block, length), 1) < iota((block, length), 0) + index * block
            counts = dot(jnp.where(earlier, 1.0, 0.0).astype(bf16), wide_low)
            span = slice(index * block, (index + 1) * block)
            rank = jnp.sum(wide[span] * counts, axis=1, keepdims=True).astype(jnp.int32)
            out_ref[span, :] = picks[span] * capacity + rank


def find_slots(routes_one, routes_two, experts, capacity):
    length = routes_one.shape[0]
    rows = jnp.concatenate([routes_one.reshape(1, length), routes_two.reshape(1, length)], axis=0)
    cols = jnp.concatenate([routes_one, routes_two], axis=1)
    return run(
        functools.partial(slots_kernel, experts, capacity),
        (rows, cols),
        [VMEM, VMEM],
        [
            shape_of((8, length), jnp.int32),
            shape_of((length, 1), jnp.int32),
            shape_of((length, 1), jnp.int32),
        ],
        flops=8 * length * length * 128,
        name="slots",
    )


def dispatch(low_ref, slot_row, out_ref):
    slots, width = out_ref.shape
    length = low_ref.shape[0]
    block = slots // 4

    def step(index):
        ids = iota((block, length), 0) + index * block
        onehot = jnp.where(ids == slot_row, 1.0, 0.0).astype(bf16)
        out_ref[rows_at(index, block), :] = dot(onehot, low_ref[...]).astype(bf16)

    loop(4, step)


def collect(slot_col, table_ref):
    rows = slot_col.shape[0]
    slots = table_ref.shape[0]
    onehot = jnp.where(iota((rows, slots), 1) == slot_col, 1.0, 0.0).astype(bf16)
    return dot(onehot, table_ref[...])


def route_block(low, embed, router_ref, picks, experts):
    width = low.shape[1]
    logits = dot(low, router_ref[:width, :]) + dot(embed, router_ref[width:, :])
    lanes = iota(logits.shape, 1)
    inside = lanes < experts
    logits = jnp.where(inside, logits, masked_score)
    raised = jnp.where(inside, jnp.exp(logits - jnp.max(logits, axis=1, keepdims=True)), 0.0)
    probs = raised / jnp.sum(raised, axis=1, keepdims=True)
    gate = jnp.sum(jnp.where(lanes == picks, probs, 0.0), axis=1, keepdims=True)
    return probs, gate


BLOCK = 256


def front_kernel(
    experts, hidden_ref, embed_ref, gain_ref, router_ref, picks_ref, slot_row_ref,
    out_ref, probs_ref, gate_ref, low_ref,
):
    length = hidden_ref.shape[0]

    def step(index):
        at = rows_at(index, BLOCK)
        standard, unused = normalize(hidden_ref[at, :].astype(f32))
        low = (standard * gain_ref[0:1, :]).astype(bf16)
        low_ref[at, :] = low
        probs, gate = route_block(low, embed_ref[at, :], router_ref, picks_ref[at, :], experts)
        probs_ref[at, :] = probs
        gate_ref[at, :] = gate

    loop(length // BLOCK, step)
    dispatch(low_ref, slot_row_ref[0:1, :], out_ref)


def expert_forward_kernel(x_ref, in_ref, out_ref, y_ref):
    slots = x_ref.shape[0]
    block = slots // 4

    def step(index):
        at = rows_at(index, block)
        inner = dot(x_ref[at, :], in_ref[...])
        hidden = (inner * sigmoid(inner)).astype(bf16)
        y_ref[at, :] = dot(hidden, out_ref[...]).astype(bf16)

    loop(4, step)


def expert_forward(received, weight_in, weight_out):
    slots, width = received.shape
    return run(
        expert_forward_kernel,
        (received, weight_in, weight_out),
        [VMEM] * 3,
        [shape_of((slots, width), bf16)],
        flops=4 * slots * width * weight_in.shape[1],
        name="experts",
    )[0]


def expert_backward_kernel(x_ref, dy_ref, in_ref, out_ref, dx_ref, hidden_ref, dinner_ref):
    slots = x_ref.shape[0]
    block = slots // 4

    def step(index):
        at = rows_at(index, block)
        inner = dot(x_ref[at, :], in_ref[...])
        gates = sigmoid(inner)
        hidden = inner * gates
        hidden_ref[at, :] = hidden.astype(bf16)
        d_hidden = dot_t(dy_ref[at, :], out_ref[...])
        d_inner = (d_hidden * (gates + hidden * (1.0 - gates))).astype(bf16)
        dinner_ref[at, :] = d_inner
        dx_ref[at, :] = dot_t(d_inner, in_ref[...]).astype(bf16)

    loop(4, step)


def expert_backward(received, d_result, weight_in, weight_out):
    slots, width = received.shape
    inner = weight_in.shape[1]
    return run(
        expert_backward_kernel,
        (received, d_result, weight_in, weight_out),
        [VMEM] * 4,
        [
            shape_of((slots, width), bf16),
            shape_of((slots, inner), bf16),
            shape_of((slots, inner), bf16),
        ],
        flops=6 * slots * width * inner,
        name="experts_back",
    )


def tile_window(starts_ref, first, length):
    count = starts_ref.shape[1]
    low = jnp.int32(0)
    high = jnp.int32(length)
    for k in range(1, count):
        low = jnp.where(starts_ref[0, k] <= first, starts_ref[0, k], low)
    for k in range(count - 1, 0, -1):
        high = jnp.where(starts_ref[0, k] > first + (TILE - 1), starts_ref[0, k], high)
    return low // TILE, (high + (TILE - 1)) // TILE


def numbers_at(starts_ref, positions):
    total = jnp.zeros(positions.shape, jnp.int32)
    for k in range(1, starts_ref.shape[1]):
        total = total + jnp.where(positions >= starts_ref[0, k], 1, 0)
    return total


def same_tile(starts_ref, first_query, first_key):
    rows = numbers_at(starts_ref, iota((TILE, TILE), 0) + first_query)
    cols = numbers_at(starts_ref, iota((TILE, TILE), 1) + first_key)
    return rows == cols


def chunk_rows(query_tile, key_tile, extra, length, mirrored=False):
    tiles = length // TILE
    index = tiles - 1 - query_tile + key_tile + extra - tiles // 2
    index = jnp.clip(index, 0, tiles - 1)
    if mirrored:
        index = tiles - 1 - index
    return pl.ds(pl.multiple_of(index * TILE, TILE), TILE)


def halves(values):
    left = iota(values.shape, 1) < TILE // 2
    zero = jnp.zeros_like(values)
    return jnp.concatenate(
        [jnp.where(left, values, zero), jnp.where(left, zero, values)], axis=0
    )


def skew(values):
    return jnp.concatenate(
        [
            pltpu.roll(values[:TILE], 1, 1, stride=1, stride_axis=0),
            pltpu.roll(values[TILE:], 1, 1, stride=1, stride_axis=0),
        ],
        axis=0,
    )


def mirror(values):
    flip = iota((TILE, TILE), 0) + iota((TILE, TILE), 1) == TILE - 1
    return dot(values, jnp.where(flip, 1.0, 0.0).astype(bf16))


def twice(values):
    return jnp.concatenate([values, values], axis=0)


PAIRS = H // 2


def attend_forward(
    starts_ref, qu_ref, qv_ref, k_ref, v_ref, t_ref, context_ref, logs_ref,
    qum, qvm, scores, rolled, peaks, sums, mixed,
):
    length = qu_ref.shape[0]
    tiles = length // TILE

    def query_step(tile):
        first = tile * TILE
        at = rows_at(tile, TILE)
        low, high = tile_window(starts_ref, first, length)
        chunk = chunk_rows(tile, low, 0, length)
        for p in range(PAIRS):
            lanes = slice(p * TILE, (p + 1) * TILE)
            qum[p] = halves(qu_ref[at, lanes])
            qvm[p] = halves(qv_ref[at, lanes])
            rolled[p] = skew(dot_t(qvm[p], t_ref[chunk, lanes]))
            peaks[p] = jnp.full((2 * TILE, TILE), masked_score, f32)
            sums[p] = jnp.zeros((2 * TILE, TILE), f32)
            mixed[p] = jnp.zeros((2 * TILE, TILE), f32)
        lower = twice(iota((TILE, TILE), 1) <= iota((TILE, TILE), 0))

        def score_step(key, carry):
            keys = rows_at(key, TILE)
            same = twice(same_tile(starts_ref, first, key * TILE))
            chunk = chunk_rows(tile, key, 1, length)
            for p in range(PAIRS):
                lanes = slice(p * TILE, (p + 1) * TILE)
                content = dot_t(qum[p], k_ref[keys, lanes])
                fresh = skew(dot_t(qvm[p], t_ref[chunk, lanes]))
                value = content + jnp.where(lower, rolled[p], fresh)
                value = jnp.where(same, value, masked_score)
                rolled[p] = fresh
                scores[key, p] = value
                peaks[p] = jnp.maximum(peaks[p], value)
            return carry

        lax.fori_loop(low, high, score_step, 0)
        for p in range(PAIRS):
            peaks[p] = jnp.broadcast_to(
                jnp.max(peaks[p], axis=1, keepdims=True), (2 * TILE, TILE)
            )

        def value_step(key, carry):
            keys = rows_at(key, TILE)
            for p in range(PAIRS):
                lanes = slice(p * TILE, (p + 1) * TILE)
                raised = jnp.exp(scores[key, p] - peaks[p])
                sums[p] = sums[p] + raised
                mixed[p] = mixed[p] + dot(raised.astype(bf16), v_ref[keys, lanes])
            return carry

        lax.fori_loop(low, high, value_step, 0)
        left = iota((TILE, TILE), 1) < TILE // 2
        logs = jnp.zeros((TILE, TILE), f32)
        lane = iota((TILE, TILE), 1)
        for p in range(PAIRS):
            lanes = slice(p * TILE, (p + 1) * TILE)
            total = jnp.sum(sums[p], axis=1, keepdims=True)
            result = mixed[p] * (1.0 / total)
            context_ref[at, lanes] = jnp.where(left, result[:TILE], result[TILE:]).astype(bf16)
            logsum = peaks[p] + jnp.log(total)
            logs = jnp.where(lane == 2 * p, logsum[:TILE], logs)
            logs = jnp.where(lane == 2 * p + 1, logsum[TILE:], logs)
        logs_ref[at, :] = logs

    loop(tiles, query_step)


def attend_scratch(length):
    pair = (PAIRS, 2 * TILE, TILE)
    return [
        pltpu.VMEM(pair, bf16),
        pltpu.VMEM(pair, bf16),
        pltpu.VMEM((length // TILE,) + pair, f32),
        pltpu.VMEM(pair, f32),
        pltpu.VMEM(pair, f32),
        pltpu.VMEM(pair, f32),
        pltpu.VMEM(pair, f32),
    ]


def attend_backward(
    starts_ref, qu_ref, qv_ref, k_ref, v_ref, t_ref, mirrored_ref, context_ref, logs_ref, dcontext_ref,
    dm_ref, dk_ref, dv_ref, dt_ref, dbias_ref,
    qum, qvm, dcm, logs, deltas, rolled, unrolled, dqu, dqv,
):
    length, width = qu_ref.shape
    tiles = length // TILE
    scale = 1.0 / math.sqrt(width // H)
    dk_ref[...] = jnp.zeros_like(dk_ref)
    dv_ref[...] = jnp.zeros_like(dv_ref)
    dt_ref[...] = jnp.zeros_like(dt_ref)
    dbias_ref[...] = jnp.zeros_like(dbias_ref)

    def query_step(tile):
        first = tile * TILE
        at = rows_at(tile, TILE)
        low, high = tile_window(starts_ref, first, length)
        chunk = chunk_rows(tile, low, 0, length)
        lanes_all = iota((TILE, TILE), 1)
        logs_tile = logs_ref[at, :]
        for p in range(PAIRS):
            lanes = slice(p * TILE, (p + 1) * TILE)
            qum[p] = halves(qu_ref[at, lanes])
            qvm[p] = halves(qv_ref[at, lanes])
            upstream = halves(dcontext_ref[at, lanes])
            dcm[p] = upstream
            delta = jnp.sum(
                upstream.astype(f32) * twice(context_ref[at, lanes].astype(f32)),
                axis=1,
                keepdims=True,
            )
            deltas[p] = jnp.broadcast_to(delta, (2 * TILE, TILE))
            logs[p, :TILE] = jnp.broadcast_to(logs_tile[:, 2 * p : 2 * p + 1], (TILE, TILE))
            logs[p, TILE:] = jnp.broadcast_to(logs_tile[:, 2 * p + 1 : 2 * p + 2], (TILE, TILE))
            rolled[p] = skew(dot_t(qvm[p], t_ref[chunk, lanes]))
            unrolled[p] = jnp.zeros((2 * TILE, TILE), f32)
            dqu[p] = jnp.zeros((2 * TILE, TILE), f32)
            dqv[p] = jnp.zeros((2 * TILE, TILE), f32)
        lower = twice(iota((TILE, TILE), 1) <= iota((TILE, TILE), 0))

        def step(key, carry):
            keys = rows_at(key, TILE)
            same = twice(same_tile(starts_ref, first, key * TILE))
            before = chunk_rows(tile, key, 0, length, True)
            after = chunk_rows(tile, key, 1, length)
            for p in range(PAIRS):
                lanes = slice(p * TILE, (p + 1) * TILE)
                content = dot_t(qum[p], k_ref[keys, lanes])
                fresh = skew(dot_t(qvm[p], t_ref[after, lanes]))
                value = content + jnp.where(lower, rolled[p], fresh)
                rolled[p] = fresh
                probs = jnp.where(same, jnp.exp(value - logs[p]), 0.0)
                dprobs = dot_t(dcm[p], v_ref[keys, lanes])
                dscores = probs * (dprobs - deltas[p])
                dlow = dscores.astype(bf16)
                dv_ref[keys, lanes] += t_dot(probs.astype(bf16), dcm[p])
                dk_ref[keys, lanes] += t_dot(dlow, qum[p])
                dqu[p] += dot(dlow, k_ref[keys, lanes])
                turned = skew(mirror(dlow))
                moved = jnp.where(lower, turned, unrolled[p]).astype(bf16)
                unrolled[p] = turned
                dqv[p] += dot(moved, mirrored_ref[before, lanes])
                dt_ref[before, lanes] += t_dot(moved, qvm[p])
            return carry

        lax.fori_loop(low, high, step, 0)
        last = chunk_rows(tile, high, 0, length, True)
        left = iota((TILE, TILE), 1) < TILE // 2
        for p in range(PAIRS):
            lanes = slice(p * TILE, (p + 1) * TILE)
            moved = jnp.where(lower, 0.0, unrolled[p]).astype(bf16)
            dq = dqv[p] + dot(moved, mirrored_ref[last, lanes])
            dt_ref[last, lanes] += t_dot(moved, qvm[p])
            part_u = jnp.where(left, dqu[p, :TILE], dqu[p, TILE:]) * scale
            part_v = jnp.where(left, dq[:TILE], dq[TILE:]) * scale
            dbias_ref[0:1, lanes] += column_sum(part_u)
            dbias_ref[1:2, lanes] += column_sum(part_v)
            dm_ref[at, lanes] = (part_u + part_v).astype(bf16)

    loop(tiles, query_step)

    def finish(index):
        at = rows_at(index, BLOCK)
        dm_ref[at, width : 2 * width] = dk_ref[at, :].astype(bf16)
        dm_ref[at, 2 * width : 3 * width] = dv_ref[at, :].astype(bf16)

    loop(length // BLOCK, finish)


def attend_back_scratch():
    pair = (PAIRS, 2 * TILE, TILE)
    return [pltpu.VMEM(pair, bf16) for unused in range(3)] + [
        pltpu.VMEM(pair, f32) for unused in range(6)
    ]


def dense_parts(dense_ref):
    width = dense_ref.shape[0]
    cuts = (0, 3, 4, 5, 6, 8)
    return [
        dense_ref.at[:, pl.ds(start * width, (stop - start) * width)]
        for start, stop in zip(cuts[:-1], cuts[1:])
    ]


EDGE = 16


def middle_kernel(
    starts_ref, hidden_ref, returned_ref, slot_ref, gate_ref, gains_ref, dense_ref, bias_ref,
    taps_ref, sinus_ref,
    h1_ref, h2_ref, qu_ref, qv_ref, k_ref, v_ref, t_ref, context_ref, logs_ref, conv_ref, sums_ref,
    padded, *attend,
):
    length, width = h1_ref.shape
    scale = 1.0 / math.sqrt(width // H)
    in_ref, place_ref, mix_ref, unused, point_ref = dense_parts(dense_ref)

    def queries_step(index):
        at = rows_at(index, BLOCK)
        picked = collect(slot_ref[at, :], returned_ref)
        h1 = hidden_ref[at, :].astype(f32) + 0.5 * gate_ref[at, :] * picked
        h1_ref[at, :] = h1
        standard, unused = normalize(h1)
        low = (standard * gains_ref[1:2, :]).astype(bf16)
        queries = dot(low, in_ref[:, :width])
        qu_ref[at, :] = ((queries + bias_ref[0:1, :]).astype(bf16).astype(f32) * scale).astype(bf16)
        qv_ref[at, :] = ((queries + bias_ref[1:2, :]).astype(bf16).astype(f32) * scale).astype(bf16)
        k_ref[at, :] = dot(low, in_ref[:, width : 2 * width]).astype(bf16)
        v_ref[at, :] = dot(low, in_ref[:, 2 * width :]).astype(bf16)
        t_ref[at, :] = dot(sinus_ref[at, :], place_ref[...]).astype(bf16)

    loop(length // BLOCK, queries_step)
    attend_forward(
        starts_ref, qu_ref, qv_ref, k_ref, v_ref, t_ref, context_ref, logs_ref, *attend
    )
    padded[:EDGE, :] = jnp.zeros((EDGE, width), f32)
    padded[EDGE + length :, :] = jnp.zeros((EDGE, width), f32)

    def gates_step(index):
        at = rows_at(index, BLOCK)
        h2 = h1_ref[at, :] + dot(context_ref[at, :], mix_ref[...])
        h2_ref[at, :] = h2
        standard, unused = normalize(h2)
        low = (standard * gains_ref[2:3, :]).astype(bf16)
        value = dot(low, point_ref[:, :width])
        gates = dot(low, point_ref[:, width:])
        padded[pl.ds(pl.multiple_of(index * BLOCK + EDGE, EDGE), BLOCK), :] = value * sigmoid(gates)

    loop(length // BLOCK, gates_step)
    sums_ref[...] = jnp.zeros_like(sums_ref)
    taps = taps_ref.shape[0] - 1
    reach = taps // 2
    frames = starts_ref[0, starts_ref.shape[1] - 1]

    def conv_step(index):
        first = index * TILE
        place = iota((TILE, TILE), 0) + first
        here = numbers_at(starts_ref, place)
        valid = place < frames
        totals = [jnp.zeros((TILE, TILE), f32) for unused in range(width // TILE)]
        around = pl.ds(pl.multiple_of(first, TILE), TILE + 2 * EDGE)
        for tap in range(taps):
            same = numbers_at(starts_ref, place + (tap - reach)) == here
            for part in range(width // TILE):
                lanes = slice(part * TILE, (part + 1) * TILE)
                near = padded[around, lanes][EDGE + tap - reach : EDGE + tap - reach + TILE]
                totals[part] = totals[part] + jnp.where(same, near, 0.0) * taps_ref[tap : tap + 1, lanes]
        for part in range(width // TILE):
            lanes = slice(part * TILE, (part + 1) * TILE)
            conv_ref[rows_at(index, TILE), lanes] = totals[part]
            kept = jnp.where(valid, totals[part], 0.0)
            sums_ref[0:1, lanes] += column_sum(kept)
            sums_ref[1:2, lanes] += column_sum(kept * kept)

    loop(length // TILE, conv_step)
    sums_ref[2:3, :] = jnp.zeros((1, width), f32) + frames.astype(f32)


def batch_block(conv, totals_ref, back_ref):
    count = totals_ref[2:3, :]
    mean = totals_ref[0:1, :] / count
    variance = totals_ref[1:2, :] / count - mean * mean
    inverse = lax.rsqrt(variance + epsilon)
    centred = conv - mean
    standard = centred * inverse
    batched = standard * back_ref[0:1, :] + back_ref[1:2, :]
    return centred, standard, inverse, batched


def second_kernel(
    experts, h2_ref, conv_ref, totals_ref, batch_ref, point_ref, embed_ref, gains_ref, router_ref,
    picks_ref, slot_row_ref,
    h3_ref, active_ref, out_ref, probs_ref, gate_ref, low_ref,
):
    length = h2_ref.shape[0]

    def step(index):
        at = rows_at(index, BLOCK)
        unused, unused, unused, batched = batch_block(conv_ref[at, :], totals_ref, batch_ref)
        active = (batched * sigmoid(batched)).astype(bf16)
        active_ref[at, :] = active
        h3 = h2_ref[at, :] + dot(active, point_ref[...])
        h3_ref[at, :] = h3
        standard, unused = normalize(h3)
        low = (standard * gains_ref[3:4, :]).astype(bf16)
        low_ref[at, :] = low
        probs, gate = route_block(low, embed_ref[at, :], router_ref, picks_ref[at, :], experts)
        probs_ref[at, :] = probs
        gate_ref[at, :] = gate

    loop(length // BLOCK, step)
    dispatch(low_ref, slot_row_ref[1:2, :], out_ref)


def gate_back(upstream, picked, gate, probs, picks):
    d_gate = 0.5 * jnp.sum(upstream * picked, axis=1, keepdims=True)
    onehot = jnp.where(iota(probs.shape, 1) == picks, 1.0, 0.0)
    return (d_gate * gate) * (onehot - probs)


def turn_kernel(
    h3_ref, returned_ref, slot_ref, gate_ref, probs_ref, picks_ref, slot_row_ref, gains_ref,
    cotangent_ref,
    output_ref, d4_ref, out_ref, dlogits_ref, dgain_ref, low_ref,
):
    length = h3_ref.shape[0]
    dgain_ref[...] = jnp.zeros_like(dgain_ref)

    def step(index):
        at = rows_at(index, BLOCK)
        picked = collect(slot_ref[at, :], returned_ref)
        gate = gate_ref[at, :]
        h4 = h3_ref[at, :] + 0.5 * gate * picked
        standard, inverse = normalize(h4)
        gain = gains_ref[4:5, :]
        output_ref[at, :] = (standard * gain).astype(bf16)
        upstream = cotangent_ref[at, :].astype(f32)
        dgain_ref[0:1, :] += column_sum(upstream * standard)
        d4 = normalize_back(standard, inverse, gain, upstream)
        d4_ref[at, :] = d4
        dlogits_ref[at, :] = gate_back(d4, picked, gate, probs_ref[at, :], picks_ref[at, :])
        low_ref[at, :] = (0.5 * gate * d4).astype(bf16)

    loop(length // BLOCK, step)
    dispatch(low_ref, slot_row_ref[1:2, :], out_ref)


def router_back(dlogits, low, embed, router_ref, drouter_ref):
    width = low.shape[1]
    high = dlogits.astype(bf16)
    rest = (dlogits - high.astype(f32)).astype(bf16)
    d_low = dot_t(high, router_ref[:width, :]) + dot_t(rest, router_ref[:width, :])
    d_embed = dot_t(high, router_ref[width:, :]) + dot_t(rest, router_ref[width:, :])
    turned = jnp.transpose(dlogits)[:8, :]
    turned_high = turned.astype(bf16)
    turned_rest = (turned - turned_high.astype(f32)).astype(bf16)
    drouter_ref[:, :width] += dot(turned_high, low) + dot(turned_rest, low)
    drouter_ref[:, width:] += dot(turned_high, embed) + dot(turned_rest, embed)
    return d_low, d_embed


def second_back_kernel(
    dsent_ref, slot_ref, dlogits_ref, h3_ref, d4_ref, embed_ref, router_ref, gains_ref,
    conv_ref, totals_ref, batch_ref, point_ref,
    d3_ref, dlow_ref, dz_ref, dembed_ref, drouter_ref, small_ref, sums_ref,
):
    length = h3_ref.shape[0]
    drouter_ref[...] = jnp.zeros_like(drouter_ref)
    small_ref[...] = jnp.zeros_like(small_ref)
    sums_ref[...] = jnp.zeros_like(sums_ref)

    def step(index):
        at = rows_at(index, BLOCK)
        standard, inverse = normalize(h3_ref[at, :])
        gain = gains_ref[3:4, :]
        low = (standard * gain).astype(bf16)
        d_low, d_embed = router_back(
            dlogits_ref[at, :], low, embed_ref[at, :], router_ref, drouter_ref
        )
        dembed_ref[at, :] = d_embed
        d_norm = collect(slot_ref[at, :], dsent_ref) + d_low
        small_ref[0:1, :] += column_sum(d_norm * standard)
        d3 = d4_ref[at, :] + normalize_back(standard, inverse, gain, d_norm)
        d3_ref[at, :] = d3
        d3_low = d3.astype(bf16)
        dlow_ref[at, :] = d3_low
        centred, normed, unused, batched = batch_block(conv_ref[at, :], totals_ref, batch_ref)
        gates = sigmoid(batched)
        d_batched = dot_t(d3_low, point_ref[...]) * (gates + batched * gates * (1.0 - gates))
        small_ref[1:2, :] += column_sum(d_batched * normed)
        small_ref[2:3, :] += column_sum(d_batched)
        d_z = d_batched * batch_ref[0:1, :]
        dz_ref[at, :] = d_z
        sums_ref[0:1, :] += column_sum(d_z)
        sums_ref[1:2, :] += column_sum(d_z * centred)

    loop(length // BLOCK, step)


def middle_back_kernel(
    starts_ref, conv_ref, dz_ref, totals_ref, dsums_ref, batch_ref, d3_ref, h1_ref, h2_ref, gains_ref,
    dense_ref, taps_ref, sinus_ref, qu_ref, qv_ref, k_ref, v_ref, t_ref, context_ref, logs_ref,
    returned_ref, slot_ref, gate_ref, probs_ref, picks_ref, slot_row_ref,
    d1_ref, out_ref, dlogits_ref, n2_ref, n3_ref, dg_ref, d2low_ref, dm_ref, dtable_ref, small_ref,
    dtaps_ref,
    padded, linear, dcontext_ref, low_ref, mirrored_ref, *attend,
):
    length, width = h1_ref.shape
    d2_ref = d1_ref
    dt_ref = padded.at[pl.ds(0, length)]
    dk_ref = linear.at[:, pl.ds(0, width)]
    dv_ref = linear.at[:, pl.ds(width, width)]
    in_ref, place_ref, mix_ref, unused, point_ref = dense_parts(dense_ref)
    taps = taps_ref.shape[0] - 1
    reach = taps // 2
    frames = starts_ref[0, starts_ref.shape[1] - 1]
    small_ref[...] = jnp.zeros_like(small_ref)
    dtaps_ref[...] = jnp.zeros_like(dtaps_ref)
    padded[:EDGE, :] = jnp.zeros((EDGE, width), f32)
    padded[EDGE + length :, :] = jnp.zeros((EDGE, width), f32)

    def conv_step(index):
        at = rows_at(index, BLOCK)
        centred, unused, inverse, unused = batch_block(conv_ref[at, :], totals_ref, batch_ref)
        count = totals_ref[2:3, :]
        d_variance = -0.5 * inverse * inverse * inverse * dsums_ref[1:2, :]
        inside = (iota((BLOCK, 1), 0) + index * BLOCK) < frames
        shared = (2.0 * d_variance * centred - inverse * dsums_ref[0:1, :]) / count
        d_conv = inverse * dz_ref[at, :] + jnp.where(inside, shared, 0.0)
        padded[pl.ds(pl.multiple_of(index * BLOCK + EDGE, EDGE), BLOCK), :] = d_conv
        standard, unused = normalize(h2_ref[at, :])
        low = (standard * gains_ref[2:3, :]).astype(bf16)
        n3_ref[at, :] = low
        value = dot(low, point_ref[:, :width])
        linear[at, :width] = value
        linear[at, width:] = sigmoid(dot(low, point_ref[:, width:]))

    loop(length // BLOCK, conv_step)

    def turn_step(index):
        first = index * TILE
        at = rows_at(index, TILE)
        place = iota((TILE, TILE), 0) + first
        here = numbers_at(starts_ref, place)
        parts = width // TILE
        totals = [jnp.zeros((TILE, TILE), f32) for unused in range(parts)]
        values = [linear[at, part * TILE : (part + 1) * TILE] for part in range(parts)]
        gates = [linear[at, width + part * TILE : width + (part + 1) * TILE] for part in range(parts)]
        around = pl.ds(pl.multiple_of(first, TILE), TILE + 2 * EDGE)
        for tap in range(taps):
            same = numbers_at(starts_ref, place - (tap - reach)) == here
            for part in range(parts):
                lanes = slice(part * TILE, (part + 1) * TILE)
                near = padded[around, lanes][EDGE - tap + reach : EDGE - tap + reach + TILE]
                near = jnp.where(same, near, 0.0)
                totals[part] = totals[part] + near * taps_ref[tap : tap + 1, lanes]
                dtaps_ref[tap : tap + 1, lanes] += column_sum(near * (values[part] * gates[part]))
        for part in range(parts):
            lanes = slice(part * TILE, (part + 1) * TILE)
            other = slice(width + part * TILE, width + (part + 1) * TILE)
            gate = gates[part]
            dg_ref[at, lanes] = (totals[part] * gate).astype(bf16)
            dg_ref[at, other] = (totals[part] * values[part] * gate * (1.0 - gate)).astype(bf16)

    loop(length // TILE, turn_step)

    def gates_step(index):
        at = rows_at(index, BLOCK)
        d_norm = dot_t(dg_ref[at, :], point_ref[...])
        standard, inverse = normalize(h2_ref[at, :])
        small_ref[0:1, :] += column_sum(d_norm * standard)
        d2 = d3_ref[at, :] + normalize_back(standard, inverse, gains_ref[2:3, :], d_norm)
        d2_ref[at, :] = d2
        low = d2.astype(bf16)
        d2low_ref[at, :] = low
        dcontext_ref[at, :] = dot_t(low, mix_ref[...]).astype(bf16)
        mirrored_ref[at, :] = dot(sinus_ref[at, :], place_ref[...]).astype(bf16)

    loop(length // BLOCK, gates_step)
    attend_backward(
        starts_ref, qu_ref, qv_ref, k_ref, v_ref, t_ref, mirrored_ref, context_ref, logs_ref, dcontext_ref,
        dm_ref, dk_ref, dv_ref, dt_ref, small_ref.at[pl.ds(8, 8)], *attend
    )

    def queries_step(index):
        at = rows_at(index, BLOCK)
        dtable_ref[at, :] = dt_ref[at, :].astype(bf16)
        d_norm = dot_t(dm_ref[at, :], in_ref[...])
        standard, inverse = normalize(h1_ref[at, :])
        gain = gains_ref[1:2, :]
        n2_ref[at, :] = (standard * gain).astype(bf16)
        small_ref[1:2, :] += column_sum(d_norm * standard)
        d1 = d2_ref[at, :] + normalize_back(standard, inverse, gain, d_norm)
        d1_ref[at, :] = d1
        picked = collect(slot_ref[at, :], returned_ref)
        gate = gate_ref[at, :]
        dlogits_ref[at, :] = gate_back(d1, picked, gate, probs_ref[at, :], picks_ref[at, :])
        low_ref[at, :] = (0.5 * gate * d1).astype(bf16)

    loop(length // BLOCK, queries_step)
    dispatch(low_ref, slot_row_ref[0:1, :], out_ref)


def last_kernel(
    dsent_ref, slot_ref, dlogits_ref, hidden_ref, d1_ref, embed_ref, router_ref, gains_ref, dembed_two_ref,
    d0_ref, dembed_ref, drouter_ref, small_ref,
):
    length = hidden_ref.shape[0]
    drouter_ref[...] = jnp.zeros_like(drouter_ref)
    small_ref[...] = jnp.zeros_like(small_ref)

    def step(index):
        at = rows_at(index, BLOCK)
        standard, inverse = normalize(hidden_ref[at, :].astype(f32))
        gain = gains_ref[0:1, :]
        low = (standard * gain).astype(bf16)
        d_low, d_embed = router_back(
            dlogits_ref[at, :], low, embed_ref[at, :], router_ref, drouter_ref
        )
        dembed_ref[at, :] = d_embed + dembed_two_ref[at, :]
        d_norm = collect(slot_ref[at, :], dsent_ref) + d_low
        small_ref[0:1, :] += column_sum(d_norm * standard)
        d0_ref[at, :] = d1_ref[at, :] + normalize_back(standard, inverse, gain, d_norm)

    loop(length // BLOCK, step)


def gather_small(values, devices):
    spread = jnp.broadcast_to(values[None], (devices,) + values.shape)
    return lax.all_to_all(spread, BOTH, split_axis=0, concat_axis=0, tiled=True)


def sum_small(values, devices):
    return jnp.sum(gather_small(values, devices), axis=0)


def exchange(values, experts):
    slots, width = values.shape
    parted = values.reshape(experts, slots // experts, width)
    moved = lax.all_to_all(parted, "expert", split_axis=0, concat_axis=0, tiled=True)
    return moved.reshape(slots, width)


def rows_product(left, right):
    return lax.dot_general(left, right, (((0,), (0,)), ((), ())), preferred_element_type=f32)


def expert_sums(received, d_result, hidden, d_inner):
    grad_out = rows_product(hidden, d_result).astype(bf16)
    grad_in = rows_product(received, d_inner).astype(bf16)
    return (
        lax.psum_scatter(grad_in, "dp", scatter_dimension=0, tiled=True).astype(f32)[None],
        lax.psum_scatter(grad_out, "dp", scatter_dimension=0, tiled=True).astype(f32)[None],
    )


def sinus_rows(length, width, upward):
    distance = (length // 2 - 1 - np.arange(length)).astype(np.float32)
    distance = distance[::-1] if upward else distance
    rates = np.exp(
        np.arange(width // 2).astype(np.float32) * np.float32(-2.0 * math.log(10000.0) / width)
    ).astype(np.float32)
    angles = (distance[:, None] * rates[None, :]).astype(np.float64)
    table = np.concatenate([np.sin(angles), np.cos(angles)], axis=1)
    return jnp.asarray(table.astype(np.float32)).astype(bf16)


def body(
    devices,
    inputs,
    embedding,
    cotangent,
    first_routes,
    second_routes,
    segment_starts,
    norm_gains,
    first_router,
    second_router,
    first_in,
    first_out,
    second_in,
    second_out,
    attention_in,
    position_weight,
    position_bias,
    attention_out,
    pointwise_in,
    depthwise_kernel,
    batch_gain,
    batch_bias,
    pointwise_out,
):
    length, width = inputs.shape
    experts = first_router.shape[1]
    capacity = 17 * length // (16 * experts)
    slots = experts * capacity
    inner = first_in.shape[2]
    share = norm_gains.shape[1]
    taps = depthwise_kernel.shape[0]
    feats = first_router.shape[0]

    rows = jnp.concatenate(
        [norm_gains, position_bias, depthwise_kernel, batch_gain[None], batch_bias[None]], axis=0
    )
    count = rows.shape[0]
    flat = jnp.concatenate(
        [rows.reshape(-1), first_router.T.reshape(-1), second_router.T.reshape(-1)]
    ).astype(f32)
    small = gather_small(flat, devices)
    rows_all = small[:, : count * share].reshape(devices, count, share)
    rows_all = rows_all.transpose(1, 0, 2).reshape(count, devices * share)
    routers = small[:, count * share :].reshape(devices, 2, experts, feats)
    routers = routers.transpose(1, 2, 0, 3).reshape(2, experts, devices * feats)
    routers = jnp.pad(routers, ((0, 0), (0, TILE - experts), (0, 0)))
    routers = routers.transpose(0, 2, 1).astype(bf16)
    gains = jnp.pad(rows_all[0:5], ((0, 3), (0, 0)))
    bias = jnp.pad(rows_all[5:7], ((0, 6), (0, 0)))
    kernel_taps = jnp.pad(rows_all[7 : 7 + taps], ((0, 1), (0, 0)))
    batch = jnp.pad(rows_all[7 + taps : 9 + taps], ((0, 6), (0, 0)))

    packed = jnp.concatenate(
        [attention_in, position_weight, attention_out, pointwise_out, pointwise_in], axis=1
    )
    dense = lax.all_gather(packed, BOTH, axis=0, tiled=True)
    point_out = dense[:, 5 * width : 6 * width]

    first_pair = (
        lax.all_gather(first_in[0], "dp", axis=0, tiled=True),
        lax.all_gather(first_out[0], "dp", axis=0, tiled=True),
    )
    second_pair = (
        lax.all_gather(second_in[0], "dp", axis=0, tiled=True),
        lax.all_gather(second_out[0], "dp", axis=0, tiled=True),
    )

    slot_rows, slot_one, slot_two = find_slots(first_routes, second_routes, experts, capacity)
    sinus = sinus_rows(length, width, False)
    mirrored = sinus_rows(length, width, True)
    row_low = shape_of((length, width), bf16)
    row_full = shape_of((length, width), f32)
    lane_full = shape_of((length, TILE), f32)
    slot_low = shape_of((slots, width), bf16)
    column = shape_of((length, 1), f32)
    eight = shape_of((8, width), f32)
    low_scratch = pltpu.VMEM((length, width), bf16)

    sent_one, probs_one, gate_one = run(
        functools.partial(front_kernel, experts),
        (inputs, embedding, gains, routers[0], first_routes, slot_rows),
        [VMEM] * 6,
        [slot_low, lane_full, column],
        [low_scratch],
        flops=4 * slots * length * width,
        name="front",
    )
    received_one = exchange(sent_one, experts)
    result_one = expert_forward(received_one, *first_pair)
    returned_one = exchange(result_one, experts)

    edge_scratch = pltpu.VMEM((length + 2 * EDGE, width), f32)
    (
        h1, h2, query_u, query_v, keys, values, table, context, logs, convolved, sums,
    ) = run(
        middle_kernel,
        (
            segment_starts, inputs, returned_one, slot_one, gate_one, gains, dense, bias, kernel_taps, sinus,
        ),
        [SMEM] + [VMEM] * 9,
        [row_full, row_full] + [row_low] * 6 + [lane_full, row_full, eight],
        [edge_scratch] + attend_scratch(length),
        flops=16 * length * length * width,
        name="middle",
    )
    totals = sum_small(sums, devices)

    h3, active, sent_two, probs_two, gate_two = run(
        functools.partial(second_kernel, experts),
        (
            h2, convolved, totals, batch, point_out, embedding, gains, routers[1], second_routes, slot_rows,
        ),
        [VMEM] * 10,
        [row_full, row_low, slot_low, lane_full, column],
        [low_scratch],
        flops=4 * slots * length * width,
        name="second",
    )
    received_two = exchange(sent_two, experts)
    result_two = expert_forward(received_two, *second_pair)
    returned_two = exchange(result_two, experts)

    output, d4, d_sent_two, dlogits_two, dgain_five = run(
        turn_kernel,
        (
            h3, returned_two, slot_two, gate_two, probs_two, second_routes, slot_rows, gains, cotangent,
        ),
        [VMEM] * 9,
        [row_low, row_full, slot_low, lane_full, eight],
        [low_scratch],
        flops=4 * slots * length * width,
        name="turn",
    )
    d_result_two = exchange(d_sent_two, experts)
    d_received_two, hidden_two, d_inner_two = expert_backward(
        received_two, d_result_two, *second_pair
    )
    d_back_two = exchange(d_received_two, experts)
    d_second_in, d_second_out = expert_sums(received_two, d_result_two, hidden_two, d_inner_two)

    router_shape = shape_of((8, 2 * width), f32)
    d3, d3_low, d_z, dembed_two, drouter_two, small_two, dsums_part = run(
        second_back_kernel,
        (
            d_back_two, slot_two, dlogits_two, h3, d4, embedding, routers[1], gains, convolved, totals,
            batch, point_out,
        ),
        [VMEM] * 12,
        [row_full, row_low, row_full, row_full, router_shape, eight, eight],
        flops=4 * slots * length * width,
        name="second_back",
    )
    dsums = sum_small(dsums_part, devices)
    d_pointwise_out = rows_product(active, d3_low)

    (
        d1, d_sent_one, dlogits_one, normed_two, normed_three, d_gates, d2_low, d_mixed, d_table, small_mid,
        d_taps,
    ) = run(
        middle_back_kernel,
        (
            segment_starts, convolved, d_z, totals, dsums, batch, d3, h1, h2, gains, dense, kernel_taps, mirrored, query_u, query_v, keys, values, table, context, logs, returned_one, slot_one, gate_one,
            probs_one, first_routes, slot_rows,
        ),
        [SMEM] + [VMEM] * 25,
        [
            row_full, slot_low, lane_full, row_low, row_low, shape_of((length, 2 * width), bf16), row_low,
            shape_of((length, 3 * width), bf16), row_low, shape_of((16, width), f32),
            shape_of((16, width), f32),
        ],
        [
            edge_scratch, pltpu.VMEM((length, 2 * width), f32), low_scratch, low_scratch, low_scratch,
        ]
        + attend_back_scratch(),
        flops=32 * length * length * width,
        name="middle_back",
    )
    d_result_one = exchange(d_sent_one, experts)
    d_received_one, hidden_one, d_inner_one = expert_backward(received_one, d_result_one, *first_pair)
    d_back_one = exchange(d_received_one, experts)
    d_first_in, d_first_out = expert_sums(received_one, d_result_one, hidden_one, d_inner_one)

    d_start, d_embed, drouter_one, small_one = run(
        last_kernel,
        (
            d_back_one, slot_one, dlogits_one, inputs, d1, embedding, routers[0], gains, dembed_two,
        ),
        [VMEM] * 9,
        [row_full, row_full, router_shape, eight],
        flops=4 * slots * length * width,
        name="last",
    )

    dense_grad = jnp.concatenate(
        [
            rows_product(normed_two, d_mixed),
            rows_product(mirrored, d_table),
            rows_product(context, d2_low),
            d_pointwise_out,
            rows_product(normed_three, d_gates),
        ],
        axis=1,
    ).astype(bf16)
    dense_share = lax.psum_scatter(dense_grad, BOTH, scatter_dimension=0, tiled=True).astype(f32)

    rows_grad = jnp.concatenate(
        [
            small_one[0:1], small_mid[1:2], small_mid[0:1], small_two[0:1], dgain_five[0:1],
            small_mid[8:10], d_taps[:taps], small_two[1:3],
        ],
        axis=0,
    )
    rows_grad = rows_grad.reshape(count, devices, share).transpose(1, 0, 2).reshape(devices, -1)
    routers_grad = jnp.stack([drouter_one[:experts], drouter_two[:experts]])
    routers_grad = routers_grad.reshape(2 * experts, devices, feats).transpose(1, 0, 2).reshape(devices, -1)
    small_grad = jnp.concatenate([rows_grad, routers_grad], axis=1)
    small_share = jnp.sum(
        lax.all_to_all(small_grad, BOTH, split_axis=0, concat_axis=0, tiled=True), axis=0
    )
    rows_share = small_share[: count * share].reshape(count, share)
    routers_share = small_share[count * share :].reshape(2, experts, feats).transpose(0, 2, 1)

    return (
        output,
        d_start,
        d_embed,
        rows_share[0:5],
        routers_share[0],
        routers_share[1],
        d_first_in,
        d_first_out,
        d_second_in,
        d_second_out,
        dense_share[:, : 3 * width],
        dense_share[:, 3 * width : 4 * width],
        rows_share[5:7],
        dense_share[:, 4 * width : 5 * width],
        dense_share[:, 6 * width : 8 * width],
        rows_share[7 : 7 + taps],
        rows_share[7 + taps],
        rows_share[8 + taps],
        dense_share[:, 5 * width : 6 * width],
    )


def solution(mesh):
    split = P(BOTH, None)
    wide = P(None, BOTH)
    bank = P("expert", "dp", None)
    line = P(BOTH)
    in_specs = (
        (split,) * 6
        + (wide, split, split)
        + (bank,) * 4
        + (split, split, wide, split, split, wide, line, line, split)
    )
    out_specs = (
        (split,) * 3
        + (wide, split, split)
        + (bank,) * 4
        + (split, split, wide, split, split, wide, line, line, split)
    )
    return jax.shard_map(
        functools.partial(body, mesh.size),
        mesh=mesh,
        in_specs=in_specs,
        out_specs=out_specs,
        check_vma=False,
    )
```

```python
import functools
import math

import jax
import jax.numpy as jnp
import numpy as np
from jax import lax
from jax.experimental import pallas as pl
from jax.experimental.pallas import tpu as pltpu
from jax.sharding import PartitionSpec as P

H = 8
TILE = 128
epsilon = 1e-05
masked_score = -1e30
BOTH = ("dp", "expert")
f32 = jnp.float32
bf16 = jnp.bfloat16

VMEM = pl.BlockSpec(memory_space=pltpu.VMEM)
SMEM = pl.BlockSpec(memory_space=pltpu.SMEM)


def shape_of(dims, kind):
    return jax.ShapeDtypeStruct(dims, kind)


def run(kernel, args, in_specs, outs, scratch=(), flops=0, name=None, limit=56):
    moved = sum(math.prod(a.shape) * a.dtype.itemsize for a in list(args) + list(outs))
    results = pl.pallas_call(
        kernel,
        out_shape=outs,
        in_specs=in_specs,
        out_specs=[VMEM] * len(outs),
        scratch_shapes=list(scratch),
        compiler_params=pltpu.CompilerParams(vmem_limit_bytes=limit * 2**20),
        cost_estimate=pl.CostEstimate(flops=flops, bytes_accessed=moved, transcendentals=0),
        name=name,
    )(*args)
    return list(results)


def dot(left, right):
    return lax.dot_general(left, right, (((1,), (0,)), ((), ())), preferred_element_type=f32)


def dot_t(left, right):
    return lax.dot_general(left, right, (((1,), (1,)), ((), ())), preferred_element_type=f32)


def t_dot(left, right):
    return lax.dot_general(left, right, (((0,), (0,)), ((), ())), preferred_element_type=f32)


def iota(dims, axis):
    return lax.broadcasted_iota(jnp.int32, dims, axis)


def normalize(values):
    center = values - jnp.mean(values, axis=-1, keepdims=True)
    spread = jnp.mean(center * center, axis=-1, keepdims=True)
    inverse = lax.rsqrt(spread + epsilon)
    return center * inverse, inverse


def normalize_back(standard, inverse, gain, upstream):
    scaled = upstream * gain
    first = jnp.mean(scaled, axis=-1, keepdims=True)
    second = jnp.mean(scaled * standard, axis=-1, keepdims=True)
    return inverse * (scaled - first - standard * second)


def column_sum(values):
    return jnp.sum(values, axis=0, keepdims=True)


def sigmoid(values):
    return 1.0 / (1.0 + jnp.exp(-values))


def loop(count, body):
    def step(index, carry):
        body(index)
        return carry

    lax.fori_loop(0, count, step, 0)


def rows_at(index, size):
    return pl.ds(pl.multiple_of(index * size, size), size)


def slots_kernel(experts, capacity, rows_ref, cols_ref, slot_row_ref, slot_one_ref, slot_two_ref):
    length = rows_ref.shape[1]
    block = 256
    slot_row_ref[...] = jnp.zeros_like(slot_row_ref)
    for half, out_ref in enumerate((slot_one_ref, slot_two_ref)):
        chosen = rows_ref[half : half + 1, :]
        onehot = jnp.where(iota((8, length), 0) == chosen, 1.0, 0.0)
        onehot_low = onehot.astype(bf16)
        for index in range(length // block):
            earlier = iota((length, block), 0) < iota((length, block), 1) + index * block
            counts = dot(onehot_low, jnp.where(earlier, 1.0, 0.0).astype(bf16))
            span = slice(index * block, (index + 1) * block)
            rank = column_sum(onehot[:, span] * counts).astype(jnp.int32)
            slot_row_ref[half : half + 1, span] = chosen[:, span] * capacity + rank
        picks = cols_ref[:, half : half + 1]
        wide = jnp.where(iota((length, TILE), 1) == picks, 1.0, 0.0)
        wide_low = wide.astype(bf16)
        for index in range(length // block):
            earlier = iota((block, length), 1) < iota((block, length), 0) + index * block
            counts = dot(jnp.where(earlier, 1.0, 0.0).astype(bf16), wide_low)
            span = slice(index * block, (index + 1) * block)
            rank = jnp.sum(wide[span] * counts, axis=1, keepdims=True).astype(jnp.int32)
            out_ref[span, :] = picks[span] * capacity + rank


def find_slots(routes_one, routes_two, experts, capacity):
    length = routes_one.shape[0]
    rows = jnp.concatenate([routes_one.reshape(1, length), routes_two.reshape(1, length)], axis=0)
    cols = jnp.concatenate([routes_one, routes_two], axis=1)
    return run(
        functools.partial(slots_kernel, experts, capacity),
        (rows, cols),
        [VMEM, VMEM],
        [
            shape_of((8, length), jnp.int32),
            shape_of((length, 1), jnp.int32),
            shape_of((length, 1), jnp.int32),
        ],
        flops=8 * length * length * 128,
        name="slots",
    )


PARTS = 4


def dispatch(low_ref, slot_row, out_refs):
    block = out_refs[0].shape[0]
    length = low_ref.shape[0]
    for index, out_ref in enumerate(out_refs):
        ids = iota((block, length), 0) + index * block
        onehot = jnp.where(ids == slot_row, 1.0, 0.0).astype(bf16)
        out_ref[...] = dot(onehot, low_ref[...]).astype(bf16)


def join_blocks(block_refs, whole_ref):
    block = block_refs[0].shape[0]
    for index, block_ref in enumerate(block_refs):
        whole_ref[index * block : (index + 1) * block, :] = block_ref[...]


def collect(slot_col, table_ref):
    rows = slot_col.shape[0]
    slots = table_ref.shape[0]
    onehot = jnp.where(iota((rows, slots), 1) == slot_col, 1.0, 0.0).astype(bf16)
    return dot(onehot, table_ref[...])


def route_block(low, embed, router_ref, picks, experts):
    width = low.shape[1]
    logits = dot(low, router_ref[:width, :]) + dot(embed, router_ref[width:, :])
    lanes = iota(logits.shape, 1)
    inside = lanes < experts
    logits = jnp.where(inside, logits, masked_score)
    raised = jnp.where(inside, jnp.exp(logits - jnp.max(logits, axis=1, keepdims=True)), 0.0)
    probs = raised / jnp.sum(raised, axis=1, keepdims=True)
    gate = jnp.sum(jnp.where(lanes == picks, probs, 0.0), axis=1, keepdims=True)
    return probs, gate


BLOCK = 256


def front_kernel(
    experts, hidden_ref, embed_ref, gain_ref, router_ref, picks_ref, slot_row_ref, *refs,
):
    out_refs, (probs_ref, gate_ref, low_ref) = refs[:PARTS], refs[PARTS:]
    length = hidden_ref.shape[0]

    def step(index):
        at = rows_at(index, BLOCK)
        standard, unused = normalize(hidden_ref[at, :].astype(f32))
        low = (standard * gain_ref[0:1, :]).astype(bf16)
        low_ref[at, :] = low
        probs, gate = route_block(low, embed_ref[at, :], router_ref, picks_ref[at, :], experts)
        probs_ref[at, :] = probs
        gate_ref[at, :] = gate

    loop(length // BLOCK, step)
    dispatch(low_ref, slot_row_ref[0:1, :], out_refs)


def expert_forward_kernel(count, in_ref, out_ref, *refs):
    for x_ref, y_ref in zip(refs[:count], refs[count:]):
        inner = dot(x_ref[...], in_ref[...])
        hidden = (inner * sigmoid(inner)).astype(bf16)
        y_ref[...] = dot(hidden, out_ref[...]).astype(bf16)


def expert_forward(received, weight_in, weight_out):
    block, width = received[0].shape
    count = len(received)
    return run(
        functools.partial(expert_forward_kernel, count),
        (weight_in, weight_out) + tuple(received),
        [VMEM] * (2 + count),
        [shape_of((block, width), bf16)] * count,
        flops=4 * count * block * width * weight_in.shape[1],
        name="experts",
        limit=32,
    )


def expert_backward_kernel(count, in_ref, out_ref, *refs):
    x_refs, dy_refs, dx_refs = refs[:count], refs[count : 2 * count], refs[2 * count : 3 * count]
    hidden_refs, dinner_refs = refs[3 * count : 4 * count], refs[4 * count :]
    for x_ref, dy_ref, dx_ref, hidden_ref, dinner_ref in zip(
        x_refs, dy_refs, dx_refs, hidden_refs, dinner_refs
    ):
        inner = dot(x_ref[...], in_ref[...])
        gates = sigmoid(inner)
        hidden = inner * gates
        hidden_ref[...] = hidden.astype(bf16)
        d_hidden = dot_t(dy_ref[...], out_ref[...])
        d_inner = (d_hidden * (gates + hidden * (1.0 - gates))).astype(bf16)
        dinner_ref[...] = d_inner
        dx_ref[...] = dot_t(d_inner, in_ref[...]).astype(bf16)


def expert_backward(received, d_result, weight_in, weight_out):
    block, width = received[0].shape
    inner = weight_in.shape[1]
    count = len(received)
    outs = run(
        functools.partial(expert_backward_kernel, count),
        (weight_in, weight_out) + tuple(received) + tuple(d_result),
        [VMEM] * (2 + 2 * count),
        [shape_of((block, width), bf16)] * count + [shape_of((block, inner), bf16)] * (2 * count),
        flops=6 * count * block * width * inner,
        name="experts_back",
        limit=40,
    )
    return outs[:count], outs[count : 2 * count], outs[2 * count :]


def tile_window(starts_ref, first, length):
    count = starts_ref.shape[1]
    low = jnp.int32(0)
    high = jnp.int32(length)
    for k in range(1, count):
        low = jnp.where(starts_ref[0, k] <= first, starts_ref[0, k], low)
    for k in range(count - 1, 0, -1):
        high = jnp.where(starts_ref[0, k] > first + (TILE - 1), starts_ref[0, k], high)
    return low // TILE, (high + (TILE - 1)) // TILE


def numbers_at(starts_ref, positions):
    total = jnp.zeros(positions.shape, jnp.int32)
    for k in range(1, starts_ref.shape[1]):
        total = total + jnp.where(positions >= starts_ref[0, k], 1, 0)
    return total


def same_tile(starts_ref, first_query, first_key):
    rows = numbers_at(starts_ref, iota((TILE, TILE), 0) + first_query)
    cols = numbers_at(starts_ref, iota((TILE, TILE), 1) + first_key)
    return rows == cols


def chunk_rows(query_tile, key_tile, extra, length, mirrored=False):
    tiles = length // TILE
    index = tiles - 1 - query_tile + key_tile + extra - tiles // 2
    index = jnp.clip(index, 0, tiles - 1)
    if mirrored:
        index = tiles - 1 - index
    return pl.ds(pl.multiple_of(index * TILE, TILE), TILE)


def halves(values):
    left = iota(values.shape, 1) < TILE // 2
    zero = jnp.zeros_like(values)
    return jnp.concatenate(
        [jnp.where(left, values, zero), jnp.where(left, zero, values)], axis=0
    )


def skew(values):
    return jnp.concatenate(
        [
            pltpu.roll(values[:TILE], 1, 1, stride=1, stride_axis=0),
            pltpu.roll(values[TILE:], 1, 1, stride=1, stride_axis=0),
        ],
        axis=0,
    )


def mirror(values):
    flip = iota((TILE, TILE), 0) + iota((TILE, TILE), 1) == TILE - 1
    return dot(values, jnp.where(flip, 1.0, 0.0).astype(bf16))


def twice(values):
    return jnp.concatenate([values, values], axis=0)


PAIRS = H // 2


def attend_forward(
    starts_ref, qu_ref, qv_ref, k_ref, v_ref, t_ref, context_ref, logs_ref,
    qum, qvm, scores, rolled, peaks, sums, mixed,
):
    length = qu_ref.shape[0]
    tiles = length // TILE

    def query_step(tile):
        first = tile * TILE
        at = rows_at(tile, TILE)
        low, high = tile_window(starts_ref, first, length)
        chunk = chunk_rows(tile, low, 0, length)
        for p in range(PAIRS):
            lanes = slice(p * TILE, (p + 1) * TILE)
            qum[p] = halves(qu_ref[at, lanes])
            qvm[p] = halves(qv_ref[at, lanes])
            rolled[p] = skew(dot_t(qvm[p], t_ref[chunk, lanes]))
            peaks[p] = jnp.full((2 * TILE, TILE), masked_score, f32)
            sums[p] = jnp.zeros((2 * TILE, TILE), f32)
            mixed[p] = jnp.zeros((2 * TILE, TILE), f32)
        lower = twice(iota((TILE, TILE), 1) <= iota((TILE, TILE), 0))

        def score_step(key, carry):
            keys = rows_at(key, TILE)
            same = twice(same_tile(starts_ref, first, key * TILE))
            chunk = chunk_rows(tile, key, 1, length)
            for p in range(PAIRS):
                lanes = slice(p * TILE, (p + 1) * TILE)
                content = dot_t(qum[p], k_ref[keys, lanes])
                fresh = skew(dot_t(qvm[p], t_ref[chunk, lanes]))
                value = content + jnp.where(lower, rolled[p], fresh)
                value = jnp.where(same, value, masked_score)
                rolled[p] = fresh
                scores[key, p] = value
                peaks[p] = jnp.maximum(peaks[p], value)
            return carry

        lax.fori_loop(low, high, score_step, 0)
        for p in range(PAIRS):
            peaks[p] = jnp.broadcast_to(
                jnp.max(peaks[p], axis=1, keepdims=True), (2 * TILE, TILE)
            )

        def value_step(key, carry):
            keys = rows_at(key, TILE)
            for p in range(PAIRS):
                lanes = slice(p * TILE, (p + 1) * TILE)
                raised = jnp.exp(scores[key, p] - peaks[p])
                sums[p] = sums[p] + raised
                mixed[p] = mixed[p] + dot(raised.astype(bf16), v_ref[keys, lanes])
            return carry

        lax.fori_loop(low, high, value_step, 0)
        left = iota((TILE, TILE), 1) < TILE // 2
        logs = jnp.zeros((TILE, TILE), f32)
        lane = iota((TILE, TILE), 1)
        for p in range(PAIRS):
            lanes = slice(p * TILE, (p + 1) * TILE)
            total = jnp.sum(sums[p], axis=1, keepdims=True)
            result = mixed[p] * (1.0 / total)
            context_ref[at, lanes] = jnp.where(left, result[:TILE], result[TILE:]).astype(bf16)
            logsum = peaks[p] + jnp.log(total)
            logs = jnp.where(lane == 2 * p, logsum[:TILE], logs)
            logs = jnp.where(lane == 2 * p + 1, logsum[TILE:], logs)
        logs_ref[at, :] = logs

    loop(tiles, query_step)


def attend_scratch(length):
    pair = (PAIRS, 2 * TILE, TILE)
    return [
        pltpu.VMEM(pair, bf16),
        pltpu.VMEM(pair, bf16),
        pltpu.VMEM((length // TILE,) + pair, f32),
        pltpu.VMEM(pair, f32),
        pltpu.VMEM(pair, f32),
        pltpu.VMEM(pair, f32),
        pltpu.VMEM(pair, f32),
    ]


def attend_backward(
    starts_ref, qu_ref, qv_ref, k_ref, v_ref, t_ref, mirrored_ref, context_ref, logs_ref, dcontext_ref,
    dm_ref, dk_ref, dv_ref, dt_ref, dbias_ref,
    qum, qvm, dcm, logs, deltas, rolled, unrolled, dqu, dqv,
):
    length, width = qu_ref.shape
    tiles = length // TILE
    scale = 1.0 / math.sqrt(width // H)
    dk_ref[...] = jnp.zeros_like(dk_ref)
    dv_ref[...] = jnp.zeros_like(dv_ref)
    dt_ref[...] = jnp.zeros_like(dt_ref)
    dbias_ref[...] = jnp.zeros_like(dbias_ref)

    def query_step(tile):
        first = tile * TILE
        at = rows_at(tile, TILE)
        low, high = tile_window(starts_ref, first, length)
        chunk = chunk_rows(tile, low, 0, length)
        lanes_all = iota((TILE, TILE), 1)
        logs_tile = logs_ref[at, :]
        for p in range(PAIRS):
            lanes = slice(p * TILE, (p + 1) * TILE)
            qum[p] = halves(qu_ref[at, lanes])
            qvm[p] = halves(qv_ref[at, lanes])
            upstream = halves(dcontext_ref[at, lanes])
            dcm[p] = upstream
            delta = jnp.sum(
                upstream.astype(f32) * twice(context_ref[at, lanes].astype(f32)),
                axis=1,
                keepdims=True,
            )
            deltas[p] = jnp.broadcast_to(delta, (2 * TILE, TILE))
            logs[p, :TILE] = jnp.broadcast_to(logs_tile[:, 2 * p : 2 * p + 1], (TILE, TILE))
            logs[p, TILE:] = jnp.broadcast_to(logs_tile[:, 2 * p + 1 : 2 * p + 2], (TILE, TILE))
            rolled[p] = skew(dot_t(qvm[p], t_ref[chunk, lanes]))
            unrolled[p] = jnp.zeros((2 * TILE, TILE), f32)
            dqu[p] = jnp.zeros((2 * TILE, TILE), f32)
            dqv[p] = jnp.zeros((2 * TILE, TILE), f32)
        lower = twice(iota((TILE, TILE), 1) <= iota((TILE, TILE), 0))

        def step(key, carry):
            keys = rows_at(key, TILE)
            same = twice(same_tile(starts_ref, first, key * TILE))
            before = chunk_rows(tile, key, 0, length, True)
            after = chunk_rows(tile, key, 1, length)
            for p in range(PAIRS):
                lanes = slice(p * TILE, (p + 1) * TILE)
                content = dot_t(qum[p], k_ref[keys, lanes])
                fresh = skew(dot_t(qvm[p], t_ref[after, lanes]))
                value = content + jnp.where(lower, rolled[p], fresh)
                rolled[p] = fresh
                probs = jnp.where(same, jnp.exp(value - logs[p]), 0.0)
                dprobs = dot_t(dcm[p], v_ref[keys, lanes])
                dscores = probs * (dprobs - deltas[p])
                dlow = dscores.astype(bf16)
                dv_ref[keys, lanes] += t_dot(probs.astype(bf16), dcm[p])
                dk_ref[keys, lanes] += t_dot(dlow, qum[p])
                dqu[p] += dot(dlow, k_ref[keys, lanes])
                turned = skew(mirror(dlow))
                moved = jnp.where(lower, turned, unrolled[p]).astype(bf16)
                unrolled[p] = turned
                dqv[p] += dot(moved, mirrored_ref[before, lanes])
                dt_ref[before, lanes] += t_dot(moved, qvm[p])
            return carry

        lax.fori_loop(low, high, step, 0)
        last = chunk_rows(tile, high, 0, length, True)
        left = iota((TILE, TILE), 1) < TILE // 2
        for p in range(PAIRS):
            lanes = slice(p * TILE, (p + 1) * TILE)
            moved = jnp.where(lower, 0.0, unrolled[p]).astype(bf16)
            dq = dqv[p] + dot(moved, mirrored_ref[last, lanes])
            dt_ref[last, lanes] += t_dot(moved, qvm[p])
            part_u = jnp.where(left, dqu[p, :TILE], dqu[p, TILE:]) * scale
            part_v = jnp.where(left, dq[:TILE], dq[TILE:]) * scale
            dbias_ref[0:1, lanes] += column_sum(part_u)
            dbias_ref[1:2, lanes] += column_sum(part_v)
            dm_ref[at, lanes] = (part_u + part_v).astype(bf16)

    loop(tiles, query_step)

    def finish(index):
        at = rows_at(index, BLOCK)
        dm_ref[at, width : 2 * width] = dk_ref[at, :].astype(bf16)
        dm_ref[at, 2 * width : 3 * width] = dv_ref[at, :].astype(bf16)

    loop(length // BLOCK, finish)


def attend_back_scratch():
    pair = (PAIRS, 2 * TILE, TILE)
    return [pltpu.VMEM(pair, bf16) for unused in range(3)] + [
        pltpu.VMEM(pair, f32) for unused in range(6)
    ]


def dense_parts(dense_ref):
    width = dense_ref.shape[0]
    cuts = (0, 3, 4, 5, 6, 8)
    return [
        dense_ref.at[:, pl.ds(start * width, (stop - start) * width)]
        for start, stop in zip(cuts[:-1], cuts[1:])
    ]


EDGE = 16


def middle_kernel(
    starts_ref, hidden_ref, slot_ref, gate_ref, gains_ref, dense_ref, bias_ref, taps_ref, sinus_ref,
    *refs,
):
    returned_refs, refs = refs[:PARTS], refs[PARTS:]
    h1_ref, h2_ref, qu_ref, qv_ref, k_ref, v_ref, t_ref, context_ref, logs_ref = refs[:9]
    conv_ref, sums_ref, padded, sums, returned_ref = refs[9:14]
    attend = refs[14:]
    join_blocks(returned_refs, returned_ref)
    length, width = h1_ref.shape
    scale = 1.0 / math.sqrt(width // H)
    in_ref, place_ref, mix_ref, unused, point_ref = dense_parts(dense_ref)

    def queries_step(index):
        at = rows_at(index, BLOCK)
        picked = collect(slot_ref[at, :], returned_ref)
        h1 = hidden_ref[at, :].astype(f32) + 0.5 * gate_ref[at, :] * picked
        h1_ref[at, :] = h1
        standard, unused = normalize(h1)
        low = (standard * gains_ref[1:2, :]).astype(bf16)
        queries = dot(low, in_ref[:, :width])
        qu_ref[at, :] = ((queries + bias_ref[0:1, :]).astype(bf16).astype(f32) * scale).astype(bf16)
        qv_ref[at, :] = ((queries + bias_ref[1:2, :]).astype(bf16).astype(f32) * scale).astype(bf16)
        k_ref[at, :] = dot(low, in_ref[:, width : 2 * width]).astype(bf16)
        v_ref[at, :] = dot(low, in_ref[:, 2 * width :]).astype(bf16)
        t_ref[at, :] = dot(sinus_ref[at, :], place_ref[...]).astype(bf16)

    loop(length // BLOCK, queries_step)
    attend_forward(
        starts_ref, qu_ref, qv_ref, k_ref, v_ref, t_ref, context_ref, logs_ref, *attend
    )
    padded[:EDGE, :] = jnp.zeros((EDGE, width), f32)
    padded[EDGE + length :, :] = jnp.zeros((EDGE, width), f32)

    def gates_step(index):
        at = rows_at(index, BLOCK)
        h2 = h1_ref[at, :] + dot(context_ref[at, :], mix_ref[...])
        h2_ref[at, :] = h2
        standard, unused = normalize(h2)
        low = (standard * gains_ref[2:3, :]).astype(bf16)
        value = dot(low, point_ref[:, :width])
        gates = dot(low, point_ref[:, width:])
        padded[pl.ds(pl.multiple_of(index * BLOCK + EDGE, EDGE), BLOCK), :] = value * sigmoid(gates)

    loop(length // BLOCK, gates_step)
    sums[...] = jnp.zeros_like(sums)
    taps = taps_ref.shape[0] - 1
    reach = taps // 2
    frames = starts_ref[0, starts_ref.shape[1] - 1]

    def conv_step(index):
        first = index * TILE
        place = iota((TILE, TILE), 0) + first
        here = numbers_at(starts_ref, place)
        valid = place < frames
        totals = [jnp.zeros((TILE, TILE), f32) for unused in range(width // TILE)]
        around = pl.ds(pl.multiple_of(first, TILE), TILE + 2 * EDGE)
        for tap in range(taps):
            same = numbers_at(starts_ref, place + (tap - reach)) == here
            for part in range(width // TILE):
                lanes = slice(part * TILE, (part + 1) * TILE)
                near = padded[around, lanes][EDGE + tap - reach : EDGE + tap - reach + TILE]
                totals[part] = totals[part] + jnp.where(same, near, 0.0) * taps_ref[tap : tap + 1, lanes]
        for part in range(width // TILE):
            lanes = slice(part * TILE, (part + 1) * TILE)
            conv_ref[rows_at(index, TILE), lanes] = totals[part]
            kept = jnp.where(valid, totals[part], 0.0)
            sums[0:1, lanes] += column_sum(kept)
            sums[1:2, lanes] += column_sum(kept * kept)

    loop(length // TILE, conv_step)
    copies = sums_ref.shape[0]
    sums_ref[:, :width] = jnp.broadcast_to(sums[0:1, :], (copies, width))
    sums_ref[:, width : 2 * width] = jnp.broadcast_to(sums[1:2, :], (copies, width))
    sums_ref[:, 2 * width :] = jnp.zeros((copies, width), f32) + frames.astype(f32)


def batch_totals(totals_ref, width):
    totals = column_sum(totals_ref[...])
    count = totals[:, 2 * width :]
    mean = totals[:, :width] / count
    variance = totals[:, width : 2 * width] / count - mean * mean
    return mean, lax.rsqrt(variance + epsilon), count


def batch_block(conv, mean, inverse, batch_ref):
    centred = conv - mean
    standard = centred * inverse
    batched = standard * batch_ref[0:1, :] + batch_ref[1:2, :]
    return centred, standard, batched


def second_kernel(
    experts, h2_ref, conv_ref, totals_ref, batch_ref, point_ref, embed_ref, gains_ref, router_ref,
    picks_ref, slot_row_ref, *refs,
):
    out_refs, refs = refs[:PARTS], refs[PARTS:]
    h3_ref, active_ref, probs_ref, gate_ref, stats_ref, low_ref = refs
    length, width = h2_ref.shape
    mean, inverse, count = batch_totals(totals_ref, width)
    stats_ref[0:1, :] = mean
    stats_ref[1:2, :] = inverse
    stats_ref[2:3, :] = count

    def step(index):
        at = rows_at(index, BLOCK)
        unused, unused, batched = batch_block(conv_ref[at, :], mean, inverse, batch_ref)
        active = (batched * sigmoid(batched)).astype(bf16)
        active_ref[at, :] = active
        h3 = h2_ref[at, :] + dot(active, point_ref[...])
        h3_ref[at, :] = h3
        standard, unused = normalize(h3)
        low = (standard * gains_ref[3:4, :]).astype(bf16)
        low_ref[at, :] = low
        probs, gate = route_block(low, embed_ref[at, :], router_ref, picks_ref[at, :], experts)
        probs_ref[at, :] = probs
        gate_ref[at, :] = gate

    loop(length // BLOCK, step)
    dispatch(low_ref, slot_row_ref[1:2, :], out_refs)


def gate_back(upstream, picked, gate, probs, picks):
    d_gate = 0.5 * jnp.sum(upstream * picked, axis=1, keepdims=True)
    onehot = jnp.where(iota(probs.shape, 1) == picks, 1.0, 0.0)
    return (d_gate * gate) * (onehot - probs)


def turn_kernel(
    h3_ref, slot_ref, gate_ref, probs_ref, picks_ref, slot_row_ref, gains_ref, cotangent_ref, *refs,
):
    returned_refs, out_refs, refs = refs[:PARTS], refs[PARTS : 2 * PARTS], refs[2 * PARTS :]
    output_ref, d4_ref, dlogits_ref, dgain_ref, low_ref, returned_ref = refs
    length = h3_ref.shape[0]
    join_blocks(returned_refs, returned_ref)
    dgain_ref[...] = jnp.zeros_like(dgain_ref)

    def step(index):
        at = rows_at(index, BLOCK)
        picked = collect(slot_ref[at, :], returned_ref)
        gate = gate_ref[at, :]
        h4 = h3_ref[at, :] + 0.5 * gate * picked
        standard, inverse = normalize(h4)
        gain = gains_ref[4:5, :]
        output_ref[at, :] = (standard * gain).astype(bf16)
        upstream = cotangent_ref[at, :].astype(f32)
        dgain_ref[0:1, :] += column_sum(upstream * standard)
        d4 = normalize_back(standard, inverse, gain, upstream)
        d4_ref[at, :] = d4
        dlogits_ref[at, :] = gate_back(d4, picked, gate, probs_ref[at, :], picks_ref[at, :])
        low_ref[at, :] = (0.5 * gate * d4).astype(bf16)

    loop(length // BLOCK, step)
    dispatch(low_ref, slot_row_ref[1:2, :], out_refs)


def router_back(dlogits, low, embed, router_ref, drouter_ref):
    width = low.shape[1]
    high = dlogits.astype(bf16)
    rest = (dlogits - high.astype(f32)).astype(bf16)
    d_low = dot_t(high, router_ref[:width, :]) + dot_t(rest, router_ref[:width, :])
    d_embed = dot_t(high, router_ref[width:, :]) + dot_t(rest, router_ref[width:, :])
    turned = jnp.transpose(dlogits)[:8, :]
    turned_high = turned.astype(bf16)
    turned_rest = (turned - turned_high.astype(f32)).astype(bf16)
    drouter_ref[:, :width] += dot(turned_high, low) + dot(turned_rest, low)
    drouter_ref[:, width:] += dot(turned_high, embed) + dot(turned_rest, embed)
    return d_low, d_embed


def second_back_kernel(
    slot_ref, dlogits_ref, h3_ref, d4_ref, embed_ref, router_ref, gains_ref, conv_ref, stats_ref,
    batch_ref, point_ref, *refs,
):
    dsent_refs, refs = refs[:PARTS], refs[PARTS:]
    d3_ref, dlow_ref, dz_ref, dembed_ref, drouter_ref, small_ref, sums_ref, sums, dsent_ref = refs
    length, width = h3_ref.shape
    drouter_ref[...] = jnp.zeros_like(drouter_ref)
    small_ref[...] = jnp.zeros_like(small_ref)
    sums[...] = jnp.zeros_like(sums)
    join_blocks(dsent_refs, dsent_ref)
    mean, batch_inverse = stats_ref[0:1, :], stats_ref[1:2, :]

    def step(index):
        at = rows_at(index, BLOCK)
        standard, inverse = normalize(h3_ref[at, :])
        gain = gains_ref[3:4, :]
        low = (standard * gain).astype(bf16)
        d_low, d_embed = router_back(
            dlogits_ref[at, :], low, embed_ref[at, :], router_ref, drouter_ref
        )
        dembed_ref[at, :] = d_embed
        d_norm = collect(slot_ref[at, :], dsent_ref) + d_low
        small_ref[0:1, :] += column_sum(d_norm * standard)
        d3 = d4_ref[at, :] + normalize_back(standard, inverse, gain, d_norm)
        d3_ref[at, :] = d3
        d3_low = d3.astype(bf16)
        dlow_ref[at, :] = d3_low
        centred, normed, batched = batch_block(conv_ref[at, :], mean, batch_inverse, batch_ref)
        gates = sigmoid(batched)
        d_batched = dot_t(d3_low, point_ref[...]) * (gates + batched * gates * (1.0 - gates))
        small_ref[1:2, :] += column_sum(d_batched * normed)
        small_ref[2:3, :] += column_sum(d_batched)
        d_z = d_batched * batch_ref[0:1, :]
        dz_ref[at, :] = d_z
        sums[0:1, :] += column_sum(d_z)
        sums[1:2, :] += column_sum(d_z * centred)

    loop(length // BLOCK, step)
    copies = sums_ref.shape[0]
    sums_ref[:, :width] = jnp.broadcast_to(sums[0:1, :], (copies, width))
    sums_ref[:, width:] = jnp.broadcast_to(sums[1:2, :], (copies, width))


def middle_back_kernel(
    starts_ref, conv_ref, dz_ref, stats_ref, dsums_ref, batch_ref, d3_ref, h1_ref, h2_ref, gains_ref,
    dense_ref, taps_ref, sinus_ref, qu_ref, qv_ref, k_ref, v_ref, t_ref, context_ref, logs_ref,
    slot_ref, gate_ref, probs_ref, picks_ref, slot_row_ref, *refs,
):
    returned_refs, out_refs, refs = refs[:PARTS], refs[PARTS : 2 * PARTS], refs[2 * PARTS :]
    d1_ref, dlogits_ref, n2_ref, n3_ref, dg_ref, d2low_ref, dm_ref, dtable_ref = refs[:8]
    small_ref, dtaps_ref, padded, linear, dcontext_ref, low_ref, mirrored_ref, returned_ref = refs[8:16]
    attend = refs[16:]
    length, width = h1_ref.shape
    d2_ref = d1_ref
    dt_ref = padded.at[pl.ds(0, length)]
    dk_ref = linear.at[:, pl.ds(0, width)]
    dv_ref = linear.at[:, pl.ds(width, width)]
    in_ref, place_ref, mix_ref, unused, point_ref = dense_parts(dense_ref)
    taps = taps_ref.shape[0] - 1
    reach = taps // 2
    frames = starts_ref[0, starts_ref.shape[1] - 1]
    small_ref[...] = jnp.zeros_like(small_ref)
    dtaps_ref[...] = jnp.zeros_like(dtaps_ref)
    join_blocks(returned_refs, returned_ref)
    mean, batch_inverse, count = stats_ref[0:1, :], stats_ref[1:2, :], stats_ref[2:3, :]
    dsums = column_sum(dsums_ref[...])
    d_variance = -0.5 * batch_inverse * batch_inverse * batch_inverse * dsums[:, width:]
    padded[:EDGE, :] = jnp.zeros((EDGE, width), f32)
    padded[EDGE + length :, :] = jnp.zeros((EDGE, width), f32)

    def conv_step(index):
        at = rows_at(index, BLOCK)
        centred = conv_ref[at, :] - mean
        inside = (iota((BLOCK, 1), 0) + index * BLOCK) < frames
        shared = (2.0 * d_variance * centred - batch_inverse * dsums[:, :width]) / count
        d_conv = batch_inverse * dz_ref[at, :] + jnp.where(inside, shared, 0.0)
        padded[pl.ds(pl.multiple_of(index * BLOCK + EDGE, EDGE), BLOCK), :] = d_conv
        standard, unused = normalize(h2_ref[at, :])
        low = (standard * gains_ref[2:3, :]).astype(bf16)
        n3_ref[at, :] = low
        value = dot(low, point_ref[:, :width])
        linear[at, :width] = value
        linear[at, width:] = sigmoid(dot(low, point_ref[:, width:]))

    loop(length // BLOCK, conv_step)

    def turn_step(index):
        first = index * TILE
        at = rows_at(index, TILE)
        place = iota((TILE, TILE), 0) + first
        here = numbers_at(starts_ref, place)
        parts = width // TILE
        totals = [jnp.zeros((TILE, TILE), f32) for unused in range(parts)]
        values = [linear[at, part * TILE : (part + 1) * TILE] for part in range(parts)]
        gates = [linear[at, width + part * TILE : width + (part + 1) * TILE] for part in range(parts)]
        around = pl.ds(pl.multiple_of(first, TILE), TILE + 2 * EDGE)
        for tap in range(taps):
            same = numbers_at(starts_ref, place - (tap - reach)) == here
            for part in range(parts):
                lanes = slice(part * TILE, (part + 1) * TILE)
                near = padded[around, lanes][EDGE - tap + reach : EDGE - tap + reach + TILE]
                near = jnp.where(same, near, 0.0)
                totals[part] = totals[part] + near * taps_ref[tap : tap + 1, lanes]
                dtaps_ref[tap : tap + 1, lanes] += column_sum(near * (values[part] * gates[part]))
        for part in range(parts):
            lanes = slice(part * TILE, (part + 1) * TILE)
            other = slice(width + part * TILE, width + (part + 1) * TILE)
            gate = gates[part]
            dg_ref[at, lanes] = (totals[part] * gate).astype(bf16)
            dg_ref[at, other] = (totals[part] * values[part] * gate * (1.0 - gate)).astype(bf16)

    loop(length // TILE, turn_step)

    def gates_step(index):
        at = rows_at(index, BLOCK)
        d_norm = dot_t(dg_ref[at, :], point_ref[...])
        standard, inverse = normalize(h2_ref[at, :])
        small_ref[0:1, :] += column_sum(d_norm * standard)
        d2 = d3_ref[at, :] + normalize_back(standard, inverse, gains_ref[2:3, :], d_norm)
        d2_ref[at, :] = d2
        low = d2.astype(bf16)
        d2low_ref[at, :] = low
        dcontext_ref[at, :] = dot_t(low, mix_ref[...]).astype(bf16)
        mirrored_ref[at, :] = dot(sinus_ref[at, :], place_ref[...]).astype(bf16)

    loop(length // BLOCK, gates_step)
    attend_backward(
        starts_ref, qu_ref, qv_ref, k_ref, v_ref, t_ref, mirrored_ref, context_ref, logs_ref, dcontext_ref,
        dm_ref, dk_ref, dv_ref, dt_ref, small_ref.at[pl.ds(8, 8)], *attend
    )

    def queries_step(index):
        at = rows_at(index, BLOCK)
        dtable_ref[at, :] = dt_ref[at, :].astype(bf16)
        d_norm = dot_t(dm_ref[at, :], in_ref[...])
        standard, inverse = normalize(h1_ref[at, :])
        gain = gains_ref[1:2, :]
        n2_ref[at, :] = (standard * gain).astype(bf16)
        small_ref[1:2, :] += column_sum(d_norm * standard)
        d1 = d2_ref[at, :] + normalize_back(standard, inverse, gain, d_norm)
        d1_ref[at, :] = d1
        picked = collect(slot_ref[at, :], returned_ref)
        gate = gate_ref[at, :]
        dlogits_ref[at, :] = gate_back(d1, picked, gate, probs_ref[at, :], picks_ref[at, :])
        low_ref[at, :] = (0.5 * gate * d1).astype(bf16)

    loop(length // BLOCK, queries_step)
    dispatch(low_ref, slot_row_ref[0:1, :], out_refs)


def last_kernel(
    slot_ref, dlogits_ref, hidden_ref, d1_ref, embed_ref, router_ref, gains_ref, dembed_two_ref, *refs,
):
    dsent_refs, refs = refs[:PARTS], refs[PARTS:]
    d0_ref, dembed_ref, drouter_ref, small_ref, dsent_ref = refs
    length = hidden_ref.shape[0]
    join_blocks(dsent_refs, dsent_ref)
    drouter_ref[...] = jnp.zeros_like(drouter_ref)
    small_ref[...] = jnp.zeros_like(small_ref)

    def step(index):
        at = rows_at(index, BLOCK)
        standard, inverse = normalize(hidden_ref[at, :].astype(f32))
        gain = gains_ref[0:1, :]
        low = (standard * gain).astype(bf16)
        d_low, d_embed = router_back(
            dlogits_ref[at, :], low, embed_ref[at, :], router_ref, drouter_ref
        )
        dembed_ref[at, :] = d_embed + dembed_two_ref[at, :]
        d_norm = collect(slot_ref[at, :], dsent_ref) + d_low
        small_ref[0:1, :] += column_sum(d_norm * standard)
        d0_ref[at, :] = d1_ref[at, :] + normalize_back(standard, inverse, gain, d_norm)

    loop(length // BLOCK, step)


def backward_parts(received, d_result, pair):
    parts = [
        expert_backward(received[start:stop], d_result[start:stop], *pair)
        for start, stop in ((0, 2), (2, 3), (3, PARTS))
    ]
    return [sum((part[k] for part in parts), []) for k in range(3)]


def gather_small(values):
    return lax.all_to_all(values, BOTH, split_axis=0, concat_axis=0, tiled=True)


def across(values, axis, size, offset):
    return lax.ppermute(values, axis, [(i, i ^ offset) for i in range(size)])


def exchange(blocks, experts):
    per = experts // PARTS
    moved = []
    for index, block in enumerate(blocks):
        rows = block.shape[0] // per
        pieces = []
        for k in range(index * per, (index + 1) * per):
            piece = block[(k - index * per) * rows : (k - index * per + 1) * rows]
            pieces.append(across(piece, "expert", experts, k) if k else piece)
        moved.append(pieces[0] if per == 1 else jnp.concatenate(pieces, axis=0))
    return moved


def ring_place(index, size):
    return jnp.where(index % 2 == 0, index // 2, size - 1 - index // 2)


def ring_member(place, size):
    place = (place + 2 * size) % size
    return jnp.where(place < size // 2, 2 * place, 2 * (size - 1 - place) + 1)


def ring_pairs(size, forward):
    order = list(range(0, size, 2)) + list(range(size - 1, 0, -2))
    step = 1 if forward else -1
    return [(order[k], order[(k + step) % size]) for k in range(size)]


def ring_gather(shards, size):
    found = []
    for number, shard in enumerate(shards):
        ahead = size // 2 if number % 2 == 0 else (size - 1) // 2
        pieces = [None] * size
        pieces[0] = shard
        found.append((pieces, ahead))
    for step in range(1, size // 2 + 1):
        for pieces, ahead in found:
            if step <= ahead:
                pieces[step] = lax.ppermute(pieces[step - 1], "dp", ring_pairs(size, False))
            if step <= size - 1 - ahead:
                pieces[-step] = lax.ppermute(pieces[-step + 1 or 0], "dp", ring_pairs(size, True))
    return [pieces for pieces, unused in found]


def assemble_kernel(count, order_ref, *refs):
    size = (len(refs) - 1 - count) // count
    sems = refs[-1]
    copies = []
    for number in range(count):
        target = refs[count * size + number]
        for offset in range(size):
            piece = refs[number * size + offset]
            rows = piece.shape[0]
            start = pl.multiple_of(order_ref[offset] * rows, 16)
            copies.append(
                pltpu.make_async_copy(
                    piece, target.at[pl.ds(start, rows)], sems.at[number * size + offset]
                )
            )
    for copy in copies:
        copy.start()
    for copy in copies:
        copy.wait()


def assemble(shards, size):
    place = ring_place(lax.axis_index("dp"), size)
    order = ring_member(place + jnp.arange(size, dtype=jnp.int32), size).astype(jnp.int32)
    groups = ring_gather(shards, size)
    count = len(groups)
    anywhere = pl.BlockSpec(memory_space=pl.ANY)
    return pl.pallas_call(
        functools.partial(assemble_kernel, count),
        out_shape=[
            shape_of((size * shard.shape[0],) + shard.shape[1:], shard.dtype) for shard in shards
        ],
        in_specs=[SMEM] + [anywhere] * (count * size),
        out_specs=[VMEM] * count,
        scratch_shapes=[pltpu.SemaphoreType.DMA((count * size,))],
        name="assemble",
    )(order, *[piece for pieces in groups for piece in pieces])


def keep_half(values, axis, bit, size, offset, mesh_axis):
    mine = lax.dynamic_index_in_dim(values, bit, axis, keepdims=False)
    theirs = lax.dynamic_index_in_dim(values, 1 - bit, axis, keepdims=False)
    arrived = across(theirs, mesh_axis, size, offset)
    return (mine.astype(f32) + arrived.astype(f32)).astype(bf16)


def keep_one(values, place, size, stride, mesh_axis):
    total = lax.dynamic_index_in_dim(values, place, 0, keepdims=False).astype(f32)
    for k in range(1, values.shape[0]):
        theirs = lax.dynamic_index_in_dim(values, place ^ k, 0, keepdims=False)
        total = total + across(theirs, mesh_axis, size, k * stride).astype(f32)
    return total


def scatter_groups(values, size):
    me = lax.axis_index("dp")
    rows, width = values.shape
    values = values.reshape(size // 2, 2, rows // size, width)
    values = keep_half(values, 1, me % 2, size, 1, "dp")
    return keep_one(values, me // 2, size, 2, "dp")


def scatter_dense(grad, groups, experts):
    rows, width = grad.shape
    me, group = lax.axis_index("expert"), lax.axis_index("dp")
    rows = rows // (groups * experts)
    values = grad.reshape(groups // 2, 2, experts // 2, 2, rows, width)
    values = keep_half(values, 3, me % 2, experts, 1, "expert")
    values = keep_half(values, 1, group % 2, groups, 1, "dp")
    values = keep_one(values, group // 2, groups, 2, "dp").astype(bf16)
    return keep_one(values, me // 2, experts, 2, "expert")


def rows_product(left, right):
    return lax.dot_general(left, right, (((0,), (0,)), ((), ())), preferred_element_type=f32)


def expert_grads(received, d_result, hidden, d_inner):
    received, d_result, hidden, d_inner = (
        jnp.concatenate(blocks, axis=0) for blocks in (received, d_result, hidden, d_inner)
    )
    return rows_product(received, d_inner).astype(bf16), rows_product(hidden, d_result).astype(bf16)


def scatter_offloaded(grad_in, grad_out):
    return (
        lax.psum_scatter(grad_in, "dp", scatter_dimension=0, tiled=True).astype(f32)[None],
        lax.psum_scatter(grad_out, "dp", scatter_dimension=0, tiled=True).astype(f32)[None],
    )


def scatter_direct(grad_in, grad_out, size):
    half_in, half_out = grad_in.shape[1] // 2, grad_out.shape[1] // 2
    sums = [
        scatter_groups(part, size)
        for part in (
            grad_out[:, :half_out], grad_out[:, half_out:], grad_in[:, :half_in], grad_in[:, half_in:],
        )
    ]
    return (
        jnp.concatenate(sums[2:], axis=1)[None],
        jnp.concatenate(sums[:2], axis=1)[None],
    )


def sinus_rows(length, width, upward):
    distance = (length // 2 - 1 - np.arange(length)).astype(np.float32)
    distance = distance[::-1] if upward else distance
    rates = np.exp(
        np.arange(width // 2).astype(np.float32) * np.float32(-2.0 * math.log(10000.0) / width)
    ).astype(np.float32)
    angles = (distance[:, None] * rates[None, :]).astype(np.float64)
    table = np.concatenate([np.sin(angles), np.cos(angles)], axis=1)
    return jnp.asarray(table.astype(np.float32)).astype(bf16)


def body(
    groups,
    inputs,
    embedding,
    cotangent,
    first_routes,
    second_routes,
    segment_starts,
    norm_gains,
    first_router,
    second_router,
    first_in,
    first_out,
    second_in,
    second_out,
    attention_in,
    position_weight,
    position_bias,
    attention_out,
    pointwise_in,
    depthwise_kernel,
    batch_gain,
    batch_bias,
    pointwise_out,
):
    length, width = inputs.shape
    experts = first_router.shape[1]
    devices = groups * experts
    capacity = 17 * length // (16 * experts)
    slots = experts * capacity
    inner = first_in.shape[2]
    share = norm_gains.shape[1]
    taps = depthwise_kernel.shape[0]
    feats = first_router.shape[0]

    rows = jnp.concatenate(
        [norm_gains, position_bias, depthwise_kernel, batch_gain[None], batch_bias[None]], axis=0
    )
    count = rows.shape[0]
    flat = jnp.concatenate(
        [rows.reshape(-1), first_router.T.reshape(-1), second_router.T.reshape(-1)]
    ).astype(f32)
    small = gather_small(jnp.broadcast_to(flat[None], (devices,) + flat.shape))
    rows_all = small[:, : count * share].reshape(devices, count, share)
    rows_all = rows_all.transpose(1, 0, 2).reshape(count, devices * share)
    routers = small[:, count * share :].reshape(devices, 2, experts, feats)
    routers = routers.transpose(1, 2, 0, 3).reshape(2, experts, devices * feats)
    routers = jnp.pad(routers, ((0, 0), (0, TILE - experts), (0, 0)))
    routers = routers.transpose(0, 2, 1).astype(bf16)
    gains = jnp.pad(rows_all[0:5], ((0, 3), (0, 0)))
    bias = jnp.pad(rows_all[5:7], ((0, 6), (0, 0)))
    kernel_taps = jnp.pad(rows_all[7 : 7 + taps], ((0, 1), (0, 0)))
    batch = jnp.pad(rows_all[7 + taps : 9 + taps], ((0, 6), (0, 0)))

    packed = jnp.concatenate(
        [attention_in, position_weight, attention_out, pointwise_out, pointwise_in], axis=1
    )
    dense = lax.all_gather(packed, BOTH, axis=0, tiled=True)
    point_out = dense[:, 5 * width : 6 * width]

    first_pair = assemble((first_in[0], first_out[0]), groups)
    second_pair = (
        lax.all_gather(second_in[0], "dp", axis=0, tiled=True),
        lax.all_gather(second_out[0], "dp", axis=0, tiled=True),
    )

    me = lax.axis_index("expert")
    slot_rows, slot_one, slot_two = find_slots(
        first_routes ^ me, second_routes ^ me, experts, capacity
    )
    sinus = sinus_rows(length, width, False)
    mirrored = sinus_rows(length, width, True)
    row_low = shape_of((length, width), bf16)
    row_full = shape_of((length, width), f32)
    lane_full = shape_of((length, TILE), f32)
    block_low = shape_of((slots // PARTS, width), bf16)
    slots_scratch = pltpu.VMEM((slots, width), bf16)
    sums_scratch = pltpu.VMEM((8, width), f32)
    column = shape_of((length, 1), f32)
    eight = shape_of((8, width), f32)
    low_scratch = pltpu.VMEM((length, width), bf16)

    *sent_one, probs_one, gate_one = run(
        functools.partial(front_kernel, experts),
        (inputs, embedding, gains, routers[0], first_routes, slot_rows),
        [VMEM] * 6,
        [block_low] * PARTS + [lane_full, column],
        [low_scratch],
        flops=4 * slots * length * width,
        name="front",
    )
    received_one = exchange(sent_one, experts)
    result_one = (
        expert_forward(received_one[:2], *first_pair)
        + expert_forward(received_one[2:3], *first_pair)
        + expert_forward(received_one[3:], *first_pair)
    )
    returned_one = exchange(result_one, experts)

    edge_scratch = pltpu.VMEM((length + 2 * EDGE, width), f32)
    (
        h1, h2, query_u, query_v, keys, values, table, context, logs, convolved, sums,
    ) = run(
        middle_kernel,
        (
            segment_starts, inputs, slot_one, gate_one, gains, dense, bias, kernel_taps, sinus,
            *returned_one,
        ),
        [SMEM] + [VMEM] * (8 + PARTS),
        [row_full, row_full] + [row_low] * 6 + [lane_full, row_full, shape_of((devices, 3 * width), f32)],
        [edge_scratch, sums_scratch, slots_scratch] + attend_scratch(length),
        flops=16 * length * length * width,
        name="middle",
    )
    totals = gather_small(sums)

    *sent_two, h3, active, probs_two, gate_two, stats = run(
        functools.partial(second_kernel, experts),
        (
            h2, convolved, totals, batch, point_out, embedding, gains, routers[1], second_routes, slot_rows,
        ),
        [VMEM] * 10,
        [block_low] * PARTS + [row_full, row_low, lane_full, column, eight],
        [low_scratch],
        flops=4 * slots * length * width,
        name="second",
    )
    received_two = exchange(sent_two, experts)
    result_two = (
        expert_forward(received_two[:2], *second_pair)
        + expert_forward(received_two[2:3], *second_pair)
        + expert_forward(received_two[3:], *second_pair)
    )
    returned_two = exchange(result_two, experts)

    *d_sent_two, output, d4, dlogits_two, dgain_five = run(
        turn_kernel,
        (
            h3, slot_two, gate_two, probs_two, second_routes, slot_rows, gains, cotangent, *returned_two,
        ),
        [VMEM] * (8 + PARTS),
        [block_low] * PARTS + [row_low, row_full, lane_full, eight],
        [low_scratch, slots_scratch],
        flops=4 * slots * length * width,
        name="turn",
    )
    d_result_two = exchange(d_sent_two, experts)
    d_received_two, hidden_two, d_inner_two = backward_parts(received_two, d_result_two, second_pair)
    d_back_two = exchange(d_received_two, experts)
    d_second_in, d_second_out = scatter_offloaded(
        *expert_grads(received_two, d_result_two, hidden_two, d_inner_two)
    )

    router_shape = shape_of((8, 2 * width), f32)
    d3, d3_low, d_z, dembed_two, drouter_two, small_two, dsums_part = run(
        second_back_kernel,
        (
            slot_two, dlogits_two, h3, d4, embedding, routers[1], gains, convolved, stats, batch, point_out,
            *d_back_two,
        ),
        [VMEM] * (11 + PARTS),
        [row_full, row_low, row_full, row_full, router_shape, eight, shape_of((devices, 2 * width), f32)],
        [sums_scratch, slots_scratch],
        flops=4 * slots * length * width,
        name="second_back",
    )
    dsums = gather_small(dsums_part)
    d_pointwise_out = rows_product(active, d3_low)

    (
        *d_sent_one, d1, dlogits_one, normed_two, normed_three, d_gates, d2_low, d_mixed, d_table, small_mid,
        d_taps,
    ) = run(
        middle_back_kernel,
        (
            segment_starts, convolved, d_z, stats, dsums, batch, d3, h1, h2, gains, dense, kernel_taps, mirrored, query_u, query_v, keys, values, table, context, logs, slot_one, gate_one, probs_one,
            first_routes, slot_rows, *returned_one,
        ),
        [SMEM] + [VMEM] * (24 + PARTS),
        [block_low] * PARTS
        + [
            row_full, lane_full, row_low, row_low, shape_of((length, 2 * width), bf16), row_low,
            shape_of((length, 3 * width), bf16), row_low, shape_of((16, width), f32),
            shape_of((16, width), f32),
        ],
        [
            edge_scratch, pltpu.VMEM((length, 2 * width), f32), low_scratch, low_scratch, low_scratch,
            slots_scratch,
        ]
        + attend_back_scratch(),
        flops=32 * length * length * width,
        name="middle_back",
    )
    d_result_one = exchange(d_sent_one, experts)
    d_received_one, hidden_one, d_inner_one = backward_parts(received_one, d_result_one, first_pair)
    d_back_one = exchange(d_received_one, experts)
    d_first_in, d_first_out = scatter_direct(
        *expert_grads(received_one, d_result_one, hidden_one, d_inner_one), groups
    )

    d_start, d_embed, drouter_one, small_one = run(
        last_kernel,
        (
            slot_one, dlogits_one, inputs, d1, embedding, routers[0], gains, dembed_two, *d_back_one,
        ),
        [VMEM] * (8 + PARTS),
        [row_full, row_full, router_shape, eight],
        [slots_scratch],
        flops=4 * slots * length * width,
        name="last",
    )

    dense_grad = jnp.concatenate(
        [
            rows_product(normed_two, d_mixed),
            rows_product(mirrored, d_table),
            rows_product(context, d2_low),
            d_pointwise_out,
            rows_product(normed_three, d_gates),
        ],
        axis=1,
    ).astype(bf16)
    dense_share = scatter_dense(dense_grad, groups, experts)

    rows_grad = jnp.concatenate(
        [
            small_one[0:1], small_mid[1:2], small_mid[0:1], small_two[0:1], dgain_five[0:1],
            small_mid[8:10], d_taps[:taps], small_two[1:3],
        ],
        axis=0,
    )
    rows_grad = rows_grad.reshape(count, devices, share).transpose(1, 0, 2).reshape(devices, -1)
    routers_grad = jnp.stack([drouter_one[:experts], drouter_two[:experts]])
    routers_grad = routers_grad.reshape(2 * experts, devices, feats).transpose(1, 0, 2).reshape(devices, -1)
    small_grad = jnp.concatenate([rows_grad, routers_grad], axis=1)
    small_share = jnp.sum(
        lax.all_to_all(small_grad, BOTH, split_axis=0, concat_axis=0, tiled=True), axis=0
    )
    rows_share = small_share[: count * share].reshape(count, share)
    routers_share = small_share[count * share :].reshape(2, experts, feats).transpose(0, 2, 1)

    return (
        output,
        d_start,
        d_embed,
        rows_share[0:5],
        routers_share[0],
        routers_share[1],
        d_first_in,
        d_first_out,
        d_second_in,
        d_second_out,
        dense_share[:, : 3 * width],
        dense_share[:, 3 * width : 4 * width],
        rows_share[5:7],
        dense_share[:, 4 * width : 5 * width],
        dense_share[:, 6 * width : 8 * width],
        rows_share[7 : 7 + taps],
        rows_share[7 + taps],
        rows_share[8 + taps],
        dense_share[:, 5 * width : 6 * width],
    )


def solution(mesh):
    split = P(BOTH, None)
    wide = P(None, BOTH)
    bank = P("expert", "dp", None)
    line = P(BOTH)
    in_specs = (
        (split,) * 6
        + (wide, split, split)
        + (bank,) * 4
        + (split, split, wide, split, split, wide, line, line, split)
    )
    out_specs = (
        (split,) * 3
        + (wide, split, split)
        + (bank,) * 4
        + (split, split, wide, split, split, wide, line, line, split)
    )
    return jax.shard_map(
        functools.partial(body, mesh.shape["dp"]),
        mesh=mesh,
        in_specs=in_specs,
        out_specs=out_specs,
        check_vma=False,
    )
```

```python
import functools
import math

import jax
import jax.numpy as jnp
import numpy as np
from jax import lax
from jax.experimental import pallas as pl
from jax.experimental.pallas import tpu as pltpu
from jax.sharding import PartitionSpec as P

H = 8
TILE = 128
epsilon = 1e-05
masked_score = -1e30
BOTH = ("dp", "expert")
f32 = jnp.float32
bf16 = jnp.bfloat16

VMEM = pl.BlockSpec(memory_space=pltpu.VMEM)
SMEM = pl.BlockSpec(memory_space=pltpu.SMEM)


def shape_of(dims, kind):
    return jax.ShapeDtypeStruct(dims, kind)


def run(kernel, args, in_specs, outs, scratch=(), flops=0, name=None, limit=56):
    moved = sum(math.prod(a.shape) * a.dtype.itemsize for a in list(args) + list(outs))
    results = pl.pallas_call(
        kernel,
        out_shape=outs,
        in_specs=in_specs,
        out_specs=[VMEM] * len(outs),
        scratch_shapes=list(scratch),
        compiler_params=pltpu.CompilerParams(vmem_limit_bytes=limit * 2**20),
        cost_estimate=pl.CostEstimate(flops=flops, bytes_accessed=moved, transcendentals=0),
        name=name,
    )(*args)
    return list(results)


def dot(left, right):
    return lax.dot_general(left, right, (((1,), (0,)), ((), ())), preferred_element_type=f32)


def dot_t(left, right):
    return lax.dot_general(left, right, (((1,), (1,)), ((), ())), preferred_element_type=f32)


def t_dot(left, right):
    return lax.dot_general(left, right, (((0,), (0,)), ((), ())), preferred_element_type=f32)


def iota(dims, axis):
    return lax.broadcasted_iota(jnp.int32, dims, axis)


def normalize(values):
    center = values - jnp.mean(values, axis=-1, keepdims=True)
    spread = jnp.mean(center * center, axis=-1, keepdims=True)
    inverse = lax.rsqrt(spread + epsilon)
    return center * inverse, inverse


def normalize_back(standard, inverse, gain, upstream):
    scaled = upstream * gain
    first = jnp.mean(scaled, axis=-1, keepdims=True)
    second = jnp.mean(scaled * standard, axis=-1, keepdims=True)
    return inverse * (scaled - first - standard * second)


def column_sum(values):
    return jnp.sum(values, axis=0, keepdims=True)


def sigmoid(values):
    return 1.0 / (1.0 + jnp.exp(-values))


def loop(count, body):
    def step(index, carry):
        body(index)
        return carry

    lax.fori_loop(0, count, step, 0)


def rows_at(index, size):
    return pl.ds(pl.multiple_of(index * size, size), size)


def slots_kernel(capacity, offset_ref, one_ref, two_ref, rows_ref, cols_ref, stack):
    length = rows_ref.shape[1]
    block = 256
    stack[...] = jnp.zeros_like(stack)
    for half, chosen_ref in enumerate((one_ref, two_ref)):
        chosen = chosen_ref[...]
        near = chosen ^ offset_ref[0]
        onehot = jnp.where(iota((8, length), 0) == near, 1.0, 0.0)
        onehot_low = onehot.astype(bf16)
        for index in range(length // block):
            earlier = iota((length, block), 0) < iota((length, block), 1) + index * block
            counts = dot(onehot_low, jnp.where(earlier, 1.0, 0.0).astype(bf16))
            span = slice(index * block, (index + 1) * block)
            rank = column_sum(onehot[:, span] * counts)
            stack[half : half + 1, span] = (near[:, span] * capacity).astype(f32) + rank
        stack[2 + half : 3 + half, :] = chosen.astype(f32)
    rows_ref[...] = stack[:8, :].astype(jnp.int32)
    for index in range(length // TILE):
        span = slice(index * TILE, (index + 1) * TILE)
        cols_ref[span, :] = jnp.transpose(stack[:, span]).astype(jnp.int32)


def find_slots(routes_one, routes_two, offset, capacity):
    length = routes_one.shape[0]
    return run(
        functools.partial(slots_kernel, capacity),
        (offset.reshape(1), routes_one.reshape(1, length), routes_two.reshape(1, length)),
        [SMEM, VMEM, VMEM],
        [shape_of((8, length), jnp.int32), shape_of((length, TILE), jnp.int32)],
        [pltpu.VMEM((TILE, length), f32)],
        flops=8 * length * length * 128,
        name="slots",
    )


PARTS = 4


def dispatch(low_ref, slot_row, out_refs):
    block = out_refs[0].shape[0]
    length = low_ref.shape[0]
    for index, out_ref in enumerate(out_refs):
        ids = iota((block, length), 0) + index * block
        onehot = jnp.where(ids == slot_row, 1.0, 0.0).astype(bf16)
        out_ref[...] = dot(onehot, low_ref[...]).astype(bf16)


def join_blocks(block_refs, whole_ref):
    block = block_refs[0].shape[0]
    for index, block_ref in enumerate(block_refs):
        whole_ref[index * block : (index + 1) * block, :] = block_ref[...]


def collect(slot_col, table_ref):
    rows = slot_col.shape[0]
    slots = table_ref.shape[0]
    onehot = jnp.where(iota((rows, slots), 1) == slot_col, 1.0, 0.0).astype(bf16)
    return dot(onehot, table_ref[...])


def route_block(low, embed, router_ref, picks, experts):
    width = low.shape[1]
    logits = dot(low, router_ref[:width, :]) + dot(embed, router_ref[width:, :])
    lanes = iota(logits.shape, 1)
    inside = lanes < experts
    logits = jnp.where(inside, logits, masked_score)
    raised = jnp.where(inside, jnp.exp(logits - jnp.max(logits, axis=1, keepdims=True)), 0.0)
    probs = raised / jnp.sum(raised, axis=1, keepdims=True)
    gate = jnp.sum(jnp.where(lanes == picks, probs, 0.0), axis=1, keepdims=True)
    return probs, gate


BLOCK = 256


def front_kernel(
    experts, hidden_ref, embed_ref, gain_ref, router_ref, cols_ref, slot_row_ref, *refs,
):
    out_refs, (probs_ref, gate_ref, low_ref) = refs[:PARTS], refs[PARTS:]
    length = hidden_ref.shape[0]

    def step(index):
        at = rows_at(index, BLOCK)
        standard, unused = normalize(hidden_ref[at, :].astype(f32))
        low = (standard * gain_ref[0:1, :]).astype(bf16)
        low_ref[at, :] = low
        probs, gate = route_block(low, embed_ref[at, :], router_ref, cols_ref[at, 2:3], experts)
        probs_ref[at, :] = probs
        gate_ref[at, :] = gate

    loop(length // BLOCK, step)
    dispatch(low_ref, slot_row_ref[0:1, :], out_refs)


def expert_forward_kernel(count, in_ref, out_ref, *refs):
    for x_ref, y_ref in zip(refs[:count], refs[count:]):
        inner = dot(x_ref[...], in_ref[...])
        hidden = (inner * sigmoid(inner)).astype(bf16)
        y_ref[...] = dot(hidden, out_ref[...]).astype(bf16)


def expert_forward(received, weight_in, weight_out):
    block, width = received[0].shape
    count = len(received)
    return run(
        functools.partial(expert_forward_kernel, count),
        (weight_in, weight_out) + tuple(received),
        [VMEM] * (2 + count),
        [shape_of((block, width), bf16)] * count,
        flops=4 * count * block * width * weight_in.shape[1],
        name="experts",
        limit=32,
    )


def forward_in_turn(received, pair):
    near, far = lax.optimization_barrier((expert_forward(received[:2], *pair), received[2:]))
    return near + expert_forward(far[:1], *pair) + expert_forward(far[1:], *pair)


def expert_backward_kernel(count, in_ref, out_ref, *refs):
    x_refs, dy_refs, refs = refs[:count], refs[count : 2 * count], refs[2 * count :]
    extra, refs = refs[: len(refs) - 3 * count], refs[len(refs) - 3 * count :]
    if extra:
        normed_ref, mixed_ref, table_ref, sinus_ref, grad_ref = extra
        width = normed_ref.shape[1]
        for part in range(3):
            lanes = slice(part * width, (part + 1) * width)
            grad_ref[:, lanes] = t_dot(normed_ref[...], mixed_ref[:, lanes]).astype(bf16)
        grad_ref[:, 3 * width :] = jnp.transpose(dot(table_ref[...], sinus_ref[...])).astype(bf16)
    dx_refs, hidden_refs, dinner_refs = refs[:count], refs[count : 2 * count], refs[2 * count :]
    for x_ref, dy_ref, dx_ref, hidden_ref, dinner_ref in zip(
        x_refs, dy_refs, dx_refs, hidden_refs, dinner_refs
    ):
        inner = dot(x_ref[...], in_ref[...])
        gates = sigmoid(inner)
        hidden = inner * gates
        hidden_ref[...] = hidden.astype(bf16)
        d_hidden = dot_t(dy_ref[...], out_ref[...])
        d_inner = (d_hidden * (gates + hidden * (1.0 - gates))).astype(bf16)
        dinner_ref[...] = d_inner
        dx_ref[...] = dot_t(d_inner, in_ref[...]).astype(bf16)


def expert_backward(received, d_result, weight_in, weight_out, extra=()):
    block, width = received[0].shape
    inner = weight_in.shape[1]
    count = len(received)
    more = [shape_of((width, 4 * width), bf16)] if extra else []
    outs = run(
        functools.partial(expert_backward_kernel, count),
        (weight_in, weight_out) + tuple(received) + tuple(d_result) + tuple(extra),
        [VMEM] * (2 + 2 * count + len(extra)),
        more + [shape_of((block, width), bf16)] * count + [shape_of((block, inner), bf16)] * (2 * count),
        flops=6 * count * block * width * inner,
        name="experts_back",
        limit=48 if extra else 40,
    )
    more, outs = outs[: len(more)], outs[len(more) :]
    return more, outs[:count], outs[count : 2 * count], outs[2 * count :]


def backward_in_turn(received, d_result, pair, extra=()):
    near, far = lax.optimization_barrier(
        (expert_backward(received[:2], d_result[:2], *pair, extra), d_result[2:])
    )
    parts = [
        near,
        expert_backward(received[2:3], far[:1], *pair),
        expert_backward(received[3:], far[1:], *pair),
    ]
    return [sum((list(part[k]) for part in parts), []) for k in range(4)]


def tile_window(starts_ref, first, length):
    count = starts_ref.shape[1]
    low = jnp.int32(0)
    high = jnp.int32(length)
    for k in range(1, count):
        low = jnp.where(starts_ref[0, k] <= first, starts_ref[0, k], low)
    for k in range(count - 1, 0, -1):
        high = jnp.where(starts_ref[0, k] > first + (TILE - 1), starts_ref[0, k], high)
    low = low // TILE
    steps = ((high + (TILE - 1)) // TILE - low + 1) // 2
    return jnp.minimum(low, length // TILE - 2 * steps), steps


def numbers_at(starts_ref, positions):
    total = jnp.zeros(positions.shape, jnp.int32)
    for k in range(1, starts_ref.shape[1]):
        total = total + jnp.where(positions >= starts_ref[0, k], 1, 0)
    return total


def same_tile(starts_ref, first_query, first_key):
    rows = numbers_at(starts_ref, iota((TILE, TILE), 0) + first_query)
    cols = numbers_at(starts_ref, iota((TILE, TILE), 1) + first_key)
    return rows == cols


PAD = 2


def chunk_rows(query_tile, key_tile, length, count, mirrored=False):
    tiles = length // TILE
    index = tiles - 1 - query_tile + key_tile - (tiles // 2 - PAD)
    if mirrored:
        index = tiles + 2 * PAD - count - index
    index = jnp.clip(index, 0, tiles + 2 * PAD - count)
    return pl.ds(pl.multiple_of(index * TILE, TILE), count * TILE)


def halves(values):
    left = iota(values.shape, 1) < TILE // 2
    zero = jnp.zeros_like(values)
    return jnp.concatenate(
        [jnp.where(left, values, zero), jnp.where(left, zero, values)], axis=0
    )


def turned_halves(values):
    turned = jnp.transpose(values)
    top = iota(turned.shape, 0) < TILE // 2
    zero = jnp.zeros_like(turned)
    return jnp.concatenate([jnp.where(top, turned, zero), jnp.where(top, zero, turned)], axis=1)


def skew(values):
    return jnp.concatenate(
        [
            pltpu.roll(values[:TILE], 1, 1, stride=1, stride_axis=0),
            pltpu.roll(values[TILE:], 1, 1, stride=1, stride_axis=0),
        ],
        axis=0,
    )


def mirror(values):
    row, col = iota((2 * TILE, 2 * TILE), 0), iota((2 * TILE, 2 * TILE), 1)
    flip = (row % TILE + col % TILE == TILE - 1) & (row // TILE == col // TILE)
    return dot(values, jnp.where(flip, 1.0, 0.0).astype(bf16))


def twice(values):
    return jnp.concatenate([values, values], axis=0)


PAIRS = H // 2


def attend_forward(
    starts_ref, qu_ref, qv_ref, k_ref, v_ref, t_ref, context_ref, logs_ref,
    qum, qvm, scores, rolled, peaks, sums, mixed,
):
    length = qu_ref.shape[0]
    tiles = length // TILE

    def query_step(tile):
        first = tile * TILE
        at = rows_at(tile, TILE)
        low, steps = tile_window(starts_ref, first, length)
        chunk = chunk_rows(tile, low, length, 1)
        for p in range(PAIRS):
            lanes = slice(p * TILE, (p + 1) * TILE)
            qum[p] = halves(qu_ref[at, lanes])
            qvm[p] = halves(qv_ref[at, lanes])
            rolled[p] = skew(dot_t(qvm[p], t_ref[chunk, lanes]))
            peaks[p] = jnp.full((2 * TILE, TILE), masked_score, f32)
            sums[p] = jnp.zeros((2 * TILE, TILE), f32)
            mixed[p] = jnp.zeros((2 * TILE, TILE), f32)
        lower = twice(iota((TILE, TILE), 1) <= iota((TILE, TILE), 0))

        def score_step(step, carry):
            key = low + 2 * step
            keys = pl.ds(pl.multiple_of(key * TILE, TILE), 2 * TILE)
            same_one = twice(same_tile(starts_ref, first, key * TILE))
            same_two = twice(same_tile(starts_ref, first, key * TILE + TILE))
            chunks = chunk_rows(tile, key + 1, length, 2)
            for p in range(PAIRS):
                lanes = slice(p * TILE, (p + 1) * TILE)
                content = dot_t(qum[p], k_ref[keys, lanes])
                fresh = dot_t(qvm[p], t_ref[chunks, lanes])
                one, two = skew(fresh[:, :TILE]), skew(fresh[:, TILE:])
                value_one = content[:, :TILE] + jnp.where(lower, rolled[p], one)
                value_two = content[:, TILE:] + jnp.where(lower, one, two)
                value_one = jnp.where(same_one, value_one, masked_score)
                value_two = jnp.where(same_two, value_two, masked_score)
                rolled[p] = two
                scores[2 * step, p] = value_one
                scores[2 * step + 1, p] = value_two
                peaks[p] = jnp.maximum(peaks[p], jnp.maximum(value_one, value_two))
            return carry

        lax.fori_loop(0, steps, score_step, 0)
        for p in range(PAIRS):
            peaks[p] = jnp.broadcast_to(
                jnp.max(peaks[p], axis=1, keepdims=True), (2 * TILE, TILE)
            )

        def value_step(step, carry):
            keys = pl.ds(pl.multiple_of((low + 2 * step) * TILE, TILE), 2 * TILE)
            for p in range(PAIRS):
                lanes = slice(p * TILE, (p + 1) * TILE)
                one = jnp.exp(scores[2 * step, p] - peaks[p])
                two = jnp.exp(scores[2 * step + 1, p] - peaks[p])
                sums[p] += one + two
                raised = jnp.concatenate([one.astype(bf16), two.astype(bf16)], axis=1)
                mixed[p] += dot(raised, v_ref[keys, lanes])
            return carry

        lax.fori_loop(0, steps, value_step, 0)
        left = iota((TILE, TILE), 1) < TILE // 2
        logs = jnp.zeros((TILE, TILE), f32)
        lane = iota((TILE, TILE), 1)
        for p in range(PAIRS):
            lanes = slice(p * TILE, (p + 1) * TILE)
            total = jnp.sum(sums[p], axis=1, keepdims=True)
            result = mixed[p] * (1.0 / total)
            context_ref[at, lanes] = jnp.where(left, result[:TILE], result[TILE:]).astype(bf16)
            logsum = peaks[p] + jnp.log(total)
            logs = jnp.where(lane == 2 * p, logsum[:TILE], logs)
            logs = jnp.where(lane == 2 * p + 1, logsum[TILE:], logs)
        logs_ref[at, :] = logs

    loop(tiles, query_step)


def attend_scratch(length):
    pair = (PAIRS, 2 * TILE, TILE)
    return [
        pltpu.VMEM(pair, bf16),
        pltpu.VMEM(pair, bf16),
        pltpu.VMEM((length // TILE,) + pair, f32),
        pltpu.VMEM(pair, f32),
        pltpu.VMEM(pair, f32),
        pltpu.VMEM(pair, f32),
        pltpu.VMEM(pair, f32),
    ]


def attend_backward(
    starts_ref, qu_ref, qv_ref, k_ref, v_ref, t_ref, mirrored_ref, context_ref, logs_ref, dcontext_ref,
    dm_ref, dk_ref, dv_ref, dt_ref, dbias_ref,
    qum, qvm, dcm, qut, qvt, dct, logs, deltas, rolled, unrolled, dqu, dqv,
):
    length, width = qu_ref.shape
    tiles = length // TILE
    scale = 1.0 / math.sqrt(width // H)
    dk_ref[...] = jnp.zeros_like(dk_ref)
    dv_ref[...] = jnp.zeros_like(dv_ref)
    dt_ref[...] = jnp.zeros_like(dt_ref)
    dbias_ref[...] = jnp.zeros_like(dbias_ref)

    def query_step(tile):
        first = tile * TILE
        at = rows_at(tile, TILE)
        low, steps = tile_window(starts_ref, first, length)
        chunk = chunk_rows(tile, low, length, 1)
        logs_tile = logs_ref[at, :]
        for p in range(PAIRS):
            lanes = slice(p * TILE, (p + 1) * TILE)
            query_u = halves(qu_ref[at, lanes])
            query_v = halves(qv_ref[at, lanes])
            upstream = halves(dcontext_ref[at, lanes])
            qum[p] = query_u
            qvm[p] = query_v
            dcm[p] = upstream
            qut[p] = turned_halves(qu_ref[at, lanes])
            qvt[p] = turned_halves(qv_ref[at, lanes])
            dct[p] = turned_halves(dcontext_ref[at, lanes])
            delta = jnp.sum(
                upstream.astype(f32) * twice(context_ref[at, lanes].astype(f32)),
                axis=1,
                keepdims=True,
            )
            deltas[p] = jnp.broadcast_to(delta, (2 * TILE, TILE))
            logs[p, :TILE] = jnp.broadcast_to(logs_tile[:, 2 * p : 2 * p + 1], (TILE, TILE))
            logs[p, TILE:] = jnp.broadcast_to(logs_tile[:, 2 * p + 1 : 2 * p + 2], (TILE, TILE))
            rolled[p] = skew(dot_t(query_v, t_ref[chunk, lanes]))
            unrolled[p] = jnp.zeros((2 * TILE, TILE), f32)
            dqu[p] = jnp.zeros((2 * TILE, TILE), f32)
            dqv[p] = jnp.zeros((2 * TILE, TILE), f32)
        lower = twice(iota((TILE, TILE), 1) <= iota((TILE, TILE), 0))

        def step_body(step, carry):
            key = low + 2 * step
            keys = pl.ds(pl.multiple_of(key * TILE, TILE), 2 * TILE)
            same_one = twice(same_tile(starts_ref, first, key * TILE))
            same_two = twice(same_tile(starts_ref, first, key * TILE + TILE))
            before = chunk_rows(tile, key, length, 2, True)
            after = chunk_rows(tile, key + 1, length, 2)
            for p in range(PAIRS):
                lanes = slice(p * TILE, (p + 1) * TILE)
                content = dot_t(qum[p], k_ref[keys, lanes])
                fresh = dot_t(qvm[p], t_ref[after, lanes])
                one, two = skew(fresh[:, :TILE]), skew(fresh[:, TILE:])
                value_one = content[:, :TILE] + jnp.where(lower, rolled[p], one)
                value_two = content[:, TILE:] + jnp.where(lower, one, two)
                rolled[p] = two
                probs_one = jnp.where(same_one, jnp.exp(value_one - logs[p]), 0.0)
                probs_two = jnp.where(same_two, jnp.exp(value_two - logs[p]), 0.0)
                probs = jnp.concatenate([probs_one.astype(bf16), probs_two.astype(bf16)], axis=1)
                dprobs = dot_t(dcm[p], v_ref[keys, lanes])
                dlow_one = (probs_one * (dprobs[:, :TILE] - deltas[p])).astype(bf16)
                dlow_two = (probs_two * (dprobs[:, TILE:] - deltas[p])).astype(bf16)
                dlow = jnp.concatenate([dlow_one, dlow_two], axis=1)
                dv_ref[lanes, keys] += dot(dct[p], probs)
                dk_ref[lanes, keys] += dot(qut[p], dlow)
                dqu[p] += dot(dlow, k_ref[keys, lanes])
                mirrored = mirror(dlow)
                one, two = skew(mirrored[:, :TILE]), skew(mirrored[:, TILE:])
                moved = jnp.concatenate(
                    [
                        jnp.where(lower, two, one).astype(bf16),
                        jnp.where(lower, one, unrolled[p]).astype(bf16),
                    ],
                    axis=1,
                )
                unrolled[p] = two
                dt_ref[lanes, before] += dot(qvt[p], moved)
                dqv[p] += dot(moved, mirrored_ref[before, lanes])
            return carry

        lax.fori_loop(0, steps, step_body, 0)
        last = chunk_rows(tile, low + 2 * steps, length, 1, True)
        left = iota((TILE, TILE), 1) < TILE // 2
        for p in range(PAIRS):
            lanes = slice(p * TILE, (p + 1) * TILE)
            moved = jnp.where(lower, 0.0, unrolled[p]).astype(bf16)
            dt_ref[lanes, last] += dot(qvt[p], moved)
            full_u = dqu[p]
            full_v = dqv[p] + dot(moved, mirrored_ref[last, lanes])
            part_u = jnp.where(left, full_u[:TILE], full_u[TILE:]) * scale
            part_v = jnp.where(left, full_v[:TILE], full_v[TILE:]) * scale
            dbias_ref[0:1, lanes] += column_sum(part_u)
            dbias_ref[1:2, lanes] += column_sum(part_v)
            dm_ref[at, lanes] = (part_u + part_v).astype(bf16)

    loop(tiles, query_step)

    def finish(index):
        at = rows_at(index, TILE)
        for p in range(PAIRS):
            lanes = slice(p * TILE, (p + 1) * TILE)
            key_lanes = slice(width + p * TILE, width + (p + 1) * TILE)
            value_lanes = slice(2 * width + p * TILE, 2 * width + (p + 1) * TILE)
            dm_ref[at, key_lanes] = jnp.transpose(dk_ref[lanes, at].astype(bf16))
            dm_ref[at, value_lanes] = jnp.transpose(dv_ref[lanes, at].astype(bf16))

    loop(tiles, finish)


def attend_back_scratch():
    pair = (PAIRS, 2 * TILE, TILE)
    turned = (PAIRS, TILE, 2 * TILE)
    return [pltpu.VMEM(dims, bf16) for dims in (pair,) * 3 + (turned,) * 3] + [
        pltpu.VMEM(pair, f32) for unused in range(6)
    ]


def dense_parts(dense_ref):
    width = dense_ref.shape[0]
    cuts = (0, 3, 4, 5, 6, 8)
    return [
        dense_ref.at[:, pl.ds(start * width, (stop - start) * width)]
        for start, stop in zip(cuts[:-1], cuts[1:])
    ]


def spread_rows(rows_ref, out_ref):
    width = rows_ref.shape[1]
    for row in range(out_ref.shape[2] // width):
        lanes = slice(row * width, (row + 1) * width)
        out_ref[:, :, lanes] = jnp.broadcast_to(
            rows_ref[row : row + 1, :][None], (out_ref.shape[0], 1, width)
        )


EDGE = 16


def middle_kernel(
    starts_ref, hidden_ref, cols_ref, gate_ref, gains_ref, dense_ref, bias_ref, taps_ref, sinus_ref,
    *refs,
):
    returned_refs, refs = refs[:PARTS], refs[PARTS:]
    h1_ref, h2_ref, qu_ref, qv_ref, k_ref, v_ref, t_ref, context_ref, logs_ref = refs[:9]
    conv_ref, sums_ref, padded, sums, returned_ref = refs[9:14]
    attend = refs[14:]
    join_blocks(returned_refs, returned_ref)
    length, width = h1_ref.shape
    scale = 1.0 / math.sqrt(width // H)
    in_ref, place_ref, mix_ref, unused, point_ref = dense_parts(dense_ref)

    def queries_step(index):
        at = rows_at(index, BLOCK)
        picked = collect(cols_ref[at, 0:1], returned_ref)
        h1 = hidden_ref[at, :].astype(f32) + 0.5 * gate_ref[at, :] * picked
        h1_ref[at, :] = h1
        standard, unused = normalize(h1)
        low = (standard * gains_ref[1:2, :]).astype(bf16)
        queries = dot(low, in_ref[:, :width])
        qu_ref[at, :] = ((queries + bias_ref[0:1, :]).astype(bf16).astype(f32) * scale).astype(bf16)
        qv_ref[at, :] = ((queries + bias_ref[1:2, :]).astype(bf16).astype(f32) * scale).astype(bf16)
        k_ref[at, :] = dot(low, in_ref[:, width : 2 * width]).astype(bf16)
        v_ref[at, :] = dot(low, in_ref[:, 2 * width :]).astype(bf16)
        table_at = pl.ds(pl.multiple_of(index * BLOCK + edge, TILE), BLOCK)
        t_ref[table_at, :] = dot(sinus_ref[at, :], place_ref[...]).astype(bf16)

    edge = PAD * TILE
    t_ref[:edge, :] = jnp.zeros((edge, width), bf16)
    t_ref[edge + length :, :] = jnp.zeros((edge, width), bf16)
    loop(length // BLOCK, queries_step)
    attend_forward(
        starts_ref, qu_ref, qv_ref, k_ref, v_ref, t_ref, context_ref, logs_ref, *attend
    )
    padded[:EDGE, :] = jnp.zeros((EDGE, width), f32)
    padded[EDGE + length :, :] = jnp.zeros((EDGE, width), f32)

    def gates_step(index):
        at = rows_at(index, BLOCK)
        h2 = h1_ref[at, :] + dot(context_ref[at, :], mix_ref[...])
        h2_ref[at, :] = h2
        standard, unused = normalize(h2)
        low = (standard * gains_ref[2:3, :]).astype(bf16)
        value = dot(low, point_ref[:, :width])
        gates = dot(low, point_ref[:, width:])
        padded[pl.ds(pl.multiple_of(index * BLOCK + EDGE, EDGE), BLOCK), :] = value * sigmoid(gates)

    loop(length // BLOCK, gates_step)
    sums[...] = jnp.zeros_like(sums)
    taps = taps_ref.shape[0] - 1
    reach = taps // 2
    frames = starts_ref[0, starts_ref.shape[1] - 1]

    def conv_step(index):
        first = index * TILE
        place = iota((TILE, TILE), 0) + first
        here = numbers_at(starts_ref, place)
        valid = place < frames
        totals = [jnp.zeros((TILE, TILE), f32) for unused in range(width // TILE)]
        around = pl.ds(pl.multiple_of(first, TILE), TILE + 2 * EDGE)
        for tap in range(taps):
            same = numbers_at(starts_ref, place + (tap - reach)) == here
            for part in range(width // TILE):
                lanes = slice(part * TILE, (part + 1) * TILE)
                near = padded[around, lanes][EDGE + tap - reach : EDGE + tap - reach + TILE]
                totals[part] = totals[part] + jnp.where(same, near, 0.0) * taps_ref[tap : tap + 1, lanes]
        for part in range(width // TILE):
            lanes = slice(part * TILE, (part + 1) * TILE)
            conv_ref[rows_at(index, TILE), lanes] = totals[part]
            kept = jnp.where(valid, totals[part], 0.0)
            sums[0:1, lanes] += column_sum(kept)
            sums[1:2, lanes] += column_sum(kept * kept)

    loop(length // TILE, conv_step)
    sums[2:3, :] = jnp.zeros((1, width), f32) + frames.astype(f32)
    spread_rows(sums, sums_ref)


def batch_totals(totals_ref, width):
    totals = jnp.sum(totals_ref[...], axis=0)
    count = totals[:, 2 * width :]
    mean = totals[:, :width] / count
    variance = totals[:, width : 2 * width] / count - mean * mean
    return mean, lax.rsqrt(variance + epsilon), count


def batch_block(conv, mean, inverse, batch_ref):
    centred = conv - mean
    standard = centred * inverse
    batched = standard * batch_ref[0:1, :] + batch_ref[1:2, :]
    return centred, standard, batched


def second_kernel(
    experts, h2_ref, conv_ref, totals_ref, batch_ref, point_ref, embed_ref, gains_ref, router_ref,
    cols_ref, slot_row_ref, *refs,
):
    out_refs, refs = refs[:PARTS], refs[PARTS:]
    h3_ref, active_ref, probs_ref, gate_ref, stats_ref, low_ref = refs
    length, width = h2_ref.shape
    mean, inverse, count = batch_totals(totals_ref, width)
    stats_ref[0:1, :] = mean
    stats_ref[1:2, :] = inverse
    stats_ref[2:3, :] = count

    def step(index):
        at = rows_at(index, BLOCK)
        unused, unused, batched = batch_block(conv_ref[at, :], mean, inverse, batch_ref)
        active = (batched * sigmoid(batched)).astype(bf16)
        active_ref[at, :] = active
        h3 = h2_ref[at, :] + dot(active, point_ref[...])
        h3_ref[at, :] = h3
        standard, unused = normalize(h3)
        low = (standard * gains_ref[3:4, :]).astype(bf16)
        low_ref[at, :] = low
        probs, gate = route_block(low, embed_ref[at, :], router_ref, cols_ref[at, 3:4], experts)
        probs_ref[at, :] = probs
        gate_ref[at, :] = gate

    loop(length // BLOCK, step)
    dispatch(low_ref, slot_row_ref[1:2, :], out_refs)


def gate_back(upstream, picked, gate, probs, picks):
    d_gate = 0.5 * jnp.sum(upstream * picked, axis=1, keepdims=True)
    onehot = jnp.where(iota(probs.shape, 1) == picks, 1.0, 0.0)
    return (d_gate * gate) * (onehot - probs)


def turn_kernel(
    h3_ref, cols_ref, gate_ref, probs_ref, slot_row_ref, gains_ref, cotangent_ref, *refs,
):
    returned_refs, out_refs, refs = refs[:PARTS], refs[PARTS : 2 * PARTS], refs[2 * PARTS :]
    output_ref, d4_ref, dlogits_ref, dgain_ref, low_ref, returned_ref = refs
    length = h3_ref.shape[0]
    join_blocks(returned_refs, returned_ref)
    dgain_ref[...] = jnp.zeros_like(dgain_ref)

    def step(index):
        at = rows_at(index, BLOCK)
        picked = collect(cols_ref[at, 1:2], returned_ref)
        gate = gate_ref[at, :]
        h4 = h3_ref[at, :] + 0.5 * gate * picked
        standard, inverse = normalize(h4)
        gain = gains_ref[4:5, :]
        output_ref[at, :] = (standard * gain).astype(bf16)
        upstream = cotangent_ref[at, :].astype(f32)
        dgain_ref[0:1, :] += column_sum(upstream * standard)
        d4 = normalize_back(standard, inverse, gain, upstream)
        d4_ref[at, :] = d4
        dlogits_ref[at, :] = gate_back(d4, picked, gate, probs_ref[at, :], cols_ref[at, 3:4])
        low_ref[at, :] = (0.5 * gate * d4).astype(bf16)

    loop(length // BLOCK, step)
    dispatch(low_ref, slot_row_ref[1:2, :], out_refs)


def router_back(dlogits, low, embed, router_ref, drouter_ref):
    width = low.shape[1]
    high = dlogits.astype(bf16)
    rest = (dlogits - high.astype(f32)).astype(bf16)
    d_low = dot_t(high, router_ref[:width, :]) + dot_t(rest, router_ref[:width, :])
    d_embed = dot_t(high, router_ref[width:, :]) + dot_t(rest, router_ref[width:, :])
    turned = jnp.transpose(dlogits)[:8, :]
    turned_high = turned.astype(bf16)
    turned_rest = (turned - turned_high.astype(f32)).astype(bf16)
    drouter_ref[:, :width] += dot(turned_high, low) + dot(turned_rest, low)
    drouter_ref[:, width:] += dot(turned_high, embed) + dot(turned_rest, embed)
    return d_low, d_embed


def second_back_kernel(
    cols_ref, dlogits_ref, h3_ref, d4_ref, embed_ref, router_ref, gains_ref, conv_ref, stats_ref,
    batch_ref, point_ref, *refs,
):
    dsent_refs, refs = refs[:PARTS], refs[PARTS:]
    d3_ref, dlow_ref, dz_ref, dembed_ref, drouter_ref, small_ref, sums_ref, sums, dsent_ref = refs
    length, width = h3_ref.shape
    drouter_ref[...] = jnp.zeros_like(drouter_ref)
    small_ref[...] = jnp.zeros_like(small_ref)
    sums[...] = jnp.zeros_like(sums)
    join_blocks(dsent_refs, dsent_ref)
    mean, batch_inverse = stats_ref[0:1, :], stats_ref[1:2, :]

    def step(index):
        at = rows_at(index, BLOCK)
        standard, inverse = normalize(h3_ref[at, :])
        gain = gains_ref[3:4, :]
        low = (standard * gain).astype(bf16)
        d_low, d_embed = router_back(
            dlogits_ref[at, :], low, embed_ref[at, :], router_ref, drouter_ref
        )
        dembed_ref[at, :] = d_embed
        d_norm = collect(cols_ref[at, 1:2], dsent_ref) + d_low
        small_ref[0:1, :] += column_sum(d_norm * standard)
        d3 = d4_ref[at, :] + normalize_back(standard, inverse, gain, d_norm)
        d3_ref[at, :] = d3
        d3_low = d3.astype(bf16)
        dlow_ref[at, :] = d3_low
        centred, normed, batched = batch_block(conv_ref[at, :], mean, batch_inverse, batch_ref)
        gates = sigmoid(batched)
        d_batched = dot_t(d3_low, point_ref[...]) * (gates + batched * gates * (1.0 - gates))
        small_ref[1:2, :] += column_sum(d_batched * normed)
        small_ref[2:3, :] += column_sum(d_batched)
        d_z = d_batched * batch_ref[0:1, :]
        dz_ref[at, :] = d_z
        sums[0:1, :] += column_sum(d_z)
        sums[1:2, :] += column_sum(d_z * centred)

    loop(length // BLOCK, step)
    spread_rows(sums, sums_ref)


def conv_back_kernel(
    starts_ref, conv_ref, dz_ref, stats_ref, dsums_ref, d3_ref, h2_ref, gains_ref, dense_ref, taps_ref,
    d2_ref, d2low_ref, dcontext_ref, n3_ref, dg_ref, small_ref, dtaps_ref, padded, linear,
):
    length, width = h2_ref.shape
    unused, unused, mix_ref, unused, point_ref = dense_parts(dense_ref)
    taps = taps_ref.shape[0] - 1
    reach = taps // 2
    frames = starts_ref[0, starts_ref.shape[1] - 1]
    small_ref[...] = jnp.zeros_like(small_ref)
    dtaps_ref[...] = jnp.zeros_like(dtaps_ref)
    mean, batch_inverse, count = stats_ref[0:1, :], stats_ref[1:2, :], stats_ref[2:3, :]
    dsums = jnp.sum(dsums_ref[...], axis=0)
    d_variance = -0.5 * batch_inverse * batch_inverse * batch_inverse * dsums[:, width:]
    padded[:EDGE, :] = jnp.zeros((EDGE, width), f32)
    padded[EDGE + length :, :] = jnp.zeros((EDGE, width), f32)

    def conv_step(index):
        at = rows_at(index, BLOCK)
        centred = conv_ref[at, :] - mean
        inside = (iota((BLOCK, 1), 0) + index * BLOCK) < frames
        shared = (2.0 * d_variance * centred - batch_inverse * dsums[:, :width]) / count
        d_conv = batch_inverse * dz_ref[at, :] + jnp.where(inside, shared, 0.0)
        padded[pl.ds(pl.multiple_of(index * BLOCK + EDGE, EDGE), BLOCK), :] = d_conv
        standard, unused = normalize(h2_ref[at, :])
        low = (standard * gains_ref[2:3, :]).astype(bf16)
        n3_ref[at, :] = low
        value = dot(low, point_ref[:, :width])
        linear[at, :width] = value
        linear[at, width:] = sigmoid(dot(low, point_ref[:, width:]))

    loop(length // BLOCK, conv_step)

    def turn_step(index):
        first = index * TILE
        at = rows_at(index, TILE)
        place = iota((TILE, TILE), 0) + first
        here = numbers_at(starts_ref, place)
        parts = width // TILE
        totals = [jnp.zeros((TILE, TILE), f32) for unused in range(parts)]
        values = [linear[at, part * TILE : (part + 1) * TILE] for part in range(parts)]
        gates = [linear[at, width + part * TILE : width + (part + 1) * TILE] for part in range(parts)]
        around = pl.ds(pl.multiple_of(first, TILE), TILE + 2 * EDGE)
        for tap in range(taps):
            same = numbers_at(starts_ref, place - (tap - reach)) == here
            for part in range(parts):
                lanes = slice(part * TILE, (part + 1) * TILE)
                near = padded[around, lanes][EDGE - tap + reach : EDGE - tap + reach + TILE]
                near = jnp.where(same, near, 0.0)
                totals[part] = totals[part] + near * taps_ref[tap : tap + 1, lanes]
                dtaps_ref[tap : tap + 1, lanes] += column_sum(near * (values[part] * gates[part]))
        for part in range(parts):
            lanes = slice(part * TILE, (part + 1) * TILE)
            other = slice(width + part * TILE, width + (part + 1) * TILE)
            gate = gates[part]
            dg_ref[at, lanes] = (totals[part] * gate).astype(bf16)
            dg_ref[at, other] = (totals[part] * values[part] * gate * (1.0 - gate)).astype(bf16)

    loop(length // TILE, turn_step)

    def gates_step(index):
        at = rows_at(index, BLOCK)
        d_norm = dot_t(dg_ref[at, :], point_ref[...])
        standard, inverse = normalize(h2_ref[at, :])
        small_ref[0:1, :] += column_sum(d_norm * standard)
        d2 = d3_ref[at, :] + normalize_back(standard, inverse, gains_ref[2:3, :], d_norm)
        d2_ref[at, :] = d2
        low = d2.astype(bf16)
        d2low_ref[at, :] = low
        dcontext_ref[at, :] = dot_t(low, mix_ref[...]).astype(bf16)

    loop(length // BLOCK, gates_step)


def attend_back_kernel(
    starts_ref, d2_ref, dcontext_ref, h1_ref, gains_ref, dense_ref, sinus_ref, qu_ref, qv_ref, k_ref, v_ref,
    t_ref, context_ref, logs_ref, cols_ref, gate_ref, probs_ref, slot_row_ref, *refs,
):
    returned_refs, out_refs, refs = refs[:PARTS], refs[PARTS : 2 * PARTS], refs[2 * PARTS :]
    d1_ref, dlogits_ref, n2_ref, dm_ref, dtable_ref, small_ref = refs[:6]
    low_ref, mirrored_ref, returned_ref, dk_ref, dv_ref, dt_ref = refs[6:12]
    attend = refs[12:]
    length, width = h1_ref.shape
    in_ref, place_ref, unused, unused, unused = dense_parts(dense_ref)
    small_ref[...] = jnp.zeros_like(small_ref)
    join_blocks(returned_refs, returned_ref)

    def table_step(index):
        at = rows_at(index, BLOCK)
        table_at = pl.ds(pl.multiple_of(index * BLOCK + edge, TILE), BLOCK)
        mirrored_ref[table_at, :] = dot(sinus_ref[at, :], place_ref[...]).astype(bf16)

    edge = PAD * TILE
    mirrored_ref[:edge, :] = jnp.zeros((edge, width), bf16)
    mirrored_ref[edge + length :, :] = jnp.zeros((edge, width), bf16)
    loop(length // BLOCK, table_step)
    attend_backward(
        starts_ref, qu_ref, qv_ref, k_ref, v_ref, t_ref, mirrored_ref, context_ref, logs_ref, dcontext_ref,
        dm_ref, dk_ref, dv_ref, dt_ref, small_ref.at[pl.ds(8, 8)], *attend
    )

    def queries_step(index):
        at = rows_at(index, BLOCK)
        d_norm = dot_t(dm_ref[at, :], in_ref[...])
        standard, inverse = normalize(h1_ref[at, :])
        gain = gains_ref[1:2, :]
        n2_ref[at, :] = (standard * gain).astype(bf16)
        small_ref[1:2, :] += column_sum(d_norm * standard)
        d1 = d2_ref[at, :] + normalize_back(standard, inverse, gain, d_norm)
        d1_ref[at, :] = d1
        picked = collect(cols_ref[at, 0:1], returned_ref)
        gate = gate_ref[at, :]
        dlogits_ref[at, :] = gate_back(d1, picked, gate, probs_ref[at, :], cols_ref[at, 2:3])
        low_ref[at, :] = (0.5 * gate * d1).astype(bf16)

    loop(length // BLOCK, queries_step)
    dtable_ref[...] = dt_ref[:, PAD * TILE : PAD * TILE + length].astype(bf16)
    dispatch(low_ref, slot_row_ref[0:1, :], out_refs)


def last_kernel(
    cols_ref, dlogits_ref, hidden_ref, d1_ref, embed_ref, router_ref, gains_ref, dembed_two_ref,
    drouter_two_ref, mid_ref, conv_ref, two_ref, five_ref, taps_ref, *refs,
):
    dsent_refs, refs = refs[:PARTS], refs[PARTS:]
    d0_ref, dembed_ref, routers_ref, small_ref, dsent_ref = refs
    length = hidden_ref.shape[0]
    taps = small_ref.shape[0] - 9
    join_blocks(dsent_refs, dsent_ref)
    drouter_ref = routers_ref.at[pl.ds(0, 8)]
    drouter_ref[...] = jnp.zeros_like(drouter_ref)
    routers_ref[8:, :] = drouter_two_ref[...]
    small_ref[0:1, :] = jnp.zeros_like(small_ref[0:1, :])
    small_ref[1:2, :] = mid_ref[1:2, :]
    small_ref[2:3, :] = conv_ref[0:1, :]
    small_ref[3:4, :] = two_ref[0:1, :]
    small_ref[4:5, :] = five_ref[0:1, :]
    small_ref[5:7, :] = mid_ref[8:10, :]
    small_ref[7 : 7 + taps, :] = taps_ref[:taps, :]
    small_ref[7 + taps :, :] = two_ref[1:3, :]

    def step(index):
        at = rows_at(index, BLOCK)
        standard, inverse = normalize(hidden_ref[at, :].astype(f32))
        gain = gains_ref[0:1, :]
        low = (standard * gain).astype(bf16)
        d_low, d_embed = router_back(
            dlogits_ref[at, :], low, embed_ref[at, :], router_ref, drouter_ref
        )
        dembed_ref[at, :] = d_embed + dembed_two_ref[at, :]
        d_norm = collect(cols_ref[at, 0:1], dsent_ref) + d_low
        small_ref[0:1, :] += column_sum(d_norm * standard)
        d0_ref[at, :] = d1_ref[at, :] + normalize_back(standard, inverse, gain, d_norm)

    loop(length // BLOCK, step)


def gather_small(values):
    return lax.all_to_all(values, BOTH, split_axis=0, concat_axis=0, tiled=True)


def across(values, axis, size, offset):
    if not offset:
        return values
    return lax.ppermute(values, axis, [(i, i ^ offset) for i in range(size)])


def exchange(blocks, experts):
    per = experts // PARTS
    moved = []
    for index, block in enumerate(blocks):
        rows = block.shape[0] // per
        pieces = []
        for k in range(index * per, (index + 1) * per):
            piece = block[(k - index * per) * rows : (k - index * per + 1) * rows]
            pieces.append(across(piece, "expert", experts, k))
        moved.append(pieces[0] if per == 1 else jnp.concatenate(pieces, axis=0))
    return moved


def ring_place(index, size):
    return jnp.where(index % 2 == 0, index // 2, size - 1 - index // 2)


def ring_member(place, size):
    place = (place + 2 * size) % size
    return jnp.where(place < size // 2, 2 * place, 2 * (size - 1 - place) + 1)


def ring_pairs(size, forward):
    order = list(range(0, size, 2)) + list(range(size - 1, 0, -2))
    step = 1 if forward else -1
    return [(order[k], order[(k + step) % size]) for k in range(size)]


def ring_gather(shards, size):
    found = []
    for number, shard in enumerate(shards):
        ahead = size // 2 if number % 2 == 0 else (size - 1) // 2
        pieces = [None] * size
        pieces[0] = shard
        found.append((pieces, ahead))
    for step in range(1, size // 2 + 1):
        for pieces, ahead in found:
            if step <= ahead:
                pieces[step] = lax.ppermute(pieces[step - 1], "dp", ring_pairs(size, False))
            if step <= size - 1 - ahead:
                pieces[-step] = lax.ppermute(pieces[-step + 1 or 0], "dp", ring_pairs(size, True))
    return [pieces for pieces, unused in found]


def assemble_kernel(count, order_ref, *refs):
    size = (len(refs) - 1 - count) // count
    sems = refs[-1]
    copies = []
    for number in range(count):
        target = refs[count * size + number]
        for offset in range(size):
            piece = refs[number * size + offset]
            rows = piece.shape[0]
            start = pl.multiple_of(order_ref[offset] * rows, 16)
            copies.append(
                pltpu.make_async_copy(
                    piece, target.at[pl.ds(start, rows)], sems.at[number * size + offset]
                )
            )
    for copy in copies:
        copy.start()
    for copy in copies:
        copy.wait()


def assemble(shards, size):
    place = ring_place(lax.axis_index("dp"), size)
    order = ring_member(place + jnp.arange(size, dtype=jnp.int32), size).astype(jnp.int32)
    groups = ring_gather(shards, size)
    count = len(groups)
    anywhere = pl.BlockSpec(memory_space=pl.ANY)
    return pl.pallas_call(
        functools.partial(assemble_kernel, count),
        out_shape=[
            shape_of((size * shard.shape[0],) + shard.shape[1:], shard.dtype) for shard in shards
        ],
        in_specs=[SMEM] + [anywhere] * (count * size),
        out_specs=[VMEM] * count,
        scratch_shapes=[pltpu.SemaphoreType.DMA((count * size,))],
        name="assemble",
    )(order, *[piece for pieces in groups for piece in pieces])


def keep_half(values, axis, bit, size, offset, mesh_axis):
    mine = lax.dynamic_index_in_dim(values, bit, axis, keepdims=False)
    theirs = lax.dynamic_index_in_dim(values, 1 - bit, axis, keepdims=False)
    arrived = across(theirs, mesh_axis, size, offset)
    return (mine.astype(f32) + arrived.astype(f32)).astype(bf16)


def own_parts(values, place, size, stride, mesh_axis):
    parts = [lax.dynamic_index_in_dim(values, place, 0, keepdims=False)]
    for k in range(1, values.shape[0]):
        theirs = lax.dynamic_index_in_dim(values, place ^ k, 0, keepdims=False)
        parts.append(across(theirs, mesh_axis, size, k * stride))
    return parts


def add_up(parts):
    total = parts[0].astype(f32)
    for part in parts[1:]:
        total = total + part.astype(f32)
    return total


def keep_one(values, place, size, stride, mesh_axis):
    return add_up(own_parts(values, place, size, stride, mesh_axis))


def near_half(values):
    groups = values.shape[0]
    values = values.reshape((groups // 2, 2) + values.shape[1:])
    return keep_half(values, 1, lax.axis_index("dp") % 2, groups, 1, "dp")


def expert_parts(values, experts):
    me = lax.axis_index("expert")
    return [
        across(lax.dynamic_index_in_dim(values, me ^ k, 1, keepdims=False), "expert", experts, k)
        for k in range(experts)
    ]


def rows_product(left, right):
    return lax.dot_general(left, right, (((0,), (0,)), ((), ())), preferred_element_type=f32)


def blocks_product(left, right):
    left, right = jnp.concatenate(left, axis=0), jnp.concatenate(right, axis=0)
    return rows_product(left, right).astype(bf16)


def scatter_offloaded(grad_in, grad_out):
    return (
        lax.psum_scatter(grad_in, "dp", scatter_dimension=0, tiled=True).astype(f32)[None],
        lax.psum_scatter(grad_out, "dp", scatter_dimension=0, tiled=True).astype(f32)[None],
    )


def split_columns(values):
    middle = values.shape[1] // 2
    return [values[:, :middle], values[:, middle:]]


def sinus_rows(length, width, upward):
    distance = (length // 2 - 1 - np.arange(length)).astype(np.float32)
    distance = distance[::-1] if upward else distance
    rates = np.exp(
        np.arange(width // 2).astype(np.float32) * np.float32(-2.0 * math.log(10000.0) / width)
    ).astype(np.float32)
    angles = (distance[:, None] * rates[None, :]).astype(np.float64)
    table = np.concatenate([np.sin(angles), np.cos(angles)], axis=1)
    return jnp.asarray(table.astype(np.float32)).astype(bf16)


def body(
    groups,
    inputs,
    embedding,
    cotangent,
    first_routes,
    second_routes,
    segment_starts,
    norm_gains,
    first_router,
    second_router,
    first_in,
    first_out,
    second_in,
    second_out,
    attention_in,
    position_weight,
    position_bias,
    attention_out,
    pointwise_in,
    depthwise_kernel,
    batch_gain,
    batch_bias,
    pointwise_out,
):
    length, width = inputs.shape
    experts = first_router.shape[1]
    devices = groups * experts
    capacity = 17 * length // (16 * experts)
    slots = experts * capacity
    inner = first_in.shape[2]
    share = norm_gains.shape[1]
    taps = depthwise_kernel.shape[0]
    feats = first_router.shape[0]

    rows = jnp.concatenate(
        [norm_gains, position_bias, depthwise_kernel, batch_gain[None], batch_bias[None]], axis=0
    )
    count = rows.shape[0]
    flat = jnp.concatenate(
        [rows.reshape(-1), first_router.T.reshape(-1), second_router.T.reshape(-1)]
    ).astype(f32)
    small = gather_small(jnp.broadcast_to(flat[None], (devices,) + flat.shape))
    rows_all = small[:, : count * share].reshape(devices, count, share)
    rows_all = rows_all.transpose(1, 0, 2).reshape(count, devices * share)
    routers = small[:, count * share :].reshape(devices, 2, experts, feats)
    routers = routers.transpose(1, 2, 0, 3).reshape(2, experts, devices * feats)
    routers = jnp.pad(routers, ((0, 0), (0, TILE - experts), (0, 0)))
    routers = routers.transpose(0, 2, 1).astype(bf16)
    gains = jnp.pad(rows_all[0:5], ((0, 3), (0, 0)))
    bias = jnp.pad(rows_all[5:7], ((0, 6), (0, 0)))
    kernel_taps = jnp.pad(rows_all[7 : 7 + taps], ((0, 1), (0, 0)))
    batch = jnp.pad(rows_all[7 + taps : 9 + taps], ((0, 6), (0, 0)))

    packed = jnp.concatenate(
        [attention_in, position_weight, attention_out, pointwise_out, pointwise_in], axis=1
    )
    dense = lax.all_gather(packed, BOTH, axis=0, tiled=True)
    point_out = dense[:, 5 * width : 6 * width]

    first_pair = assemble((first_in[0], first_out[0]), groups)
    second_pair = (
        lax.all_gather(second_in[0], "dp", axis=0, tiled=True),
        lax.all_gather(second_out[0], "dp", axis=0, tiled=True),
    )

    me = lax.axis_index("expert")
    slot_rows, slot_cols = find_slots(first_routes, second_routes, me, capacity)
    sinus = sinus_rows(length, width, False)
    mirrored = sinus_rows(length, width, True)
    row_low = shape_of((length, width), bf16)
    row_full = shape_of((length, width), f32)
    lane_full = shape_of((length, TILE), f32)
    table_low = shape_of((length + 2 * PAD * TILE, width), bf16)
    block_low = shape_of((slots // PARTS, width), bf16)
    slots_scratch = pltpu.VMEM((slots, width), bf16)
    sums_scratch = pltpu.VMEM((8, width), f32)
    column = shape_of((length, 1), f32)
    eight = shape_of((8, width), f32)
    low_scratch = pltpu.VMEM((length, width), bf16)

    *sent_one, probs_one, gate_one = run(
        functools.partial(front_kernel, experts),
        (inputs, embedding, gains, routers[0], slot_cols, slot_rows),
        [VMEM] * 6,
        [block_low] * PARTS + [lane_full, column],
        [low_scratch],
        flops=4 * slots * length * width,
        name="front",
    )
    received_one = exchange(sent_one, experts)
    result_one = forward_in_turn(received_one, first_pair)
    returned_one = exchange(result_one, experts)

    edge_scratch = pltpu.VMEM((length + 2 * EDGE, width), f32)
    (
        h1, h2, query_u, query_v, keys, values, table, context, logs, convolved, sums,
    ) = run(
        middle_kernel,
        (
            segment_starts, inputs, slot_cols, gate_one, gains, dense, bias, kernel_taps, sinus,
            *returned_one,
        ),
        [SMEM] + [VMEM] * (8 + PARTS),
        [row_full, row_full]
        + [row_low] * 4
        + [table_low, row_low, lane_full, row_full, shape_of((devices, 1, 3 * width), f32)],
        [edge_scratch, sums_scratch, slots_scratch] + attend_scratch(length),
        flops=16 * length * length * width,
        name="middle",
    )
    totals = gather_small(sums)

    *sent_two, h3, active, probs_two, gate_two, stats = run(
        functools.partial(second_kernel, experts),
        (
            h2, convolved, totals, batch, point_out, embedding, gains, routers[1], slot_cols, slot_rows,
        ),
        [VMEM] * 10,
        [block_low] * PARTS + [row_full, row_low, lane_full, column, eight],
        [low_scratch],
        flops=4 * slots * length * width,
        name="second",
    )
    received_two = exchange(sent_two, experts)
    result_two = forward_in_turn(received_two, second_pair)
    returned_two = exchange(result_two, experts)

    *d_sent_two, output, d4, dlogits_two, dgain_five = run(
        turn_kernel,
        (
            h3, slot_cols, gate_two, probs_two, slot_rows, gains, cotangent, *returned_two,
        ),
        [VMEM] * (7 + PARTS),
        [block_low] * PARTS + [row_low, row_full, lane_full, eight],
        [low_scratch, slots_scratch],
        flops=4 * slots * length * width,
        name="turn",
    )
    d_result_two = exchange(d_sent_two, experts)
    unused, d_received_two, hidden_two, d_inner_two = backward_in_turn(
        received_two, d_result_two, second_pair
    )
    d_back_two = exchange(d_received_two, experts)
    grad_in_two, grad_out_two, *d_back_two = lax.optimization_barrier(
        (
            blocks_product(received_two, d_inner_two), blocks_product(hidden_two, d_result_two), *d_back_two,
        )
    )
    d_second_in, d_second_out = scatter_offloaded(grad_in_two, grad_out_two)

    router_shape = shape_of((8, 2 * width), f32)
    d3, d3_low, d_z, dembed_two, drouter_two, small_two, dsums_part = run(
        second_back_kernel,
        (
            slot_cols, dlogits_two, h3, d4, embedding, routers[1], gains, convolved, stats, batch, point_out,
            *d_back_two,
        ),
        [VMEM] * (11 + PARTS),
        [row_full, row_low, row_full, row_full, router_shape, eight, shape_of((devices, 1, 2 * width), f32)],
        [sums_scratch, slots_scratch],
        flops=4 * slots * length * width,
        name="second_back",
    )
    dsums = gather_small(dsums_part)
    d_pointwise_out = rows_product(active, d3_low)

    d2, d2_low, d_context, normed_three, d_gates, small_conv, d_taps = run(
        conv_back_kernel,
        (segment_starts, convolved, d_z, stats, dsums, d3, h2, gains, dense, kernel_taps),
        [SMEM] + [VMEM] * 9,
        [
            row_full, row_low, row_low, row_low, shape_of((length, 2 * width), bf16), eight,
            shape_of((16, width), f32),
        ],
        [edge_scratch, pltpu.VMEM((length, 2 * width), f32)],
        flops=6 * length * width * width,
        name="conv_back",
    )
    value_grad, gates_grad = split_columns(rows_product(normed_three, d_gates))
    early = jnp.stack(
        [
            part.astype(bf16).reshape(groups, experts, width // devices, width)
            for part in (rows_product(context, d2_low), d_pointwise_out, value_grad, gates_grad)
        ],
        axis=2,
    )
    early = expert_parts(early, experts)
    *d_sent_one, d1, dlogits_one, normed_two, d_mixed, d_table, small_mid = run(
        attend_back_kernel,
        (
            segment_starts, d2, d_context, h1, gains, dense, mirrored, query_u, query_v, keys, values, table,
            context, logs, slot_cols, gate_one, probs_one, slot_rows, *returned_one,
        ),
        [SMEM] + [VMEM] * (17 + PARTS),
        [block_low] * PARTS
        + [
            row_full, lane_full, row_low, shape_of((length, 3 * width), bf16),
            shape_of((width, length), bf16), shape_of((16, width), f32),
        ],
        [
            low_scratch, pltpu.VMEM(table_low.shape, bf16), slots_scratch,
            pltpu.VMEM((width, length), f32), pltpu.VMEM((width, length), f32),
            pltpu.VMEM((width, length + 2 * PAD * TILE), f32),
        ]
        + attend_back_scratch(),
        flops=32 * length * length * width,
        name="attend_back",
    )
    early, *d_sent_one = lax.optimization_barrier((early, *d_sent_one))
    d_result_one = exchange(d_sent_one, experts)
    (late,), d_received_one, hidden_one, d_inner_one = backward_in_turn(
        received_one, d_result_one, first_pair, (normed_two, d_mixed, d_table, mirrored)
    )
    late = expert_parts(late.reshape(groups, experts, width // devices, 4 * width), experts)
    d_back_one = exchange(d_received_one, experts)
    early = add_up(early).astype(bf16).reshape(groups, -1, width)
    grad_out = blocks_product(hidden_one, d_result_one).reshape(groups, -1, width)
    near_out = near_half(jnp.concatenate([grad_out, early], axis=1))
    grad_in = blocks_product(received_one, d_inner_one).reshape(groups, -1, inner)
    near_out, grad_in, late, d_second_in, d_second_out, d_back_one = lax.optimization_barrier(
        (near_out, grad_in, late, d_second_in, d_second_out, d_back_one)
    )
    far_out = own_parts(near_out, lax.axis_index("dp") // 2, groups, 2, "dp")
    late = add_up(late).astype(bf16)
    near_in = near_half(jnp.concatenate([grad_in, late], axis=1))
    d_start, d_embed, routers_grad, rows_grad = run(
        last_kernel,
        (
            slot_cols, dlogits_one, inputs, d1, embedding, routers[0], gains, dembed_two,
            drouter_two, small_mid, small_conv, small_two, dgain_five, d_taps, *d_back_one,
        ),
        [VMEM] * (14 + PARTS),
        [row_full, row_full, shape_of((16, 2 * width), f32), shape_of((count, width), f32)],
        [slots_scratch],
        flops=4 * slots * length * width,
        name="last",
    )

    near_in, far_out, routers_grad, rows_grad = lax.optimization_barrier(
        (near_in, far_out, routers_grad, rows_grad)
    )
    out_sum = add_up(far_out)
    in_sum = add_up(own_parts(near_in, lax.axis_index("dp") // 2, groups, 2, "dp"))
    d_first_out = out_sum[None, : first_out.shape[1]]
    d_first_in = in_sum[None, : first_in.shape[1]]
    late_share = in_sum[first_in.shape[1] :]
    early_share = out_sum[first_out.shape[1] :].reshape(4, width // devices, width)
    early_share = jnp.concatenate([early_share[k] for k in range(4)], axis=1)
    rows_grad = rows_grad.reshape(count, devices, share).transpose(1, 0, 2).reshape(devices, -1)
    routers_grad = routers_grad.reshape(2, 8, devices, feats)[:, :experts]
    routers_grad = routers_grad.transpose(2, 0, 1, 3).reshape(devices, -1)
    small_grad = jnp.concatenate([rows_grad, routers_grad], axis=1)
    small_share = jnp.sum(
        lax.all_to_all(small_grad, BOTH, split_axis=0, concat_axis=0, tiled=True), axis=0
    )
    rows_share = small_share[: count * share].reshape(count, share)
    routers_share = small_share[count * share :].reshape(2, experts, feats).transpose(0, 2, 1)

    return (
        output,
        d_start,
        d_embed,
        rows_share[0:5],
        routers_share[0],
        routers_share[1],
        d_first_in,
        d_first_out,
        d_second_in,
        d_second_out,
        late_share[:, : 3 * width],
        late_share[:, 3 * width :],
        rows_share[5:7],
        early_share[:, :width],
        early_share[:, 2 * width :],
        rows_share[7 : 7 + taps],
        rows_share[7 + taps],
        rows_share[8 + taps],
        early_share[:, width : 2 * width],
    )


def solution(mesh):
    split = P(BOTH, None)
    wide = P(None, BOTH)
    bank = P("expert", "dp", None)
    line = P(BOTH)
    in_specs = (
        (split,) * 6
        + (wide, split, split)
        + (bank,) * 4
        + (split, split, wide, split, split, wide, line, line, split)
    )
    out_specs = (
        (split,) * 3
        + (wide, split, split)
        + (bank,) * 4
        + (split, split, wide, split, split, wide, line, line, split)
    )
    return jax.shard_map(
        functools.partial(body, mesh.shape["dp"]),
        mesh=mesh,
        in_specs=in_specs,
        out_specs=out_specs,
        check_vma=False,
    )
```

```python
import functools
import math

import jax
import jax.numpy as jnp
import numpy as np
from jax import lax
from jax.experimental import pallas as pl
from jax.experimental.pallas import tpu as pltpu
from jax.sharding import PartitionSpec as P

H = 8
TILE = 128
epsilon = 1e-05
masked_score = -1e30
BOTH = ("dp", "expert")
f32 = jnp.float32
bf16 = jnp.bfloat16

VMEM = pl.BlockSpec(memory_space=pltpu.VMEM)
SMEM = pl.BlockSpec(memory_space=pltpu.SMEM)


def shape_of(dims, kind):
    return jax.ShapeDtypeStruct(dims, kind)


def run(kernel, args, in_specs, outs, scratch=(), flops=0, name=None, limit=56):
    moved = sum(math.prod(a.shape) * a.dtype.itemsize for a in list(args) + list(outs))
    results = pl.pallas_call(
        kernel,
        out_shape=outs,
        in_specs=in_specs,
        out_specs=[VMEM] * len(outs),
        scratch_shapes=list(scratch),
        compiler_params=pltpu.CompilerParams(vmem_limit_bytes=limit * 2**20),
        cost_estimate=pl.CostEstimate(flops=flops, bytes_accessed=moved, transcendentals=0),
        name=name,
    )(*args)
    return list(results)


def dot(left, right):
    return lax.dot_general(left, right, (((1,), (0,)), ((), ())), preferred_element_type=f32)


def dot_t(left, right):
    return lax.dot_general(left, right, (((1,), (1,)), ((), ())), preferred_element_type=f32)


def t_dot(left, right):
    return lax.dot_general(left, right, (((0,), (0,)), ((), ())), preferred_element_type=f32)


def iota(dims, axis):
    return lax.broadcasted_iota(jnp.int32, dims, axis)


def normalize(values):
    center = values - jnp.mean(values, axis=-1, keepdims=True)
    spread = jnp.mean(center * center, axis=-1, keepdims=True)
    inverse = lax.rsqrt(spread + epsilon)
    return center * inverse, inverse


def normalize_back(standard, inverse, gain, upstream):
    scaled = upstream * gain
    first = jnp.mean(scaled, axis=-1, keepdims=True)
    second = jnp.mean(scaled * standard, axis=-1, keepdims=True)
    return inverse * (scaled - first - standard * second)


def column_sum(values):
    return jnp.sum(values, axis=0, keepdims=True)


def sigmoid(values):
    return 1.0 / (1.0 + jnp.exp(-values))


def loop(count, body):
    def step(index, carry):
        body(index)
        return carry

    lax.fori_loop(0, count, step, 0)


def rows_at(index, size):
    return pl.ds(pl.multiple_of(index * size, size), size)


def slots_kernel(capacity, offset_ref, one_ref, two_ref, rows_ref, cols_ref, stack):
    length = rows_ref.shape[1]
    block = 256
    stack[...] = jnp.zeros_like(stack)
    for half, chosen_ref in enumerate((one_ref, two_ref)):
        chosen = chosen_ref[...]
        near = chosen ^ offset_ref[0]
        onehot = jnp.where(iota((8, length), 0) == near, 1.0, 0.0)
        onehot_low = onehot.astype(bf16)
        for index in range(length // block):
            earlier = iota((length, block), 0) < iota((length, block), 1) + index * block
            counts = dot(onehot_low, jnp.where(earlier, 1.0, 0.0).astype(bf16))
            span = slice(index * block, (index + 1) * block)
            rank = column_sum(onehot[:, span] * counts)
            stack[half : half + 1, span] = (near[:, span] * capacity).astype(f32) + rank
        stack[2 + half : 3 + half, :] = chosen.astype(f32)
    rows_ref[...] = stack[:8, :].astype(jnp.int32)
    for index in range(length // TILE):
        span = slice(index * TILE, (index + 1) * TILE)
        cols_ref[span, :] = jnp.transpose(stack[:, span]).astype(jnp.int32)


def find_slots(routes_one, routes_two, offset, capacity):
    length = routes_one.shape[0]
    return run(
        functools.partial(slots_kernel, capacity),
        (offset.reshape(1), routes_one.reshape(1, length), routes_two.reshape(1, length)),
        [SMEM, VMEM, VMEM],
        [shape_of((8, length), jnp.int32), shape_of((length, TILE), jnp.int32)],
        [pltpu.VMEM((TILE, length), f32)],
        flops=8 * length * length * 128,
        name="slots",
    )


PARTS = 4


def dispatch(low_ref, slot_row, out_refs):
    block = out_refs[0].shape[0]
    length = low_ref.shape[0]
    for index, out_ref in enumerate(out_refs):
        ids = iota((block, length), 0) + index * block
        onehot = jnp.where(ids == slot_row, 1.0, 0.0).astype(bf16)
        out_ref[...] = dot(onehot, low_ref[...]).astype(bf16)


def join_blocks(block_refs, whole_ref):
    block = block_refs[0].shape[0]
    for index, block_ref in enumerate(block_refs):
        whole_ref[index * block : (index + 1) * block, :] = block_ref[...]


def collect(slot_col, table_ref):
    rows = slot_col.shape[0]
    slots = table_ref.shape[0]
    onehot = jnp.where(iota((rows, slots), 1) == slot_col, 1.0, 0.0).astype(bf16)
    return dot(onehot, table_ref[...])


def route_block(low, embed, router_ref, picks, experts):
    width = low.shape[1]
    logits = dot(low, router_ref[:width, :]) + dot(embed, router_ref[width:, :])
    lanes = iota(logits.shape, 1)
    inside = lanes < experts
    logits = jnp.where(inside, logits, masked_score)
    raised = jnp.where(inside, jnp.exp(logits - jnp.max(logits, axis=1, keepdims=True)), 0.0)
    probs = raised / jnp.sum(raised, axis=1, keepdims=True)
    gate = jnp.sum(jnp.where(lanes == picks, probs, 0.0), axis=1, keepdims=True)
    return probs, gate


BLOCK = 256


def front_kernel(
    experts, hidden_ref, embed_ref, gain_ref, router_ref, cols_ref, slot_row_ref, *refs,
):
    out_refs, (probs_ref, gate_ref, low_ref) = refs[:PARTS], refs[PARTS:]
    length = hidden_ref.shape[0]

    def step(index):
        at = rows_at(index, BLOCK)
        standard, unused = normalize(hidden_ref[at, :].astype(f32))
        low = (standard * gain_ref[0:1, :]).astype(bf16)
        low_ref[at, :] = low
        probs, gate = route_block(low, embed_ref[at, :], router_ref, cols_ref[at, 2:3], experts)
        probs_ref[at, :] = probs
        gate_ref[at, :] = gate

    loop(length // BLOCK, step)
    dispatch(low_ref, slot_row_ref[0:1, :], out_refs)


def expert_forward_kernel(count, in_ref, out_ref, *refs):
    for x_ref, y_ref in zip(refs[:count], refs[count:]):
        inner = dot(x_ref[...], in_ref[...])
        hidden = (inner * sigmoid(inner)).astype(bf16)
        y_ref[...] = dot(hidden, out_ref[...]).astype(bf16)


def expert_forward(received, weight_in, weight_out):
    block, width = received[0].shape
    count = len(received)
    return run(
        functools.partial(expert_forward_kernel, count),
        (weight_in, weight_out) + tuple(received),
        [VMEM] * (2 + count),
        [shape_of((block, width), bf16)] * count,
        flops=4 * count * block * width * weight_in.shape[1],
        name="experts",
        limit=32,
    )


def forward_in_turn(received, pair):
    near, far = lax.optimization_barrier((expert_forward(received[:2], *pair), received[2:]))
    return near + expert_forward(far[:1], *pair) + expert_forward(far[1:], *pair)


def expert_backward_kernel(count, in_ref, out_ref, *refs):
    x_refs, dy_refs, refs = refs[:count], refs[count : 2 * count], refs[2 * count :]
    extra, refs = refs[: len(refs) - 3 * count], refs[len(refs) - 3 * count :]
    if extra:
        normed_ref, mixed_ref, table_ref, sinus_ref, grad_ref = extra
        width = normed_ref.shape[1]
        for part in range(3):
            lanes = slice(part * width, (part + 1) * width)
            grad_ref[:, lanes] = t_dot(normed_ref[...], mixed_ref[:, lanes]).astype(bf16)
        grad_ref[:, 3 * width :] = jnp.transpose(dot(table_ref[...], sinus_ref[...])).astype(bf16)
    dx_refs, hidden_refs, dinner_refs = refs[:count], refs[count : 2 * count], refs[2 * count :]
    for x_ref, dy_ref, dx_ref, hidden_ref, dinner_ref in zip(
        x_refs, dy_refs, dx_refs, hidden_refs, dinner_refs
    ):
        inner = dot(x_ref[...], in_ref[...])
        gates = sigmoid(inner)
        hidden = inner * gates
        hidden_ref[...] = hidden.astype(bf16)
        d_hidden = dot_t(dy_ref[...], out_ref[...])
        d_inner = (d_hidden * (gates + hidden * (1.0 - gates))).astype(bf16)
        dinner_ref[...] = d_inner
        dx_ref[...] = dot_t(d_inner, in_ref[...]).astype(bf16)


def expert_backward(received, d_result, weight_in, weight_out, extra=()):
    block, width = received[0].shape
    inner = weight_in.shape[1]
    count = len(received)
    more = [shape_of((width, 4 * width), bf16)] if extra else []
    outs = run(
        functools.partial(expert_backward_kernel, count),
        (weight_in, weight_out) + tuple(received) + tuple(d_result) + tuple(extra),
        [VMEM] * (2 + 2 * count + len(extra)),
        more + [shape_of((block, width), bf16)] * count + [shape_of((block, inner), bf16)] * (2 * count),
        flops=6 * count * block * width * inner,
        name="experts_back",
        limit=48 if extra else 40,
    )
    more, outs = outs[: len(more)], outs[len(more) :]
    return more, outs[:count], outs[count : 2 * count], outs[2 * count :]


def backward_in_turn(received, d_result, pair, extra=()):
    near, far = lax.optimization_barrier(
        (expert_backward(received[:2], d_result[:2], *pair, extra), d_result[2:])
    )
    parts = [
        near,
        expert_backward(received[2:3], far[:1], *pair),
        expert_backward(received[3:], far[1:], *pair),
    ]
    return [sum((list(part[k]) for part in parts), []) for k in range(4)]


def tile_window(starts_ref, first, length):
    count = starts_ref.shape[1]
    low = jnp.int32(0)
    high = jnp.int32(length)
    for k in range(1, count):
        low = jnp.where(starts_ref[0, k] <= first, starts_ref[0, k], low)
    for k in range(count - 1, 0, -1):
        high = jnp.where(starts_ref[0, k] > first + (TILE - 1), starts_ref[0, k], high)
    low = low // TILE
    steps = ((high + (TILE - 1)) // TILE - low + 1) // 2
    return jnp.minimum(low, length // TILE - 2 * steps), steps


def numbers_at(starts_ref, positions):
    total = jnp.zeros(positions.shape, jnp.int32)
    for k in range(1, starts_ref.shape[1]):
        total = total + jnp.where(positions >= starts_ref[0, k], 1, 0)
    return total


def same_tile(starts_ref, first_query, first_key):
    rows = numbers_at(starts_ref, iota((TILE, TILE), 0) + first_query)
    cols = numbers_at(starts_ref, iota((TILE, TILE), 1) + first_key)
    return rows == cols


PAD = 2


def chunk_rows(query_tile, key_tile, length, count, mirrored=False):
    tiles = length // TILE
    index = tiles - 1 - query_tile + key_tile - (tiles // 2 - PAD)
    if mirrored:
        index = tiles + 2 * PAD - count - index
    index = jnp.clip(index, 0, tiles + 2 * PAD - count)
    return pl.ds(pl.multiple_of(index * TILE, TILE), count * TILE)


def halves(values):
    left = iota(values.shape, 1) < TILE // 2
    zero = jnp.zeros_like(values)
    return jnp.concatenate(
        [jnp.where(left, values, zero), jnp.where(left, zero, values)], axis=0
    )


def turned_halves(values):
    turned = jnp.transpose(values)
    top = iota(turned.shape, 0) < TILE // 2
    zero = jnp.zeros_like(turned)
    return jnp.concatenate([jnp.where(top, turned, zero), jnp.where(top, zero, turned)], axis=1)


def skew(values):
    return jnp.concatenate(
        [
            pltpu.roll(values[:TILE], 1, 1, stride=1, stride_axis=0),
            pltpu.roll(values[TILE:], 1, 1, stride=1, stride_axis=0),
        ],
        axis=0,
    )


def mirror(values):
    row, col = iota((2 * TILE, 2 * TILE), 0), iota((2 * TILE, 2 * TILE), 1)
    flip = (row % TILE + col % TILE == TILE - 1) & (row // TILE == col // TILE)
    return dot(values, jnp.where(flip, 1.0, 0.0).astype(bf16))


def twice(values):
    return jnp.concatenate([values, values], axis=0)


PAIRS = H // 2


def attend_forward(
    starts_ref, qu_ref, qv_ref, k_ref, v_ref, t_ref, context_ref, logs_ref,
    qum, qvm, scores, rolled, peaks, sums, mixed,
):
    length = qu_ref.shape[0]
    tiles = length // TILE

    def query_step(tile):
        first = tile * TILE
        at = rows_at(tile, TILE)
        low, steps = tile_window(starts_ref, first, length)
        chunk = chunk_rows(tile, low, length, 1)
        for p in range(PAIRS):
            lanes = slice(p * TILE, (p + 1) * TILE)
            qum[p] = halves(qu_ref[at, lanes])
            qvm[p] = halves(qv_ref[at, lanes])
            rolled[p] = skew(dot_t(qvm[p], t_ref[chunk, lanes]))
            peaks[p] = jnp.full((2 * TILE, TILE), masked_score, f32)
            sums[p] = jnp.zeros((2 * TILE, TILE), f32)
            mixed[p] = jnp.zeros((2 * TILE, TILE), f32)
        lower = twice(iota((TILE, TILE), 1) <= iota((TILE, TILE), 0))

        def score_step(step, carry):
            key = low + 2 * step
            keys = pl.ds(pl.multiple_of(key * TILE, TILE), 2 * TILE)
            same_one = twice(same_tile(starts_ref, first, key * TILE))
            same_two = twice(same_tile(starts_ref, first, key * TILE + TILE))
            chunks = chunk_rows(tile, key + 1, length, 2)
            for p in range(PAIRS):
                lanes = slice(p * TILE, (p + 1) * TILE)
                content = dot_t(qum[p], k_ref[keys, lanes])
                fresh = dot_t(qvm[p], t_ref[chunks, lanes])
                one, two = skew(fresh[:, :TILE]), skew(fresh[:, TILE:])
                value_one = content[:, :TILE] + jnp.where(lower, rolled[p], one)
                value_two = content[:, TILE:] + jnp.where(lower, one, two)
                value_one = jnp.where(same_one, value_one, masked_score)
                value_two = jnp.where(same_two, value_two, masked_score)
                rolled[p] = two
                scores[2 * step, p] = value_one
                scores[2 * step + 1, p] = value_two
                peaks[p] = jnp.maximum(peaks[p], jnp.maximum(value_one, value_two))
            return carry

        lax.fori_loop(0, steps, score_step, 0)
        for p in range(PAIRS):
            peaks[p] = jnp.broadcast_to(
                jnp.max(peaks[p], axis=1, keepdims=True), (2 * TILE, TILE)
            )

        def value_step(step, carry):
            keys = pl.ds(pl.multiple_of((low + 2 * step) * TILE, TILE), 2 * TILE)
            for p in range(PAIRS):
                lanes = slice(p * TILE, (p + 1) * TILE)
                one = jnp.exp(scores[2 * step, p] - peaks[p])
                two = jnp.exp(scores[2 * step + 1, p] - peaks[p])
                sums[p] += one + two
                raised = jnp.concatenate([one.astype(bf16), two.astype(bf16)], axis=1)
                mixed[p] += dot(raised, v_ref[keys, lanes])
            return carry

        lax.fori_loop(0, steps, value_step, 0)
        left = iota((TILE, TILE), 1) < TILE // 2
        logs = jnp.zeros((TILE, TILE), f32)
        lane = iota((TILE, TILE), 1)
        for p in range(PAIRS):
            lanes = slice(p * TILE, (p + 1) * TILE)
            total = jnp.sum(sums[p], axis=1, keepdims=True)
            result = mixed[p] * (1.0 / total)
            context_ref[at, lanes] = jnp.where(left, result[:TILE], result[TILE:]).astype(bf16)
            logsum = peaks[p] + jnp.log(total)
            logs = jnp.where(lane == 2 * p, logsum[:TILE], logs)
            logs = jnp.where(lane == 2 * p + 1, logsum[TILE:], logs)
        logs_ref[at, :] = logs

    loop(tiles, query_step)


def attend_scratch(length):
    pair = (PAIRS, 2 * TILE, TILE)
    return [
        pltpu.VMEM(pair, bf16),
        pltpu.VMEM(pair, bf16),
        pltpu.VMEM((length // TILE,) + pair, f32),
        pltpu.VMEM(pair, f32),
        pltpu.VMEM(pair, f32),
        pltpu.VMEM(pair, f32),
        pltpu.VMEM(pair, f32),
    ]


def attend_backward(
    starts_ref, qu_ref, qv_ref, k_ref, v_ref, t_ref, mirrored_ref, context_ref, logs_ref, dcontext_ref,
    dm_ref, dk_ref, dv_ref, dt_ref, dbias_ref,
    qum, qvm, dcm, qut, qvt, dct, logs, deltas, rolled, unrolled, dqu, dqv,
):
    length, width = qu_ref.shape
    tiles = length // TILE
    scale = 1.0 / math.sqrt(width // H)
    dk_ref[...] = jnp.zeros_like(dk_ref)
    dv_ref[...] = jnp.zeros_like(dv_ref)
    dt_ref[...] = jnp.zeros_like(dt_ref)
    dbias_ref[...] = jnp.zeros_like(dbias_ref)

    def query_step(tile):
        first = tile * TILE
        at = rows_at(tile, TILE)
        low, steps = tile_window(starts_ref, first, length)
        chunk = chunk_rows(tile, low, length, 1)
        logs_tile = logs_ref[at, :]
        for p in range(PAIRS):
            lanes = slice(p * TILE, (p + 1) * TILE)
            query_u = halves(qu_ref[at, lanes])
            query_v = halves(qv_ref[at, lanes])
            upstream = halves(dcontext_ref[at, lanes])
            qum[p] = query_u
            qvm[p] = query_v
            dcm[p] = upstream
            qut[p] = turned_halves(qu_ref[at, lanes])
            qvt[p] = turned_halves(qv_ref[at, lanes])
            dct[p] = turned_halves(dcontext_ref[at, lanes])
            delta = jnp.sum(
                upstream.astype(f32) * twice(context_ref[at, lanes].astype(f32)),
                axis=1,
                keepdims=True,
            )
            deltas[p] = jnp.broadcast_to(delta, (2 * TILE, TILE))
            logs[p, :TILE] = jnp.broadcast_to(logs_tile[:, 2 * p : 2 * p + 1], (TILE, TILE))
            logs[p, TILE:] = jnp.broadcast_to(logs_tile[:, 2 * p + 1 : 2 * p + 2], (TILE, TILE))
            rolled[p] = skew(dot_t(query_v, t_ref[chunk, lanes]))
            unrolled[p] = jnp.zeros((2 * TILE, TILE), f32)
            dqu[p] = jnp.zeros((2 * TILE, TILE), f32)
            dqv[p] = jnp.zeros((2 * TILE, TILE), f32)
        lower = twice(iota((TILE, TILE), 1) <= iota((TILE, TILE), 0))

        def step_body(step, carry):
            key = low + 2 * step
            keys = pl.ds(pl.multiple_of(key * TILE, TILE), 2 * TILE)
            same_one = twice(same_tile(starts_ref, first, key * TILE))
            same_two = twice(same_tile(starts_ref, first, key * TILE + TILE))
            before = chunk_rows(tile, key, length, 2, True)
            after = chunk_rows(tile, key + 1, length, 2)
            for p in range(PAIRS):
                lanes = slice(p * TILE, (p + 1) * TILE)
                content = dot_t(qum[p], k_ref[keys, lanes])
                fresh = dot_t(qvm[p], t_ref[after, lanes])
                one, two = skew(fresh[:, :TILE]), skew(fresh[:, TILE:])
                value_one = content[:, :TILE] + jnp.where(lower, rolled[p], one)
                value_two = content[:, TILE:] + jnp.where(lower, one, two)
                rolled[p] = two
                probs_one = jnp.where(same_one, jnp.exp(value_one - logs[p]), 0.0)
                probs_two = jnp.where(same_two, jnp.exp(value_two - logs[p]), 0.0)
                probs = jnp.concatenate([probs_one.astype(bf16), probs_two.astype(bf16)], axis=1)
                dprobs = dot_t(dcm[p], v_ref[keys, lanes])
                dlow_one = (probs_one * (dprobs[:, :TILE] - deltas[p])).astype(bf16)
                dlow_two = (probs_two * (dprobs[:, TILE:] - deltas[p])).astype(bf16)
                dlow = jnp.concatenate([dlow_one, dlow_two], axis=1)
                dv_ref[lanes, keys] += dot(dct[p], probs)
                dk_ref[lanes, keys] += dot(qut[p], dlow)
                dqu[p] += dot(dlow, k_ref[keys, lanes])
                mirrored = mirror(dlow)
                one, two = skew(mirrored[:, :TILE]), skew(mirrored[:, TILE:])
                moved = jnp.concatenate(
                    [
                        jnp.where(lower, two, one).astype(bf16),
                        jnp.where(lower, one, unrolled[p]).astype(bf16),
                    ],
                    axis=1,
                )
                unrolled[p] = two
                dt_ref[lanes, before] += dot(qvt[p], moved)
                dqv[p] += dot(moved, mirrored_ref[before, lanes])
            return carry

        lax.fori_loop(0, steps, step_body, 0)
        last = chunk_rows(tile, low + 2 * steps, length, 1, True)
        left = iota((TILE, TILE), 1) < TILE // 2
        for p in range(PAIRS):
            lanes = slice(p * TILE, (p + 1) * TILE)
            moved = jnp.where(lower, 0.0, unrolled[p]).astype(bf16)
            dt_ref[lanes, last] += dot(qvt[p], moved)
            full_u = dqu[p]
            full_v = dqv[p] + dot(moved, mirrored_ref[last, lanes])
            part_u = jnp.where(left, full_u[:TILE], full_u[TILE:]) * scale
            part_v = jnp.where(left, full_v[:TILE], full_v[TILE:]) * scale
            dbias_ref[0:1, lanes] += column_sum(part_u)
            dbias_ref[1:2, lanes] += column_sum(part_v)
            dm_ref[at, lanes] = (part_u + part_v).astype(bf16)

    loop(tiles, query_step)

    def finish(index):
        at = rows_at(index, TILE)
        for p in range(PAIRS):
            lanes = slice(p * TILE, (p + 1) * TILE)
            key_lanes = slice(width + p * TILE, width + (p + 1) * TILE)
            value_lanes = slice(2 * width + p * TILE, 2 * width + (p + 1) * TILE)
            dm_ref[at, key_lanes] = jnp.transpose(dk_ref[lanes, at].astype(bf16))
            dm_ref[at, value_lanes] = jnp.transpose(dv_ref[lanes, at].astype(bf16))

    loop(tiles, finish)


def attend_back_scratch():
    pair = (PAIRS, 2 * TILE, TILE)
    turned = (PAIRS, TILE, 2 * TILE)
    return [pltpu.VMEM(dims, bf16) for dims in (pair,) * 3 + (turned,) * 3] + [
        pltpu.VMEM(pair, f32) for unused in range(6)
    ]


def dense_parts(dense_ref):
    width = dense_ref.shape[0]
    cuts = (0, 3, 4, 5, 6, 8)
    return [
        dense_ref.at[:, pl.ds(start * width, (stop - start) * width)]
        for start, stop in zip(cuts[:-1], cuts[1:])
    ]


def shifted(values, reach, taps):
    rows = values.shape[0]
    found = {}
    for rest in range(8):
        starts = [EDGE - reach + k for k in range(taps) if (EDGE - reach + k) % 8 == rest]
        turned = pltpu.roll(values, (rows - rest) % rows, 0) if rest else values
        for start in starts:
            found[start - EDGE + reach] = turned[start - rest : start - rest + rows - 2 * EDGE]
    return [found[k] for k in range(taps)]


def at_edges(starts_ref, length, step):
    for k in range(1, starts_ref.shape[1]):
        edge = starts_ref[0, k]

        @pl.when(edge < length)
        def unused():
            start = jnp.minimum((edge - 8) // 8 * 8, length - 2 * EDGE)
            start = pl.multiple_of(start, 8)
            step(start, iota((2 * EDGE, TILE), 0) + start)


def spread_rows(rows_ref, out_ref):
    width = rows_ref.shape[1]
    for row in range(out_ref.shape[2] // width):
        lanes = slice(row * width, (row + 1) * width)
        out_ref[:, :, lanes] = jnp.broadcast_to(
            rows_ref[row : row + 1, :][None], (out_ref.shape[0], 1, width)
        )


EDGE = 16


def middle_kernel(
    starts_ref, hidden_ref, cols_ref, gate_ref, gains_ref, dense_ref, bias_ref, taps_ref, sinus_ref,
    *refs,
):
    returned_refs, refs = refs[:PARTS], refs[PARTS:]
    h1_ref, h2_ref, qu_ref, qv_ref, k_ref, v_ref, t_ref, context_ref, logs_ref = refs[:9]
    conv_ref, sums_ref, padded, sums, returned_ref = refs[9:14]
    attend = refs[14:]
    join_blocks(returned_refs, returned_ref)
    length, width = h1_ref.shape
    scale = 1.0 / math.sqrt(width // H)
    in_ref, place_ref, mix_ref, unused, point_ref = dense_parts(dense_ref)

    def queries_step(index):
        at = rows_at(index, BLOCK)
        picked = collect(cols_ref[at, 0:1], returned_ref)
        h1 = hidden_ref[at, :].astype(f32) + 0.5 * gate_ref[at, :] * picked
        h1_ref[at, :] = h1
        standard, unused = normalize(h1)
        low = (standard * gains_ref[1:2, :]).astype(bf16)
        queries = dot(low, in_ref[:, :width])
        qu_ref[at, :] = ((queries + bias_ref[0:1, :]).astype(bf16).astype(f32) * scale).astype(bf16)
        qv_ref[at, :] = ((queries + bias_ref[1:2, :]).astype(bf16).astype(f32) * scale).astype(bf16)
        k_ref[at, :] = dot(low, in_ref[:, width : 2 * width]).astype(bf16)
        v_ref[at, :] = dot(low, in_ref[:, 2 * width :]).astype(bf16)
        table_at = pl.ds(pl.multiple_of(index * BLOCK + edge, TILE), BLOCK)
        t_ref[table_at, :] = dot(sinus_ref[at, :], place_ref[...]).astype(bf16)

    edge = PAD * TILE
    t_ref[:edge, :] = jnp.zeros((edge, width), bf16)
    t_ref[edge + length :, :] = jnp.zeros((edge, width), bf16)
    loop(length // BLOCK, queries_step)
    attend_forward(
        starts_ref, qu_ref, qv_ref, k_ref, v_ref, t_ref, context_ref, logs_ref, *attend
    )
    padded[:EDGE, :] = jnp.zeros((EDGE, width), f32)
    padded[EDGE + length :, :] = jnp.zeros((EDGE, width), f32)

    def gates_step(index):
        at = rows_at(index, BLOCK)
        h2 = h1_ref[at, :] + dot(context_ref[at, :], mix_ref[...])
        h2_ref[at, :] = h2
        standard, unused = normalize(h2)
        low = (standard * gains_ref[2:3, :]).astype(bf16)
        value = dot(low, point_ref[:, :width])
        gates = dot(low, point_ref[:, width:])
        padded[pl.ds(pl.multiple_of(index * BLOCK + EDGE, EDGE), BLOCK), :] = value * sigmoid(gates)

    loop(length // BLOCK, gates_step)
    sums[...] = jnp.zeros_like(sums)
    taps = taps_ref.shape[0] - 1
    reach = taps // 2
    frames = starts_ref[0, starts_ref.shape[1] - 1]

    def conv_step(index):
        first = index * TILE
        around = pl.ds(pl.multiple_of(first, TILE), TILE + 2 * EDGE)
        for part in range(width // TILE):
            lanes = slice(part * TILE, (part + 1) * TILE)
            total = jnp.zeros((TILE, TILE), f32)
            for tap, near in enumerate(shifted(padded[around, lanes], reach, taps)):
                total = total + near * taps_ref[tap : tap + 1, lanes]
            conv_ref[rows_at(index, TILE), lanes] = total

    loop(length // TILE, conv_step)

    def edge_step(start, place):
        here = numbers_at(starts_ref, place)
        masks = [numbers_at(starts_ref, place + (tap - reach)) == here for tap in range(taps)]
        around = pl.ds(start, 2 * EDGE + 2 * EDGE)
        for part in range(width // TILE):
            lanes = slice(part * TILE, (part + 1) * TILE)
            total = jnp.zeros(place.shape, f32)
            for tap, near in enumerate(shifted(padded[around, lanes], reach, taps)):
                total = total + jnp.where(masks[tap], near, 0.0) * taps_ref[tap : tap + 1, lanes]
            conv_ref[pl.ds(start, 2 * EDGE), lanes] = total

    at_edges(starts_ref, length, edge_step)

    def sums_step(index):
        at = rows_at(index, BLOCK)
        inside = (iota((BLOCK, 1), 0) + index * BLOCK) < frames
        kept = jnp.where(inside, conv_ref[at, :], 0.0)
        sums[0:1, :] += column_sum(kept)
        sums[1:2, :] += column_sum(kept * kept)

    loop(length // BLOCK, sums_step)
    sums[2:3, :] = jnp.zeros((1, width), f32) + frames.astype(f32)
    spread_rows(sums, sums_ref)


def batch_totals(totals_ref, width):
    totals = jnp.sum(totals_ref[...], axis=0)
    count = totals[:, 2 * width :]
    mean = totals[:, :width] / count
    variance = totals[:, width : 2 * width] / count - mean * mean
    return mean, lax.rsqrt(variance + epsilon), count


def batch_block(conv, mean, inverse, batch_ref):
    centred = conv - mean
    standard = centred * inverse
    batched = standard * batch_ref[0:1, :] + batch_ref[1:2, :]
    return centred, standard, batched


def second_kernel(
    experts, h2_ref, conv_ref, totals_ref, batch_ref, point_ref, embed_ref, gains_ref, router_ref,
    cols_ref, slot_row_ref, *refs,
):
    out_refs, refs = refs[:PARTS], refs[PARTS:]
    h3_ref, active_ref, probs_ref, gate_ref, stats_ref, low_ref = refs
    length, width = h2_ref.shape
    mean, inverse, count = batch_totals(totals_ref, width)
    stats_ref[0:1, :] = mean
    stats_ref[1:2, :] = inverse
    stats_ref[2:3, :] = count

    def step(index):
        at = rows_at(index, BLOCK)
        unused, unused, batched = batch_block(conv_ref[at, :], mean, inverse, batch_ref)
        active = (batched * sigmoid(batched)).astype(bf16)
        active_ref[at, :] = active
        h3 = h2_ref[at, :] + dot(active, point_ref[...])
        h3_ref[at, :] = h3
        standard, unused = normalize(h3)
        low = (standard * gains_ref[3:4, :]).astype(bf16)
        low_ref[at, :] = low
        probs, gate = route_block(low, embed_ref[at, :], router_ref, cols_ref[at, 3:4], experts)
        probs_ref[at, :] = probs
        gate_ref[at, :] = gate

    loop(length // BLOCK, step)
    dispatch(low_ref, slot_row_ref[1:2, :], out_refs)


def gate_back(upstream, picked, gate, probs, picks):
    d_gate = 0.5 * jnp.sum(upstream * picked, axis=1, keepdims=True)
    onehot = jnp.where(iota(probs.shape, 1) == picks, 1.0, 0.0)
    return (d_gate * gate) * (onehot - probs)


def turn_kernel(
    h3_ref, cols_ref, gate_ref, probs_ref, slot_row_ref, gains_ref, cotangent_ref, *refs,
):
    returned_refs, out_refs, refs = refs[:PARTS], refs[PARTS : 2 * PARTS], refs[2 * PARTS :]
    output_ref, d4_ref, dlogits_ref, dgain_ref, low_ref, returned_ref = refs
    length = h3_ref.shape[0]
    join_blocks(returned_refs, returned_ref)
    dgain_ref[...] = jnp.zeros_like(dgain_ref)

    def step(index):
        at = rows_at(index, BLOCK)
        picked = collect(cols_ref[at, 1:2], returned_ref)
        gate = gate_ref[at, :]
        h4 = h3_ref[at, :] + 0.5 * gate * picked
        standard, inverse = normalize(h4)
        gain = gains_ref[4:5, :]
        output_ref[at, :] = (standard * gain).astype(bf16)
        upstream = cotangent_ref[at, :].astype(f32)
        dgain_ref[0:1, :] += column_sum(upstream * standard)
        d4 = normalize_back(standard, inverse, gain, upstream)
        d4_ref[at, :] = d4
        dlogits_ref[at, :] = gate_back(d4, picked, gate, probs_ref[at, :], cols_ref[at, 3:4])
        low_ref[at, :] = (0.5 * gate * d4).astype(bf16)

    loop(length // BLOCK, step)
    dispatch(low_ref, slot_row_ref[1:2, :], out_refs)


def router_back(dlogits, low, embed, router_ref, drouter_ref):
    width = low.shape[1]
    high = dlogits.astype(bf16)
    rest = (dlogits - high.astype(f32)).astype(bf16)
    d_low = dot_t(high, router_ref[:width, :]) + dot_t(rest, router_ref[:width, :])
    d_embed = dot_t(high, router_ref[width:, :]) + dot_t(rest, router_ref[width:, :])
    turned = jnp.transpose(dlogits)[:8, :]
    turned_high = turned.astype(bf16)
    turned_rest = (turned - turned_high.astype(f32)).astype(bf16)
    drouter_ref[:, :width] += dot(turned_high, low) + dot(turned_rest, low)
    drouter_ref[:, width:] += dot(turned_high, embed) + dot(turned_rest, embed)
    return d_low, d_embed


def second_back_kernel(
    cols_ref, dlogits_ref, h3_ref, d4_ref, embed_ref, router_ref, gains_ref, conv_ref, stats_ref,
    batch_ref, point_ref, *refs,
):
    dsent_refs, refs = refs[:PARTS], refs[PARTS:]
    d3_ref, dlow_ref, dz_ref, dembed_ref, drouter_ref, small_ref, sums_ref, sums, dsent_ref = refs
    length, width = h3_ref.shape
    drouter_ref[...] = jnp.zeros_like(drouter_ref)
    small_ref[...] = jnp.zeros_like(small_ref)
    sums[...] = jnp.zeros_like(sums)
    join_blocks(dsent_refs, dsent_ref)
    mean, batch_inverse = stats_ref[0:1, :], stats_ref[1:2, :]

    def step(index):
        at = rows_at(index, BLOCK)
        standard, inverse = normalize(h3_ref[at, :])
        gain = gains_ref[3:4, :]
        low = (standard * gain).astype(bf16)
        d_low, d_embed = router_back(
            dlogits_ref[at, :], low, embed_ref[at, :], router_ref, drouter_ref
        )
        dembed_ref[at, :] = d_embed
        d_norm = collect(cols_ref[at, 1:2], dsent_ref) + d_low
        small_ref[0:1, :] += column_sum(d_norm * standard)
        d3 = d4_ref[at, :] + normalize_back(standard, inverse, gain, d_norm)
        d3_ref[at, :] = d3
        d3_low = d3.astype(bf16)
        dlow_ref[at, :] = d3_low
        centred, normed, batched = batch_block(conv_ref[at, :], mean, batch_inverse, batch_ref)
        gates = sigmoid(batched)
        d_batched = dot_t(d3_low, point_ref[...]) * (gates + batched * gates * (1.0 - gates))
        small_ref[1:2, :] += column_sum(d_batched * normed)
        small_ref[2:3, :] += column_sum(d_batched)
        d_z = d_batched * batch_ref[0:1, :]
        dz_ref[at, :] = d_z
        sums[0:1, :] += column_sum(d_z)
        sums[1:2, :] += column_sum(d_z * centred)

    loop(length // BLOCK, step)
    spread_rows(sums, sums_ref)


def conv_back_kernel(
    starts_ref, conv_ref, dz_ref, stats_ref, dsums_ref, d3_ref, h2_ref, gains_ref, dense_ref, taps_ref,
    d2_ref, d2low_ref, dcontext_ref, n3_ref, dg_ref, small_ref, dtaps_ref, padded, linear, dtaps, edge_grad,
):
    length, width = h2_ref.shape
    unused, unused, mix_ref, unused, point_ref = dense_parts(dense_ref)
    taps = taps_ref.shape[0] - 1
    reach = taps // 2
    frames = starts_ref[0, starts_ref.shape[1] - 1]
    small_ref[...] = jnp.zeros_like(small_ref)
    dtaps[...] = jnp.zeros_like(dtaps)
    mean, batch_inverse, count = stats_ref[0:1, :], stats_ref[1:2, :], stats_ref[2:3, :]
    dsums = jnp.sum(dsums_ref[...], axis=0)
    d_variance = -0.5 * batch_inverse * batch_inverse * batch_inverse * dsums[:, width:]
    padded[:EDGE, :] = jnp.zeros((EDGE, width), f32)
    padded[EDGE + length :, :] = jnp.zeros((EDGE, width), f32)

    def conv_step(index):
        at = rows_at(index, BLOCK)
        centred = conv_ref[at, :] - mean
        inside = (iota((BLOCK, 1), 0) + index * BLOCK) < frames
        shared = (2.0 * d_variance * centred - batch_inverse * dsums[:, :width]) / count
        d_conv = batch_inverse * dz_ref[at, :] + jnp.where(inside, shared, 0.0)
        padded[pl.ds(pl.multiple_of(index * BLOCK + EDGE, EDGE), BLOCK), :] = d_conv
        standard, unused = normalize(h2_ref[at, :])
        low = (standard * gains_ref[2:3, :]).astype(bf16)
        n3_ref[at, :] = low
        value = dot(low, point_ref[:, :width])
        linear[at, :width] = value
        linear[at, width:] = sigmoid(dot(low, point_ref[:, width:]))

    loop(length // BLOCK, conv_step)

    def turn_step(index):
        at = rows_at(index, TILE)
        around = pl.ds(pl.multiple_of(index * TILE, TILE), TILE + 2 * EDGE)
        for part in range(width // TILE):
            lanes = slice(part * TILE, (part + 1) * TILE)
            other = slice(width + part * TILE, width + (part + 1) * TILE)
            value, gate = linear[at, lanes], linear[at, other]
            passed = value * gate
            total = jnp.zeros((TILE, TILE), f32)
            for step, near in enumerate(shifted(padded[around, lanes], reach, taps)):
                tap = taps - 1 - step
                total = total + near * taps_ref[tap : tap + 1, lanes]
                dtaps[tap, :, lanes] += jnp.sum((near * passed).reshape(TILE // 8, 8, TILE), axis=0)
            dg_ref[at, lanes] = (total * gate).astype(bf16)
            dg_ref[at, other] = (total * passed * (1.0 - gate)).astype(bf16)

    def edge_step(start, place):
        rows = 2 * EDGE
        at = pl.ds(start, rows)
        here = numbers_at(starts_ref, place)
        masks = [numbers_at(starts_ref, place - (reach - tap)) == here for tap in range(taps)]
        around = pl.ds(start, rows + 2 * EDGE)
        for part in range(width // TILE):
            lanes = slice(part * TILE, (part + 1) * TILE)
            other = slice(width + part * TILE, width + (part + 1) * TILE)
            value, gate = linear[at, lanes], linear[at, other]
            passed = value * gate
            total = jnp.zeros((rows, TILE), f32)
            for step, near in enumerate(shifted(padded[around, lanes], reach, taps)):
                tap = taps - 1 - step
                total = total + jnp.where(masks[step], near, 0.0) * taps_ref[tap : tap + 1, lanes]
                extra = jnp.where(masks[step], 0.0, near) * passed
                dtaps[tap, :, lanes] -= jnp.sum(extra.reshape(rows // 8, 8, TILE), axis=0)
            edge_grad[:, lanes] = total * gate
            edge_grad[:, other] = total * passed * (1.0 - gate)
        low = pl.multiple_of(jnp.minimum(start // 16 * 16, length - rows - 16), 16)
        wide = pl.ds(low, rows + 16)
        shift = start - low
        whole = dg_ref[wide, :].astype(f32)
        grad = edge_grad[...]
        zero = jnp.zeros((16, 2 * width), f32)
        head = jnp.concatenate([grad, zero], axis=0)
        middle = jnp.concatenate([zero[:8], grad, zero[:8]], axis=0)
        tail = jnp.concatenate([zero, grad], axis=0)
        place = iota((rows + 16, 1), 0) - shift
        moved = jnp.where(shift == 0, head, jnp.where(shift == 8, middle, tail))
        inside = (place >= 0) & (place < rows)
        dg_ref[wide, :] = jnp.where(inside, moved, whole).astype(bf16)

    loop(length // TILE, turn_step)
    at_edges(starts_ref, length, edge_step)
    dtaps_ref[...] = jnp.sum(dtaps[...], axis=1)

    def gates_step(index):
        at = rows_at(index, BLOCK)
        d_norm = dot_t(dg_ref[at, :], point_ref[...])
        standard, inverse = normalize(h2_ref[at, :])
        small_ref[0:1, :] += column_sum(d_norm * standard)
        d2 = d3_ref[at, :] + normalize_back(standard, inverse, gains_ref[2:3, :], d_norm)
        d2_ref[at, :] = d2
        low = d2.astype(bf16)
        d2low_ref[at, :] = low
        dcontext_ref[at, :] = dot_t(low, mix_ref[...]).astype(bf16)

    loop(length // BLOCK, gates_step)


def attend_back_kernel(
    starts_ref, d2_ref, dcontext_ref, h1_ref, gains_ref, dense_ref, sinus_ref, qu_ref, qv_ref, k_ref, v_ref,
    t_ref, context_ref, logs_ref, cols_ref, gate_ref, probs_ref, slot_row_ref, *refs,
):
    returned_refs, out_refs, refs = refs[:PARTS], refs[PARTS : 2 * PARTS], refs[2 * PARTS :]
    d1_ref, dlogits_ref, n2_ref, dm_ref, dtable_ref, small_ref = refs[:6]
    low_ref, mirrored_ref, returned_ref, dk_ref, dv_ref, dt_ref = refs[6:12]
    attend = refs[12:]
    length, width = h1_ref.shape
    in_ref, place_ref, unused, unused, unused = dense_parts(dense_ref)
    small_ref[...] = jnp.zeros_like(small_ref)
    join_blocks(returned_refs, returned_ref)

    def table_step(index):
        at = rows_at(index, BLOCK)
        table_at = pl.ds(pl.multiple_of(index * BLOCK + edge, TILE), BLOCK)
        mirrored_ref[table_at, :] = dot(sinus_ref[at, :], place_ref[...]).astype(bf16)

    edge = PAD * TILE
    mirrored_ref[:edge, :] = jnp.zeros((edge, width), bf16)
    mirrored_ref[edge + length :, :] = jnp.zeros((edge, width), bf16)
    loop(length // BLOCK, table_step)
    attend_backward(
        starts_ref, qu_ref, qv_ref, k_ref, v_ref, t_ref, mirrored_ref, context_ref, logs_ref, dcontext_ref,
        dm_ref, dk_ref, dv_ref, dt_ref, small_ref.at[pl.ds(8, 8)], *attend
    )

    def queries_step(index):
        at = rows_at(index, BLOCK)
        d_norm = dot_t(dm_ref[at, :], in_ref[...])
        standard, inverse = normalize(h1_ref[at, :])
        gain = gains_ref[1:2, :]
        n2_ref[at, :] = (standard * gain).astype(bf16)
        small_ref[1:2, :] += column_sum(d_norm * standard)
        d1 = d2_ref[at, :] + normalize_back(standard, inverse, gain, d_norm)
        d1_ref[at, :] = d1
        picked = collect(cols_ref[at, 0:1], returned_ref)
        gate = gate_ref[at, :]
        dlogits_ref[at, :] = gate_back(d1, picked, gate, probs_ref[at, :], cols_ref[at, 2:3])
        low_ref[at, :] = (0.5 * gate * d1).astype(bf16)

    loop(length // BLOCK, queries_step)
    dtable_ref[...] = dt_ref[:, PAD * TILE : PAD * TILE + length].astype(bf16)
    dispatch(low_ref, slot_row_ref[0:1, :], out_refs)


def last_kernel(
    cols_ref, dlogits_ref, hidden_ref, d1_ref, embed_ref, router_ref, gains_ref, dembed_two_ref,
    drouter_two_ref, mid_ref, conv_ref, two_ref, five_ref, taps_ref, *refs,
):
    dsent_refs, refs = refs[:PARTS], refs[PARTS:]
    d0_ref, dembed_ref, routers_ref, small_ref, dsent_ref = refs
    length = hidden_ref.shape[0]
    taps = small_ref.shape[0] - 9
    join_blocks(dsent_refs, dsent_ref)
    drouter_ref = routers_ref.at[pl.ds(0, 8)]
    drouter_ref[...] = jnp.zeros_like(drouter_ref)
    routers_ref[8:, :] = drouter_two_ref[...]
    small_ref[0:1, :] = jnp.zeros_like(small_ref[0:1, :])
    small_ref[1:2, :] = mid_ref[1:2, :]
    small_ref[2:3, :] = conv_ref[0:1, :]
    small_ref[3:4, :] = two_ref[0:1, :]
    small_ref[4:5, :] = five_ref[0:1, :]
    small_ref[5:7, :] = mid_ref[8:10, :]
    small_ref[7 : 7 + taps, :] = taps_ref[:taps, :]
    small_ref[7 + taps :, :] = two_ref[1:3, :]

    def step(index):
        at = rows_at(index, BLOCK)
        standard, inverse = normalize(hidden_ref[at, :].astype(f32))
        gain = gains_ref[0:1, :]
        low = (standard * gain).astype(bf16)
        d_low, d_embed = router_back(
            dlogits_ref[at, :], low, embed_ref[at, :], router_ref, drouter_ref
        )
        dembed_ref[at, :] = d_embed + dembed_two_ref[at, :]
        d_norm = collect(cols_ref[at, 0:1], dsent_ref) + d_low
        small_ref[0:1, :] += column_sum(d_norm * standard)
        d0_ref[at, :] = d1_ref[at, :] + normalize_back(standard, inverse, gain, d_norm)

    loop(length // BLOCK, step)


def gather_small(values):
    return lax.all_to_all(values, BOTH, split_axis=0, concat_axis=0, tiled=True)


def across(values, axis, size, offset):
    if not offset:
        return values
    return lax.ppermute(values, axis, [(i, i ^ offset) for i in range(size)])


def exchange(blocks, experts):
    per = experts // PARTS
    moved = []
    for index, block in enumerate(blocks):
        rows = block.shape[0] // per
        pieces = []
        for k in range(index * per, (index + 1) * per):
            piece = block[(k - index * per) * rows : (k - index * per + 1) * rows]
            pieces.append(across(piece, "expert", experts, k))
        moved.append(pieces[0] if per == 1 else jnp.concatenate(pieces, axis=0))
    return moved


def ring_place(index, size):
    return jnp.where(index % 2 == 0, index // 2, size - 1 - index // 2)


def ring_member(place, size):
    place = (place + 2 * size) % size
    return jnp.where(place < size // 2, 2 * place, 2 * (size - 1 - place) + 1)


def ring_pairs(size, forward):
    order = list(range(0, size, 2)) + list(range(size - 1, 0, -2))
    step = 1 if forward else -1
    return [(order[k], order[(k + step) % size]) for k in range(size)]


def ring_gather(shards, size):
    found = []
    for number, shard in enumerate(shards):
        ahead = size // 2 if number % 2 == 0 else (size - 1) // 2
        pieces = [None] * size
        pieces[0] = shard
        found.append((pieces, ahead))
    for step in range(1, size // 2 + 1):
        for pieces, ahead in found:
            if step <= ahead:
                pieces[step] = lax.ppermute(pieces[step - 1], "dp", ring_pairs(size, False))
            if step <= size - 1 - ahead:
                pieces[-step] = lax.ppermute(pieces[-step + 1 or 0], "dp", ring_pairs(size, True))
    return [pieces for pieces, unused in found]


def assemble_kernel(count, order_ref, *refs):
    size = (len(refs) - 1 - count) // count
    sems = refs[-1]
    copies = []
    for number in range(count):
        target = refs[count * size + number]
        for offset in range(size):
            piece = refs[number * size + offset]
            rows = piece.shape[0]
            start = pl.multiple_of(order_ref[offset] * rows, 16)
            copies.append(
                pltpu.make_async_copy(
                    piece, target.at[pl.ds(start, rows)], sems.at[number * size + offset]
                )
            )
    for copy in copies:
        copy.start()
    for copy in copies:
        copy.wait()


def assemble(shards, size):
    place = ring_place(lax.axis_index("dp"), size)
    order = ring_member(place + jnp.arange(size, dtype=jnp.int32), size).astype(jnp.int32)
    groups = ring_gather(shards, size)
    count = len(groups)
    anywhere = pl.BlockSpec(memory_space=pl.ANY)
    return pl.pallas_call(
        functools.partial(assemble_kernel, count),
        out_shape=[
            shape_of((size * shard.shape[0],) + shard.shape[1:], shard.dtype) for shard in shards
        ],
        in_specs=[SMEM] + [anywhere] * (count * size),
        out_specs=[VMEM] * count,
        scratch_shapes=[pltpu.SemaphoreType.DMA((count * size,))],
        name="assemble",
    )(order, *[piece for pieces in groups for piece in pieces])


def keep_half(values, axis, bit, size, offset, mesh_axis):
    mine = lax.dynamic_index_in_dim(values, bit, axis, keepdims=False)
    theirs = lax.dynamic_index_in_dim(values, 1 - bit, axis, keepdims=False)
    arrived = across(theirs, mesh_axis, size, offset)
    return (mine.astype(f32) + arrived.astype(f32)).astype(bf16)


def own_parts(values, place, size, stride, mesh_axis):
    parts = [lax.dynamic_index_in_dim(values, place, 0, keepdims=False)]
    for k in range(1, values.shape[0]):
        theirs = lax.dynamic_index_in_dim(values, place ^ k, 0, keepdims=False)
        parts.append(across(theirs, mesh_axis, size, k * stride))
    return parts


def add_up(parts):
    total = parts[0].astype(f32)
    for part in parts[1:]:
        total = total + part.astype(f32)
    return total


def keep_one(values, place, size, stride, mesh_axis):
    return add_up(own_parts(values, place, size, stride, mesh_axis))


def near_half(values):
    groups = values.shape[0]
    values = values.reshape((groups // 2, 2) + values.shape[1:])
    return keep_half(values, 1, lax.axis_index("dp") % 2, groups, 1, "dp")


def expert_parts(values, experts):
    me = lax.axis_index("expert")
    return [
        across(lax.dynamic_index_in_dim(values, me ^ k, 1, keepdims=False), "expert", experts, k)
        for k in range(experts)
    ]


def rows_product(left, right):
    return lax.dot_general(left, right, (((0,), (0,)), ((), ())), preferred_element_type=f32)


def blocks_product(left, right):
    left, right = jnp.concatenate(left, axis=0), jnp.concatenate(right, axis=0)
    return rows_product(left, right).astype(bf16)


def scatter_offloaded(grad_in, grad_out):
    return (
        lax.psum_scatter(grad_in, "dp", scatter_dimension=0, tiled=True).astype(f32)[None],
        lax.psum_scatter(grad_out, "dp", scatter_dimension=0, tiled=True).astype(f32)[None],
    )


def split_columns(values):
    middle = values.shape[1] // 2
    return [values[:, :middle], values[:, middle:]]


def sinus_rows(length, width, upward):
    distance = (length // 2 - 1 - np.arange(length)).astype(np.float32)
    distance = distance[::-1] if upward else distance
    rates = np.exp(
        np.arange(width // 2).astype(np.float32) * np.float32(-2.0 * math.log(10000.0) / width)
    ).astype(np.float32)
    angles = (distance[:, None] * rates[None, :]).astype(np.float64)
    table = np.concatenate([np.sin(angles), np.cos(angles)], axis=1)
    return jnp.asarray(table.astype(np.float32)).astype(bf16)


def body(
    groups,
    inputs,
    embedding,
    cotangent,
    first_routes,
    second_routes,
    segment_starts,
    norm_gains,
    first_router,
    second_router,
    first_in,
    first_out,
    second_in,
    second_out,
    attention_in,
    position_weight,
    position_bias,
    attention_out,
    pointwise_in,
    depthwise_kernel,
    batch_gain,
    batch_bias,
    pointwise_out,
):
    length, width = inputs.shape
    experts = first_router.shape[1]
    devices = groups * experts
    capacity = 17 * length // (16 * experts)
    slots = experts * capacity
    inner = first_in.shape[2]
    share = norm_gains.shape[1]
    taps = depthwise_kernel.shape[0]
    feats = first_router.shape[0]

    rows = jnp.concatenate(
        [norm_gains, position_bias, depthwise_kernel, batch_gain[None], batch_bias[None]], axis=0
    )
    count = rows.shape[0]
    flat = jnp.concatenate(
        [rows.reshape(-1), first_router.T.reshape(-1), second_router.T.reshape(-1)]
    ).astype(f32)
    small = gather_small(jnp.broadcast_to(flat[None], (devices,) + flat.shape))
    rows_all = small[:, : count * share].reshape(devices, count, share)
    rows_all = rows_all.transpose(1, 0, 2).reshape(count, devices * share)
    routers = small[:, count * share :].reshape(devices, 2, experts, feats)
    routers = routers.transpose(1, 2, 0, 3).reshape(2, experts, devices * feats)
    routers = jnp.pad(routers, ((0, 0), (0, TILE - experts), (0, 0)))
    routers = routers.transpose(0, 2, 1).astype(bf16)
    gains = jnp.pad(rows_all[0:5], ((0, 3), (0, 0)))
    bias = jnp.pad(rows_all[5:7], ((0, 6), (0, 0)))
    kernel_taps = jnp.pad(rows_all[7 : 7 + taps], ((0, 1), (0, 0)))
    batch = jnp.pad(rows_all[7 + taps : 9 + taps], ((0, 6), (0, 0)))

    packed = jnp.concatenate(
        [attention_in, position_weight, attention_out, pointwise_out, pointwise_in], axis=1
    )
    dense = lax.all_gather(packed, BOTH, axis=0, tiled=True)
    point_out = dense[:, 5 * width : 6 * width]

    first_pair = assemble((first_in[0], first_out[0]), groups)
    second_pair = (
        lax.all_gather(second_in[0], "dp", axis=0, tiled=True),
        lax.all_gather(second_out[0], "dp", axis=0, tiled=True),
    )

    me = lax.axis_index("expert")
    slot_rows, slot_cols = find_slots(first_routes, second_routes, me, capacity)
    sinus = sinus_rows(length, width, False)
    mirrored = sinus_rows(length, width, True)
    row_low = shape_of((length, width), bf16)
    row_full = shape_of((length, width), f32)
    lane_full = shape_of((length, TILE), f32)
    table_low = shape_of((length + 2 * PAD * TILE, width), bf16)
    block_low = shape_of((slots // PARTS, width), bf16)
    slots_scratch = pltpu.VMEM((slots, width), bf16)
    sums_scratch = pltpu.VMEM((8, width), f32)
    column = shape_of((length, 1), f32)
    eight = shape_of((8, width), f32)
    low_scratch = pltpu.VMEM((length, width), bf16)

    *sent_one, probs_one, gate_one = run(
        functools.partial(front_kernel, experts),
        (inputs, embedding, gains, routers[0], slot_cols, slot_rows),
        [VMEM] * 6,
        [block_low] * PARTS + [lane_full, column],
        [low_scratch],
        flops=4 * slots * length * width,
        name="front",
    )
    received_one = exchange(sent_one, experts)
    result_one = (
        expert_forward(received_one[2:3], *first_pair) + expert_forward(received_one[3:], *first_pair)
    )
    result_one = expert_forward(received_one[:2], *first_pair) + result_one
    returned_one = exchange(result_one, experts)

    edge_scratch = pltpu.VMEM((length + 2 * EDGE, width), f32)
    (
        h1, h2, query_u, query_v, keys, values, table, context, logs, convolved, sums,
    ) = run(
        middle_kernel,
        (
            segment_starts, inputs, slot_cols, gate_one, gains, dense, bias, kernel_taps, sinus,
            *returned_one,
        ),
        [SMEM] + [VMEM] * (8 + PARTS),
        [row_full, row_full]
        + [row_low] * 4
        + [table_low, row_low, lane_full, row_full, shape_of((devices, 1, 3 * width), f32)],
        [edge_scratch, sums_scratch, slots_scratch] + attend_scratch(length),
        flops=16 * length * length * width,
        name="middle",
    )
    totals = gather_small(sums)

    *sent_two, h3, active, probs_two, gate_two, stats = run(
        functools.partial(second_kernel, experts),
        (
            h2, convolved, totals, batch, point_out, embedding, gains, routers[1], slot_cols, slot_rows,
        ),
        [VMEM] * 10,
        [block_low] * PARTS + [row_full, row_low, lane_full, column, eight],
        [low_scratch],
        flops=4 * slots * length * width,
        name="second",
    )
    received_two = exchange(sent_two, experts)
    result_two = forward_in_turn(received_two, second_pair)
    returned_two = exchange(result_two, experts)

    *d_sent_two, output, d4, dlogits_two, dgain_five = run(
        turn_kernel,
        (
            h3, slot_cols, gate_two, probs_two, slot_rows, gains, cotangent, *returned_two,
        ),
        [VMEM] * (7 + PARTS),
        [block_low] * PARTS + [row_low, row_full, lane_full, eight],
        [low_scratch, slots_scratch],
        flops=4 * slots * length * width,
        name="turn",
    )
    d_result_two = exchange(d_sent_two, experts)
    unused, d_received_two, hidden_two, d_inner_two = backward_in_turn(
        received_two, d_result_two, second_pair
    )
    d_back_two = exchange(d_received_two, experts)
    grad_in_two, grad_out_two, *d_back_two = lax.optimization_barrier(
        (
            blocks_product(received_two, d_inner_two), blocks_product(hidden_two, d_result_two), *d_back_two,
        )
    )
    d_second_in, d_second_out = scatter_offloaded(grad_in_two, grad_out_two)

    router_shape = shape_of((8, 2 * width), f32)
    d3, d3_low, d_z, dembed_two, drouter_two, small_two, dsums_part = run(
        second_back_kernel,
        (
            slot_cols, dlogits_two, h3, d4, embedding, routers[1], gains, convolved, stats, batch, point_out,
            *d_back_two,
        ),
        [VMEM] * (11 + PARTS),
        [row_full, row_low, row_full, row_full, router_shape, eight, shape_of((devices, 1, 2 * width), f32)],
        [sums_scratch, slots_scratch],
        flops=4 * slots * length * width,
        name="second_back",
    )
    dsums = gather_small(dsums_part)
    d_pointwise_out = rows_product(active, d3_low)

    d2, d2_low, d_context, normed_three, d_gates, small_conv, d_taps = run(
        conv_back_kernel,
        (segment_starts, convolved, d_z, stats, dsums, d3, h2, gains, dense, kernel_taps),
        [SMEM] + [VMEM] * 9,
        [
            row_full, row_low, row_low, row_low, shape_of((length, 2 * width), bf16), eight,
            shape_of((16, width), f32),
        ],
        [
            edge_scratch, pltpu.VMEM((length, 2 * width), f32), pltpu.VMEM((16, 8, width), f32),
            pltpu.VMEM((2 * EDGE, 2 * width), f32),
        ],
        flops=6 * length * width * width,
        name="conv_back",
    )
    value_grad, gates_grad = split_columns(rows_product(normed_three, d_gates))
    early = jnp.stack(
        [
            part.astype(bf16).reshape(groups, experts, width // devices, width)
            for part in (rows_product(context, d2_low), d_pointwise_out, value_grad, gates_grad)
        ],
        axis=2,
    )
    early = expert_parts(early, experts)
    *d_sent_one, d1, dlogits_one, normed_two, d_mixed, d_table, small_mid = run(
        attend_back_kernel,
        (
            segment_starts, d2, d_context, h1, gains, dense, mirrored, query_u, query_v, keys, values, table,
            context, logs, slot_cols, gate_one, probs_one, slot_rows, *returned_one,
        ),
        [SMEM] + [VMEM] * (17 + PARTS),
        [block_low] * PARTS
        + [
            row_full, lane_full, row_low, shape_of((length, 3 * width), bf16),
            shape_of((width, length), bf16), shape_of((16, width), f32),
        ],
        [
            low_scratch, pltpu.VMEM(table_low.shape, bf16), slots_scratch,
            pltpu.VMEM((width, length), f32), pltpu.VMEM((width, length), f32),
            pltpu.VMEM((width, length + 2 * PAD * TILE), f32),
        ]
        + attend_back_scratch(),
        flops=32 * length * length * width,
        name="attend_back",
    )
    early, *d_sent_one = lax.optimization_barrier((early, *d_sent_one))
    d_result_one = exchange(d_sent_one, experts)
    (late,), d_received_one, hidden_one, d_inner_one = backward_in_turn(
        received_one, d_result_one, first_pair, (normed_two, d_mixed, d_table, mirrored)
    )
    late = expert_parts(late.reshape(groups, experts, width // devices, 4 * width), experts)
    d_back_one = exchange(d_received_one, experts)
    early = add_up(early).astype(bf16).reshape(groups, -1, width)
    grad_out = blocks_product(hidden_one, d_result_one).reshape(groups, -1, width)
    near_out = near_half(jnp.concatenate([grad_out, early], axis=1))
    grad_in = blocks_product(received_one, d_inner_one).reshape(groups, -1, inner)
    near_out, grad_in, d_back_one = lax.optimization_barrier((near_out, grad_in, d_back_one))
    far_out = own_parts(near_out, lax.axis_index("dp") // 2, groups, 2, "dp")
    near_in = near_half(grad_in)
    near_late = near_half(add_up(late).astype(bf16))
    d1, d_second_in, d_second_out = lax.optimization_barrier((d1, d_second_in, d_second_out))
    d_start, d_embed, routers_grad, rows_grad = run(
        last_kernel,
        (
            slot_cols, dlogits_one, inputs, d1, embedding, routers[0], gains, dembed_two,
            drouter_two, small_mid, small_conv, small_two, dgain_five, d_taps, *d_back_one,
        ),
        [VMEM] * (14 + PARTS),
        [row_full, row_full, shape_of((16, 2 * width), f32), shape_of((count, width), f32)],
        [slots_scratch],
        flops=4 * slots * length * width,
        name="last",
    )

    near_in, near_late, far_out, routers_grad, rows_grad = lax.optimization_barrier(
        (near_in, near_late, far_out, routers_grad, rows_grad)
    )
    near_in = jnp.concatenate([near_in, near_late], axis=1)
    out_sum = add_up(far_out)
    far_in = own_parts(near_in, lax.axis_index("dp") // 2, groups, 2, "dp")
    far_in[1], routers_grad, rows_grad = lax.optimization_barrier(
        (far_in[1], routers_grad, rows_grad)
    )
    in_sum = add_up(far_in)
    d_first_out = out_sum[None, : first_out.shape[1]]
    d_first_in = in_sum[None, : first_in.shape[1]]
    late_share = in_sum[first_in.shape[1] :]
    early_share = out_sum[first_out.shape[1] :].reshape(4, width // devices, width)
    early_share = jnp.concatenate([early_share[k] for k in range(4)], axis=1)
    rows_grad = rows_grad.reshape(count, devices, share).transpose(1, 0, 2).reshape(devices, -1)
    routers_grad = routers_grad.reshape(2, 8, devices, feats)[:, :experts]
    routers_grad = routers_grad.transpose(2, 0, 1, 3).reshape(devices, -1)
    small_grad = jnp.concatenate([rows_grad, routers_grad], axis=1)
    small_share = jnp.sum(
        lax.all_to_all(small_grad, BOTH, split_axis=0, concat_axis=0, tiled=True), axis=0
    )
    rows_share = small_share[: count * share].reshape(count, share)
    routers_share = small_share[count * share :].reshape(2, experts, feats).transpose(0, 2, 1)

    return (
        output,
        d_start,
        d_embed,
        rows_share[0:5],
        routers_share[0],
        routers_share[1],
        d_first_in,
        d_first_out,
        d_second_in,
        d_second_out,
        late_share[:, : 3 * width],
        late_share[:, 3 * width :],
        rows_share[5:7],
        early_share[:, :width],
        early_share[:, 2 * width :],
        rows_share[7 : 7 + taps],
        rows_share[7 + taps],
        rows_share[8 + taps],
        early_share[:, width : 2 * width],
    )


def solution(mesh):
    split = P(BOTH, None)
    wide = P(None, BOTH)
    bank = P("expert", "dp", None)
    line = P(BOTH)
    in_specs = (
        (split,) * 6
        + (wide, split, split)
        + (bank,) * 4
        + (split, split, wide, split, split, wide, line, line, split)
    )
    out_specs = (
        (split,) * 3
        + (wide, split, split)
        + (bank,) * 4
        + (split, split, wide, split, split, wide, line, line, split)
    )
    return jax.shard_map(
        functools.partial(body, mesh.shape["dp"]),
        mesh=mesh,
        in_specs=in_specs,
        out_specs=out_specs,
        check_vma=False,
    )
```

```python
import functools
import math

import jax
import jax.numpy as jnp
import numpy as np
from jax import lax
from jax.experimental import pallas as pl
from jax.experimental.pallas import tpu as pltpu
from jax.sharding import PartitionSpec as P

H = 8
TILE = 128
epsilon = 1e-05
masked_score = -1e30
BOTH = ("dp", "expert")
f32 = jnp.float32
bf16 = jnp.bfloat16

VMEM = pl.BlockSpec(memory_space=pltpu.VMEM)
SMEM = pl.BlockSpec(memory_space=pltpu.SMEM)


def shape_of(dims, kind):
    return jax.ShapeDtypeStruct(dims, kind)


def run(kernel, args, in_specs, outs, scratch=(), flops=0, name=None, limit=56):
    moved = sum(math.prod(a.shape) * a.dtype.itemsize for a in list(args) + list(outs))
    results = pl.pallas_call(
        kernel,
        out_shape=outs,
        in_specs=in_specs,
        out_specs=[VMEM] * len(outs),
        scratch_shapes=list(scratch),
        compiler_params=pltpu.CompilerParams(vmem_limit_bytes=limit * 2**20),
        cost_estimate=pl.CostEstimate(flops=flops, bytes_accessed=moved, transcendentals=0),
        name=name,
    )(*args)
    return list(results)


def dot(left, right):
    return lax.dot_general(left, right, (((1,), (0,)), ((), ())), preferred_element_type=f32)


def dot_t(left, right):
    return lax.dot_general(left, right, (((1,), (1,)), ((), ())), preferred_element_type=f32)


def t_dot(left, right):
    return lax.dot_general(left, right, (((0,), (0,)), ((), ())), preferred_element_type=f32)


def iota(dims, axis):
    return lax.broadcasted_iota(jnp.int32, dims, axis)


def normalize(values):
    center = values - jnp.mean(values, axis=-1, keepdims=True)
    spread = jnp.mean(center * center, axis=-1, keepdims=True)
    inverse = lax.rsqrt(spread + epsilon)
    return center * inverse, inverse


def normalize_back(standard, inverse, gain, upstream):
    scaled = upstream * gain
    first = jnp.mean(scaled, axis=-1, keepdims=True)
    second = jnp.mean(scaled * standard, axis=-1, keepdims=True)
    return inverse * (scaled - first - standard * second)


def column_sum(values):
    return jnp.sum(values, axis=0, keepdims=True)


def sigmoid(values):
    return 1.0 / (1.0 + jnp.exp(-values))


def loop(count, body):
    def step(index, carry):
        body(index)
        return carry

    lax.fori_loop(0, count, step, 0)


def rows_at(index, size):
    return pl.ds(pl.multiple_of(index * size, size), size)


def slots_kernel(capacity, offset_ref, one_ref, two_ref, rows_ref, cols_ref, stack):
    length = rows_ref.shape[1]
    block = 256
    stack[...] = jnp.zeros_like(stack)
    for half, chosen_ref in enumerate((one_ref, two_ref)):
        chosen = chosen_ref[...]
        near = chosen ^ offset_ref[0]
        onehot = jnp.where(iota((8, length), 0) == near, 1.0, 0.0)
        onehot_low = onehot.astype(bf16)
        for index in range(length // block):
            earlier = iota((length, block), 0) < iota((length, block), 1) + index * block
            counts = dot(onehot_low, jnp.where(earlier, 1.0, 0.0).astype(bf16))
            span = slice(index * block, (index + 1) * block)
            rank = column_sum(onehot[:, span] * counts)
            stack[half : half + 1, span] = (near[:, span] * capacity).astype(f32) + rank
        stack[2 + half : 3 + half, :] = chosen.astype(f32)
    rows_ref[...] = stack[:8, :].astype(jnp.int32)
    for index in range(length // TILE):
        span = slice(index * TILE, (index + 1) * TILE)
        cols_ref[span, :] = jnp.transpose(stack[:, span]).astype(jnp.int32)


def find_slots(routes_one, routes_two, offset, capacity):
    length = routes_one.shape[0]
    return run(
        functools.partial(slots_kernel, capacity),
        (offset.reshape(1), routes_one.reshape(1, length), routes_two.reshape(1, length)),
        [SMEM, VMEM, VMEM],
        [shape_of((8, length), jnp.int32), shape_of((length, TILE), jnp.int32)],
        [pltpu.VMEM((TILE, length), f32)],
        flops=8 * length * length * 128,
        name="slots",
    )


PARTS = 4


def dispatch(low_ref, slot_row, out_refs):
    block = out_refs[0].shape[0]
    length = low_ref.shape[0]
    for index, out_ref in enumerate(out_refs):
        ids = iota((block, length), 0) + index * block
        onehot = jnp.where(ids == slot_row, 1.0, 0.0).astype(bf16)
        out_ref[...] = dot(onehot, low_ref[...]).astype(bf16)


def join_blocks(block_refs, whole_ref):
    block = block_refs[0].shape[0]
    for index, block_ref in enumerate(block_refs):
        whole_ref[index * block : (index + 1) * block, :] = block_ref[...]


def collect(slot_col, table_ref):
    rows = slot_col.shape[0]
    slots = table_ref.shape[0]
    onehot = jnp.where(iota((rows, slots), 1) == slot_col, 1.0, 0.0).astype(bf16)
    return dot(onehot, table_ref[...])


def route_block(low, embed, router_ref, picks, experts):
    width = low.shape[1]
    logits = dot(low, router_ref[:width, :]) + dot(embed, router_ref[width:, :])
    lanes = iota(logits.shape, 1)
    inside = lanes < experts
    logits = jnp.where(inside, logits, masked_score)
    raised = jnp.where(inside, jnp.exp(logits - jnp.max(logits, axis=1, keepdims=True)), 0.0)
    probs = raised / jnp.sum(raised, axis=1, keepdims=True)
    gate = jnp.sum(jnp.where(lanes == picks, probs, 0.0), axis=1, keepdims=True)
    return probs, gate


BLOCK = 256


def front_kernel(
    experts, hidden_ref, embed_ref, gain_ref, router_ref, cols_ref, slot_row_ref, *refs,
):
    out_refs, (probs_ref, gate_ref, low_ref) = refs[:PARTS], refs[PARTS:]
    length = hidden_ref.shape[0]

    def step(index):
        at = rows_at(index, BLOCK)
        standard, unused = normalize(hidden_ref[at, :].astype(f32))
        low = (standard * gain_ref[0:1, :]).astype(bf16)
        low_ref[at, :] = low
        probs, gate = route_block(low, embed_ref[at, :], router_ref, cols_ref[at, 2:3], experts)
        probs_ref[at, :] = probs
        gate_ref[at, :] = gate

    loop(length // BLOCK, step)
    dispatch(low_ref, slot_row_ref[0:1, :], out_refs)


def expert_forward_kernel(count, in_ref, out_ref, *refs):
    for x_ref, y_ref in zip(refs[:count], refs[count:]):
        inner = dot(x_ref[...], in_ref[...])
        hidden = (inner * sigmoid(inner)).astype(bf16)
        y_ref[...] = dot(hidden, out_ref[...]).astype(bf16)


def expert_forward(received, weight_in, weight_out):
    block, width = received[0].shape
    count = len(received)
    return run(
        functools.partial(expert_forward_kernel, count),
        (weight_in, weight_out) + tuple(received),
        [VMEM] * (2 + count),
        [shape_of((block, width), bf16)] * count,
        flops=4 * count * block * width * weight_in.shape[1],
        name="experts",
        limit=32,
    )


def forward_in_turn(received, pair):
    near, far = lax.optimization_barrier((expert_forward(received[:2], *pair), received[2:]))
    return near + expert_forward(far[:1], *pair) + expert_forward(far[1:], *pair)


def expert_backward_kernel(count, in_ref, out_ref, *refs):
    x_refs, dy_refs, refs = refs[:count], refs[count : 2 * count], refs[2 * count :]
    extra, refs = refs[: len(refs) - 3 * count], refs[len(refs) - 3 * count :]
    if extra:
        normed_ref, mixed_ref, table_ref, sinus_ref, grad_ref = extra
        width = normed_ref.shape[1]
        for part in range(3):
            lanes = slice(part * width, (part + 1) * width)
            grad_ref[:, lanes] = t_dot(normed_ref[...], mixed_ref[:, lanes]).astype(bf16)
        grad_ref[:, 3 * width :] = jnp.transpose(dot(table_ref[...], sinus_ref[...])).astype(bf16)
    dx_refs, hidden_refs, dinner_refs = refs[:count], refs[count : 2 * count], refs[2 * count :]
    for x_ref, dy_ref, dx_ref, hidden_ref, dinner_ref in zip(
        x_refs, dy_refs, dx_refs, hidden_refs, dinner_refs
    ):
        inner = dot(x_ref[...], in_ref[...])
        gates = sigmoid(inner)
        hidden = inner * gates
        hidden_ref[...] = hidden.astype(bf16)
        d_hidden = dot_t(dy_ref[...], out_ref[...])
        d_inner = (d_hidden * (gates + hidden * (1.0 - gates))).astype(bf16)
        dinner_ref[...] = d_inner
        dx_ref[...] = dot_t(d_inner, in_ref[...]).astype(bf16)


def expert_backward(received, d_result, weight_in, weight_out, extra=()):
    block, width = received[0].shape
    inner = weight_in.shape[1]
    count = len(received)
    more = [shape_of((width, 4 * width), bf16)] if extra else []
    outs = run(
        functools.partial(expert_backward_kernel, count),
        (weight_in, weight_out) + tuple(received) + tuple(d_result) + tuple(extra),
        [VMEM] * (2 + 2 * count + len(extra)),
        more + [shape_of((block, width), bf16)] * count + [shape_of((block, inner), bf16)] * (2 * count),
        flops=6 * count * block * width * inner,
        name="experts_back",
        limit=48 if extra else 40,
    )
    more, outs = outs[: len(more)], outs[len(more) :]
    return more, outs[:count], outs[count : 2 * count], outs[2 * count :]


def backward_in_turn(received, d_result, pair, extra=()):
    near, far = lax.optimization_barrier(
        (expert_backward(received[:2], d_result[:2], *pair, extra), d_result[2:])
    )
    parts = [
        near,
        expert_backward(received[2:3], far[:1], *pair),
        expert_backward(received[3:], far[1:], *pair),
    ]
    return [sum((list(part[k]) for part in parts), []) for k in range(4)]


def tile_window(starts_ref, first, length):
    count = starts_ref.shape[1]
    low = jnp.int32(0)
    high = jnp.int32(length)
    for k in range(1, count):
        low = jnp.where(starts_ref[0, k] <= first, starts_ref[0, k], low)
    for k in range(count - 1, 0, -1):
        high = jnp.where(starts_ref[0, k] > first + (TILE - 1), starts_ref[0, k], high)
    low = low // TILE
    steps = ((high + (TILE - 1)) // TILE - low + 1) // 2
    return jnp.minimum(low, length // TILE - 2 * steps), steps


def numbers_at(starts_ref, positions):
    total = jnp.zeros(positions.shape, jnp.int32)
    for k in range(1, starts_ref.shape[1]):
        total = total + jnp.where(positions >= starts_ref[0, k], 1, 0)
    return total


def same_tile(starts_ref, first_query, first_key):
    rows = numbers_at(starts_ref, iota((TILE, TILE), 0) + first_query)
    cols = numbers_at(starts_ref, iota((TILE, TILE), 1) + first_key)
    return rows == cols


PAD = 2


def chunk_rows(query_tile, key_tile, length, count, mirrored=False):
    tiles = length // TILE
    index = tiles - 1 - query_tile + key_tile - (tiles // 2 - PAD)
    if mirrored:
        index = tiles + 2 * PAD - count - index
    index = jnp.clip(index, 0, tiles + 2 * PAD - count)
    return pl.ds(pl.multiple_of(index * TILE, TILE), count * TILE)


def halves(values):
    left = iota(values.shape, 1) < TILE // 2
    zero = jnp.zeros_like(values)
    return jnp.concatenate(
        [jnp.where(left, values, zero), jnp.where(left, zero, values)], axis=0
    )


def turned_halves(values):
    turned = jnp.transpose(values)
    top = iota(turned.shape, 0) < TILE // 2
    zero = jnp.zeros_like(turned)
    return jnp.concatenate([jnp.where(top, turned, zero), jnp.where(top, zero, turned)], axis=1)


def skew(values):
    return jnp.concatenate(
        [
            pltpu.roll(values[:TILE], 1, 1, stride=1, stride_axis=0),
            pltpu.roll(values[TILE:], 1, 1, stride=1, stride_axis=0),
        ],
        axis=0,
    )


def mirror(values):
    row, col = iota((2 * TILE, 2 * TILE), 0), iota((2 * TILE, 2 * TILE), 1)
    flip = (row % TILE + col % TILE == TILE - 1) & (row // TILE == col // TILE)
    return dot(values, jnp.where(flip, 1.0, 0.0).astype(bf16))


def twice(values):
    return jnp.concatenate([values, values], axis=0)


PAIRS = H // 2


def attend_forward(
    starts_ref, qu_ref, qv_ref, k_ref, v_ref, t_ref, context_ref, logs_ref,
    qum, qvm, scores, rolled, peaks, sums, mixed,
):
    length = qu_ref.shape[0]
    tiles = length // TILE

    def query_step(tile):
        first = tile * TILE
        at = rows_at(tile, TILE)
        low, steps = tile_window(starts_ref, first, length)
        chunk = chunk_rows(tile, low, length, 1)
        for p in range(PAIRS):
            lanes = slice(p * TILE, (p + 1) * TILE)
            qum[p] = halves(qu_ref[at, lanes])
            qvm[p] = halves(qv_ref[at, lanes])
            rolled[p] = skew(dot_t(qvm[p], t_ref[chunk, lanes]))
            peaks[p] = jnp.full((2 * TILE, TILE), masked_score, f32)
            sums[p] = jnp.zeros((2 * TILE, TILE), f32)
            mixed[p] = jnp.zeros((2 * TILE, TILE), f32)
        lower = twice(iota((TILE, TILE), 1) <= iota((TILE, TILE), 0))

        def score_step(step, carry):
            key = low + 2 * step
            keys = pl.ds(pl.multiple_of(key * TILE, TILE), 2 * TILE)
            same_one = twice(same_tile(starts_ref, first, key * TILE))
            same_two = twice(same_tile(starts_ref, first, key * TILE + TILE))
            chunks = chunk_rows(tile, key + 1, length, 2)
            for p in range(PAIRS):
                lanes = slice(p * TILE, (p + 1) * TILE)
                content = dot_t(qum[p], k_ref[keys, lanes])
                fresh = dot_t(qvm[p], t_ref[chunks, lanes])
                one, two = skew(fresh[:, :TILE]), skew(fresh[:, TILE:])
                value_one = content[:, :TILE] + jnp.where(lower, rolled[p], one)
                value_two = content[:, TILE:] + jnp.where(lower, one, two)
                value_one = jnp.where(same_one, value_one, masked_score)
                value_two = jnp.where(same_two, value_two, masked_score)
                rolled[p] = two
                scores[2 * step, p] = value_one
                scores[2 * step + 1, p] = value_two
                peaks[p] = jnp.maximum(peaks[p], jnp.maximum(value_one, value_two))
            return carry

        lax.fori_loop(0, steps, score_step, 0)
        for p in range(PAIRS):
            peaks[p] = jnp.broadcast_to(
                jnp.max(peaks[p], axis=1, keepdims=True), (2 * TILE, TILE)
            )

        def value_step(step, carry):
            keys = pl.ds(pl.multiple_of((low + 2 * step) * TILE, TILE), 2 * TILE)
            for p in range(PAIRS):
                lanes = slice(p * TILE, (p + 1) * TILE)
                one = jnp.exp(scores[2 * step, p] - peaks[p])
                two = jnp.exp(scores[2 * step + 1, p] - peaks[p])
                sums[p] += one + two
                raised = jnp.concatenate([one.astype(bf16), two.astype(bf16)], axis=1)
                mixed[p] += dot(raised, v_ref[keys, lanes])
            return carry

        lax.fori_loop(0, steps, value_step, 0)
        left = iota((TILE, TILE), 1) < TILE // 2
        logs = jnp.zeros((TILE, TILE), f32)
        lane = iota((TILE, TILE), 1)
        for p in range(PAIRS):
            lanes = slice(p * TILE, (p + 1) * TILE)
            total = jnp.sum(sums[p], axis=1, keepdims=True)
            result = mixed[p] * (1.0 / total)
            context_ref[at, lanes] = jnp.where(left, result[:TILE], result[TILE:]).astype(bf16)
            logsum = peaks[p] + jnp.log(total)
            logs = jnp.where(lane == 2 * p, logsum[:TILE], logs)
            logs = jnp.where(lane == 2 * p + 1, logsum[TILE:], logs)
        logs_ref[at, :] = logs

    loop(tiles, query_step)


def attend_scratch(length):
    pair = (PAIRS, 2 * TILE, TILE)
    return [
        pltpu.VMEM(pair, bf16),
        pltpu.VMEM(pair, bf16),
        pltpu.VMEM((length // TILE,) + pair, f32),
        pltpu.VMEM(pair, f32),
        pltpu.VMEM(pair, f32),
        pltpu.VMEM(pair, f32),
        pltpu.VMEM(pair, f32),
    ]


STRIP = 32


def strips():
    return [
        (slice(head * TILE + row, head * TILE + row + STRIP), row)
        for head in range(2)
        for row in range(0, TILE, STRIP)
    ]


def skew_strip(values, row):
    return pltpu.roll(values, 1 + row, 1, stride=1, stride_axis=0)


def attend_backward(
    starts_ref, qu_ref, qv_ref, k_ref, v_ref, t_ref, mirrored_ref, context_ref, logs_ref, dcontext_ref,
    dm_ref, dk_ref, dv_ref, dt_ref, dbias_ref,
    qum, qvm, dcm, qut, qvt, dct, logs, deltas, rolled, unrolled, dqu, dqv, first_s, second_s, third_s,
    probs_s, dlow_s, moved_s,
):
    length, width = qu_ref.shape
    tiles = length // TILE
    scale = 1.0 / math.sqrt(width // H)
    dk_ref[...] = jnp.zeros_like(dk_ref)
    dv_ref[...] = jnp.zeros_like(dv_ref)
    dt_ref[...] = jnp.zeros_like(dt_ref)
    dbias_ref[...] = jnp.zeros_like(dbias_ref)

    def query_step(tile):
        first = tile * TILE
        at = rows_at(tile, TILE)
        low, steps = tile_window(starts_ref, first, length)
        chunk = chunk_rows(tile, low, length, 1)
        logs_tile = logs_ref[at, :]
        for p in range(PAIRS):
            lanes = slice(p * TILE, (p + 1) * TILE)
            query_u = halves(qu_ref[at, lanes])
            query_v = halves(qv_ref[at, lanes])
            upstream = halves(dcontext_ref[at, lanes])
            qum[p] = query_u
            qvm[p] = query_v
            dcm[p] = upstream
            qut[p] = turned_halves(qu_ref[at, lanes])
            qvt[p] = turned_halves(qv_ref[at, lanes])
            dct[p] = turned_halves(dcontext_ref[at, lanes])
            delta = jnp.sum(
                upstream.astype(f32) * twice(context_ref[at, lanes].astype(f32)),
                axis=1,
                keepdims=True,
            )
            deltas[p] = jnp.broadcast_to(delta, (2 * TILE, TILE))
            logs[p, :TILE] = jnp.broadcast_to(logs_tile[:, 2 * p : 2 * p + 1], (TILE, TILE))
            logs[p, TILE:] = jnp.broadcast_to(logs_tile[:, 2 * p + 1 : 2 * p + 2], (TILE, TILE))
            rolled[p] = skew(dot_t(query_v, t_ref[chunk, lanes]))
            unrolled[p] = jnp.zeros((2 * TILE, TILE), f32)
            dqu[p] = jnp.zeros((2 * TILE, TILE), f32)
            dqv[p] = jnp.zeros((2 * TILE, TILE), f32)
        lower = twice(iota((TILE, TILE), 1) <= iota((TILE, TILE), 0))

        def step_body(step, carry):
            key = low + 2 * step
            keys = pl.ds(pl.multiple_of(key * TILE, TILE), 2 * TILE)
            same_one = same_tile(starts_ref, first, key * TILE)
            same_two = same_tile(starts_ref, first, key * TILE + TILE)
            before = chunk_rows(tile, key, length, 2, True)
            after = chunk_rows(tile, key + 1, length, 2)
            for p in range(PAIRS):
                lanes = slice(p * TILE, (p + 1) * TILE)
                first_s[p] = dot_t(qum[p], k_ref[keys, lanes])
                second_s[p] = dot_t(qvm[p], t_ref[after, lanes])
                third_s[p] = dot_t(dcm[p], v_ref[keys, lanes])
            for p in range(PAIRS):
                for rows, row in strips():
                    near = iota((STRIP, TILE), 1) <= iota((STRIP, TILE), 0) + row
                    span = slice(row, row + STRIP)
                    one = skew_strip(second_s[p, rows, :TILE], row)
                    two = skew_strip(second_s[p, rows, TILE:], row)
                    value_one = first_s[p, rows, :TILE] + jnp.where(near, rolled[p, rows], one)
                    value_two = first_s[p, rows, TILE:] + jnp.where(near, one, two)
                    rolled[p, rows] = two
                    log, delta = logs[p, rows], deltas[p, rows]
                    probs_one = jnp.where(same_one[span], jnp.exp(value_one - log), 0.0)
                    probs_two = jnp.where(same_two[span], jnp.exp(value_two - log), 0.0)
                    probs_s[p, rows, :TILE] = probs_one.astype(bf16)
                    probs_s[p, rows, TILE:] = probs_two.astype(bf16)
                    dlow_s[p, rows, :TILE] = (probs_one * (third_s[p, rows, :TILE] - delta)).astype(bf16)
                    dlow_s[p, rows, TILE:] = (probs_two * (third_s[p, rows, TILE:] - delta)).astype(bf16)
            for p in range(PAIRS):
                lanes = slice(p * TILE, (p + 1) * TILE)
                second_s[p] = mirror(dlow_s[p])
                dv_ref[lanes, keys] += dot(dct[p], probs_s[p])
                dk_ref[lanes, keys] += dot(qut[p], dlow_s[p])
                dqu[p] += dot(dlow_s[p], k_ref[keys, lanes])
            for p in range(PAIRS):
                for rows, row in strips():
                    near = iota((STRIP, TILE), 1) <= iota((STRIP, TILE), 0) + row
                    one = skew_strip(second_s[p, rows, :TILE], row)
                    two = skew_strip(second_s[p, rows, TILE:], row)
                    moved_s[p, rows, :TILE] = jnp.where(near, two, one).astype(bf16)
                    moved_s[p, rows, TILE:] = jnp.where(near, one, unrolled[p, rows]).astype(bf16)
                    unrolled[p, rows] = two
            for p in range(PAIRS):
                lanes = slice(p * TILE, (p + 1) * TILE)
                dt_ref[lanes, before] += dot(qvt[p], moved_s[p])
                dqv[p] += dot(moved_s[p], mirrored_ref[before, lanes])
            return carry

        lax.fori_loop(0, steps, step_body, 0)
        last = chunk_rows(tile, low + 2 * steps, length, 1, True)
        left = iota((TILE, TILE), 1) < TILE // 2
        for p in range(PAIRS):
            lanes = slice(p * TILE, (p + 1) * TILE)
            moved = jnp.where(lower, 0.0, unrolled[p]).astype(bf16)
            dt_ref[lanes, last] += dot(qvt[p], moved)
            full_u = dqu[p]
            full_v = dqv[p] + dot(moved, mirrored_ref[last, lanes])
            part_u = jnp.where(left, full_u[:TILE], full_u[TILE:]) * scale
            part_v = jnp.where(left, full_v[:TILE], full_v[TILE:]) * scale
            dbias_ref[0:1, lanes] += column_sum(part_u)
            dbias_ref[1:2, lanes] += column_sum(part_v)
            dm_ref[at, lanes] = (part_u + part_v).astype(bf16)

    loop(tiles, query_step)

    def finish(index):
        at = rows_at(index, TILE)
        for p in range(PAIRS):
            lanes = slice(p * TILE, (p + 1) * TILE)
            key_lanes = slice(width + p * TILE, width + (p + 1) * TILE)
            value_lanes = slice(2 * width + p * TILE, 2 * width + (p + 1) * TILE)
            dm_ref[at, key_lanes] = jnp.transpose(dk_ref[lanes, at].astype(bf16))
            dm_ref[at, value_lanes] = jnp.transpose(dv_ref[lanes, at].astype(bf16))

    loop(tiles, finish)


def attend_back_scratch():
    pair = (PAIRS, 2 * TILE, TILE)
    turned = (PAIRS, TILE, 2 * TILE)
    square = (PAIRS, 2 * TILE, 2 * TILE)
    return (
        [pltpu.VMEM(dims, bf16) for dims in (pair,) * 3 + (turned,) * 3]
        + [pltpu.VMEM(dims, f32) for dims in (pair,) * 6 + (square,) * 3]
        + [pltpu.VMEM(square, bf16) for unused in range(3)]
    )


def dense_parts(dense_ref):
    width = dense_ref.shape[0]
    cuts = (0, 3, 4, 5, 6, 8)
    return [
        dense_ref.at[:, pl.ds(start * width, (stop - start) * width)]
        for start, stop in zip(cuts[:-1], cuts[1:])
    ]


def shifted(values, reach, taps):
    rows = values.shape[0]
    found = {}
    for rest in range(8):
        starts = [EDGE - reach + k for k in range(taps) if (EDGE - reach + k) % 8 == rest]
        turned = pltpu.roll(values, (rows - rest) % rows, 0) if rest else values
        for start in starts:
            found[start - EDGE + reach] = turned[start - rest : start - rest + rows - 2 * EDGE]
    return [found[k] for k in range(taps)]


def at_edges(starts_ref, length, step):
    for k in range(1, starts_ref.shape[1]):
        edge = starts_ref[0, k]

        @pl.when(edge < length)
        def unused():
            start = jnp.minimum((edge - 8) // 8 * 8, length - 2 * EDGE)
            start = pl.multiple_of(start, 8)
            step(start, iota((2 * EDGE, TILE), 0) + start)


def spread_rows(rows_ref, out_ref):
    width = rows_ref.shape[1]
    for row in range(out_ref.shape[2] // width):
        lanes = slice(row * width, (row + 1) * width)
        out_ref[:, :, lanes] = jnp.broadcast_to(
            rows_ref[row : row + 1, :][None], (out_ref.shape[0], 1, width)
        )


EDGE = 16


def middle_kernel(
    starts_ref, hidden_ref, cols_ref, gate_ref, gains_ref, dense_ref, bias_ref, taps_ref, sinus_ref,
    *refs,
):
    returned_refs, refs = refs[:PARTS], refs[PARTS:]
    h1_ref, h2_ref, qu_ref, qv_ref, k_ref, v_ref, t_ref, context_ref, logs_ref = refs[:9]
    conv_ref, sums_ref, padded, sums, returned_ref = refs[9:14]
    attend = refs[14:]
    join_blocks(returned_refs, returned_ref)
    length, width = h1_ref.shape
    scale = 1.0 / math.sqrt(width // H)
    in_ref, place_ref, mix_ref, unused, point_ref = dense_parts(dense_ref)

    def queries_step(index):
        at = rows_at(index, BLOCK)
        picked = collect(cols_ref[at, 0:1], returned_ref)
        h1 = hidden_ref[at, :].astype(f32) + 0.5 * gate_ref[at, :] * picked
        h1_ref[at, :] = h1
        standard, unused = normalize(h1)
        low = (standard * gains_ref[1:2, :]).astype(bf16)
        queries = dot(low, in_ref[:, :width])
        qu_ref[at, :] = ((queries + bias_ref[0:1, :]).astype(bf16).astype(f32) * scale).astype(bf16)
        qv_ref[at, :] = ((queries + bias_ref[1:2, :]).astype(bf16).astype(f32) * scale).astype(bf16)
        k_ref[at, :] = dot(low, in_ref[:, width : 2 * width]).astype(bf16)
        v_ref[at, :] = dot(low, in_ref[:, 2 * width :]).astype(bf16)
        table_at = pl.ds(pl.multiple_of(index * BLOCK + edge, TILE), BLOCK)
        t_ref[table_at, :] = dot(sinus_ref[at, :], place_ref[...]).astype(bf16)

    edge = PAD * TILE
    t_ref[:edge, :] = jnp.zeros((edge, width), bf16)
    t_ref[edge + length :, :] = jnp.zeros((edge, width), bf16)
    loop(length // BLOCK, queries_step)
    attend_forward(
        starts_ref, qu_ref, qv_ref, k_ref, v_ref, t_ref, context_ref, logs_ref, *attend
    )
    padded[:EDGE, :] = jnp.zeros((EDGE, width), f32)
    padded[EDGE + length :, :] = jnp.zeros((EDGE, width), f32)

    def gates_step(index):
        at = rows_at(index, BLOCK)
        h2 = h1_ref[at, :] + dot(context_ref[at, :], mix_ref[...])
        h2_ref[at, :] = h2
        standard, unused = normalize(h2)
        low = (standard * gains_ref[2:3, :]).astype(bf16)
        value = dot(low, point_ref[:, :width])
        gates = dot(low, point_ref[:, width:])
        padded[pl.ds(pl.multiple_of(index * BLOCK + EDGE, EDGE), BLOCK), :] = value * sigmoid(gates)

    loop(length // BLOCK, gates_step)
    sums[...] = jnp.zeros_like(sums)
    taps = taps_ref.shape[0] - 1
    reach = taps // 2
    frames = starts_ref[0, starts_ref.shape[1] - 1]

    def conv_step(index):
        first = index * TILE
        around = pl.ds(pl.multiple_of(first, TILE), TILE + 2 * EDGE)
        for part in range(width // TILE):
            lanes = slice(part * TILE, (part + 1) * TILE)
            total = jnp.zeros((TILE, TILE), f32)
            for tap, near in enumerate(shifted(padded[around, lanes], reach, taps)):
                total = total + near * taps_ref[tap : tap + 1, lanes]
            conv_ref[rows_at(index, TILE), lanes] = total

    loop(length // TILE, conv_step)

    def edge_step(start, place):
        here = numbers_at(starts_ref, place)
        masks = [numbers_at(starts_ref, place + (tap - reach)) == here for tap in range(taps)]
        around = pl.ds(start, 2 * EDGE + 2 * EDGE)
        for part in range(width // TILE):
            lanes = slice(part * TILE, (part + 1) * TILE)
            total = jnp.zeros(place.shape, f32)
            for tap, near in enumerate(shifted(padded[around, lanes], reach, taps)):
                total = total + jnp.where(masks[tap], near, 0.0) * taps_ref[tap : tap + 1, lanes]
            conv_ref[pl.ds(start, 2 * EDGE), lanes] = total

    at_edges(starts_ref, length, edge_step)

    def sums_step(index):
        at = rows_at(index, BLOCK)
        inside = (iota((BLOCK, 1), 0) + index * BLOCK) < frames
        kept = jnp.where(inside, conv_ref[at, :], 0.0)
        sums[0:1, :] += column_sum(kept)
        sums[1:2, :] += column_sum(kept * kept)

    loop(length // BLOCK, sums_step)
    sums[2:3, :] = jnp.zeros((1, width), f32) + frames.astype(f32)
    spread_rows(sums, sums_ref)


def batch_totals(totals_ref, width):
    totals = jnp.sum(totals_ref[...], axis=0)
    count = totals[:, 2 * width :]
    mean = totals[:, :width] / count
    variance = totals[:, width : 2 * width] / count - mean * mean
    return mean, lax.rsqrt(variance + epsilon), count


def batch_block(conv, mean, inverse, batch_ref):
    centred = conv - mean
    standard = centred * inverse
    batched = standard * batch_ref[0:1, :] + batch_ref[1:2, :]
    return centred, standard, batched


def second_kernel(
    experts, h2_ref, conv_ref, totals_ref, batch_ref, point_ref, embed_ref, gains_ref, router_ref,
    cols_ref, slot_row_ref, *refs,
):
    out_refs, refs = refs[:PARTS], refs[PARTS:]
    h3_ref, active_ref, probs_ref, gate_ref, stats_ref, low_ref = refs
    length, width = h2_ref.shape
    mean, inverse, count = batch_totals(totals_ref, width)
    stats_ref[0:1, :] = mean
    stats_ref[1:2, :] = inverse
    stats_ref[2:3, :] = count

    def step(index):
        at = rows_at(index, BLOCK)
        unused, unused, batched = batch_block(conv_ref[at, :], mean, inverse, batch_ref)
        active = (batched * sigmoid(batched)).astype(bf16)
        active_ref[at, :] = active
        h3 = h2_ref[at, :] + dot(active, point_ref[...])
        h3_ref[at, :] = h3
        standard, unused = normalize(h3)
        low = (standard * gains_ref[3:4, :]).astype(bf16)
        low_ref[at, :] = low
        probs, gate = route_block(low, embed_ref[at, :], router_ref, cols_ref[at, 3:4], experts)
        probs_ref[at, :] = probs
        gate_ref[at, :] = gate

    loop(length // BLOCK, step)
    dispatch(low_ref, slot_row_ref[1:2, :], out_refs)


def gate_back(upstream, picked, gate, probs, picks):
    d_gate = 0.5 * jnp.sum(upstream * picked, axis=1, keepdims=True)
    onehot = jnp.where(iota(probs.shape, 1) == picks, 1.0, 0.0)
    return (d_gate * gate) * (onehot - probs)


def turn_kernel(
    h3_ref, cols_ref, gate_ref, probs_ref, slot_row_ref, gains_ref, cotangent_ref, *refs,
):
    returned_refs, out_refs, refs = refs[:PARTS], refs[PARTS : 2 * PARTS], refs[2 * PARTS :]
    output_ref, d4_ref, dlogits_ref, dgain_ref, low_ref, returned_ref = refs
    length = h3_ref.shape[0]
    join_blocks(returned_refs, returned_ref)
    dgain_ref[...] = jnp.zeros_like(dgain_ref)

    def step(index):
        at = rows_at(index, BLOCK)
        picked = collect(cols_ref[at, 1:2], returned_ref)
        gate = gate_ref[at, :]
        h4 = h3_ref[at, :] + 0.5 * gate * picked
        standard, inverse = normalize(h4)
        gain = gains_ref[4:5, :]
        output_ref[at, :] = (standard * gain).astype(bf16)
        upstream = cotangent_ref[at, :].astype(f32)
        dgain_ref[0:1, :] += column_sum(upstream * standard)
        d4 = normalize_back(standard, inverse, gain, upstream)
        d4_ref[at, :] = d4
        dlogits_ref[at, :] = gate_back(d4, picked, gate, probs_ref[at, :], cols_ref[at, 3:4])
        low_ref[at, :] = (0.5 * gate * d4).astype(bf16)

    loop(length // BLOCK, step)
    dispatch(low_ref, slot_row_ref[1:2, :], out_refs)


def router_back(dlogits, low, embed, router_ref, drouter_ref):
    width = low.shape[1]
    high = dlogits.astype(bf16)
    rest = (dlogits - high.astype(f32)).astype(bf16)
    d_low = dot_t(high, router_ref[:width, :]) + dot_t(rest, router_ref[:width, :])
    d_embed = dot_t(high, router_ref[width:, :]) + dot_t(rest, router_ref[width:, :])
    turned = jnp.transpose(dlogits)[:8, :]
    turned_high = turned.astype(bf16)
    turned_rest = (turned - turned_high.astype(f32)).astype(bf16)
    drouter_ref[:, :width] += dot(turned_high, low) + dot(turned_rest, low)
    drouter_ref[:, width:] += dot(turned_high, embed) + dot(turned_rest, embed)
    return d_low, d_embed


def second_back_kernel(
    cols_ref, dlogits_ref, h3_ref, d4_ref, embed_ref, router_ref, gains_ref, conv_ref, stats_ref,
    batch_ref, point_ref, *refs,
):
    dsent_refs, refs = refs[:PARTS], refs[PARTS:]
    d3_ref, dlow_ref, dz_ref, dembed_ref, drouter_ref, small_ref, sums_ref, sums, dsent_ref = refs
    length, width = h3_ref.shape
    drouter_ref[...] = jnp.zeros_like(drouter_ref)
    small_ref[...] = jnp.zeros_like(small_ref)
    sums[...] = jnp.zeros_like(sums)
    join_blocks(dsent_refs, dsent_ref)
    mean, batch_inverse = stats_ref[0:1, :], stats_ref[1:2, :]

    def step(index):
        at = rows_at(index, BLOCK)
        standard, inverse = normalize(h3_ref[at, :])
        gain = gains_ref[3:4, :]
        low = (standard * gain).astype(bf16)
        d_low, d_embed = router_back(
            dlogits_ref[at, :], low, embed_ref[at, :], router_ref, drouter_ref
        )
        dembed_ref[at, :] = d_embed
        d_norm = collect(cols_ref[at, 1:2], dsent_ref) + d_low
        small_ref[0:1, :] += column_sum(d_norm * standard)
        d3 = d4_ref[at, :] + normalize_back(standard, inverse, gain, d_norm)
        d3_ref[at, :] = d3
        d3_low = d3.astype(bf16)
        dlow_ref[at, :] = d3_low
        centred, normed, batched = batch_block(conv_ref[at, :], mean, batch_inverse, batch_ref)
        gates = sigmoid(batched)
        d_batched = dot_t(d3_low, point_ref[...]) * (gates + batched * gates * (1.0 - gates))
        small_ref[1:2, :] += column_sum(d_batched * normed)
        small_ref[2:3, :] += column_sum(d_batched)
        d_z = d_batched * batch_ref[0:1, :]
        dz_ref[at, :] = d_z
        sums[0:1, :] += column_sum(d_z)
        sums[1:2, :] += column_sum(d_z * centred)

    loop(length // BLOCK, step)
    spread_rows(sums, sums_ref)


def conv_back_kernel(
    starts_ref, conv_ref, dz_ref, stats_ref, dsums_ref, d3_ref, h2_ref, gains_ref, dense_ref, taps_ref,
    d2_ref, d2low_ref, dcontext_ref, n3_ref, dg_ref, small_ref, dtaps_ref, padded, linear, dtaps, edge_grad,
):
    length, width = h2_ref.shape
    unused, unused, mix_ref, unused, point_ref = dense_parts(dense_ref)
    taps = taps_ref.shape[0] - 1
    reach = taps // 2
    frames = starts_ref[0, starts_ref.shape[1] - 1]
    small_ref[...] = jnp.zeros_like(small_ref)
    dtaps[...] = jnp.zeros_like(dtaps)
    mean, batch_inverse, count = stats_ref[0:1, :], stats_ref[1:2, :], stats_ref[2:3, :]
    dsums = jnp.sum(dsums_ref[...], axis=0)
    d_variance = -0.5 * batch_inverse * batch_inverse * batch_inverse * dsums[:, width:]
    padded[:EDGE, :] = jnp.zeros((EDGE, width), f32)
    padded[EDGE + length :, :] = jnp.zeros((EDGE, width), f32)

    def conv_step(index):
        at = rows_at(index, BLOCK)
        centred = conv_ref[at, :] - mean
        inside = (iota((BLOCK, 1), 0) + index * BLOCK) < frames
        shared = (2.0 * d_variance * centred - batch_inverse * dsums[:, :width]) / count
        d_conv = batch_inverse * dz_ref[at, :] + jnp.where(inside, shared, 0.0)
        padded[pl.ds(pl.multiple_of(index * BLOCK + EDGE, EDGE), BLOCK), :] = d_conv
        standard, unused = normalize(h2_ref[at, :])
        low = (standard * gains_ref[2:3, :]).astype(bf16)
        n3_ref[at, :] = low
        value = dot(low, point_ref[:, :width])
        linear[at, :width] = value
        linear[at, width:] = sigmoid(dot(low, point_ref[:, width:]))

    loop(length // BLOCK, conv_step)

    def turn_step(index):
        at = rows_at(index, TILE)
        around = pl.ds(pl.multiple_of(index * TILE, TILE), TILE + 2 * EDGE)
        for part in range(width // TILE):
            lanes = slice(part * TILE, (part + 1) * TILE)
            other = slice(width + part * TILE, width + (part + 1) * TILE)
            value, gate = linear[at, lanes], linear[at, other]
            passed = value * gate
            total = jnp.zeros((TILE, TILE), f32)
            for step, near in enumerate(shifted(padded[around, lanes], reach, taps)):
                tap = taps - 1 - step
                total = total + near * taps_ref[tap : tap + 1, lanes]
                dtaps[tap, :, lanes] += jnp.sum((near * passed).reshape(TILE // 8, 8, TILE), axis=0)
            dg_ref[at, lanes] = (total * gate).astype(bf16)
            dg_ref[at, other] = (total * passed * (1.0 - gate)).astype(bf16)

    def edge_step(start, place):
        rows = 2 * EDGE
        at = pl.ds(start, rows)
        here = numbers_at(starts_ref, place)
        masks = [numbers_at(starts_ref, place - (reach - tap)) == here for tap in range(taps)]
        around = pl.ds(start, rows + 2 * EDGE)
        for part in range(width // TILE):
            lanes = slice(part * TILE, (part + 1) * TILE)
            other = slice(width + part * TILE, width + (part + 1) * TILE)
            value, gate = linear[at, lanes], linear[at, other]
            passed = value * gate
            total = jnp.zeros((rows, TILE), f32)
            for step, near in enumerate(shifted(padded[around, lanes], reach, taps)):
                tap = taps - 1 - step
                total = total + jnp.where(masks[step], near, 0.0) * taps_ref[tap : tap + 1, lanes]
                extra = jnp.where(masks[step], 0.0, near) * passed
                dtaps[tap, :, lanes] -= jnp.sum(extra.reshape(rows // 8, 8, TILE), axis=0)
            edge_grad[:, lanes] = total * gate
            edge_grad[:, other] = total * passed * (1.0 - gate)
        low = pl.multiple_of(jnp.minimum(start // 16 * 16, length - rows - 16), 16)
        wide = pl.ds(low, rows + 16)
        shift = start - low
        whole = dg_ref[wide, :].astype(f32)
        grad = edge_grad[...]
        zero = jnp.zeros((16, 2 * width), f32)
        head = jnp.concatenate([grad, zero], axis=0)
        middle = jnp.concatenate([zero[:8], grad, zero[:8]], axis=0)
        tail = jnp.concatenate([zero, grad], axis=0)
        place = iota((rows + 16, 1), 0) - shift
        moved = jnp.where(shift == 0, head, jnp.where(shift == 8, middle, tail))
        inside = (place >= 0) & (place < rows)
        dg_ref[wide, :] = jnp.where(inside, moved, whole).astype(bf16)

    loop(length // TILE, turn_step)
    at_edges(starts_ref, length, edge_step)
    dtaps_ref[...] = jnp.sum(dtaps[...], axis=1)

    def gates_step(index):
        at = rows_at(index, BLOCK)
        d_norm = dot_t(dg_ref[at, :], point_ref[...])
        standard, inverse = normalize(h2_ref[at, :])
        small_ref[0:1, :] += column_sum(d_norm * standard)
        d2 = d3_ref[at, :] + normalize_back(standard, inverse, gains_ref[2:3, :], d_norm)
        d2_ref[at, :] = d2
        low = d2.astype(bf16)
        d2low_ref[at, :] = low
        dcontext_ref[at, :] = dot_t(low, mix_ref[...]).astype(bf16)

    loop(length // BLOCK, gates_step)


def attend_back_kernel(
    starts_ref, d2_ref, dcontext_ref, h1_ref, gains_ref, dense_ref, sinus_ref, qu_ref, qv_ref, k_ref, v_ref,
    t_ref, context_ref, logs_ref, cols_ref, gate_ref, probs_ref, slot_row_ref, *refs,
):
    returned_refs, out_refs, refs = refs[:PARTS], refs[PARTS : 2 * PARTS], refs[2 * PARTS :]
    d1_ref, dlogits_ref, n2_ref, dm_ref, dtable_ref, small_ref = refs[:6]
    low_ref, mirrored_ref, returned_ref, dk_ref, dv_ref, dt_ref = refs[6:12]
    attend = refs[12:]
    length, width = h1_ref.shape
    in_ref, place_ref, unused, unused, unused = dense_parts(dense_ref)
    small_ref[...] = jnp.zeros_like(small_ref)
    join_blocks(returned_refs, returned_ref)

    def table_step(index):
        at = rows_at(index, BLOCK)
        table_at = pl.ds(pl.multiple_of(index * BLOCK + edge, TILE), BLOCK)
        mirrored_ref[table_at, :] = dot(sinus_ref[at, :], place_ref[...]).astype(bf16)

    edge = PAD * TILE
    mirrored_ref[:edge, :] = jnp.zeros((edge, width), bf16)
    mirrored_ref[edge + length :, :] = jnp.zeros((edge, width), bf16)
    loop(length // BLOCK, table_step)
    attend_backward(
        starts_ref, qu_ref, qv_ref, k_ref, v_ref, t_ref, mirrored_ref, context_ref, logs_ref, dcontext_ref,
        dm_ref, dk_ref, dv_ref, dt_ref, small_ref.at[pl.ds(8, 8)], *attend
    )

    def queries_step(index):
        at = rows_at(index, BLOCK)
        d_norm = dot_t(dm_ref[at, :], in_ref[...])
        standard, inverse = normalize(h1_ref[at, :])
        gain = gains_ref[1:2, :]
        n2_ref[at, :] = (standard * gain).astype(bf16)
        small_ref[1:2, :] += column_sum(d_norm * standard)
        d1 = d2_ref[at, :] + normalize_back(standard, inverse, gain, d_norm)
        d1_ref[at, :] = d1
        picked = collect(cols_ref[at, 0:1], returned_ref)
        gate = gate_ref[at, :]
        dlogits_ref[at, :] = gate_back(d1, picked, gate, probs_ref[at, :], cols_ref[at, 2:3])
        low_ref[at, :] = (0.5 * gate * d1).astype(bf16)

    loop(length // BLOCK, queries_step)
    dtable_ref[...] = dt_ref[:, PAD * TILE : PAD * TILE + length].astype(bf16)
    dispatch(low_ref, slot_row_ref[0:1, :], out_refs)


def last_kernel(
    cols_ref, dlogits_ref, hidden_ref, d1_ref, embed_ref, router_ref, gains_ref, dembed_two_ref,
    drouter_two_ref, mid_ref, conv_ref, two_ref, five_ref, taps_ref, in_low_ref, out_low_ref, *refs,
):
    dsent_refs, refs = refs[:PARTS], refs[PARTS:]
    d0_ref, dembed_ref, routers_ref, small_ref, in_ref, out_ref, dsent_ref = refs
    in_ref[...] = in_low_ref[...].astype(f32)
    out_ref[...] = out_low_ref[...].astype(f32)
    length = hidden_ref.shape[0]
    taps = small_ref.shape[0] - 9
    join_blocks(dsent_refs, dsent_ref)
    drouter_ref = routers_ref.at[pl.ds(0, 8)]
    drouter_ref[...] = jnp.zeros_like(drouter_ref)
    routers_ref[8:, :] = drouter_two_ref[...]
    small_ref[0:1, :] = jnp.zeros_like(small_ref[0:1, :])
    small_ref[1:2, :] = mid_ref[1:2, :]
    small_ref[2:3, :] = conv_ref[0:1, :]
    small_ref[3:4, :] = two_ref[0:1, :]
    small_ref[4:5, :] = five_ref[0:1, :]
    small_ref[5:7, :] = mid_ref[8:10, :]
    small_ref[7 : 7 + taps, :] = taps_ref[:taps, :]
    small_ref[7 + taps :, :] = two_ref[1:3, :]

    def step(index):
        at = rows_at(index, BLOCK)
        standard, inverse = normalize(hidden_ref[at, :].astype(f32))
        gain = gains_ref[0:1, :]
        low = (standard * gain).astype(bf16)
        d_low, d_embed = router_back(
            dlogits_ref[at, :], low, embed_ref[at, :], router_ref, drouter_ref
        )
        dembed_ref[at, :] = d_embed + dembed_two_ref[at, :]
        d_norm = collect(cols_ref[at, 0:1], dsent_ref) + d_low
        small_ref[0:1, :] += column_sum(d_norm * standard)
        d0_ref[at, :] = d1_ref[at, :] + normalize_back(standard, inverse, gain, d_norm)

    loop(length // BLOCK, step)


def gather_small(values):
    return lax.all_to_all(values, BOTH, split_axis=0, concat_axis=0, tiled=True)


def across(values, axis, size, offset):
    if not offset:
        return values
    return lax.ppermute(values, axis, [(i, i ^ offset) for i in range(size)])


def exchange(blocks, experts):
    per = experts // PARTS
    moved = []
    for index, block in enumerate(blocks):
        rows = block.shape[0] // per
        pieces = []
        for k in range(index * per, (index + 1) * per):
            piece = block[(k - index * per) * rows : (k - index * per + 1) * rows]
            pieces.append(across(piece, "expert", experts, k))
        moved.append(pieces[0] if per == 1 else jnp.concatenate(pieces, axis=0))
    return moved


def ring_place(index, size):
    return jnp.where(index % 2 == 0, index // 2, size - 1 - index // 2)


def ring_member(place, size):
    place = (place + 2 * size) % size
    return jnp.where(place < size // 2, 2 * place, 2 * (size - 1 - place) + 1)


def ring_pairs(size, forward):
    order = list(range(0, size, 2)) + list(range(size - 1, 0, -2))
    step = 1 if forward else -1
    return [(order[k], order[(k + step) % size]) for k in range(size)]


def ring_gather(shards, size):
    found = []
    for number, shard in enumerate(shards):
        ahead = size // 2 if number % 2 == 0 else (size - 1) // 2
        pieces = [None] * size
        pieces[0] = shard
        found.append((pieces, ahead))
    for step in range(1, size // 2 + 1):
        for pieces, ahead in found:
            if step <= ahead:
                pieces[step] = lax.ppermute(pieces[step - 1], "dp", ring_pairs(size, False))
            if step <= size - 1 - ahead:
                pieces[-step] = lax.ppermute(pieces[-step + 1 or 0], "dp", ring_pairs(size, True))
    return [pieces for pieces, unused in found]


def assemble_kernel(count, order_ref, *refs):
    size = (len(refs) - 1 - count) // count
    sems = refs[-1]
    copies = []
    for number in range(count):
        target = refs[count * size + number]
        for offset in range(size):
            piece = refs[number * size + offset]
            rows = piece.shape[0]
            start = pl.multiple_of(order_ref[offset] * rows, 16)
            copies.append(
                pltpu.make_async_copy(
                    piece, target.at[pl.ds(start, rows)], sems.at[number * size + offset]
                )
            )
    for copy in copies:
        copy.start()
    for copy in copies:
        copy.wait()


def assemble(shards, size):
    place = ring_place(lax.axis_index("dp"), size)
    order = ring_member(place + jnp.arange(size, dtype=jnp.int32), size).astype(jnp.int32)
    groups = ring_gather(shards, size)
    count = len(groups)
    anywhere = pl.BlockSpec(memory_space=pl.ANY)
    return pl.pallas_call(
        functools.partial(assemble_kernel, count),
        out_shape=[
            shape_of((size * shard.shape[0],) + shard.shape[1:], shard.dtype) for shard in shards
        ],
        in_specs=[SMEM] + [anywhere] * (count * size),
        out_specs=[VMEM] * count,
        scratch_shapes=[pltpu.SemaphoreType.DMA((count * size,))],
        name="assemble",
    )(order, *[piece for pieces in groups for piece in pieces])


def own_parts(values, place, size, stride, mesh_axis):
    parts = [lax.dynamic_index_in_dim(values, place, 0, keepdims=False)]
    for k in range(1, values.shape[0]):
        theirs = lax.dynamic_index_in_dim(values, place ^ k, 0, keepdims=False)
        parts.append(across(theirs, mesh_axis, size, k * stride))
    return parts


def add_up(parts):
    total = parts[0].astype(f32)
    for part in parts[1:]:
        total = total + part.astype(f32)
    return total


def keep_one(values, place, size, stride, mesh_axis):
    return add_up(own_parts(values, place, size, stride, mesh_axis))


def near_parts(values):
    groups = values.shape[0]
    values = values.reshape((groups // 2, 2) + values.shape[1:])
    bit = lax.axis_index("dp") % 2
    mine = lax.dynamic_index_in_dim(values, bit, 1, keepdims=False)
    theirs = lax.dynamic_index_in_dim(values, 1 - bit, 1, keepdims=False)
    return [mine, across(theirs, "dp", groups, 1)]


def near_half(values):
    return add_up(near_parts(values)).astype(bf16)


def expert_parts(values, experts):
    me = lax.axis_index("expert")
    return [
        across(lax.dynamic_index_in_dim(values, me ^ k, 1, keepdims=False), "expert", experts, k)
        for k in range(experts)
    ]


def rows_product(left, right):
    return lax.dot_general(left, right, (((0,), (0,)), ((), ())), preferred_element_type=f32)


def blocks_product(left, right):
    left, right = jnp.concatenate(left, axis=0), jnp.concatenate(right, axis=0)
    return rows_product(left, right).astype(bf16)


def scatter_offloaded(grad_in, grad_out):
    return (
        lax.psum_scatter(grad_in, "dp", scatter_dimension=0, tiled=True),
        lax.psum_scatter(grad_out, "dp", scatter_dimension=0, tiled=True),
    )


def split_columns(values):
    middle = values.shape[1] // 2
    return [values[:, :middle], values[:, middle:]]


def sinus_rows(length, width, upward):
    distance = (length // 2 - 1 - np.arange(length)).astype(np.float32)
    distance = distance[::-1] if upward else distance
    rates = np.exp(
        np.arange(width // 2).astype(np.float32) * np.float32(-2.0 * math.log(10000.0) / width)
    ).astype(np.float32)
    angles = (distance[:, None] * rates[None, :]).astype(np.float64)
    table = np.concatenate([np.sin(angles), np.cos(angles)], axis=1)
    return jnp.asarray(table.astype(np.float32)).astype(bf16)


def body(
    groups,
    inputs,
    embedding,
    cotangent,
    first_routes,
    second_routes,
    segment_starts,
    norm_gains,
    first_router,
    second_router,
    first_in,
    first_out,
    second_in,
    second_out,
    attention_in,
    position_weight,
    position_bias,
    attention_out,
    pointwise_in,
    depthwise_kernel,
    batch_gain,
    batch_bias,
    pointwise_out,
):
    length, width = inputs.shape
    experts = first_router.shape[1]
    devices = groups * experts
    capacity = 17 * length // (16 * experts)
    slots = experts * capacity
    inner = first_in.shape[2]
    share = norm_gains.shape[1]
    taps = depthwise_kernel.shape[0]
    feats = first_router.shape[0]

    rows = jnp.concatenate(
        [norm_gains, position_bias, depthwise_kernel, batch_gain[None], batch_bias[None]], axis=0
    )
    count = rows.shape[0]
    flat = jnp.concatenate(
        [rows.reshape(-1), first_router.T.reshape(-1), second_router.T.reshape(-1)]
    ).astype(f32)
    small = gather_small(jnp.broadcast_to(flat[None], (devices,) + flat.shape))
    rows_all = small[:, : count * share].reshape(devices, count, share)
    rows_all = rows_all.transpose(1, 0, 2).reshape(count, devices * share)
    routers = small[:, count * share :].reshape(devices, 2, experts, feats)
    routers = routers.transpose(1, 2, 0, 3).reshape(2, experts, devices * feats)
    routers = jnp.pad(routers, ((0, 0), (0, TILE - experts), (0, 0)))
    routers = routers.transpose(0, 2, 1).astype(bf16)
    gains = jnp.pad(rows_all[0:5], ((0, 3), (0, 0)))
    bias = jnp.pad(rows_all[5:7], ((0, 6), (0, 0)))
    kernel_taps = jnp.pad(rows_all[7 : 7 + taps], ((0, 1), (0, 0)))
    batch = jnp.pad(rows_all[7 + taps : 9 + taps], ((0, 6), (0, 0)))

    packed = jnp.concatenate(
        [attention_in, position_weight, attention_out, pointwise_out, pointwise_in], axis=1
    )
    dense = lax.all_gather(packed, BOTH, axis=0, tiled=True)
    point_out = dense[:, 5 * width : 6 * width]

    first_pair = assemble((first_in[0], first_out[0]), groups)
    second_pair = (
        lax.all_gather(second_in[0], "dp", axis=0, tiled=True),
        lax.all_gather(second_out[0], "dp", axis=0, tiled=True),
    )

    me = lax.axis_index("expert")
    slot_rows, slot_cols = find_slots(first_routes, second_routes, me, capacity)
    sinus = sinus_rows(length, width, False)
    mirrored = sinus_rows(length, width, True)
    row_low = shape_of((length, width), bf16)
    row_full = shape_of((length, width), f32)
    lane_full = shape_of((length, TILE), f32)
    table_low = shape_of((length + 2 * PAD * TILE, width), bf16)
    block_low = shape_of((slots // PARTS, width), bf16)
    slots_scratch = pltpu.VMEM((slots, width), bf16)
    sums_scratch = pltpu.VMEM((8, width), f32)
    column = shape_of((length, 1), f32)
    eight = shape_of((8, width), f32)
    low_scratch = pltpu.VMEM((length, width), bf16)

    *sent_one, probs_one, gate_one = run(
        functools.partial(front_kernel, experts),
        (inputs, embedding, gains, routers[0], slot_cols, slot_rows),
        [VMEM] * 6,
        [block_low] * PARTS + [lane_full, column],
        [low_scratch],
        flops=4 * slots * length * width,
        name="front",
    )
    received_one = exchange(sent_one, experts)
    result_one = (
        expert_forward(received_one[2:3], *first_pair) + expert_forward(received_one[3:], *first_pair)
    )
    result_one = expert_forward(received_one[:2], *first_pair) + result_one
    returned_one = exchange(result_one, experts)

    edge_scratch = pltpu.VMEM((length + 2 * EDGE, width), f32)
    (
        h1, h2, query_u, query_v, keys, values, table, context, logs, convolved, sums,
    ) = run(
        middle_kernel,
        (
            segment_starts, inputs, slot_cols, gate_one, gains, dense, bias, kernel_taps, sinus,
            *returned_one,
        ),
        [SMEM] + [VMEM] * (8 + PARTS),
        [row_full, row_full]
        + [row_low] * 4
        + [table_low, row_low, lane_full, row_full, shape_of((devices, 1, 3 * width), f32)],
        [edge_scratch, sums_scratch, slots_scratch] + attend_scratch(length),
        flops=16 * length * length * width,
        name="middle",
    )
    totals = gather_small(sums)

    *sent_two, h3, active, probs_two, gate_two, stats = run(
        functools.partial(second_kernel, experts),
        (
            h2, convolved, totals, batch, point_out, embedding, gains, routers[1], slot_cols, slot_rows,
        ),
        [VMEM] * 10,
        [block_low] * PARTS + [row_full, row_low, lane_full, column, eight],
        [low_scratch],
        flops=4 * slots * length * width,
        name="second",
    )
    received_two = exchange(sent_two, experts)
    result_two = forward_in_turn(received_two, second_pair)
    returned_two = exchange(result_two, experts)

    *d_sent_two, output, d4, dlogits_two, dgain_five = run(
        turn_kernel,
        (
            h3, slot_cols, gate_two, probs_two, slot_rows, gains, cotangent, *returned_two,
        ),
        [VMEM] * (7 + PARTS),
        [block_low] * PARTS + [row_low, row_full, lane_full, eight],
        [low_scratch, slots_scratch],
        flops=4 * slots * length * width,
        name="turn",
    )
    d_result_two = exchange(d_sent_two, experts)
    unused, d_received_two, hidden_two, d_inner_two = backward_in_turn(
        received_two, d_result_two, second_pair
    )
    d_back_two = exchange(d_received_two, experts)
    grad_in_two, grad_out_two, *d_back_two = lax.optimization_barrier(
        (
            blocks_product(received_two, d_inner_two), blocks_product(hidden_two, d_result_two), *d_back_two,
        )
    )
    d_second_in, d_second_out = scatter_offloaded(grad_in_two, grad_out_two)

    router_shape = shape_of((8, 2 * width), f32)
    d3, d3_low, d_z, dembed_two, drouter_two, small_two, dsums_part = run(
        second_back_kernel,
        (
            slot_cols, dlogits_two, h3, d4, embedding, routers[1], gains, convolved, stats, batch, point_out,
            *d_back_two,
        ),
        [VMEM] * (11 + PARTS),
        [row_full, row_low, row_full, row_full, router_shape, eight, shape_of((devices, 1, 2 * width), f32)],
        [sums_scratch, slots_scratch],
        flops=4 * slots * length * width,
        name="second_back",
    )
    dsums = gather_small(dsums_part)
    d_pointwise_out = rows_product(active, d3_low)

    d2, d2_low, d_context, normed_three, d_gates, small_conv, d_taps = run(
        conv_back_kernel,
        (segment_starts, convolved, d_z, stats, dsums, d3, h2, gains, dense, kernel_taps),
        [SMEM] + [VMEM] * 9,
        [
            row_full, row_low, row_low, row_low, shape_of((length, 2 * width), bf16), eight,
            shape_of((16, width), f32),
        ],
        [
            edge_scratch, pltpu.VMEM((length, 2 * width), f32), pltpu.VMEM((16, 8, width), f32),
            pltpu.VMEM((2 * EDGE, 2 * width), f32),
        ],
        flops=6 * length * width * width,
        name="conv_back",
    )
    value_grad, gates_grad = split_columns(rows_product(normed_three, d_gates))
    early = jnp.stack(
        [
            part.astype(bf16).reshape(groups, experts, width // devices, width)
            for part in (rows_product(context, d2_low), d_pointwise_out, value_grad, gates_grad)
        ],
        axis=2,
    )
    early = expert_parts(early, experts)
    *d_sent_one, d1, dlogits_one, normed_two, d_mixed, d_table, small_mid = run(
        attend_back_kernel,
        (
            segment_starts, d2, d_context, h1, gains, dense, mirrored, query_u, query_v, keys, values, table,
            context, logs, slot_cols, gate_one, probs_one, slot_rows, *returned_one,
        ),
        [SMEM] + [VMEM] * (17 + PARTS),
        [block_low] * PARTS
        + [
            row_full, lane_full, row_low, shape_of((length, 3 * width), bf16),
            shape_of((width, length), bf16), shape_of((16, width), f32),
        ],
        [
            low_scratch, pltpu.VMEM(table_low.shape, bf16), slots_scratch,
            pltpu.VMEM((width, length), f32), pltpu.VMEM((width, length), f32),
            pltpu.VMEM((width, length + 2 * PAD * TILE), f32),
        ]
        + attend_back_scratch(),
        flops=32 * length * length * width,
        name="attend_back",
    )
    early, *d_sent_one = lax.optimization_barrier((early, *d_sent_one))
    d_result_one = exchange(d_sent_one, experts)
    (late,), d_received_one, hidden_one, d_inner_one = backward_in_turn(
        received_one, d_result_one, first_pair, (normed_two, d_mixed, d_table, mirrored)
    )
    late = expert_parts(late.reshape(groups, experts, width // devices, 4 * width), experts)
    d_back_one = exchange(d_received_one, experts)
    early = add_up(early).astype(bf16).reshape(groups, -1, width)
    grad_out = blocks_product(hidden_one, d_result_one).reshape(groups, -1, width)
    near_out = near_half(jnp.concatenate([grad_out, early], axis=1))
    grad_in = blocks_product(received_one, d_inner_one).reshape(groups, -1, inner)
    near_out, grad_in, late, d_back_one = lax.optimization_barrier(
        (near_out, grad_in, late, d_back_one)
    )
    far_out = own_parts(near_out, lax.axis_index("dp") // 2, groups, 2, "dp")
    near_in = near_parts(grad_in)
    d_start, d_embed, routers_grad, rows_grad, d_second_in, d_second_out = run(
        last_kernel,
        (
            slot_cols, dlogits_one, inputs, d1, embedding, routers[0], gains, dembed_two,
            drouter_two, small_mid, small_conv, small_two, dgain_five, d_taps, d_second_in, d_second_out,
            *d_back_one,
        ),
        [VMEM] * (16 + PARTS),
        [
            row_full, row_full, shape_of((16, 2 * width), f32), shape_of((count, width), f32),
            shape_of(first_in.shape[1:], f32), shape_of(first_out.shape[1:], f32),
        ],
        [slots_scratch],
        flops=4 * slots * length * width,
        name="last",
    )

    near_in, late, far_out, routers_grad, rows_grad = lax.optimization_barrier(
        (near_in, late, far_out, routers_grad, rows_grad)
    )
    near_in = add_up(near_in).astype(bf16)
    near_late = near_half(add_up(late).astype(bf16))
    late_share = add_up(own_parts(near_late, lax.axis_index("dp") // 2, groups, 2, "dp"))
    out_sum = add_up(far_out)
    far_in = own_parts(near_in, lax.axis_index("dp") // 2, groups, 2, "dp")
    far_in[1], routers_grad, rows_grad = lax.optimization_barrier(
        (far_in[1], routers_grad, rows_grad)
    )
    in_sum = add_up(far_in)
    d_first_out = out_sum[None, : first_out.shape[1]]
    d_first_in = in_sum[None]
    early_share = out_sum[first_out.shape[1] :].reshape(4, width // devices, width)
    early_share = jnp.concatenate([early_share[k] for k in range(4)], axis=1)
    rows_grad = rows_grad.reshape(count, devices, share).transpose(1, 0, 2).reshape(devices, -1)
    routers_grad = routers_grad.reshape(2, 8, devices, feats)[:, :experts]
    routers_grad = routers_grad.transpose(2, 0, 1, 3).reshape(devices, -1)
    small_grad = jnp.concatenate([rows_grad, routers_grad], axis=1)
    small_share = jnp.sum(
        lax.all_to_all(small_grad, BOTH, split_axis=0, concat_axis=0, tiled=True), axis=0
    )
    rows_share = small_share[: count * share].reshape(count, share)
    routers_share = small_share[count * share :].reshape(2, experts, feats).transpose(0, 2, 1)

    return (
        output,
        d_start,
        d_embed,
        rows_share[0:5],
        routers_share[0],
        routers_share[1],
        d_first_in,
        d_first_out,
        d_second_in[None],
        d_second_out[None],
        late_share[:, : 3 * width],
        late_share[:, 3 * width :],
        rows_share[5:7],
        early_share[:, :width],
        early_share[:, 2 * width :],
        rows_share[7 : 7 + taps],
        rows_share[7 + taps],
        rows_share[8 + taps],
        early_share[:, width : 2 * width],
    )


def solution(mesh):
    split = P(BOTH, None)
    wide = P(None, BOTH)
    bank = P("expert", "dp", None)
    line = P(BOTH)
    in_specs = (
        (split,) * 6
        + (wide, split, split)
        + (bank,) * 4
        + (split, split, wide, split, split, wide, line, line, split)
    )
    out_specs = (
        (split,) * 3
        + (wide, split, split)
        + (bank,) * 4
        + (split, split, wide, split, split, wide, line, line, split)
    )
    return jax.shard_map(
        functools.partial(body, mesh.shape["dp"]),
        mesh=mesh,
        in_specs=in_specs,
        out_specs=out_specs,
        check_vma=False,
    )
```

```python
import functools
import math

import jax
import jax.numpy as jnp
import numpy as np
from jax import lax
from jax.experimental import pallas as pl
from jax.experimental.pallas import tpu as pltpu
from jax.sharding import PartitionSpec as P

H = 8
TILE = 128
epsilon = 1e-05
masked_score = -1e30
BOTH = ("dp", "expert")
f32 = jnp.float32
bf16 = jnp.bfloat16

VMEM = pl.BlockSpec(memory_space=pltpu.VMEM)
SMEM = pl.BlockSpec(memory_space=pltpu.SMEM)


def shape_of(dims, kind):
    return jax.ShapeDtypeStruct(dims, kind)


def run(kernel, args, in_specs, outs, scratch=(), flops=0, name=None, limit=56):
    moved = sum(math.prod(a.shape) * a.dtype.itemsize for a in list(args) + list(outs))
    results = pl.pallas_call(
        kernel,
        out_shape=outs,
        in_specs=in_specs,
        out_specs=[VMEM] * len(outs),
        scratch_shapes=list(scratch),
        compiler_params=pltpu.CompilerParams(vmem_limit_bytes=limit * 2**20),
        cost_estimate=pl.CostEstimate(flops=flops, bytes_accessed=moved, transcendentals=0),
        name=name,
    )(*args)
    return list(results)


def dot(left, right):
    return lax.dot_general(left, right, (((1,), (0,)), ((), ())), preferred_element_type=f32)


def dot_t(left, right):
    return lax.dot_general(left, right, (((1,), (1,)), ((), ())), preferred_element_type=f32)


def t_dot(left, right):
    return lax.dot_general(left, right, (((0,), (0,)), ((), ())), preferred_element_type=f32)


def iota(dims, axis):
    return lax.broadcasted_iota(jnp.int32, dims, axis)


def normalize(values):
    center = values - jnp.mean(values, axis=-1, keepdims=True)
    spread = jnp.mean(center * center, axis=-1, keepdims=True)
    inverse = lax.rsqrt(spread + epsilon)
    return center * inverse, inverse


def normalize_back(standard, inverse, gain, upstream):
    scaled = upstream * gain
    first = jnp.mean(scaled, axis=-1, keepdims=True)
    second = jnp.mean(scaled * standard, axis=-1, keepdims=True)
    return inverse * (scaled - first - standard * second)


def column_sum(values):
    return jnp.sum(values, axis=0, keepdims=True)


def sigmoid(values):
    return 1.0 / (1.0 + jnp.exp(-values))


def loop(count, body):
    if count <= 4:
        for index in range(count):
            body(index)
        return

    def step(index, carry):
        body(index)
        return carry

    lax.fori_loop(0, count, step, 0)


def span_at(start, size, step):
    if isinstance(start, int):
        return slice(start, start + size)
    return pl.ds(pl.multiple_of(start, step), size)


def rows_at(index, size):
    if isinstance(index, int):
        return slice(index * size, (index + 1) * size)
    return pl.ds(pl.multiple_of(index * size, size), size)


def slots_kernel(capacity, offset_ref, one_ref, two_ref, rows_ref, cols_ref, stack):
    length = rows_ref.shape[1]
    block = 256
    stack[...] = jnp.zeros_like(stack)
    for half, chosen_ref in enumerate((one_ref, two_ref)):
        chosen = chosen_ref[...]
        near = chosen ^ offset_ref[0]
        onehot = jnp.where(iota((8, length), 0) == near, 1.0, 0.0)
        onehot_low = onehot.astype(bf16)
        for index in range(length // block):
            earlier = iota((length, block), 0) < iota((length, block), 1) + index * block
            counts = dot(onehot_low, jnp.where(earlier, 1.0, 0.0).astype(bf16))
            span = slice(index * block, (index + 1) * block)
            rank = column_sum(onehot[:, span] * counts)
            stack[half : half + 1, span] = (near[:, span] * capacity).astype(f32) + rank
        stack[2 + half : 3 + half, :] = chosen.astype(f32)
    rows_ref[...] = stack[:8, :].astype(jnp.int32)
    for index in range(length // TILE):
        span = slice(index * TILE, (index + 1) * TILE)
        cols_ref[span, :] = jnp.transpose(stack[:, span]).astype(jnp.int32)


def find_slots(routes_one, routes_two, offset, capacity):
    length = routes_one.shape[0]
    return run(
        functools.partial(slots_kernel, capacity),
        (offset.reshape(1), routes_one.reshape(1, length), routes_two.reshape(1, length)),
        [SMEM, VMEM, VMEM],
        [shape_of((8, length), jnp.int32), shape_of((length, TILE), jnp.int32)],
        [pltpu.VMEM((TILE, length), f32)],
        flops=8 * length * length * 128,
        name="slots",
    )


PARTS = 4


def dispatch(low_ref, slot_row, out_refs):
    block = out_refs[0].shape[0]
    length = low_ref.shape[0]
    for index, out_ref in enumerate(out_refs):
        ids = iota((block, length), 0) + index * block
        onehot = jnp.where(ids == slot_row, 1.0, 0.0).astype(bf16)
        out_ref[...] = dot(onehot, low_ref[...]).astype(bf16)


def join_blocks(block_refs, whole_ref):
    block = block_refs[0].shape[0]
    for index, block_ref in enumerate(block_refs):
        whole_ref[index * block : (index + 1) * block, :] = block_ref[...]


def collect(slot_col, table_ref):
    rows = slot_col.shape[0]
    slots = table_ref.shape[0]
    onehot = jnp.where(iota((rows, slots), 1) == slot_col, 1.0, 0.0).astype(bf16)
    return dot(onehot, table_ref[...])


def route_block(low, embed, router_ref, picks, experts):
    width = low.shape[1]
    logits = dot(low, router_ref[:width, :]) + dot(embed, router_ref[width:, :])
    lanes = iota(logits.shape, 1)
    inside = lanes < experts
    logits = jnp.where(inside, logits, masked_score)
    raised = jnp.where(inside, jnp.exp(logits - jnp.max(logits, axis=1, keepdims=True)), 0.0)
    probs = raised / jnp.sum(raised, axis=1, keepdims=True)
    gate = jnp.sum(jnp.where(lanes == picks, probs, 0.0), axis=1, keepdims=True)
    return probs, gate


BLOCK = 256


def front_kernel(
    experts, hidden_ref, embed_ref, gain_ref, router_ref, cols_ref, slot_row_ref, *refs,
):
    out_refs, (probs_ref, gate_ref, low_ref) = refs[:PARTS], refs[PARTS:]
    length = hidden_ref.shape[0]

    def step(index):
        at = rows_at(index, BLOCK)
        standard, unused = normalize(hidden_ref[at, :].astype(f32))
        low = (standard * gain_ref[0:1, :]).astype(bf16)
        low_ref[at, :] = low
        probs, gate = route_block(low, embed_ref[at, :], router_ref, cols_ref[at, 2:3], experts)
        probs_ref[at, :] = probs
        gate_ref[at, :] = gate

    loop(length // BLOCK, step)
    dispatch(low_ref, slot_row_ref[0:1, :], out_refs)


def expert_forward_kernel(count, in_ref, out_ref, *refs):
    for x_ref, y_ref in zip(refs[:count], refs[count:]):
        inner = dot(x_ref[...], in_ref[...])
        hidden = (inner * sigmoid(inner)).astype(bf16)
        y_ref[...] = dot(hidden, out_ref[...]).astype(bf16)


def expert_forward(received, weight_in, weight_out):
    block, width = received[0].shape
    count = len(received)
    return run(
        functools.partial(expert_forward_kernel, count),
        (weight_in, weight_out) + tuple(received),
        [VMEM] * (2 + count),
        [shape_of((block, width), bf16)] * count,
        flops=4 * count * block * width * weight_in.shape[1],
        name="experts",
        limit=32,
    )


def forward_in_turn(received, pair):
    near, far = lax.optimization_barrier((expert_forward(received[:2], *pair), received[2:]))
    return near + expert_forward(far[:1], *pair) + expert_forward(far[1:], *pair)


def expert_backward_kernel(count, in_ref, out_ref, *refs):
    x_refs, dy_refs, refs = refs[:count], refs[count : 2 * count], refs[2 * count :]
    extra, refs = refs[: len(refs) - 3 * count], refs[len(refs) - 3 * count :]
    if extra:
        normed_ref, mixed_ref, table_ref, sinus_ref, grad_ref = extra
        width = normed_ref.shape[1]
        for part in range(3):
            lanes = slice(part * width, (part + 1) * width)
            grad_ref[:, lanes] = t_dot(normed_ref[...], mixed_ref[:, lanes]).astype(bf16)
        grad_ref[:, 3 * width :] = jnp.transpose(dot(table_ref[...], sinus_ref[...])).astype(bf16)
    dx_refs, hidden_refs, dinner_refs = refs[:count], refs[count : 2 * count], refs[2 * count :]
    for x_ref, dy_ref, dx_ref, hidden_ref, dinner_ref in zip(
        x_refs, dy_refs, dx_refs, hidden_refs, dinner_refs
    ):
        inner = dot(x_ref[...], in_ref[...])
        gates = sigmoid(inner)
        hidden = inner * gates
        hidden_ref[...] = hidden.astype(bf16)
        d_hidden = dot_t(dy_ref[...], out_ref[...])
        d_inner = (d_hidden * (gates + hidden * (1.0 - gates))).astype(bf16)
        dinner_ref[...] = d_inner
        dx_ref[...] = dot_t(d_inner, in_ref[...]).astype(bf16)


def expert_backward(received, d_result, weight_in, weight_out, extra=()):
    block, width = received[0].shape
    inner = weight_in.shape[1]
    count = len(received)
    more = [shape_of((width, 4 * width), bf16)] if extra else []
    outs = run(
        functools.partial(expert_backward_kernel, count),
        (weight_in, weight_out) + tuple(received) + tuple(d_result) + tuple(extra),
        [VMEM] * (2 + 2 * count + len(extra)),
        more + [shape_of((block, width), bf16)] * count + [shape_of((block, inner), bf16)] * (2 * count),
        flops=6 * count * block * width * inner,
        name="experts_back",
        limit=48 if extra else 40,
    )
    more, outs = outs[: len(more)], outs[len(more) :]
    return more, outs[:count], outs[count : 2 * count], outs[2 * count :]


def backward_in_turn(received, d_result, pair, extra=()):
    near, far = lax.optimization_barrier(
        (expert_backward(received[:2], d_result[:2], *pair, extra), d_result[2:])
    )
    parts = [
        near,
        expert_backward(received[2:3], far[:1], *pair),
        expert_backward(received[3:], far[1:], *pair),
    ]
    return [sum((list(part[k]) for part in parts), []) for k in range(4)]


def tile_window(starts_ref, first, length):
    count = starts_ref.shape[1]
    low = jnp.int32(0)
    high = jnp.int32(length)
    for k in range(1, count):
        low = jnp.where(starts_ref[0, k] <= first, starts_ref[0, k], low)
    for k in range(count - 1, 0, -1):
        high = jnp.where(starts_ref[0, k] > first + (TILE - 1), starts_ref[0, k], high)
    low = low // TILE
    steps = ((high + (TILE - 1)) // TILE - low + 1) // 2
    return jnp.minimum(low, length // TILE - 2 * steps), steps


def numbers_at(starts_ref, positions):
    total = jnp.zeros(positions.shape, jnp.int32)
    for k in range(1, starts_ref.shape[1]):
        total = total + jnp.where(positions >= starts_ref[0, k], 1, 0)
    return total


def same_tile(starts_ref, first_query, first_key):
    rows = numbers_at(starts_ref, iota((TILE, TILE), 0) + first_query)
    cols = numbers_at(starts_ref, iota((TILE, TILE), 1) + first_key)
    return rows == cols


PAD = 2


def chunk_rows(query_tile, key_tile, length, count, mirrored=False):
    tiles = length // TILE
    index = tiles - 1 - query_tile + key_tile - (tiles // 2 - PAD)
    if mirrored:
        index = tiles + 2 * PAD - count - index
    index = jnp.clip(index, 0, tiles + 2 * PAD - count)
    return pl.ds(pl.multiple_of(index * TILE, TILE), count * TILE)


def halves(values):
    left = iota(values.shape, 1) < TILE // 2
    zero = jnp.zeros_like(values)
    return jnp.concatenate(
        [jnp.where(left, values, zero), jnp.where(left, zero, values)], axis=0
    )


def turned_halves(values):
    turned = jnp.transpose(values)
    top = iota(turned.shape, 0) < TILE // 2
    zero = jnp.zeros_like(turned)
    return jnp.concatenate([jnp.where(top, turned, zero), jnp.where(top, zero, turned)], axis=1)


def skew(values):
    return jnp.concatenate(
        [
            pltpu.roll(values[:TILE], 1, 1, stride=1, stride_axis=0),
            pltpu.roll(values[TILE:], 1, 1, stride=1, stride_axis=0),
        ],
        axis=0,
    )


def mirror(values):
    row, col = iota((2 * TILE, 2 * TILE), 0), iota((2 * TILE, 2 * TILE), 1)
    flip = (row % TILE + col % TILE == TILE - 1) & (row // TILE == col // TILE)
    return dot(values, jnp.where(flip, 1.0, 0.0).astype(bf16))


def twice(values):
    return jnp.concatenate([values, values], axis=0)


PAIRS = H // 2


def attend_forward(
    starts_ref, qu_ref, qv_ref, k_ref, v_ref, t_ref, context_ref, logs_ref,
    qum, qvm, scores, rolled, peaks, sums, mixed,
):
    length = qu_ref.shape[0]
    tiles = length // TILE

    def query_step(tile):
        first = tile * TILE
        at = rows_at(tile, TILE)
        low, steps = tile_window(starts_ref, first, length)
        chunk = chunk_rows(tile, low, length, 1)
        for p in range(PAIRS):
            lanes = slice(p * TILE, (p + 1) * TILE)
            qum[p] = halves(qu_ref[at, lanes])
            qvm[p] = halves(qv_ref[at, lanes])
            rolled[p] = skew(dot_t(qvm[p], t_ref[chunk, lanes]))
            peaks[p] = jnp.full((2 * TILE, TILE), masked_score, f32)
            sums[p] = jnp.zeros((2 * TILE, TILE), f32)
            mixed[p] = jnp.zeros((2 * TILE, TILE), f32)
        lower = twice(iota((TILE, TILE), 1) <= iota((TILE, TILE), 0))

        def score_step(step, carry):
            key = low + 2 * step
            keys = pl.ds(pl.multiple_of(key * TILE, TILE), 2 * TILE)
            same_one = twice(same_tile(starts_ref, first, key * TILE))
            same_two = twice(same_tile(starts_ref, first, key * TILE + TILE))
            chunks = chunk_rows(tile, key + 1, length, 2)
            for p in range(PAIRS):
                lanes = slice(p * TILE, (p + 1) * TILE)
                content = dot_t(qum[p], k_ref[keys, lanes])
                fresh = dot_t(qvm[p], t_ref[chunks, lanes])
                one, two = skew(fresh[:, :TILE]), skew(fresh[:, TILE:])
                value_one = content[:, :TILE] + jnp.where(lower, rolled[p], one)
                value_two = content[:, TILE:] + jnp.where(lower, one, two)
                value_one = jnp.where(same_one, value_one, masked_score)
                value_two = jnp.where(same_two, value_two, masked_score)
                rolled[p] = two
                scores[2 * step, p] = value_one
                scores[2 * step + 1, p] = value_two
                peaks[p] = jnp.maximum(peaks[p], jnp.maximum(value_one, value_two))
            return carry

        lax.fori_loop(0, steps, score_step, 0)
        for p in range(PAIRS):
            peaks[p] = jnp.broadcast_to(
                jnp.max(peaks[p], axis=1, keepdims=True), (2 * TILE, TILE)
            )

        def value_step(step, carry):
            keys = pl.ds(pl.multiple_of((low + 2 * step) * TILE, TILE), 2 * TILE)
            for p in range(PAIRS):
                lanes = slice(p * TILE, (p + 1) * TILE)
                one = jnp.exp(scores[2 * step, p] - peaks[p])
                two = jnp.exp(scores[2 * step + 1, p] - peaks[p])
                sums[p] += one + two
                raised = jnp.concatenate([one.astype(bf16), two.astype(bf16)], axis=1)
                mixed[p] += dot(raised, v_ref[keys, lanes])
            return carry

        lax.fori_loop(0, steps, value_step, 0)
        left = iota((TILE, TILE), 1) < TILE // 2
        logs = jnp.zeros((TILE, TILE), f32)
        lane = iota((TILE, TILE), 1)
        for p in range(PAIRS):
            lanes = slice(p * TILE, (p + 1) * TILE)
            total = jnp.sum(sums[p], axis=1, keepdims=True)
            result = mixed[p] * (1.0 / total)
            context_ref[at, lanes] = jnp.where(left, result[:TILE], result[TILE:]).astype(bf16)
            logsum = peaks[p] + jnp.log(total)
            logs = jnp.where(lane == 2 * p, logsum[:TILE], logs)
            logs = jnp.where(lane == 2 * p + 1, logsum[TILE:], logs)
        logs_ref[at, :] = logs

    loop(tiles, query_step)


def attend_scratch(length):
    pair = (PAIRS, 2 * TILE, TILE)
    return [
        pltpu.VMEM(pair, bf16),
        pltpu.VMEM(pair, bf16),
        pltpu.VMEM((length // TILE,) + pair, f32),
        pltpu.VMEM(pair, f32),
        pltpu.VMEM(pair, f32),
        pltpu.VMEM(pair, f32),
        pltpu.VMEM(pair, f32),
    ]


STRIP = 32


def strips():
    return [
        (slice(head * TILE + row, head * TILE + row + STRIP), row)
        for head in range(2)
        for row in range(0, TILE, STRIP)
    ]


def skew_strip(values, row):
    return pltpu.roll(values, 1 + row, 1, stride=1, stride_axis=0)


def attend_backward(
    starts_ref, qu_ref, qv_ref, k_ref, v_ref, t_ref, mirrored_ref, context_ref, logs_ref, dcontext_ref,
    dm_ref, dk_ref, dv_ref, dt_ref, dbias_ref,
    qum, qvm, dcm, qut, qvt, dct, logs, deltas, rolled, unrolled, dqu, dqv, first_s, second_s, third_s,
    probs_s, dlow_s, moved_s,
):
    length, width = qu_ref.shape
    tiles = length // TILE
    scale = 1.0 / math.sqrt(width // H)
    dk_ref[...] = jnp.zeros_like(dk_ref)
    dv_ref[...] = jnp.zeros_like(dv_ref)
    dt_ref[...] = jnp.zeros_like(dt_ref)
    dbias_ref[...] = jnp.zeros_like(dbias_ref)

    def query_step(tile):
        first = tile * TILE
        at = rows_at(tile, TILE)
        low, steps = tile_window(starts_ref, first, length)
        chunk = chunk_rows(tile, low, length, 1)
        logs_tile = logs_ref[at, :]
        for p in range(PAIRS):
            lanes = slice(p * TILE, (p + 1) * TILE)
            query_u = halves(qu_ref[at, lanes])
            query_v = halves(qv_ref[at, lanes])
            upstream = halves(dcontext_ref[at, lanes])
            qum[p] = query_u
            qvm[p] = query_v
            dcm[p] = upstream
            qut[p] = turned_halves(qu_ref[at, lanes])
            qvt[p] = turned_halves(qv_ref[at, lanes])
            dct[p] = turned_halves(dcontext_ref[at, lanes])
            delta = jnp.sum(
                upstream.astype(f32) * twice(context_ref[at, lanes].astype(f32)),
                axis=1,
                keepdims=True,
            )
            deltas[p] = jnp.broadcast_to(delta, (2 * TILE, TILE))
            logs[p, :TILE] = jnp.broadcast_to(logs_tile[:, 2 * p : 2 * p + 1], (TILE, TILE))
            logs[p, TILE:] = jnp.broadcast_to(logs_tile[:, 2 * p + 1 : 2 * p + 2], (TILE, TILE))
            rolled[p] = skew(dot_t(query_v, t_ref[chunk, lanes]))
            unrolled[p] = jnp.zeros((2 * TILE, TILE), f32)
            dqu[p] = jnp.zeros((2 * TILE, TILE), f32)
            dqv[p] = jnp.zeros((2 * TILE, TILE), f32)
        lower = twice(iota((TILE, TILE), 1) <= iota((TILE, TILE), 0))

        def step_body(step, carry):
            key = low + 2 * step
            keys = pl.ds(pl.multiple_of(key * TILE, TILE), 2 * TILE)
            same_one = same_tile(starts_ref, first, key * TILE)
            same_two = same_tile(starts_ref, first, key * TILE + TILE)
            before = chunk_rows(tile, key, length, 2, True)
            after = chunk_rows(tile, key + 1, length, 2)
            for p in range(PAIRS):
                lanes = slice(p * TILE, (p + 1) * TILE)
                first_s[p] = dot_t(qum[p], k_ref[keys, lanes])
                second_s[p] = dot_t(qvm[p], t_ref[after, lanes])
                third_s[p] = dot_t(dcm[p], v_ref[keys, lanes])
            for p in range(PAIRS):
                for rows, row in strips():
                    near = iota((STRIP, TILE), 1) <= iota((STRIP, TILE), 0) + row
                    span = slice(row, row + STRIP)
                    one = skew_strip(second_s[p, rows, :TILE], row)
                    two = skew_strip(second_s[p, rows, TILE:], row)
                    value_one = first_s[p, rows, :TILE] + jnp.where(near, rolled[p, rows], one)
                    value_two = first_s[p, rows, TILE:] + jnp.where(near, one, two)
                    rolled[p, rows] = two
                    log, delta = logs[p, rows], deltas[p, rows]
                    probs_one = jnp.where(same_one[span], jnp.exp(value_one - log), 0.0)
                    probs_two = jnp.where(same_two[span], jnp.exp(value_two - log), 0.0)
                    probs_s[p, rows, :TILE] = probs_one.astype(bf16)
                    probs_s[p, rows, TILE:] = probs_two.astype(bf16)
                    dlow_s[p, rows, :TILE] = (probs_one * (third_s[p, rows, :TILE] - delta)).astype(bf16)
                    dlow_s[p, rows, TILE:] = (probs_two * (third_s[p, rows, TILE:] - delta)).astype(bf16)
            for p in range(PAIRS):
                lanes = slice(p * TILE, (p + 1) * TILE)
                second_s[p] = mirror(dlow_s[p])
                dv_ref[lanes, keys] += dot(dct[p], probs_s[p])
                dk_ref[lanes, keys] += dot(qut[p], dlow_s[p])
                dqu[p] += dot(dlow_s[p], k_ref[keys, lanes])
            for p in range(PAIRS):
                for rows, row in strips():
                    near = iota((STRIP, TILE), 1) <= iota((STRIP, TILE), 0) + row
                    one = skew_strip(second_s[p, rows, :TILE], row)
                    two = skew_strip(second_s[p, rows, TILE:], row)
                    moved_s[p, rows, :TILE] = jnp.where(near, two, one).astype(bf16)
                    moved_s[p, rows, TILE:] = jnp.where(near, one, unrolled[p, rows]).astype(bf16)
                    unrolled[p, rows] = two
            for p in range(PAIRS):
                lanes = slice(p * TILE, (p + 1) * TILE)
                dt_ref[lanes, before] += dot(qvt[p], moved_s[p])
                dqv[p] += dot(moved_s[p], mirrored_ref[before, lanes])
            return carry

        lax.fori_loop(0, steps, step_body, 0)
        last = chunk_rows(tile, low + 2 * steps, length, 1, True)
        left = iota((TILE, TILE), 1) < TILE // 2
        for p in range(PAIRS):
            lanes = slice(p * TILE, (p + 1) * TILE)
            moved = jnp.where(lower, 0.0, unrolled[p]).astype(bf16)
            dt_ref[lanes, last] += dot(qvt[p], moved)
            full_u = dqu[p]
            full_v = dqv[p] + dot(moved, mirrored_ref[last, lanes])
            part_u = jnp.where(left, full_u[:TILE], full_u[TILE:]) * scale
            part_v = jnp.where(left, full_v[:TILE], full_v[TILE:]) * scale
            dbias_ref[0:1, lanes] += column_sum(part_u)
            dbias_ref[1:2, lanes] += column_sum(part_v)
            dm_ref[at, lanes] = (part_u + part_v).astype(bf16)

    loop(tiles, query_step)

    def finish(index):
        at = rows_at(index, TILE)
        for p in range(PAIRS):
            lanes = slice(p * TILE, (p + 1) * TILE)
            key_lanes = slice(width + p * TILE, width + (p + 1) * TILE)
            value_lanes = slice(2 * width + p * TILE, 2 * width + (p + 1) * TILE)
            dm_ref[at, key_lanes] = jnp.transpose(dk_ref[lanes, at].astype(bf16))
            dm_ref[at, value_lanes] = jnp.transpose(dv_ref[lanes, at].astype(bf16))

    loop(tiles, finish)


def attend_back_scratch():
    pair = (PAIRS, 2 * TILE, TILE)
    turned = (PAIRS, TILE, 2 * TILE)
    square = (PAIRS, 2 * TILE, 2 * TILE)
    return (
        [pltpu.VMEM(dims, bf16) for dims in (pair,) * 3 + (turned,) * 3]
        + [pltpu.VMEM(dims, f32) for dims in (pair,) * 6 + (square,) * 3]
        + [pltpu.VMEM(square, bf16) for unused in range(3)]
    )


def dense_parts(dense_ref):
    width = dense_ref.shape[0]
    cuts = (0, 3, 4, 5, 6, 8)
    return [
        dense_ref.at[:, pl.ds(start * width, (stop - start) * width)]
        for start, stop in zip(cuts[:-1], cuts[1:])
    ]


def shifted(values, reach, taps):
    rows = values.shape[0]
    found = {}
    for rest in range(8):
        starts = [EDGE - reach + k for k in range(taps) if (EDGE - reach + k) % 8 == rest]
        turned = pltpu.roll(values, (rows - rest) % rows, 0) if rest else values
        for start in starts:
            found[start - EDGE + reach] = turned[start - rest : start - rest + rows - 2 * EDGE]
    return [found[k] for k in range(taps)]


def at_edges(starts_ref, length, step):
    for k in range(1, starts_ref.shape[1]):
        edge = starts_ref[0, k]

        @pl.when(edge < length)
        def unused():
            start = jnp.minimum((edge - 8) // 8 * 8, length - 2 * EDGE)
            start = pl.multiple_of(start, 8)
            step(start, iota((2 * EDGE, TILE), 0) + start)


def spread_rows(rows_ref, out_ref):
    width = rows_ref.shape[1]
    for row in range(out_ref.shape[2] // width):
        lanes = slice(row * width, (row + 1) * width)
        out_ref[:, :, lanes] = jnp.broadcast_to(
            rows_ref[row : row + 1, :][None], (out_ref.shape[0], 1, width)
        )


EDGE = 16


def middle_kernel(
    starts_ref, hidden_ref, cols_ref, gate_ref, gains_ref, dense_ref, bias_ref, taps_ref, sinus_ref,
    *refs,
):
    returned_refs, refs = refs[:PARTS], refs[PARTS:]
    h1_ref, h2_ref, qu_ref, qv_ref, k_ref, v_ref, t_ref, context_ref, logs_ref = refs[:9]
    conv_ref, sums_ref, padded, sums, returned_ref = refs[9:14]
    attend = refs[14:]
    join_blocks(returned_refs, returned_ref)
    length, width = h1_ref.shape
    scale = 1.0 / math.sqrt(width // H)
    in_ref, place_ref, mix_ref, unused, point_ref = dense_parts(dense_ref)

    def queries_step(index):
        at = rows_at(index, BLOCK)
        picked = collect(cols_ref[at, 0:1], returned_ref)
        h1 = hidden_ref[at, :].astype(f32) + 0.5 * gate_ref[at, :] * picked
        h1_ref[at, :] = h1
        standard, unused = normalize(h1)
        low = (standard * gains_ref[1:2, :]).astype(bf16)
        queries = dot(low, in_ref[:, :width])
        qu_ref[at, :] = ((queries + bias_ref[0:1, :]).astype(bf16).astype(f32) * scale).astype(bf16)
        qv_ref[at, :] = ((queries + bias_ref[1:2, :]).astype(bf16).astype(f32) * scale).astype(bf16)
        k_ref[at, :] = dot(low, in_ref[:, width : 2 * width]).astype(bf16)
        v_ref[at, :] = dot(low, in_ref[:, 2 * width :]).astype(bf16)
        table_at = span_at(index * BLOCK + edge, BLOCK, TILE)
        t_ref[table_at, :] = dot(sinus_ref[at, :], place_ref[...]).astype(bf16)

    edge = PAD * TILE
    t_ref[:edge, :] = jnp.zeros((edge, width), bf16)
    t_ref[edge + length :, :] = jnp.zeros((edge, width), bf16)
    loop(length // BLOCK, queries_step)
    attend_forward(
        starts_ref, qu_ref, qv_ref, k_ref, v_ref, t_ref, context_ref, logs_ref, *attend
    )
    padded[:EDGE, :] = jnp.zeros((EDGE, width), f32)
    padded[EDGE + length :, :] = jnp.zeros((EDGE, width), f32)

    def gates_step(index):
        at = rows_at(index, BLOCK)
        h2 = h1_ref[at, :] + dot(context_ref[at, :], mix_ref[...])
        h2_ref[at, :] = h2
        standard, unused = normalize(h2)
        low = (standard * gains_ref[2:3, :]).astype(bf16)
        value = dot(low, point_ref[:, :width])
        gates = dot(low, point_ref[:, width:])
        padded[span_at(index * BLOCK + EDGE, BLOCK, EDGE), :] = value * sigmoid(gates)

    loop(length // BLOCK, gates_step)
    sums[...] = jnp.zeros_like(sums)
    taps = taps_ref.shape[0] - 1
    reach = taps // 2
    frames = starts_ref[0, starts_ref.shape[1] - 1]

    def conv_step(index):
        first = index * TILE
        around = pl.ds(pl.multiple_of(first, TILE), TILE + 2 * EDGE)
        for part in range(width // TILE):
            lanes = slice(part * TILE, (part + 1) * TILE)
            total = jnp.zeros((TILE, TILE), f32)
            for tap, near in enumerate(shifted(padded[around, lanes], reach, taps)):
                total = total + near * taps_ref[tap : tap + 1, lanes]
            conv_ref[rows_at(index, TILE), lanes] = total

    loop(length // TILE, conv_step)

    def edge_step(start, place):
        here = numbers_at(starts_ref, place)
        masks = [numbers_at(starts_ref, place + (tap - reach)) == here for tap in range(taps)]
        around = pl.ds(start, 2 * EDGE + 2 * EDGE)
        for part in range(width // TILE):
            lanes = slice(part * TILE, (part + 1) * TILE)
            total = jnp.zeros(place.shape, f32)
            for tap, near in enumerate(shifted(padded[around, lanes], reach, taps)):
                total = total + jnp.where(masks[tap], near, 0.0) * taps_ref[tap : tap + 1, lanes]
            conv_ref[pl.ds(start, 2 * EDGE), lanes] = total

    at_edges(starts_ref, length, edge_step)

    def sums_step(index):
        at = rows_at(index, BLOCK)
        inside = (iota((BLOCK, 1), 0) + index * BLOCK) < frames
        kept = jnp.where(inside, conv_ref[at, :], 0.0)
        sums[0:1, :] += column_sum(kept)
        sums[1:2, :] += column_sum(kept * kept)

    loop(length // BLOCK, sums_step)
    sums[2:3, :] = jnp.zeros((1, width), f32) + frames.astype(f32)
    spread_rows(sums, sums_ref)


def batch_totals(totals_ref, width):
    totals = jnp.sum(totals_ref[...], axis=0)
    count = totals[:, 2 * width :]
    mean = totals[:, :width] / count
    variance = totals[:, width : 2 * width] / count - mean * mean
    return mean, lax.rsqrt(variance + epsilon), count


def batch_block(conv, mean, inverse, batch_ref):
    centred = conv - mean
    standard = centred * inverse
    batched = standard * batch_ref[0:1, :] + batch_ref[1:2, :]
    return centred, standard, batched


def second_kernel(
    experts, h2_ref, conv_ref, totals_ref, batch_ref, point_ref, embed_ref, gains_ref, router_ref,
    cols_ref, slot_row_ref, *refs,
):
    out_refs, refs = refs[:PARTS], refs[PARTS:]
    h3_ref, active_ref, probs_ref, gate_ref, stats_ref, low_ref = refs
    length, width = h2_ref.shape
    mean, inverse, count = batch_totals(totals_ref, width)
    stats_ref[0:1, :] = mean
    stats_ref[1:2, :] = inverse
    stats_ref[2:3, :] = count

    def step(index):
        at = rows_at(index, BLOCK)
        unused, unused, batched = batch_block(conv_ref[at, :], mean, inverse, batch_ref)
        active = (batched * sigmoid(batched)).astype(bf16)
        active_ref[at, :] = active
        h3 = h2_ref[at, :] + dot(active, point_ref[...])
        h3_ref[at, :] = h3
        standard, unused = normalize(h3)
        low = (standard * gains_ref[3:4, :]).astype(bf16)
        low_ref[at, :] = low
        probs, gate = route_block(low, embed_ref[at, :], router_ref, cols_ref[at, 3:4], experts)
        probs_ref[at, :] = probs
        gate_ref[at, :] = gate

    loop(length // BLOCK, step)
    dispatch(low_ref, slot_row_ref[1:2, :], out_refs)


def gate_back(upstream, picked, gate, probs, picks):
    d_gate = 0.5 * jnp.sum(upstream * picked, axis=1, keepdims=True)
    onehot = jnp.where(iota(probs.shape, 1) == picks, 1.0, 0.0)
    return (d_gate * gate) * (onehot - probs)


def turn_kernel(
    h3_ref, cols_ref, gate_ref, probs_ref, slot_row_ref, gains_ref, cotangent_ref, *refs,
):
    returned_refs, out_refs, refs = refs[:PARTS], refs[PARTS : 2 * PARTS], refs[2 * PARTS :]
    output_ref, d4_ref, dlogits_ref, dgain_ref, low_ref, returned_ref = refs
    length = h3_ref.shape[0]
    join_blocks(returned_refs, returned_ref)
    dgain_ref[...] = jnp.zeros_like(dgain_ref)

    def step(index):
        at = rows_at(index, BLOCK)
        picked = collect(cols_ref[at, 1:2], returned_ref)
        gate = gate_ref[at, :]
        h4 = h3_ref[at, :] + 0.5 * gate * picked
        standard, inverse = normalize(h4)
        gain = gains_ref[4:5, :]
        output_ref[at, :] = (standard * gain).astype(bf16)
        upstream = cotangent_ref[at, :].astype(f32)
        dgain_ref[0:1, :] += column_sum(upstream * standard)
        d4 = normalize_back(standard, inverse, gain, upstream)
        d4_ref[at, :] = d4
        dlogits_ref[at, :] = gate_back(d4, picked, gate, probs_ref[at, :], cols_ref[at, 3:4])
        low_ref[at, :] = (0.5 * gate * d4).astype(bf16)

    loop(length // BLOCK, step)
    dispatch(low_ref, slot_row_ref[1:2, :], out_refs)


def router_back(dlogits, low, embed, router_ref, drouter_ref):
    width = low.shape[1]
    high = dlogits.astype(bf16)
    rest = (dlogits - high.astype(f32)).astype(bf16)
    d_low = dot_t(high, router_ref[:width, :]) + dot_t(rest, router_ref[:width, :])
    d_embed = dot_t(high, router_ref[width:, :]) + dot_t(rest, router_ref[width:, :])
    turned = jnp.transpose(dlogits)[:8, :]
    turned_high = turned.astype(bf16)
    turned_rest = (turned - turned_high.astype(f32)).astype(bf16)
    drouter_ref[:, :width] += dot(turned_high, low) + dot(turned_rest, low)
    drouter_ref[:, width:] += dot(turned_high, embed) + dot(turned_rest, embed)
    return d_low, d_embed


def second_back_kernel(
    cols_ref, dlogits_ref, h3_ref, d4_ref, embed_ref, router_ref, gains_ref, conv_ref, stats_ref,
    batch_ref, point_ref, *refs,
):
    dsent_refs, refs = refs[:PARTS], refs[PARTS:]
    d3_ref, dlow_ref, dz_ref, dembed_ref, drouter_ref, small_ref, sums_ref, sums, dsent_ref = refs
    length, width = h3_ref.shape
    drouter_ref[...] = jnp.zeros_like(drouter_ref)
    small_ref[...] = jnp.zeros_like(small_ref)
    sums[...] = jnp.zeros_like(sums)
    join_blocks(dsent_refs, dsent_ref)
    mean, batch_inverse = stats_ref[0:1, :], stats_ref[1:2, :]

    def step(index):
        at = rows_at(index, BLOCK)
        standard, inverse = normalize(h3_ref[at, :])
        gain = gains_ref[3:4, :]
        low = (standard * gain).astype(bf16)
        d_low, d_embed = router_back(
            dlogits_ref[at, :], low, embed_ref[at, :], router_ref, drouter_ref
        )
        dembed_ref[at, :] = d_embed
        d_norm = collect(cols_ref[at, 1:2], dsent_ref) + d_low
        small_ref[0:1, :] += column_sum(d_norm * standard)
        d3 = d4_ref[at, :] + normalize_back(standard, inverse, gain, d_norm)
        d3_ref[at, :] = d3
        d3_low = d3.astype(bf16)
        dlow_ref[at, :] = d3_low
        centred, normed, batched = batch_block(conv_ref[at, :], mean, batch_inverse, batch_ref)
        gates = sigmoid(batched)
        d_batched = dot_t(d3_low, point_ref[...]) * (gates + batched * gates * (1.0 - gates))
        small_ref[1:2, :] += column_sum(d_batched * normed)
        small_ref[2:3, :] += column_sum(d_batched)
        d_z = d_batched * batch_ref[0:1, :]
        dz_ref[at, :] = d_z
        sums[0:1, :] += column_sum(d_z)
        sums[1:2, :] += column_sum(d_z * centred)

    loop(length // BLOCK, step)
    spread_rows(sums, sums_ref)


def conv_back_kernel(
    starts_ref, conv_ref, dz_ref, stats_ref, dsums_ref, d3_ref, h2_ref, gains_ref, dense_ref, taps_ref,
    d2_ref, d2low_ref, dcontext_ref, n3_ref, dg_ref, small_ref, dtaps_ref, padded, linear, dtaps, edge_grad,
):
    length, width = h2_ref.shape
    unused, unused, mix_ref, unused, point_ref = dense_parts(dense_ref)
    taps = taps_ref.shape[0] - 1
    reach = taps // 2
    frames = starts_ref[0, starts_ref.shape[1] - 1]
    small_ref[...] = jnp.zeros_like(small_ref)
    dtaps[...] = jnp.zeros_like(dtaps)
    mean, batch_inverse, count = stats_ref[0:1, :], stats_ref[1:2, :], stats_ref[2:3, :]
    dsums = jnp.sum(dsums_ref[...], axis=0)
    d_variance = -0.5 * batch_inverse * batch_inverse * batch_inverse * dsums[:, width:]
    padded[:EDGE, :] = jnp.zeros((EDGE, width), f32)
    padded[EDGE + length :, :] = jnp.zeros((EDGE, width), f32)

    def conv_step(index):
        at = rows_at(index, BLOCK)
        centred = conv_ref[at, :] - mean
        inside = (iota((BLOCK, 1), 0) + index * BLOCK) < frames
        shared = (2.0 * d_variance * centred - batch_inverse * dsums[:, :width]) / count
        d_conv = batch_inverse * dz_ref[at, :] + jnp.where(inside, shared, 0.0)
        padded[span_at(index * BLOCK + EDGE, BLOCK, EDGE), :] = d_conv
        standard, unused = normalize(h2_ref[at, :])
        low = (standard * gains_ref[2:3, :]).astype(bf16)
        n3_ref[at, :] = low
        value = dot(low, point_ref[:, :width])
        linear[at, :width] = value
        linear[at, width:] = sigmoid(dot(low, point_ref[:, width:]))

    loop(length // BLOCK, conv_step)

    def turn_step(index):
        at = rows_at(index, TILE)
        around = pl.ds(pl.multiple_of(index * TILE, TILE), TILE + 2 * EDGE)
        for part in range(width // TILE):
            lanes = slice(part * TILE, (part + 1) * TILE)
            other = slice(width + part * TILE, width + (part + 1) * TILE)
            value, gate = linear[at, lanes], linear[at, other]
            passed = value * gate
            total = jnp.zeros((TILE, TILE), f32)
            for step, near in enumerate(shifted(padded[around, lanes], reach, taps)):
                tap = taps - 1 - step
                total = total + near * taps_ref[tap : tap + 1, lanes]
                dtaps[tap, :, lanes] += jnp.sum((near * passed).reshape(TILE // 8, 8, TILE), axis=0)
            dg_ref[at, lanes] = (total * gate).astype(bf16)
            dg_ref[at, other] = (total * passed * (1.0 - gate)).astype(bf16)

    def edge_step(start, place):
        rows = 2 * EDGE
        at = pl.ds(start, rows)
        here = numbers_at(starts_ref, place)
        masks = [numbers_at(starts_ref, place - (reach - tap)) == here for tap in range(taps)]
        around = pl.ds(start, rows + 2 * EDGE)
        for part in range(width // TILE):
            lanes = slice(part * TILE, (part + 1) * TILE)
            other = slice(width + part * TILE, width + (part + 1) * TILE)
            value, gate = linear[at, lanes], linear[at, other]
            passed = value * gate
            total = jnp.zeros((rows, TILE), f32)
            for step, near in enumerate(shifted(padded[around, lanes], reach, taps)):
                tap = taps - 1 - step
                total = total + jnp.where(masks[step], near, 0.0) * taps_ref[tap : tap + 1, lanes]
                extra = jnp.where(masks[step], 0.0, near) * passed
                dtaps[tap, :, lanes] -= jnp.sum(extra.reshape(rows // 8, 8, TILE), axis=0)
            edge_grad[:, lanes] = total * gate
            edge_grad[:, other] = total * passed * (1.0 - gate)
        low = pl.multiple_of(jnp.minimum(start // 16 * 16, length - rows - 16), 16)
        wide = pl.ds(low, rows + 16)
        shift = start - low
        whole = dg_ref[wide, :].astype(f32)
        grad = edge_grad[...]
        zero = jnp.zeros((16, 2 * width), f32)
        head = jnp.concatenate([grad, zero], axis=0)
        middle = jnp.concatenate([zero[:8], grad, zero[:8]], axis=0)
        tail = jnp.concatenate([zero, grad], axis=0)
        place = iota((rows + 16, 1), 0) - shift
        moved = jnp.where(shift == 0, head, jnp.where(shift == 8, middle, tail))
        inside = (place >= 0) & (place < rows)
        dg_ref[wide, :] = jnp.where(inside, moved, whole).astype(bf16)

    loop(length // TILE, turn_step)
    at_edges(starts_ref, length, edge_step)
    dtaps_ref[...] = jnp.sum(dtaps[...], axis=1)

    def gates_step(index):
        at = rows_at(index, BLOCK)
        d_norm = dot_t(dg_ref[at, :], point_ref[...])
        standard, inverse = normalize(h2_ref[at, :])
        small_ref[0:1, :] += column_sum(d_norm * standard)
        d2 = d3_ref[at, :] + normalize_back(standard, inverse, gains_ref[2:3, :], d_norm)
        d2_ref[at, :] = d2
        low = d2.astype(bf16)
        d2low_ref[at, :] = low
        dcontext_ref[at, :] = dot_t(low, mix_ref[...]).astype(bf16)

    loop(length // BLOCK, gates_step)


def attend_back_kernel(
    starts_ref, d2_ref, dcontext_ref, h1_ref, gains_ref, dense_ref, sinus_ref, qu_ref, qv_ref, k_ref, v_ref,
    t_ref, context_ref, logs_ref, cols_ref, gate_ref, probs_ref, slot_row_ref, *refs,
):
    returned_refs, out_refs, refs = refs[:PARTS], refs[PARTS : 2 * PARTS], refs[2 * PARTS :]
    d1_ref, dlogits_ref, n2_ref, dm_ref, dtable_ref, small_ref = refs[:6]
    low_ref, mirrored_ref, returned_ref, dk_ref, dv_ref, dt_ref = refs[6:12]
    attend = refs[12:]
    length, width = h1_ref.shape
    in_ref, place_ref, unused, unused, unused = dense_parts(dense_ref)
    small_ref[...] = jnp.zeros_like(small_ref)
    join_blocks(returned_refs, returned_ref)

    def table_step(index):
        at = rows_at(index, BLOCK)
        table_at = span_at(index * BLOCK + edge, BLOCK, TILE)
        mirrored_ref[table_at, :] = dot(sinus_ref[at, :], place_ref[...]).astype(bf16)

    edge = PAD * TILE
    mirrored_ref[:edge, :] = jnp.zeros((edge, width), bf16)
    mirrored_ref[edge + length :, :] = jnp.zeros((edge, width), bf16)
    loop(length // BLOCK, table_step)
    attend_backward(
        starts_ref, qu_ref, qv_ref, k_ref, v_ref, t_ref, mirrored_ref, context_ref, logs_ref, dcontext_ref,
        dm_ref, dk_ref, dv_ref, dt_ref, small_ref.at[pl.ds(8, 8)], *attend
    )

    def queries_step(index):
        at = rows_at(index, BLOCK)
        d_norm = dot_t(dm_ref[at, :], in_ref[...])
        standard, inverse = normalize(h1_ref[at, :])
        gain = gains_ref[1:2, :]
        n2_ref[at, :] = (standard * gain).astype(bf16)
        small_ref[1:2, :] += column_sum(d_norm * standard)
        d1 = d2_ref[at, :] + normalize_back(standard, inverse, gain, d_norm)
        d1_ref[at, :] = d1
        picked = collect(cols_ref[at, 0:1], returned_ref)
        gate = gate_ref[at, :]
        dlogits_ref[at, :] = gate_back(d1, picked, gate, probs_ref[at, :], cols_ref[at, 2:3])
        low_ref[at, :] = (0.5 * gate * d1).astype(bf16)

    loop(length // BLOCK, queries_step)
    dtable_ref[...] = dt_ref[:, PAD * TILE : PAD * TILE + length].astype(bf16)
    dispatch(low_ref, slot_row_ref[0:1, :], out_refs)


def last_kernel(
    cols_ref, dlogits_ref, hidden_ref, d1_ref, embed_ref, router_ref, gains_ref, dembed_two_ref,
    drouter_two_ref, mid_ref, conv_ref, two_ref, five_ref, taps_ref, in_low_ref, out_low_ref, *refs,
):
    dsent_refs, refs = refs[:PARTS], refs[PARTS:]
    d0_ref, dembed_ref, routers_ref, small_ref, in_ref, out_ref, dsent_ref = refs
    in_ref[...] = in_low_ref[...].astype(f32)
    out_ref[...] = out_low_ref[...].astype(f32)
    length = hidden_ref.shape[0]
    taps = small_ref.shape[0] - 9
    join_blocks(dsent_refs, dsent_ref)
    drouter_ref = routers_ref.at[pl.ds(0, 8)]
    drouter_ref[...] = jnp.zeros_like(drouter_ref)
    routers_ref[8:, :] = drouter_two_ref[...]
    small_ref[0:1, :] = jnp.zeros_like(small_ref[0:1, :])
    small_ref[1:2, :] = mid_ref[1:2, :]
    small_ref[2:3, :] = conv_ref[0:1, :]
    small_ref[3:4, :] = two_ref[0:1, :]
    small_ref[4:5, :] = five_ref[0:1, :]
    small_ref[5:7, :] = mid_ref[8:10, :]
    small_ref[7 : 7 + taps, :] = taps_ref[:taps, :]
    small_ref[7 + taps :, :] = two_ref[1:3, :]

    def step(index):
        at = rows_at(index, BLOCK)
        standard, inverse = normalize(hidden_ref[at, :].astype(f32))
        gain = gains_ref[0:1, :]
        low = (standard * gain).astype(bf16)
        d_low, d_embed = router_back(
            dlogits_ref[at, :], low, embed_ref[at, :], router_ref, drouter_ref
        )
        dembed_ref[at, :] = d_embed + dembed_two_ref[at, :]
        d_norm = collect(cols_ref[at, 0:1], dsent_ref) + d_low
        small_ref[0:1, :] += column_sum(d_norm * standard)
        d0_ref[at, :] = d1_ref[at, :] + normalize_back(standard, inverse, gain, d_norm)

    loop(length // BLOCK, step)


def gather_small(values):
    return lax.all_to_all(values, BOTH, split_axis=0, concat_axis=0, tiled=True)


def across(values, axis, size, offset):
    if not offset:
        return values
    return lax.ppermute(values, axis, [(i, i ^ offset) for i in range(size)])


def exchange(blocks, experts):
    per = experts // PARTS
    moved = []
    for index, block in enumerate(blocks):
        rows = block.shape[0] // per
        pieces = []
        for k in range(index * per, (index + 1) * per):
            piece = block[(k - index * per) * rows : (k - index * per + 1) * rows]
            pieces.append(across(piece, "expert", experts, k))
        moved.append(pieces[0] if per == 1 else jnp.concatenate(pieces, axis=0))
    return moved


def ring_place(index, size):
    return jnp.where(index % 2 == 0, index // 2, size - 1 - index // 2)


def ring_member(place, size):
    place = (place + 2 * size) % size
    return jnp.where(place < size // 2, 2 * place, 2 * (size - 1 - place) + 1)


def ring_pairs(size, forward):
    order = list(range(0, size, 2)) + list(range(size - 1, 0, -2))
    step = 1 if forward else -1
    return [(order[k], order[(k + step) % size]) for k in range(size)]


def ring_gather(shards, size):
    found = []
    for number, shard in enumerate(shards):
        ahead = size // 2 if number % 2 == 0 else (size - 1) // 2
        pieces = [None] * size
        pieces[0] = shard
        found.append((pieces, ahead))
    for step in range(1, size // 2 + 1):
        for pieces, ahead in found:
            if step <= ahead:
                pieces[step] = lax.ppermute(pieces[step - 1], "dp", ring_pairs(size, False))
            if step <= size - 1 - ahead:
                pieces[-step] = lax.ppermute(pieces[-step + 1 or 0], "dp", ring_pairs(size, True))
    return [pieces for pieces, unused in found]


def assemble_kernel(count, order_ref, *refs):
    size = (len(refs) - 1 - count) // count
    sems = refs[-1]
    copies = []
    for number in range(count):
        target = refs[count * size + number]
        for offset in range(size):
            piece = refs[number * size + offset]
            rows = piece.shape[0]
            start = pl.multiple_of(order_ref[offset] * rows, 16)
            copies.append(
                pltpu.make_async_copy(
                    piece, target.at[pl.ds(start, rows)], sems.at[number * size + offset]
                )
            )
    for copy in copies:
        copy.start()
    for copy in copies:
        copy.wait()


def assemble(shards, size):
    place = ring_place(lax.axis_index("dp"), size)
    order = ring_member(place + jnp.arange(size, dtype=jnp.int32), size).astype(jnp.int32)
    groups = ring_gather(shards, size)
    count = len(groups)
    anywhere = pl.BlockSpec(memory_space=pl.ANY)
    return pl.pallas_call(
        functools.partial(assemble_kernel, count),
        out_shape=[
            shape_of((size * shard.shape[0],) + shard.shape[1:], shard.dtype) for shard in shards
        ],
        in_specs=[SMEM] + [anywhere] * (count * size),
        out_specs=[VMEM] * count,
        scratch_shapes=[pltpu.SemaphoreType.DMA((count * size,))],
        name="assemble",
    )(order, *[piece for pieces in groups for piece in pieces])


def own_parts(values, place, size, stride, mesh_axis):
    parts = [lax.dynamic_index_in_dim(values, place, 0, keepdims=False)]
    for k in range(1, values.shape[0]):
        theirs = lax.dynamic_index_in_dim(values, place ^ k, 0, keepdims=False)
        parts.append(across(theirs, mesh_axis, size, k * stride))
    return parts


def add_up(parts):
    total = parts[0].astype(f32)
    for part in parts[1:]:
        total = total + part.astype(f32)
    return total


def keep_one(values, place, size, stride, mesh_axis):
    return add_up(own_parts(values, place, size, stride, mesh_axis))


def near_parts(values):
    groups = values.shape[0]
    values = values.reshape((groups // 2, 2) + values.shape[1:])
    bit = lax.axis_index("dp") % 2
    mine = lax.dynamic_index_in_dim(values, bit, 1, keepdims=False)
    theirs = lax.dynamic_index_in_dim(values, 1 - bit, 1, keepdims=False)
    return [mine, across(theirs, "dp", groups, 1)]


def near_half(values):
    return add_up(near_parts(values)).astype(bf16)


def expert_parts(values, experts):
    me = lax.axis_index("expert")
    return [
        across(lax.dynamic_index_in_dim(values, me ^ k, 1, keepdims=False), "expert", experts, k)
        for k in range(experts)
    ]


def rows_product(left, right):
    return lax.dot_general(left, right, (((0,), (0,)), ((), ())), preferred_element_type=f32)


def blocks_product(left, right):
    left, right = jnp.concatenate(left, axis=0), jnp.concatenate(right, axis=0)
    return rows_product(left, right).astype(bf16)


def scatter_offloaded(grad_in, grad_out):
    return (
        lax.psum_scatter(grad_in, "dp", scatter_dimension=0, tiled=True),
        lax.psum_scatter(grad_out, "dp", scatter_dimension=0, tiled=True),
    )


def split_columns(values):
    middle = values.shape[1] // 2
    return [values[:, :middle], values[:, middle:]]


def sinus_rows(length, width, upward):
    distance = (length // 2 - 1 - np.arange(length)).astype(np.float32)
    distance = distance[::-1] if upward else distance
    rates = np.exp(
        np.arange(width // 2).astype(np.float32) * np.float32(-2.0 * math.log(10000.0) / width)
    ).astype(np.float32)
    angles = (distance[:, None] * rates[None, :]).astype(np.float64)
    table = np.concatenate([np.sin(angles), np.cos(angles)], axis=1)
    return jnp.asarray(table.astype(np.float32)).astype(bf16)


def body(
    groups,
    inputs,
    embedding,
    cotangent,
    first_routes,
    second_routes,
    segment_starts,
    norm_gains,
    first_router,
    second_router,
    first_in,
    first_out,
    second_in,
    second_out,
    attention_in,
    position_weight,
    position_bias,
    attention_out,
    pointwise_in,
    depthwise_kernel,
    batch_gain,
    batch_bias,
    pointwise_out,
):
    length, width = inputs.shape
    experts = first_router.shape[1]
    devices = groups * experts
    capacity = 17 * length // (16 * experts)
    slots = experts * capacity
    inner = first_in.shape[2]
    share = norm_gains.shape[1]
    taps = depthwise_kernel.shape[0]
    feats = first_router.shape[0]

    rows = jnp.concatenate(
        [norm_gains, position_bias, depthwise_kernel, batch_gain[None], batch_bias[None]], axis=0
    )
    count = rows.shape[0]
    flat = jnp.concatenate(
        [rows.reshape(-1), first_router.T.reshape(-1), second_router.T.reshape(-1)]
    ).astype(f32)
    small = gather_small(jnp.broadcast_to(flat[None], (devices,) + flat.shape))
    rows_all = small[:, : count * share].reshape(devices, count, share)
    rows_all = rows_all.transpose(1, 0, 2).reshape(count, devices * share)
    routers = small[:, count * share :].reshape(devices, 2, experts, feats)
    routers = routers.transpose(1, 2, 0, 3).reshape(2, experts, devices * feats)
    routers = jnp.pad(routers, ((0, 0), (0, TILE - experts), (0, 0)))
    routers = routers.transpose(0, 2, 1).astype(bf16)
    gains = jnp.pad(rows_all[0:5], ((0, 3), (0, 0)))
    bias = jnp.pad(rows_all[5:7], ((0, 6), (0, 0)))
    kernel_taps = jnp.pad(rows_all[7 : 7 + taps], ((0, 1), (0, 0)))
    batch = jnp.pad(rows_all[7 + taps : 9 + taps], ((0, 6), (0, 0)))

    packed = jnp.concatenate(
        [attention_in, position_weight, attention_out, pointwise_out, pointwise_in], axis=1
    )
    dense = lax.all_gather(packed, BOTH, axis=0, tiled=True)
    point_out = dense[:, 5 * width : 6 * width]

    first_pair = assemble((first_in[0], first_out[0]), groups)
    second_pair = (
        lax.all_gather(second_in[0], "dp", axis=0, tiled=True),
        lax.all_gather(second_out[0], "dp", axis=0, tiled=True),
    )

    me = lax.axis_index("expert")
    slot_rows, slot_cols = find_slots(first_routes, second_routes, me, capacity)
    sinus = sinus_rows(length, width, False)
    mirrored = sinus_rows(length, width, True)
    row_low = shape_of((length, width), bf16)
    row_full = shape_of((length, width), f32)
    lane_full = shape_of((length, TILE), f32)
    table_low = shape_of((length + 2 * PAD * TILE, width), bf16)
    block_low = shape_of((slots // PARTS, width), bf16)
    slots_scratch = pltpu.VMEM((slots, width), bf16)
    sums_scratch = pltpu.VMEM((8, width), f32)
    column = shape_of((length, 1), f32)
    eight = shape_of((8, width), f32)
    low_scratch = pltpu.VMEM((length, width), bf16)

    *sent_one, probs_one, gate_one = run(
        functools.partial(front_kernel, experts),
        (inputs, embedding, gains, routers[0], slot_cols, slot_rows),
        [VMEM] * 6,
        [block_low] * PARTS + [lane_full, column],
        [low_scratch],
        flops=4 * slots * length * width,
        name="front",
    )
    received_one = exchange(sent_one, experts)
    result_one = (
        expert_forward(received_one[2:3], *first_pair) + expert_forward(received_one[3:], *first_pair)
    )
    result_one = expert_forward(received_one[:2], *first_pair) + result_one
    returned_one = exchange(result_one, experts)

    edge_scratch = pltpu.VMEM((length + 2 * EDGE, width), f32)
    (
        h1, h2, query_u, query_v, keys, values, table, context, logs, convolved, sums,
    ) = run(
        middle_kernel,
        (
            segment_starts, inputs, slot_cols, gate_one, gains, dense, bias, kernel_taps, sinus,
            *returned_one,
        ),
        [SMEM] + [VMEM] * (8 + PARTS),
        [row_full, row_full]
        + [row_low] * 4
        + [table_low, row_low, lane_full, row_full, shape_of((devices, 1, 3 * width), f32)],
        [edge_scratch, sums_scratch, slots_scratch] + attend_scratch(length),
        flops=16 * length * length * width,
        name="middle",
    )
    totals = gather_small(sums)

    *sent_two, h3, active, probs_two, gate_two, stats = run(
        functools.partial(second_kernel, experts),
        (
            h2, convolved, totals, batch, point_out, embedding, gains, routers[1], slot_cols, slot_rows,
        ),
        [VMEM] * 10,
        [block_low] * PARTS + [row_full, row_low, lane_full, column, eight],
        [low_scratch],
        flops=4 * slots * length * width,
        name="second",
    )
    received_two = exchange(sent_two, experts)
    result_two = forward_in_turn(received_two, second_pair)
    returned_two = exchange(result_two, experts)

    *d_sent_two, output, d4, dlogits_two, dgain_five = run(
        turn_kernel,
        (
            h3, slot_cols, gate_two, probs_two, slot_rows, gains, cotangent, *returned_two,
        ),
        [VMEM] * (7 + PARTS),
        [block_low] * PARTS + [row_low, row_full, lane_full, eight],
        [low_scratch, slots_scratch],
        flops=4 * slots * length * width,
        name="turn",
    )
    d_result_two = exchange(d_sent_two, experts)
    unused, d_received_two, hidden_two, d_inner_two = backward_in_turn(
        received_two, d_result_two, second_pair
    )
    d_back_two = exchange(d_received_two, experts)
    grad_in_two, grad_out_two, *d_back_two = lax.optimization_barrier(
        (
            blocks_product(received_two, d_inner_two), blocks_product(hidden_two, d_result_two), *d_back_two,
        )
    )
    d_second_in, d_second_out = scatter_offloaded(grad_in_two, grad_out_two)

    router_shape = shape_of((8, 2 * width), f32)
    d3, d3_low, d_z, dembed_two, drouter_two, small_two, dsums_part = run(
        second_back_kernel,
        (
            slot_cols, dlogits_two, h3, d4, embedding, routers[1], gains, convolved, stats, batch, point_out,
            *d_back_two,
        ),
        [VMEM] * (11 + PARTS),
        [row_full, row_low, row_full, row_full, router_shape, eight, shape_of((devices, 1, 2 * width), f32)],
        [sums_scratch, slots_scratch],
        flops=4 * slots * length * width,
        name="second_back",
    )
    dsums = gather_small(dsums_part)
    d_pointwise_out = rows_product(active, d3_low)

    d2, d2_low, d_context, normed_three, d_gates, small_conv, d_taps = run(
        conv_back_kernel,
        (segment_starts, convolved, d_z, stats, dsums, d3, h2, gains, dense, kernel_taps),
        [SMEM] + [VMEM] * 9,
        [
            row_full, row_low, row_low, row_low, shape_of((length, 2 * width), bf16), eight,
            shape_of((16, width), f32),
        ],
        [
            edge_scratch, pltpu.VMEM((length, 2 * width), f32), pltpu.VMEM((16, 8, width), f32),
            pltpu.VMEM((2 * EDGE, 2 * width), f32),
        ],
        flops=6 * length * width * width,
        name="conv_back",
    )
    value_grad, gates_grad = split_columns(rows_product(normed_three, d_gates))
    early = jnp.stack(
        [
            part.astype(bf16).reshape(groups, experts, width // devices, width)
            for part in (rows_product(context, d2_low), d_pointwise_out, value_grad, gates_grad)
        ],
        axis=2,
    )
    early = expert_parts(early, experts)
    *d_sent_one, d1, dlogits_one, normed_two, d_mixed, d_table, small_mid = run(
        attend_back_kernel,
        (
            segment_starts, d2, d_context, h1, gains, dense, mirrored, query_u, query_v, keys, values, table,
            context, logs, slot_cols, gate_one, probs_one, slot_rows, *returned_one,
        ),
        [SMEM] + [VMEM] * (17 + PARTS),
        [block_low] * PARTS
        + [
            row_full, lane_full, row_low, shape_of((length, 3 * width), bf16),
            shape_of((width, length), bf16), shape_of((16, width), f32),
        ],
        [
            low_scratch, pltpu.VMEM(table_low.shape, bf16), slots_scratch,
            pltpu.VMEM((width, length), f32), pltpu.VMEM((width, length), f32),
            pltpu.VMEM((width, length + 2 * PAD * TILE), f32),
        ]
        + attend_back_scratch(),
        flops=32 * length * length * width,
        name="attend_back",
    )
    early, *d_sent_one = lax.optimization_barrier((early, *d_sent_one))
    d_result_one = exchange(d_sent_one, experts)
    (late,), d_received_one, hidden_one, d_inner_one = backward_in_turn(
        received_one, d_result_one, first_pair, (normed_two, d_mixed, d_table, mirrored)
    )
    late = expert_parts(late.reshape(groups, experts, width // devices, 4 * width), experts)
    d_back_one = exchange(d_received_one, experts)
    early = add_up(early).astype(bf16).reshape(groups, -1, width)
    grad_out = blocks_product(hidden_one, d_result_one).reshape(groups, -1, width)
    near_out = near_half(jnp.concatenate([grad_out, early], axis=1))
    grad_in = blocks_product(received_one, d_inner_one).reshape(groups, -1, inner)
    near_out, grad_in, late, d_back_one = lax.optimization_barrier(
        (near_out, grad_in, late, d_back_one)
    )
    far_out = own_parts(near_out, lax.axis_index("dp") // 2, groups, 2, "dp")
    near_in = near_parts(grad_in)
    d_start, d_embed, routers_grad, rows_grad, d_second_in, d_second_out = run(
        last_kernel,
        (
            slot_cols, dlogits_one, inputs, d1, embedding, routers[0], gains, dembed_two,
            drouter_two, small_mid, small_conv, small_two, dgain_five, d_taps, d_second_in, d_second_out,
            *d_back_one,
        ),
        [VMEM] * (16 + PARTS),
        [
            row_full, row_full, shape_of((16, 2 * width), f32), shape_of((count, width), f32),
            shape_of(first_in.shape[1:], f32), shape_of(first_out.shape[1:], f32),
        ],
        [slots_scratch],
        flops=4 * slots * length * width,
        name="last",
    )

    near_in, late, far_out, routers_grad, rows_grad = lax.optimization_barrier(
        (near_in, late, far_out, routers_grad, rows_grad)
    )
    near_in = add_up(near_in).astype(bf16)
    near_late = near_half(add_up(late).astype(bf16))
    late_share = add_up(own_parts(near_late, lax.axis_index("dp") // 2, groups, 2, "dp"))
    out_sum = add_up(far_out)
    far_in = own_parts(near_in, lax.axis_index("dp") // 2, groups, 2, "dp")
    far_in[1], routers_grad, rows_grad = lax.optimization_barrier(
        (far_in[1], routers_grad, rows_grad)
    )
    in_sum = add_up(far_in)
    d_first_out = out_sum[None, : first_out.shape[1]]
    d_first_in = in_sum[None]
    early_share = out_sum[first_out.shape[1] :].reshape(4, width // devices, width)
    early_share = jnp.concatenate([early_share[k] for k in range(4)], axis=1)
    rows_grad = rows_grad.reshape(count, devices, share).transpose(1, 0, 2).reshape(devices, -1)
    routers_grad = routers_grad.reshape(2, 8, devices, feats)[:, :experts]
    routers_grad = routers_grad.transpose(2, 0, 1, 3).reshape(devices, -1)
    small_grad = jnp.concatenate([rows_grad, routers_grad], axis=1)
    small_share = jnp.sum(
        lax.all_to_all(small_grad, BOTH, split_axis=0, concat_axis=0, tiled=True), axis=0
    )
    rows_share = small_share[: count * share].reshape(count, share)
    routers_share = small_share[count * share :].reshape(2, experts, feats).transpose(0, 2, 1)

    return (
        output,
        d_start,
        d_embed,
        rows_share[0:5],
        routers_share[0],
        routers_share[1],
        d_first_in,
        d_first_out,
        d_second_in[None],
        d_second_out[None],
        late_share[:, : 3 * width],
        late_share[:, 3 * width :],
        rows_share[5:7],
        early_share[:, :width],
        early_share[:, 2 * width :],
        rows_share[7 : 7 + taps],
        rows_share[7 + taps],
        rows_share[8 + taps],
        early_share[:, width : 2 * width],
    )


def solution(mesh):
    split = P(BOTH, None)
    wide = P(None, BOTH)
    bank = P("expert", "dp", None)
    line = P(BOTH)
    in_specs = (
        (split,) * 6
        + (wide, split, split)
        + (bank,) * 4
        + (split, split, wide, split, split, wide, line, line, split)
    )
    out_specs = (
        (split,) * 3
        + (wide, split, split)
        + (bank,) * 4
        + (split, split, wide, split, split, wide, line, line, split)
    )
    return jax.shard_map(
        functools.partial(body, mesh.shape["dp"]),
        mesh=mesh,
        in_specs=in_specs,
        out_specs=out_specs,
        check_vma=False,
    )
```

```python
import functools
import math

import jax
import jax.numpy as jnp
import numpy as np
from jax import lax
from jax.experimental import pallas as pl
from jax.experimental.pallas import tpu as pltpu
from jax.sharding import PartitionSpec as P

H = 8
TILE = 128
epsilon = 1e-05
masked_score = -1e30
BOTH = ("dp", "expert")
f32 = jnp.float32
bf16 = jnp.bfloat16

VMEM = pl.BlockSpec(memory_space=pltpu.VMEM)
SMEM = pl.BlockSpec(memory_space=pltpu.SMEM)


def shape_of(dims, kind):
    return jax.ShapeDtypeStruct(dims, kind)


def run(kernel, args, in_specs, outs, scratch=(), flops=0, name=None, limit=56):
    moved = sum(math.prod(a.shape) * a.dtype.itemsize for a in list(args) + list(outs))
    results = pl.pallas_call(
        kernel,
        out_shape=outs,
        in_specs=in_specs,
        out_specs=[VMEM] * len(outs),
        scratch_shapes=list(scratch),
        compiler_params=pltpu.CompilerParams(vmem_limit_bytes=limit * 2**20),
        cost_estimate=pl.CostEstimate(flops=flops, bytes_accessed=moved, transcendentals=0),
        name=name,
    )(*args)
    return list(results)


def dot(left, right):
    return lax.dot_general(left, right, (((1,), (0,)), ((), ())), preferred_element_type=f32)


def dot_t(left, right):
    return lax.dot_general(left, right, (((1,), (1,)), ((), ())), preferred_element_type=f32)


def t_dot(left, right):
    return lax.dot_general(left, right, (((0,), (0,)), ((), ())), preferred_element_type=f32)


def iota(dims, axis):
    return lax.broadcasted_iota(jnp.int32, dims, axis)


def normalize(values):
    center = values - jnp.mean(values, axis=-1, keepdims=True)
    spread = jnp.mean(center * center, axis=-1, keepdims=True)
    inverse = lax.rsqrt(spread + epsilon)
    return center * inverse, inverse


def normalize_back(standard, inverse, gain, upstream):
    scaled = upstream * gain
    first = jnp.mean(scaled, axis=-1, keepdims=True)
    second = jnp.mean(scaled * standard, axis=-1, keepdims=True)
    return inverse * (scaled - first - standard * second)


def column_sum(values):
    return jnp.sum(values, axis=0, keepdims=True)


def sigmoid(values):
    return 1.0 / (1.0 + jnp.exp(-values))


def loop(count, body):
    if count <= 4:
        for index in range(count):
            body(index)
        return

    def step(index, carry):
        body(index)
        return carry

    lax.fori_loop(0, count, step, 0)


def span_at(start, size, step):
    if isinstance(start, int):
        return slice(start, start + size)
    return pl.ds(pl.multiple_of(start, step), size)


def rows_at(index, size):
    if isinstance(index, int):
        return slice(index * size, (index + 1) * size)
    return pl.ds(pl.multiple_of(index * size, size), size)


def slots_kernel(capacity, offset_ref, one_ref, two_ref, rows_ref, cols_ref, stack):
    length = rows_ref.shape[1]
    block = 256
    stack[...] = jnp.zeros_like(stack)
    for half, chosen_ref in enumerate((one_ref, two_ref)):
        chosen = chosen_ref[...]
        near = chosen ^ offset_ref[0]
        onehot = jnp.where(iota((8, length), 0) == near, 1.0, 0.0)
        onehot_low = onehot.astype(bf16)
        for index in range(length // block):
            earlier = iota((length, block), 0) < iota((length, block), 1) + index * block
            counts = dot(onehot_low, jnp.where(earlier, 1.0, 0.0).astype(bf16))
            span = slice(index * block, (index + 1) * block)
            rank = column_sum(onehot[:, span] * counts)
            stack[half : half + 1, span] = (near[:, span] * capacity).astype(f32) + rank
        stack[2 + half : 3 + half, :] = chosen.astype(f32)
    rows_ref[...] = stack[:8, :].astype(jnp.int32)
    for index in range(length // TILE):
        span = slice(index * TILE, (index + 1) * TILE)
        cols_ref[span, :] = jnp.transpose(stack[:, span]).astype(jnp.int32)


def find_slots(routes_one, routes_two, offset, capacity):
    length = routes_one.shape[0]
    return run(
        functools.partial(slots_kernel, capacity),
        (offset.reshape(1), routes_one.reshape(1, length), routes_two.reshape(1, length)),
        [SMEM, VMEM, VMEM],
        [shape_of((8, length), jnp.int32), shape_of((length, TILE), jnp.int32)],
        [pltpu.VMEM((TILE, length), f32)],
        flops=8 * length * length * 128,
        name="slots",
    )


PARTS = 4


def dispatch(low_ref, slot_row, out_refs):
    block = out_refs[0].shape[0]
    length = low_ref.shape[0]
    for index, out_ref in enumerate(out_refs):
        ids = iota((block, length), 0) + index * block
        onehot = jnp.where(ids == slot_row, 1.0, 0.0).astype(bf16)
        out_ref[...] = dot(onehot, low_ref[...]).astype(bf16)


def join_blocks(block_refs, whole_ref):
    block = block_refs[0].shape[0]
    for index, block_ref in enumerate(block_refs):
        whole_ref[index * block : (index + 1) * block, :] = block_ref[...]


def collect(slot_col, table_ref):
    rows = slot_col.shape[0]
    slots = table_ref.shape[0]
    onehot = jnp.where(iota((rows, slots), 1) == slot_col, 1.0, 0.0).astype(bf16)
    return dot(onehot, table_ref[...])


def route_block(low, embed, router_ref, picks, experts):
    width = low.shape[1]
    logits = dot(low, router_ref[:width, :]) + dot(embed, router_ref[width:, :])
    lanes = iota(logits.shape, 1)
    inside = lanes < experts
    logits = jnp.where(inside, logits, masked_score)
    raised = jnp.where(inside, jnp.exp(logits - jnp.max(logits, axis=1, keepdims=True)), 0.0)
    probs = raised / jnp.sum(raised, axis=1, keepdims=True)
    gate = jnp.sum(jnp.where(lanes == picks, probs, 0.0), axis=1, keepdims=True)
    return probs, gate


BLOCK = 256


def front_kernel(
    experts, hidden_ref, embed_ref, gain_ref, router_ref, cols_ref, slot_row_ref, *refs,
):
    out_refs, (probs_ref, gate_ref, low_ref) = refs[:PARTS], refs[PARTS:]
    length = hidden_ref.shape[0]

    def step(index):
        at = rows_at(index, BLOCK)
        standard, unused = normalize(hidden_ref[at, :].astype(f32))
        low = (standard * gain_ref[0:1, :]).astype(bf16)
        low_ref[at, :] = low
        probs, gate = route_block(low, embed_ref[at, :], router_ref, cols_ref[at, 2:3], experts)
        probs_ref[at, :] = probs
        gate_ref[at, :] = gate

    loop(length // BLOCK, step)
    dispatch(low_ref, slot_row_ref[0:1, :], out_refs)


def expert_forward_kernel(count, in_ref, out_ref, *refs):
    for x_ref, y_ref in zip(refs[:count], refs[count:]):
        inner = dot(x_ref[...], in_ref[...])
        hidden = (inner * sigmoid(inner)).astype(bf16)
        y_ref[...] = dot(hidden, out_ref[...]).astype(bf16)


def expert_forward(received, weight_in, weight_out):
    block, width = received[0].shape
    count = len(received)
    return run(
        functools.partial(expert_forward_kernel, count),
        (weight_in, weight_out) + tuple(received),
        [VMEM] * (2 + count),
        [shape_of((block, width), bf16)] * count,
        flops=4 * count * block * width * weight_in.shape[1],
        name="experts",
        limit=32,
    )


def expert_backward_kernel(count, in_ref, out_ref, *refs):
    x_refs, dy_refs, refs = refs[:count], refs[count : 2 * count], refs[2 * count :]
    extra, refs = refs[: len(refs) - 3 * count], refs[len(refs) - 3 * count :]
    if extra:
        normed_ref, mixed_ref, table_ref, sinus_ref, grad_ref = extra
        width = normed_ref.shape[1]
        for part in range(3):
            lanes = slice(part * width, (part + 1) * width)
            grad_ref[:, lanes] = t_dot(normed_ref[...], mixed_ref[:, lanes]).astype(bf16)
        grad_ref[:, 3 * width :] = jnp.transpose(dot(table_ref[...], sinus_ref[...])).astype(bf16)
    dx_refs, hidden_refs, dinner_refs = refs[:count], refs[count : 2 * count], refs[2 * count :]
    for x_ref, dy_ref, dx_ref, hidden_ref, dinner_ref in zip(
        x_refs, dy_refs, dx_refs, hidden_refs, dinner_refs
    ):
        inner = dot(x_ref[...], in_ref[...])
        gates = sigmoid(inner)
        hidden = inner * gates
        hidden_ref[...] = hidden.astype(bf16)
        d_hidden = dot_t(dy_ref[...], out_ref[...])
        d_inner = (d_hidden * (gates + hidden * (1.0 - gates))).astype(bf16)
        dinner_ref[...] = d_inner
        dx_ref[...] = dot_t(d_inner, in_ref[...]).astype(bf16)


def expert_backward(received, d_result, weight_in, weight_out, extra=()):
    block, width = received[0].shape
    inner = weight_in.shape[1]
    count = len(received)
    more = [shape_of((width, 4 * width), bf16)] if extra else []
    outs = run(
        functools.partial(expert_backward_kernel, count),
        (weight_in, weight_out) + tuple(received) + tuple(d_result) + tuple(extra),
        [VMEM] * (2 + 2 * count + len(extra)),
        more + [shape_of((block, width), bf16)] * count + [shape_of((block, inner), bf16)] * (2 * count),
        flops=6 * count * block * width * inner,
        name="experts_back",
        limit=48 if extra else 40,
    )
    more, outs = outs[: len(more)], outs[len(more) :]
    return more, outs[:count], outs[count : 2 * count], outs[2 * count :]


def backward_in_turn(received, d_result, pair, extra=()):
    near, far = lax.optimization_barrier(
        (expert_backward(received[:2], d_result[:2], *pair, extra), d_result[2:])
    )
    parts = [
        near,
        expert_backward(received[2:3], far[:1], *pair),
        expert_backward(received[3:], far[1:], *pair),
    ]
    return [sum((list(part[k]) for part in parts), []) for k in range(4)]


def tile_window(starts_ref, first, length):
    count = starts_ref.shape[1]
    low = jnp.int32(0)
    high = jnp.int32(length)
    for k in range(1, count):
        low = jnp.where(starts_ref[0, k] <= first, starts_ref[0, k], low)
    for k in range(count - 1, 0, -1):
        high = jnp.where(starts_ref[0, k] > first + (TILE - 1), starts_ref[0, k], high)
    low = low // TILE
    steps = ((high + (TILE - 1)) // TILE - low + 1) // 2
    return jnp.minimum(low, length // TILE - 2 * steps), steps


def numbers_at(starts_ref, positions):
    total = jnp.zeros(positions.shape, jnp.int32)
    for k in range(1, starts_ref.shape[1]):
        total = total + jnp.where(positions >= starts_ref[0, k], 1, 0)
    return total


def same_tile(starts_ref, first_query, first_key):
    rows = numbers_at(starts_ref, iota((TILE, TILE), 0) + first_query)
    cols = numbers_at(starts_ref, iota((TILE, TILE), 1) + first_key)
    return rows == cols


PAD = 2


def chunk_rows(query_tile, key_tile, length, count, mirrored=False):
    tiles = length // TILE
    index = tiles - 1 - query_tile + key_tile - (tiles // 2 - PAD)
    if mirrored:
        index = tiles + 2 * PAD - count - index
    index = jnp.clip(index, 0, tiles + 2 * PAD - count)
    return pl.ds(pl.multiple_of(index * TILE, TILE), count * TILE)


def halves(values):
    left = iota(values.shape, 1) < TILE // 2
    zero = jnp.zeros_like(values)
    return jnp.concatenate(
        [jnp.where(left, values, zero), jnp.where(left, zero, values)], axis=0
    )


def turned_halves(values):
    turned = jnp.transpose(values)
    top = iota(turned.shape, 0) < TILE // 2
    zero = jnp.zeros_like(turned)
    return jnp.concatenate([jnp.where(top, turned, zero), jnp.where(top, zero, turned)], axis=1)


def skew(values):
    return jnp.concatenate(
        [
            pltpu.roll(values[:TILE], 1, 1, stride=1, stride_axis=0),
            pltpu.roll(values[TILE:], 1, 1, stride=1, stride_axis=0),
        ],
        axis=0,
    )


def mirror(values):
    row, col = iota((2 * TILE, 2 * TILE), 0), iota((2 * TILE, 2 * TILE), 1)
    flip = (row % TILE + col % TILE == TILE - 1) & (row // TILE == col // TILE)
    return dot(values, jnp.where(flip, 1.0, 0.0).astype(bf16))


def twice(values):
    return jnp.concatenate([values, values], axis=0)


PAIRS = H // 2


def attend_forward(
    starts_ref, qu_ref, qv_ref, k_ref, v_ref, t_ref, context_ref, logs_ref,
    qum, qvm, scores, rolled, peaks, sums, mixed,
):
    length = qu_ref.shape[0]
    tiles = length // TILE

    def query_step(tile):
        first = tile * TILE
        at = rows_at(tile, TILE)
        low, steps = tile_window(starts_ref, first, length)
        chunk = chunk_rows(tile, low, length, 1)
        for p in range(PAIRS):
            lanes = slice(p * TILE, (p + 1) * TILE)
            qum[p] = halves(qu_ref[at, lanes])
            qvm[p] = halves(qv_ref[at, lanes])
            rolled[p] = skew(dot_t(qvm[p], t_ref[chunk, lanes]))
            peaks[p] = jnp.full((2 * TILE, TILE), masked_score, f32)
            sums[p] = jnp.zeros((2 * TILE, TILE), f32)
            mixed[p] = jnp.zeros((2 * TILE, TILE), f32)
        lower = twice(iota((TILE, TILE), 1) <= iota((TILE, TILE), 0))

        def score_step(step, carry):
            key = low + 2 * step
            keys = pl.ds(pl.multiple_of(key * TILE, TILE), 2 * TILE)
            same_one = twice(same_tile(starts_ref, first, key * TILE))
            same_two = twice(same_tile(starts_ref, first, key * TILE + TILE))
            chunks = chunk_rows(tile, key + 1, length, 2)
            for p in range(PAIRS):
                lanes = slice(p * TILE, (p + 1) * TILE)
                content = dot_t(qum[p], k_ref[keys, lanes])
                fresh = dot_t(qvm[p], t_ref[chunks, lanes])
                one, two = skew(fresh[:, :TILE]), skew(fresh[:, TILE:])
                value_one = content[:, :TILE] + jnp.where(lower, rolled[p], one)
                value_two = content[:, TILE:] + jnp.where(lower, one, two)
                value_one = jnp.where(same_one, value_one, masked_score)
                value_two = jnp.where(same_two, value_two, masked_score)
                rolled[p] = two
                scores[2 * step, p] = value_one
                scores[2 * step + 1, p] = value_two
                peaks[p] = jnp.maximum(peaks[p], jnp.maximum(value_one, value_two))
            return carry

        lax.fori_loop(0, steps, score_step, 0)
        for p in range(PAIRS):
            peaks[p] = jnp.broadcast_to(
                jnp.max(peaks[p], axis=1, keepdims=True), (2 * TILE, TILE)
            )

        def value_step(step, carry):
            keys = pl.ds(pl.multiple_of((low + 2 * step) * TILE, TILE), 2 * TILE)
            for p in range(PAIRS):
                lanes = slice(p * TILE, (p + 1) * TILE)
                one = jnp.exp(scores[2 * step, p] - peaks[p])
                two = jnp.exp(scores[2 * step + 1, p] - peaks[p])
                sums[p] += one + two
                raised = jnp.concatenate([one.astype(bf16), two.astype(bf16)], axis=1)
                mixed[p] += dot(raised, v_ref[keys, lanes])
            return carry

        lax.fori_loop(0, steps, value_step, 0)
        left = iota((TILE, TILE), 1) < TILE // 2
        logs = jnp.zeros((TILE, TILE), f32)
        lane = iota((TILE, TILE), 1)
        for p in range(PAIRS):
            lanes = slice(p * TILE, (p + 1) * TILE)
            total = jnp.sum(sums[p], axis=1, keepdims=True)
            result = mixed[p] * (1.0 / total)
            context_ref[at, lanes] = jnp.where(left, result[:TILE], result[TILE:]).astype(bf16)
            logsum = peaks[p] + jnp.log(total)
            logs = jnp.where(lane == 2 * p, logsum[:TILE], logs)
            logs = jnp.where(lane == 2 * p + 1, logsum[TILE:], logs)
        logs_ref[at, :] = logs

    loop(tiles, query_step)


def attend_scratch(length):
    pair = (PAIRS, 2 * TILE, TILE)
    return [
        pltpu.VMEM(pair, bf16),
        pltpu.VMEM(pair, bf16),
        pltpu.VMEM((length // TILE,) + pair, f32),
        pltpu.VMEM(pair, f32),
        pltpu.VMEM(pair, f32),
        pltpu.VMEM(pair, f32),
        pltpu.VMEM(pair, f32),
    ]


STRIP = 32


def strips():
    return [
        (slice(head * TILE + row, head * TILE + row + STRIP), row)
        for head in range(2)
        for row in range(0, TILE, STRIP)
    ]


def skew_strip(values, row):
    return pltpu.roll(values, 1 + row, 1, stride=1, stride_axis=0)


def attend_backward(
    starts_ref, qu_ref, qv_ref, k_ref, v_ref, t_ref, mirrored_ref, context_ref, logs_ref, dcontext_ref,
    dm_ref, dk_ref, dv_ref, dt_ref, dbias_ref,
    qum, qvm, dcm, qut, qvt, dct, logs, deltas, rolled, unrolled, dqu, dqv, first_s, second_s, third_s,
    probs_s, dlow_s, moved_s,
):
    length, width = qu_ref.shape
    tiles = length // TILE
    scale = 1.0 / math.sqrt(width // H)
    dk_ref[...] = jnp.zeros_like(dk_ref)
    dv_ref[...] = jnp.zeros_like(dv_ref)
    dt_ref[...] = jnp.zeros_like(dt_ref)
    dbias_ref[...] = jnp.zeros_like(dbias_ref)

    def query_step(tile):
        first = tile * TILE
        at = rows_at(tile, TILE)
        low, steps = tile_window(starts_ref, first, length)
        chunk = chunk_rows(tile, low, length, 1)
        logs_tile = logs_ref[at, :]
        for p in range(PAIRS):
            lanes = slice(p * TILE, (p + 1) * TILE)
            query_u = halves(qu_ref[at, lanes])
            query_v = halves(qv_ref[at, lanes])
            upstream = halves(dcontext_ref[at, lanes])
            qum[p] = query_u
            qvm[p] = query_v
            dcm[p] = upstream
            qut[p] = turned_halves(qu_ref[at, lanes])
            qvt[p] = turned_halves(qv_ref[at, lanes])
            dct[p] = turned_halves(dcontext_ref[at, lanes])
            delta = jnp.sum(
                upstream.astype(f32) * twice(context_ref[at, lanes].astype(f32)),
                axis=1,
                keepdims=True,
            )
            deltas[p] = jnp.broadcast_to(delta, (2 * TILE, TILE))
            logs[p, :TILE] = jnp.broadcast_to(logs_tile[:, 2 * p : 2 * p + 1], (TILE, TILE))
            logs[p, TILE:] = jnp.broadcast_to(logs_tile[:, 2 * p + 1 : 2 * p + 2], (TILE, TILE))
            rolled[p] = skew(dot_t(query_v, t_ref[chunk, lanes]))
            unrolled[p] = jnp.zeros((2 * TILE, TILE), f32)
            dqu[p] = jnp.zeros((2 * TILE, TILE), f32)
            dqv[p] = jnp.zeros((2 * TILE, TILE), f32)
        lower = twice(iota((TILE, TILE), 1) <= iota((TILE, TILE), 0))

        def step_body(step, carry):
            key = low + 2 * step
            keys = pl.ds(pl.multiple_of(key * TILE, TILE), 2 * TILE)
            same_one = same_tile(starts_ref, first, key * TILE)
            same_two = same_tile(starts_ref, first, key * TILE + TILE)
            before = chunk_rows(tile, key, length, 2, True)
            after = chunk_rows(tile, key + 1, length, 2)
            for p in range(PAIRS):
                lanes = slice(p * TILE, (p + 1) * TILE)
                first_s[p] = dot_t(qum[p], k_ref[keys, lanes])
                second_s[p] = dot_t(qvm[p], t_ref[after, lanes])
                third_s[p] = dot_t(dcm[p], v_ref[keys, lanes])
            for p in range(PAIRS):
                for rows, row in strips():
                    near = iota((STRIP, TILE), 1) <= iota((STRIP, TILE), 0) + row
                    span = slice(row, row + STRIP)
                    one = skew_strip(second_s[p, rows, :TILE], row)
                    two = skew_strip(second_s[p, rows, TILE:], row)
                    value_one = first_s[p, rows, :TILE] + jnp.where(near, rolled[p, rows], one)
                    value_two = first_s[p, rows, TILE:] + jnp.where(near, one, two)
                    rolled[p, rows] = two
                    log, delta = logs[p, rows], deltas[p, rows]
                    probs_one = jnp.where(same_one[span], jnp.exp(value_one - log), 0.0)
                    probs_two = jnp.where(same_two[span], jnp.exp(value_two - log), 0.0)
                    probs_s[p, rows, :TILE] = probs_one.astype(bf16)
                    probs_s[p, rows, TILE:] = probs_two.astype(bf16)
                    dlow_s[p, rows, :TILE] = (probs_one * (third_s[p, rows, :TILE] - delta)).astype(bf16)
                    dlow_s[p, rows, TILE:] = (probs_two * (third_s[p, rows, TILE:] - delta)).astype(bf16)
            for p in range(PAIRS):
                lanes = slice(p * TILE, (p + 1) * TILE)
                second_s[p] = mirror(dlow_s[p])
                dv_ref[lanes, keys] += dot(dct[p], probs_s[p])
                dk_ref[lanes, keys] += dot(qut[p], dlow_s[p])
                dqu[p] += dot(dlow_s[p], k_ref[keys, lanes])
            for p in range(PAIRS):
                for rows, row in strips():
                    near = iota((STRIP, TILE), 1) <= iota((STRIP, TILE), 0) + row
                    one = skew_strip(second_s[p, rows, :TILE], row)
                    two = skew_strip(second_s[p, rows, TILE:], row)
                    moved_s[p, rows, :TILE] = jnp.where(near, two, one).astype(bf16)
                    moved_s[p, rows, TILE:] = jnp.where(near, one, unrolled[p, rows]).astype(bf16)
                    unrolled[p, rows] = two
            for p in range(PAIRS):
                lanes = slice(p * TILE, (p + 1) * TILE)
                dt_ref[lanes, before] += dot(qvt[p], moved_s[p])
                dqv[p] += dot(moved_s[p], mirrored_ref[before, lanes])
            return carry

        lax.fori_loop(0, steps, step_body, 0)
        last = chunk_rows(tile, low + 2 * steps, length, 1, True)
        left = iota((TILE, TILE), 1) < TILE // 2
        for p in range(PAIRS):
            lanes = slice(p * TILE, (p + 1) * TILE)
            moved = jnp.where(lower, 0.0, unrolled[p]).astype(bf16)
            dt_ref[lanes, last] += dot(qvt[p], moved)
            full_u = dqu[p]
            full_v = dqv[p] + dot(moved, mirrored_ref[last, lanes])
            part_u = jnp.where(left, full_u[:TILE], full_u[TILE:]) * scale
            part_v = jnp.where(left, full_v[:TILE], full_v[TILE:]) * scale
            dbias_ref[0:1, lanes] += column_sum(part_u)
            dbias_ref[1:2, lanes] += column_sum(part_v)
            dm_ref[at, lanes] = (part_u + part_v).astype(bf16)

    loop(tiles, query_step)

    def finish(index):
        at = rows_at(index, TILE)
        for p in range(PAIRS):
            lanes = slice(p * TILE, (p + 1) * TILE)
            key_lanes = slice(width + p * TILE, width + (p + 1) * TILE)
            value_lanes = slice(2 * width + p * TILE, 2 * width + (p + 1) * TILE)
            dm_ref[at, key_lanes] = jnp.transpose(dk_ref[lanes, at].astype(bf16))
            dm_ref[at, value_lanes] = jnp.transpose(dv_ref[lanes, at].astype(bf16))

    loop(tiles, finish)


def attend_back_scratch():
    pair = (PAIRS, 2 * TILE, TILE)
    turned = (PAIRS, TILE, 2 * TILE)
    square = (PAIRS, 2 * TILE, 2 * TILE)
    return (
        [pltpu.VMEM(dims, bf16) for dims in (pair,) * 3 + (turned,) * 3]
        + [pltpu.VMEM(dims, f32) for dims in (pair,) * 6 + (square,) * 3]
        + [pltpu.VMEM(square, bf16) for unused in range(3)]
    )


def dense_parts(dense_ref):
    width = dense_ref.shape[0]
    cuts = (0, 3, 4, 5, 6, 8)
    return [
        dense_ref.at[:, pl.ds(start * width, (stop - start) * width)]
        for start, stop in zip(cuts[:-1], cuts[1:])
    ]


def shifted(values, reach, taps):
    rows = values.shape[0]
    found = {}
    for rest in range(8):
        starts = [EDGE - reach + k for k in range(taps) if (EDGE - reach + k) % 8 == rest]
        turned = pltpu.roll(values, (rows - rest) % rows, 0) if rest else values
        for start in starts:
            found[start - EDGE + reach] = turned[start - rest : start - rest + rows - 2 * EDGE]
    return [found[k] for k in range(taps)]


def at_edges(starts_ref, length, step):
    for k in range(1, starts_ref.shape[1]):
        edge = starts_ref[0, k]

        @pl.when(edge < length)
        def unused():
            start = jnp.minimum((edge - 8) // 8 * 8, length - 2 * EDGE)
            start = pl.multiple_of(start, 8)
            step(start, iota((2 * EDGE, TILE), 0) + start)


def spread_rows(rows_ref, out_ref):
    width = rows_ref.shape[1]
    for row in range(out_ref.shape[2] // width):
        lanes = slice(row * width, (row + 1) * width)
        out_ref[:, :, lanes] = jnp.broadcast_to(
            rows_ref[row : row + 1, :][None], (out_ref.shape[0], 1, width)
        )


EDGE = 16


def middle_kernel(
    starts_ref, hidden_ref, cols_ref, gate_ref, gains_ref, dense_ref, bias_ref, taps_ref, sinus_ref,
    *refs,
):
    returned_refs, refs = refs[:PARTS], refs[PARTS:]
    h1_ref, h2_ref, qu_ref, qv_ref, k_ref, v_ref, t_ref, context_ref, logs_ref = refs[:9]
    conv_ref, sums_ref, padded, sums, returned_ref = refs[9:14]
    attend = refs[14:]
    join_blocks(returned_refs, returned_ref)
    length, width = h1_ref.shape
    scale = 1.0 / math.sqrt(width // H)
    in_ref, place_ref, mix_ref, unused, point_ref = dense_parts(dense_ref)

    def queries_step(index):
        at = rows_at(index, BLOCK)
        picked = collect(cols_ref[at, 0:1], returned_ref)
        h1 = hidden_ref[at, :].astype(f32) + 0.5 * gate_ref[at, :] * picked
        h1_ref[at, :] = h1
        standard, unused = normalize(h1)
        low = (standard * gains_ref[1:2, :]).astype(bf16)
        queries = dot(low, in_ref[:, :width])
        qu_ref[at, :] = ((queries + bias_ref[0:1, :]).astype(bf16).astype(f32) * scale).astype(bf16)
        qv_ref[at, :] = ((queries + bias_ref[1:2, :]).astype(bf16).astype(f32) * scale).astype(bf16)
        k_ref[at, :] = dot(low, in_ref[:, width : 2 * width]).astype(bf16)
        v_ref[at, :] = dot(low, in_ref[:, 2 * width :]).astype(bf16)
        table_at = span_at(index * BLOCK + edge, BLOCK, TILE)
        t_ref[table_at, :] = dot(sinus_ref[at, :], place_ref[...]).astype(bf16)

    edge = PAD * TILE
    t_ref[:edge, :] = jnp.zeros((edge, width), bf16)
    t_ref[edge + length :, :] = jnp.zeros((edge, width), bf16)
    loop(length // BLOCK, queries_step)
    attend_forward(
        starts_ref, qu_ref, qv_ref, k_ref, v_ref, t_ref, context_ref, logs_ref, *attend
    )
    padded[:EDGE, :] = jnp.zeros((EDGE, width), f32)
    padded[EDGE + length :, :] = jnp.zeros((EDGE, width), f32)

    def gates_step(index):
        at = rows_at(index, BLOCK)
        h2 = h1_ref[at, :] + dot(context_ref[at, :], mix_ref[...])
        h2_ref[at, :] = h2
        standard, unused = normalize(h2)
        low = (standard * gains_ref[2:3, :]).astype(bf16)
        value = dot(low, point_ref[:, :width])
        gates = dot(low, point_ref[:, width:])
        padded[span_at(index * BLOCK + EDGE, BLOCK, EDGE), :] = value * sigmoid(gates)

    loop(length // BLOCK, gates_step)
    sums[...] = jnp.zeros_like(sums)
    taps = taps_ref.shape[0] - 1
    reach = taps // 2
    frames = starts_ref[0, starts_ref.shape[1] - 1]

    def conv_step(index):
        first = index * TILE
        around = pl.ds(pl.multiple_of(first, TILE), TILE + 2 * EDGE)
        for part in range(width // TILE):
            lanes = slice(part * TILE, (part + 1) * TILE)
            total = jnp.zeros((TILE, TILE), f32)
            for tap, near in enumerate(shifted(padded[around, lanes], reach, taps)):
                total = total + near * taps_ref[tap : tap + 1, lanes]
            conv_ref[rows_at(index, TILE), lanes] = total

    loop(length // TILE, conv_step)

    def edge_step(start, place):
        here = numbers_at(starts_ref, place)
        masks = [numbers_at(starts_ref, place + (tap - reach)) == here for tap in range(taps)]
        around = pl.ds(start, 2 * EDGE + 2 * EDGE)
        for part in range(width // TILE):
            lanes = slice(part * TILE, (part + 1) * TILE)
            total = jnp.zeros(place.shape, f32)
            for tap, near in enumerate(shifted(padded[around, lanes], reach, taps)):
                total = total + jnp.where(masks[tap], near, 0.0) * taps_ref[tap : tap + 1, lanes]
            conv_ref[pl.ds(start, 2 * EDGE), lanes] = total

    at_edges(starts_ref, length, edge_step)

    def sums_step(index):
        at = rows_at(index, BLOCK)
        inside = (iota((BLOCK, 1), 0) + index * BLOCK) < frames
        kept = jnp.where(inside, conv_ref[at, :], 0.0)
        sums[0:1, :] += column_sum(kept)
        sums[1:2, :] += column_sum(kept * kept)

    loop(length // BLOCK, sums_step)
    sums[2:3, :] = jnp.zeros((1, width), f32) + frames.astype(f32)
    spread_rows(sums, sums_ref)


def batch_totals(totals_ref, width):
    totals = jnp.sum(totals_ref[...], axis=0)
    count = totals[:, 2 * width :]
    mean = totals[:, :width] / count
    variance = totals[:, width : 2 * width] / count - mean * mean
    return mean, lax.rsqrt(variance + epsilon), count


def batch_block(conv, mean, inverse, batch_ref):
    centred = conv - mean
    standard = centred * inverse
    batched = standard * batch_ref[0:1, :] + batch_ref[1:2, :]
    return centred, standard, batched


def second_kernel(
    experts, h2_ref, conv_ref, totals_ref, batch_ref, point_ref, embed_ref, gains_ref, router_ref,
    cols_ref, slot_row_ref, *refs,
):
    out_refs, refs = refs[:PARTS], refs[PARTS:]
    h3_ref, active_ref, probs_ref, gate_ref, stats_ref, low_ref = refs
    length, width = h2_ref.shape
    mean, inverse, count = batch_totals(totals_ref, width)
    stats_ref[0:1, :] = mean
    stats_ref[1:2, :] = inverse
    stats_ref[2:3, :] = count

    def step(index):
        at = rows_at(index, BLOCK)
        unused, unused, batched = batch_block(conv_ref[at, :], mean, inverse, batch_ref)
        active = (batched * sigmoid(batched)).astype(bf16)
        active_ref[at, :] = active
        h3 = h2_ref[at, :] + dot(active, point_ref[...])
        h3_ref[at, :] = h3
        standard, unused = normalize(h3)
        low = (standard * gains_ref[3:4, :]).astype(bf16)
        low_ref[at, :] = low
        probs, gate = route_block(low, embed_ref[at, :], router_ref, cols_ref[at, 3:4], experts)
        probs_ref[at, :] = probs
        gate_ref[at, :] = gate

    loop(length // BLOCK, step)
    dispatch(low_ref, slot_row_ref[1:2, :], out_refs)


def gate_back(upstream, picked, gate, probs, picks):
    d_gate = 0.5 * jnp.sum(upstream * picked, axis=1, keepdims=True)
    onehot = jnp.where(iota(probs.shape, 1) == picks, 1.0, 0.0)
    return (d_gate * gate) * (onehot - probs)


def turn_kernel(
    h3_ref, cols_ref, gate_ref, probs_ref, slot_row_ref, gains_ref, cotangent_ref, *refs,
):
    returned_refs, out_refs, refs = refs[:PARTS], refs[PARTS : 2 * PARTS], refs[2 * PARTS :]
    output_ref, d4_ref, dlogits_ref, dgain_ref, low_ref, returned_ref = refs
    length = h3_ref.shape[0]
    join_blocks(returned_refs, returned_ref)
    dgain_ref[...] = jnp.zeros_like(dgain_ref)

    def step(index):
        at = rows_at(index, BLOCK)
        picked = collect(cols_ref[at, 1:2], returned_ref)
        gate = gate_ref[at, :]
        h4 = h3_ref[at, :] + 0.5 * gate * picked
        standard, inverse = normalize(h4)
        gain = gains_ref[4:5, :]
        output_ref[at, :] = (standard * gain).astype(bf16)
        upstream = cotangent_ref[at, :].astype(f32)
        dgain_ref[0:1, :] += column_sum(upstream * standard)
        d4 = normalize_back(standard, inverse, gain, upstream)
        d4_ref[at, :] = d4
        dlogits_ref[at, :] = gate_back(d4, picked, gate, probs_ref[at, :], cols_ref[at, 3:4])
        low_ref[at, :] = (0.5 * gate * d4).astype(bf16)

    loop(length // BLOCK, step)
    dispatch(low_ref, slot_row_ref[1:2, :], out_refs)


def router_back(dlogits, low, embed, router_ref, drouter_ref):
    width = low.shape[1]
    high = dlogits.astype(bf16)
    rest = (dlogits - high.astype(f32)).astype(bf16)
    d_low = dot_t(high, router_ref[:width, :]) + dot_t(rest, router_ref[:width, :])
    d_embed = dot_t(high, router_ref[width:, :]) + dot_t(rest, router_ref[width:, :])
    turned = jnp.transpose(dlogits)[:8, :]
    turned_high = turned.astype(bf16)
    turned_rest = (turned - turned_high.astype(f32)).astype(bf16)
    drouter_ref[:, :width] += dot(turned_high, low) + dot(turned_rest, low)
    drouter_ref[:, width:] += dot(turned_high, embed) + dot(turned_rest, embed)
    return d_low, d_embed


def second_back_kernel(
    cols_ref, dlogits_ref, h3_ref, d4_ref, embed_ref, router_ref, gains_ref, conv_ref, stats_ref,
    batch_ref, point_ref, *refs,
):
    dsent_refs, refs = refs[:PARTS], refs[PARTS:]
    d3_ref, dlow_ref, dz_ref, dembed_ref, drouter_ref, small_ref, sums_ref, sums, dsent_ref = refs
    length, width = h3_ref.shape
    drouter_ref[...] = jnp.zeros_like(drouter_ref)
    small_ref[...] = jnp.zeros_like(small_ref)
    sums[...] = jnp.zeros_like(sums)
    join_blocks(dsent_refs, dsent_ref)
    mean, batch_inverse = stats_ref[0:1, :], stats_ref[1:2, :]

    def step(index):
        at = rows_at(index, BLOCK)
        standard, inverse = normalize(h3_ref[at, :])
        gain = gains_ref[3:4, :]
        low = (standard * gain).astype(bf16)
        d_low, d_embed = router_back(
            dlogits_ref[at, :], low, embed_ref[at, :], router_ref, drouter_ref
        )
        dembed_ref[at, :] = d_embed
        d_norm = collect(cols_ref[at, 1:2], dsent_ref) + d_low
        small_ref[0:1, :] += column_sum(d_norm * standard)
        d3 = d4_ref[at, :] + normalize_back(standard, inverse, gain, d_norm)
        d3_ref[at, :] = d3
        d3_low = d3.astype(bf16)
        dlow_ref[at, :] = d3_low
        centred, normed, batched = batch_block(conv_ref[at, :], mean, batch_inverse, batch_ref)
        gates = sigmoid(batched)
        d_batched = dot_t(d3_low, point_ref[...]) * (gates + batched * gates * (1.0 - gates))
        small_ref[1:2, :] += column_sum(d_batched * normed)
        small_ref[2:3, :] += column_sum(d_batched)
        d_z = d_batched * batch_ref[0:1, :]
        dz_ref[at, :] = d_z
        sums[0:1, :] += column_sum(d_z)
        sums[1:2, :] += column_sum(d_z * centred)

    loop(length // BLOCK, step)
    spread_rows(sums, sums_ref)


def conv_back_kernel(
    starts_ref, conv_ref, dz_ref, stats_ref, dsums_ref, d3_ref, h2_ref, gains_ref, dense_ref, taps_ref,
    d2_ref, d2low_ref, dcontext_ref, n3_ref, dg_ref, small_ref, dtaps_ref, padded, linear, dtaps, edge_grad,
):
    length, width = h2_ref.shape
    unused, unused, mix_ref, unused, point_ref = dense_parts(dense_ref)
    taps = taps_ref.shape[0] - 1
    reach = taps // 2
    frames = starts_ref[0, starts_ref.shape[1] - 1]
    small_ref[...] = jnp.zeros_like(small_ref)
    dtaps[...] = jnp.zeros_like(dtaps)
    mean, batch_inverse, count = stats_ref[0:1, :], stats_ref[1:2, :], stats_ref[2:3, :]
    dsums = jnp.sum(dsums_ref[...], axis=0)
    d_variance = -0.5 * batch_inverse * batch_inverse * batch_inverse * dsums[:, width:]
    padded[:EDGE, :] = jnp.zeros((EDGE, width), f32)
    padded[EDGE + length :, :] = jnp.zeros((EDGE, width), f32)

    def conv_step(index):
        at = rows_at(index, BLOCK)
        centred = conv_ref[at, :] - mean
        inside = (iota((BLOCK, 1), 0) + index * BLOCK) < frames
        shared = (2.0 * d_variance * centred - batch_inverse * dsums[:, :width]) / count
        d_conv = batch_inverse * dz_ref[at, :] + jnp.where(inside, shared, 0.0)
        padded[span_at(index * BLOCK + EDGE, BLOCK, EDGE), :] = d_conv
        standard, unused = normalize(h2_ref[at, :])
        low = (standard * gains_ref[2:3, :]).astype(bf16)
        n3_ref[at, :] = low
        value = dot(low, point_ref[:, :width])
        linear[at, :width] = value
        linear[at, width:] = sigmoid(dot(low, point_ref[:, width:]))

    loop(length // BLOCK, conv_step)

    def turn_step(index):
        at = rows_at(index, TILE)
        around = pl.ds(pl.multiple_of(index * TILE, TILE), TILE + 2 * EDGE)
        for part in range(width // TILE):
            lanes = slice(part * TILE, (part + 1) * TILE)
            other = slice(width + part * TILE, width + (part + 1) * TILE)
            value, gate = linear[at, lanes], linear[at, other]
            passed = value * gate
            total = jnp.zeros((TILE, TILE), f32)
            for step, near in enumerate(shifted(padded[around, lanes], reach, taps)):
                tap = taps - 1 - step
                total = total + near * taps_ref[tap : tap + 1, lanes]
                dtaps[tap, :, lanes] += jnp.sum((near * passed).reshape(TILE // 8, 8, TILE), axis=0)
            dg_ref[at, lanes] = (total * gate).astype(bf16)
            dg_ref[at, other] = (total * passed * (1.0 - gate)).astype(bf16)

    def edge_step(start, place):
        rows = 2 * EDGE
        at = pl.ds(start, rows)
        here = numbers_at(starts_ref, place)
        masks = [numbers_at(starts_ref, place - (reach - tap)) == here for tap in range(taps)]
        around = pl.ds(start, rows + 2 * EDGE)
        for part in range(width // TILE):
            lanes = slice(part * TILE, (part + 1) * TILE)
            other = slice(width + part * TILE, width + (part + 1) * TILE)
            value, gate = linear[at, lanes], linear[at, other]
            passed = value * gate
            total = jnp.zeros((rows, TILE), f32)
            for step, near in enumerate(shifted(padded[around, lanes], reach, taps)):
                tap = taps - 1 - step
                total = total + jnp.where(masks[step], near, 0.0) * taps_ref[tap : tap + 1, lanes]
                extra = jnp.where(masks[step], 0.0, near) * passed
                dtaps[tap, :, lanes] -= jnp.sum(extra.reshape(rows // 8, 8, TILE), axis=0)
            edge_grad[:, lanes] = total * gate
            edge_grad[:, other] = total * passed * (1.0 - gate)
        low = pl.multiple_of(jnp.minimum(start // 16 * 16, length - rows - 16), 16)
        wide = pl.ds(low, rows + 16)
        shift = start - low
        whole = dg_ref[wide, :].astype(f32)
        grad = edge_grad[...]
        zero = jnp.zeros((16, 2 * width), f32)
        head = jnp.concatenate([grad, zero], axis=0)
        middle = jnp.concatenate([zero[:8], grad, zero[:8]], axis=0)
        tail = jnp.concatenate([zero, grad], axis=0)
        place = iota((rows + 16, 1), 0) - shift
        moved = jnp.where(shift == 0, head, jnp.where(shift == 8, middle, tail))
        inside = (place >= 0) & (place < rows)
        dg_ref[wide, :] = jnp.where(inside, moved, whole).astype(bf16)

    loop(length // TILE, turn_step)
    at_edges(starts_ref, length, edge_step)
    dtaps_ref[...] = jnp.sum(dtaps[...], axis=1)

    def gates_step(index):
        at = rows_at(index, BLOCK)
        d_norm = dot_t(dg_ref[at, :], point_ref[...])
        standard, inverse = normalize(h2_ref[at, :])
        small_ref[0:1, :] += column_sum(d_norm * standard)
        d2 = d3_ref[at, :] + normalize_back(standard, inverse, gains_ref[2:3, :], d_norm)
        d2_ref[at, :] = d2
        low = d2.astype(bf16)
        d2low_ref[at, :] = low
        dcontext_ref[at, :] = dot_t(low, mix_ref[...]).astype(bf16)

    loop(length // BLOCK, gates_step)


def attend_back_kernel(
    starts_ref, d2_ref, dcontext_ref, h1_ref, gains_ref, dense_ref, sinus_ref, qu_ref, qv_ref, k_ref, v_ref,
    t_ref, context_ref, logs_ref, cols_ref, gate_ref, probs_ref, slot_row_ref, *refs,
):
    returned_refs, out_refs, refs = refs[:PARTS], refs[PARTS : 2 * PARTS], refs[2 * PARTS :]
    d1_ref, dlogits_ref, n2_ref, dm_ref, dtable_ref, small_ref = refs[:6]
    low_ref, mirrored_ref, returned_ref, dk_ref, dv_ref, dt_ref = refs[6:12]
    attend = refs[12:]
    length, width = h1_ref.shape
    in_ref, place_ref, unused, unused, unused = dense_parts(dense_ref)
    small_ref[...] = jnp.zeros_like(small_ref)
    join_blocks(returned_refs, returned_ref)

    def table_step(index):
        at = rows_at(index, BLOCK)
        table_at = span_at(index * BLOCK + edge, BLOCK, TILE)
        mirrored_ref[table_at, :] = dot(sinus_ref[at, :], place_ref[...]).astype(bf16)

    edge = PAD * TILE
    mirrored_ref[:edge, :] = jnp.zeros((edge, width), bf16)
    mirrored_ref[edge + length :, :] = jnp.zeros((edge, width), bf16)
    loop(length // BLOCK, table_step)
    attend_backward(
        starts_ref, qu_ref, qv_ref, k_ref, v_ref, t_ref, mirrored_ref, context_ref, logs_ref, dcontext_ref,
        dm_ref, dk_ref, dv_ref, dt_ref, small_ref.at[pl.ds(8, 8)], *attend
    )

    def queries_step(index):
        at = rows_at(index, BLOCK)
        d_norm = dot_t(dm_ref[at, :], in_ref[...])
        standard, inverse = normalize(h1_ref[at, :])
        gain = gains_ref[1:2, :]
        n2_ref[at, :] = (standard * gain).astype(bf16)
        small_ref[1:2, :] += column_sum(d_norm * standard)
        d1 = d2_ref[at, :] + normalize_back(standard, inverse, gain, d_norm)
        d1_ref[at, :] = d1
        picked = collect(cols_ref[at, 0:1], returned_ref)
        gate = gate_ref[at, :]
        dlogits_ref[at, :] = gate_back(d1, picked, gate, probs_ref[at, :], cols_ref[at, 2:3])
        low_ref[at, :] = (0.5 * gate * d1).astype(bf16)

    loop(length // BLOCK, queries_step)
    dtable_ref[...] = dt_ref[:, PAD * TILE : PAD * TILE + length].astype(bf16)
    dispatch(low_ref, slot_row_ref[0:1, :], out_refs)


def last_kernel(
    cols_ref, dlogits_ref, hidden_ref, d1_ref, embed_ref, router_ref, gains_ref, dembed_two_ref,
    drouter_two_ref, mid_ref, conv_ref, two_ref, five_ref, taps_ref, in_low_ref, out_low_ref, *refs,
):
    dsent_refs, refs = refs[:PARTS], refs[PARTS:]
    d0_ref, dembed_ref, routers_ref, small_ref, in_ref, out_ref, dsent_ref = refs
    in_ref[...] = in_low_ref[...].astype(f32)
    out_ref[...] = out_low_ref[...].astype(f32)
    length = hidden_ref.shape[0]
    taps = small_ref.shape[0] - 9
    join_blocks(dsent_refs, dsent_ref)
    drouter_ref = routers_ref.at[pl.ds(0, 8)]
    drouter_ref[...] = jnp.zeros_like(drouter_ref)
    routers_ref[8:, :] = drouter_two_ref[...]
    small_ref[0:1, :] = jnp.zeros_like(small_ref[0:1, :])
    small_ref[1:2, :] = mid_ref[1:2, :]
    small_ref[2:3, :] = conv_ref[0:1, :]
    small_ref[3:4, :] = two_ref[0:1, :]
    small_ref[4:5, :] = five_ref[0:1, :]
    small_ref[5:7, :] = mid_ref[8:10, :]
    small_ref[7 : 7 + taps, :] = taps_ref[:taps, :]
    small_ref[7 + taps :, :] = two_ref[1:3, :]

    def step(index):
        at = rows_at(index, BLOCK)
        standard, inverse = normalize(hidden_ref[at, :].astype(f32))
        gain = gains_ref[0:1, :]
        low = (standard * gain).astype(bf16)
        d_low, d_embed = router_back(
            dlogits_ref[at, :], low, embed_ref[at, :], router_ref, drouter_ref
        )
        dembed_ref[at, :] = d_embed + dembed_two_ref[at, :]
        d_norm = collect(cols_ref[at, 0:1], dsent_ref) + d_low
        small_ref[0:1, :] += column_sum(d_norm * standard)
        d0_ref[at, :] = d1_ref[at, :] + normalize_back(standard, inverse, gain, d_norm)

    loop(length // BLOCK, step)


def gather_small(values):
    return lax.all_to_all(values, BOTH, split_axis=0, concat_axis=0, tiled=True)


def across(values, axis, size, offset):
    if not offset:
        return values
    return lax.ppermute(values, axis, [(i, i ^ offset) for i in range(size)])


def exchange(blocks, experts):
    per = experts // PARTS
    moved = []
    for index, block in enumerate(blocks):
        rows = block.shape[0] // per
        pieces = []
        for k in range(index * per, (index + 1) * per):
            piece = block[(k - index * per) * rows : (k - index * per + 1) * rows]
            pieces.append(across(piece, "expert", experts, k))
        moved.append(pieces[0] if per == 1 else jnp.concatenate(pieces, axis=0))
    return moved


def ring_place(index, size):
    return jnp.where(index % 2 == 0, index // 2, size - 1 - index // 2)


def ring_member(place, size):
    place = (place + 2 * size) % size
    return jnp.where(place < size // 2, 2 * place, 2 * (size - 1 - place) + 1)


def ring_pairs(size, forward):
    order = list(range(0, size, 2)) + list(range(size - 1, 0, -2))
    step = 1 if forward else -1
    return [(order[k], order[(k + step) % size]) for k in range(size)]


def ring_gather(shards, size):
    found = []
    for number, shard in enumerate(shards):
        ahead = size // 2 if number % 2 == 0 else (size - 1) // 2
        pieces = [None] * size
        pieces[0] = shard
        found.append((pieces, ahead))
    for step in range(1, size // 2 + 1):
        for pieces, ahead in found:
            if step <= ahead:
                pieces[step] = lax.ppermute(pieces[step - 1], "dp", ring_pairs(size, False))
            if step <= size - 1 - ahead:
                pieces[-step] = lax.ppermute(pieces[-step + 1 or 0], "dp", ring_pairs(size, True))
    return [pieces for pieces, unused in found]


def assemble_kernel(count, order_ref, *refs):
    size = (len(refs) - 1 - count) // count
    sems = refs[-1]
    copies = []
    for number in range(count):
        target = refs[count * size + number]
        for offset in range(size):
            piece = refs[number * size + offset]
            rows = piece.shape[0]
            start = pl.multiple_of(order_ref[offset] * rows, 16)
            copies.append(
                pltpu.make_async_copy(
                    piece, target.at[pl.ds(start, rows)], sems.at[number * size + offset]
                )
            )
    for copy in copies:
        copy.start()
    for copy in copies:
        copy.wait()


def assemble(shards, size):
    place = ring_place(lax.axis_index("dp"), size)
    order = ring_member(place + jnp.arange(size, dtype=jnp.int32), size).astype(jnp.int32)
    groups = ring_gather(shards, size)
    count = len(groups)
    anywhere = pl.BlockSpec(memory_space=pl.ANY)
    return pl.pallas_call(
        functools.partial(assemble_kernel, count),
        out_shape=[
            shape_of((size * shard.shape[0],) + shard.shape[1:], shard.dtype) for shard in shards
        ],
        in_specs=[SMEM] + [anywhere] * (count * size),
        out_specs=[VMEM] * count,
        scratch_shapes=[pltpu.SemaphoreType.DMA((count * size,))],
        name="assemble",
    )(order, *[piece for pieces in groups for piece in pieces])


def own_parts(values, place, size, stride, mesh_axis):
    parts = [lax.dynamic_index_in_dim(values, place, 0, keepdims=False)]
    for k in range(1, values.shape[0]):
        theirs = lax.dynamic_index_in_dim(values, place ^ k, 0, keepdims=False)
        parts.append(across(theirs, mesh_axis, size, k * stride))
    return parts


def add_up(parts):
    total = parts[0].astype(f32)
    for part in parts[1:]:
        total = total + part.astype(f32)
    return total


def keep_one(values, place, size, stride, mesh_axis):
    return add_up(own_parts(values, place, size, stride, mesh_axis))


def near_parts(values):
    groups = values.shape[0]
    values = values.reshape((groups // 2, 2) + values.shape[1:])
    bit = lax.axis_index("dp") % 2
    mine = lax.dynamic_index_in_dim(values, bit, 1, keepdims=False)
    theirs = lax.dynamic_index_in_dim(values, 1 - bit, 1, keepdims=False)
    return [mine, across(theirs, "dp", groups, 1)]


def near_half(values):
    return add_up(near_parts(values)).astype(bf16)


def expert_parts(values, experts):
    me = lax.axis_index("expert")
    return [
        across(lax.dynamic_index_in_dim(values, me ^ k, 1, keepdims=False), "expert", experts, k)
        for k in range(experts)
    ]


def rows_product(left, right):
    return lax.dot_general(left, right, (((0,), (0,)), ((), ())), preferred_element_type=f32)


def blocks_product(left, right):
    left, right = jnp.concatenate(left, axis=0), jnp.concatenate(right, axis=0)
    return rows_product(left, right).astype(bf16)


def scatter_offloaded(grad_in, grad_out):
    return (
        lax.psum_scatter(grad_in, "dp", scatter_dimension=0, tiled=True),
        lax.psum_scatter(grad_out, "dp", scatter_dimension=0, tiled=True),
    )


def split_columns(values):
    middle = values.shape[1] // 2
    return [values[:, :middle], values[:, middle:]]


def sinus_rows(length, width, upward):
    distance = (length // 2 - 1 - np.arange(length)).astype(np.float32)
    distance = distance[::-1] if upward else distance
    rates = np.exp(
        np.arange(width // 2).astype(np.float32) * np.float32(-2.0 * math.log(10000.0) / width)
    ).astype(np.float32)
    angles = (distance[:, None] * rates[None, :]).astype(np.float64)
    table = np.concatenate([np.sin(angles), np.cos(angles)], axis=1)
    return jnp.asarray(table.astype(np.float32)).astype(bf16)


def body(
    groups,
    inputs,
    embedding,
    cotangent,
    first_routes,
    second_routes,
    segment_starts,
    norm_gains,
    first_router,
    second_router,
    first_in,
    first_out,
    second_in,
    second_out,
    attention_in,
    position_weight,
    position_bias,
    attention_out,
    pointwise_in,
    depthwise_kernel,
    batch_gain,
    batch_bias,
    pointwise_out,
):
    length, width = inputs.shape
    experts = first_router.shape[1]
    devices = groups * experts
    capacity = 17 * length // (16 * experts)
    slots = experts * capacity
    inner = first_in.shape[2]
    share = norm_gains.shape[1]
    taps = depthwise_kernel.shape[0]
    feats = first_router.shape[0]

    rows = jnp.concatenate(
        [norm_gains, position_bias, depthwise_kernel, batch_gain[None], batch_bias[None]], axis=0
    )
    count = rows.shape[0]
    flat = jnp.concatenate(
        [rows.reshape(-1), first_router.T.reshape(-1), second_router.T.reshape(-1)]
    ).astype(f32)
    small = gather_small(jnp.broadcast_to(flat[None], (devices,) + flat.shape))
    rows_all = small[:, : count * share].reshape(devices, count, share)
    rows_all = rows_all.transpose(1, 0, 2).reshape(count, devices * share)
    routers = small[:, count * share :].reshape(devices, 2, experts, feats)
    routers = routers.transpose(1, 2, 0, 3).reshape(2, experts, devices * feats)
    routers = jnp.pad(routers, ((0, 0), (0, TILE - experts), (0, 0)))
    routers = routers.transpose(0, 2, 1).astype(bf16)
    gains = jnp.pad(rows_all[0:5], ((0, 3), (0, 0)))
    bias = jnp.pad(rows_all[5:7], ((0, 6), (0, 0)))
    kernel_taps = jnp.pad(rows_all[7 : 7 + taps], ((0, 1), (0, 0)))
    batch = jnp.pad(rows_all[7 + taps : 9 + taps], ((0, 6), (0, 0)))

    packed = jnp.concatenate(
        [attention_in, position_weight, attention_out, pointwise_out, pointwise_in], axis=1
    )
    dense = lax.all_gather(packed, BOTH, axis=0, tiled=True)
    point_out = dense[:, 5 * width : 6 * width]

    first_pair = assemble((first_in[0], first_out[0]), groups)
    second_pair = (
        lax.all_gather(second_in[0], "dp", axis=0, tiled=True),
        lax.all_gather(second_out[0], "dp", axis=0, tiled=True),
    )

    me = lax.axis_index("expert")
    slot_rows, slot_cols = find_slots(first_routes, second_routes, me, capacity)
    sinus = sinus_rows(length, width, False)
    mirrored = sinus_rows(length, width, True)
    row_low = shape_of((length, width), bf16)
    row_full = shape_of((length, width), f32)
    lane_full = shape_of((length, TILE), f32)
    table_low = shape_of((length + 2 * PAD * TILE, width), bf16)
    block_low = shape_of((slots // PARTS, width), bf16)
    slots_scratch = pltpu.VMEM((slots, width), bf16)
    sums_scratch = pltpu.VMEM((8, width), f32)
    column = shape_of((length, 1), f32)
    eight = shape_of((8, width), f32)
    low_scratch = pltpu.VMEM((length, width), bf16)

    *sent_one, probs_one, gate_one = run(
        functools.partial(front_kernel, experts),
        (inputs, embedding, gains, routers[0], slot_cols, slot_rows),
        [VMEM] * 6,
        [block_low] * PARTS + [lane_full, column],
        [low_scratch],
        flops=4 * slots * length * width,
        name="front",
    )
    received_one = exchange(sent_one, experts)
    result_one = (
        expert_forward(received_one[2:3], *first_pair) + expert_forward(received_one[3:], *first_pair)
    )
    result_one = expert_forward(received_one[:2], *first_pair) + result_one
    returned_one = exchange(result_one, experts)

    edge_scratch = pltpu.VMEM((length + 2 * EDGE, width), f32)
    (
        h1, h2, query_u, query_v, keys, values, table, context, logs, convolved, sums,
    ) = run(
        middle_kernel,
        (
            segment_starts, inputs, slot_cols, gate_one, gains, dense, bias, kernel_taps, sinus,
            *returned_one,
        ),
        [SMEM] + [VMEM] * (8 + PARTS),
        [row_full, row_full]
        + [row_low] * 4
        + [table_low, row_low, lane_full, row_full, shape_of((devices, 1, 3 * width), f32)],
        [edge_scratch, sums_scratch, slots_scratch] + attend_scratch(length),
        flops=16 * length * length * width,
        name="middle",
    )
    totals = gather_small(sums)

    *sent_two, h3, active, probs_two, gate_two, stats = run(
        functools.partial(second_kernel, experts),
        (
            h2, convolved, totals, batch, point_out, embedding, gains, routers[1], slot_cols, slot_rows,
        ),
        [VMEM] * 10,
        [block_low] * PARTS + [row_full, row_low, lane_full, column, eight],
        [low_scratch],
        flops=4 * slots * length * width,
        name="second",
    )
    received_two = exchange(sent_two, experts)
    result_two = (
        expert_forward(received_two[2:3], *second_pair) + expert_forward(received_two[3:], *second_pair)
    )
    result_two = expert_forward(received_two[:2], *second_pair) + result_two
    returned_two = exchange(result_two, experts)

    *d_sent_two, output, d4, dlogits_two, dgain_five = run(
        turn_kernel,
        (
            h3, slot_cols, gate_two, probs_two, slot_rows, gains, cotangent, *returned_two,
        ),
        [VMEM] * (7 + PARTS),
        [block_low] * PARTS + [row_low, row_full, lane_full, eight],
        [low_scratch, slots_scratch],
        flops=4 * slots * length * width,
        name="turn",
    )
    d_result_two = exchange(d_sent_two, experts)
    unused, d_received_two, hidden_two, d_inner_two = backward_in_turn(
        received_two, d_result_two, second_pair
    )
    d_back_two = exchange(d_received_two, experts)
    grad_in_two, grad_out_two, *d_back_two = lax.optimization_barrier(
        (
            blocks_product(received_two, d_inner_two), blocks_product(hidden_two, d_result_two), *d_back_two,
        )
    )
    d_second_in, d_second_out = scatter_offloaded(grad_in_two, grad_out_two)

    router_shape = shape_of((8, 2 * width), f32)
    d3, d3_low, d_z, dembed_two, drouter_two, small_two, dsums_part = run(
        second_back_kernel,
        (
            slot_cols, dlogits_two, h3, d4, embedding, routers[1], gains, convolved, stats, batch, point_out,
            *d_back_two,
        ),
        [VMEM] * (11 + PARTS),
        [row_full, row_low, row_full, row_full, router_shape, eight, shape_of((devices, 1, 2 * width), f32)],
        [sums_scratch, slots_scratch],
        flops=4 * slots * length * width,
        name="second_back",
    )
    dsums = gather_small(dsums_part)
    d_pointwise_out = rows_product(active, d3_low)

    d2, d2_low, d_context, normed_three, d_gates, small_conv, d_taps = run(
        conv_back_kernel,
        (segment_starts, convolved, d_z, stats, dsums, d3, h2, gains, dense, kernel_taps),
        [SMEM] + [VMEM] * 9,
        [
            row_full, row_low, row_low, row_low, shape_of((length, 2 * width), bf16), eight,
            shape_of((16, width), f32),
        ],
        [
            edge_scratch, pltpu.VMEM((length, 2 * width), f32), pltpu.VMEM((16, 8, width), f32),
            pltpu.VMEM((2 * EDGE, 2 * width), f32),
        ],
        flops=6 * length * width * width,
        name="conv_back",
    )
    value_grad, gates_grad = split_columns(rows_product(normed_three, d_gates))
    early = jnp.stack(
        [
            part.astype(bf16).reshape(groups, experts, width // devices, width)
            for part in (rows_product(context, d2_low), d_pointwise_out, value_grad, gates_grad)
        ],
        axis=2,
    )
    early = expert_parts(early, experts)
    *d_sent_one, d1, dlogits_one, normed_two, d_mixed, d_table, small_mid = run(
        attend_back_kernel,
        (
            segment_starts, d2, d_context, h1, gains, dense, mirrored, query_u, query_v, keys, values, table,
            context, logs, slot_cols, gate_one, probs_one, slot_rows, *returned_one,
        ),
        [SMEM] + [VMEM] * (17 + PARTS),
        [block_low] * PARTS
        + [
            row_full, lane_full, row_low, shape_of((length, 3 * width), bf16),
            shape_of((width, length), bf16), shape_of((16, width), f32),
        ],
        [
            low_scratch, pltpu.VMEM(table_low.shape, bf16), slots_scratch,
            pltpu.VMEM((width, length), f32), pltpu.VMEM((width, length), f32),
            pltpu.VMEM((width, length + 2 * PAD * TILE), f32),
        ]
        + attend_back_scratch(),
        flops=32 * length * length * width,
        name="attend_back",
    )
    early, *d_sent_one = lax.optimization_barrier((early, *d_sent_one))
    d_result_one = exchange(d_sent_one, experts)
    (late,), d_received_one, hidden_one, d_inner_one = backward_in_turn(
        received_one, d_result_one, first_pair, (normed_two, d_mixed, d_table, mirrored)
    )
    late = expert_parts(late.reshape(groups, experts, width // devices, 4 * width), experts)
    d_back_one = exchange(d_received_one, experts)
    early = add_up(early).astype(bf16).reshape(groups, -1, width)
    grad_out = blocks_product(hidden_one, d_result_one).reshape(groups, -1, width)
    near_out = near_half(jnp.concatenate([grad_out, early], axis=1))
    grad_in = blocks_product(received_one, d_inner_one).reshape(groups, -1, inner)
    near_out, grad_in, late, d_back_one = lax.optimization_barrier(
        (near_out, grad_in, late, d_back_one)
    )
    far_out = own_parts(near_out, lax.axis_index("dp") // 2, groups, 2, "dp")
    near_in = near_parts(grad_in)
    d_start, d_embed, routers_grad, rows_grad, d_second_in, d_second_out = run(
        last_kernel,
        (
            slot_cols, dlogits_one, inputs, d1, embedding, routers[0], gains, dembed_two,
            drouter_two, small_mid, small_conv, small_two, dgain_five, d_taps, d_second_in, d_second_out,
            *d_back_one,
        ),
        [VMEM] * (16 + PARTS),
        [
            row_full, row_full, shape_of((16, 2 * width), f32), shape_of((count, width), f32),
            shape_of(first_in.shape[1:], f32), shape_of(first_out.shape[1:], f32),
        ],
        [slots_scratch],
        flops=4 * slots * length * width,
        name="last",
    )

    near_in, late, far_out, routers_grad, rows_grad = lax.optimization_barrier(
        (near_in, late, far_out, routers_grad, rows_grad)
    )
    near_in = add_up(near_in).astype(bf16)
    near_late = near_half(add_up(late).astype(bf16))
    late_share = add_up(own_parts(near_late, lax.axis_index("dp") // 2, groups, 2, "dp"))
    out_sum = add_up(far_out)
    far_in = own_parts(near_in, lax.axis_index("dp") // 2, groups, 2, "dp")
    far_in[1], routers_grad, rows_grad = lax.optimization_barrier(
        (far_in[1], routers_grad, rows_grad)
    )
    in_sum = add_up(far_in)
    d_first_out = out_sum[None, : first_out.shape[1]]
    d_first_in = in_sum[None]
    early_share = out_sum[first_out.shape[1] :].reshape(4, width // devices, width)
    early_share = jnp.concatenate([early_share[k] for k in range(4)], axis=1)
    rows_grad = rows_grad.reshape(count, devices, share).transpose(1, 0, 2).reshape(devices, -1)
    routers_grad = routers_grad.reshape(2, 8, devices, feats)[:, :experts]
    routers_grad = routers_grad.transpose(2, 0, 1, 3).reshape(devices, -1)
    small_grad = jnp.concatenate([rows_grad, routers_grad], axis=1)
    small_share = jnp.sum(
        lax.all_to_all(small_grad, BOTH, split_axis=0, concat_axis=0, tiled=True), axis=0
    )
    rows_share = small_share[: count * share].reshape(count, share)
    routers_share = small_share[count * share :].reshape(2, experts, feats).transpose(0, 2, 1)

    return (
        output,
        d_start,
        d_embed,
        rows_share[0:5],
        routers_share[0],
        routers_share[1],
        d_first_in,
        d_first_out,
        d_second_in[None],
        d_second_out[None],
        late_share[:, : 3 * width],
        late_share[:, 3 * width :],
        rows_share[5:7],
        early_share[:, :width],
        early_share[:, 2 * width :],
        rows_share[7 : 7 + taps],
        rows_share[7 + taps],
        rows_share[8 + taps],
        early_share[:, width : 2 * width],
    )


def solution(mesh):
    split = P(BOTH, None)
    wide = P(None, BOTH)
    bank = P("expert", "dp", None)
    line = P(BOTH)
    in_specs = (
        (split,) * 6
        + (wide, split, split)
        + (bank,) * 4
        + (split, split, wide, split, split, wide, line, line, split)
    )
    out_specs = (
        (split,) * 3
        + (wide, split, split)
        + (bank,) * 4
        + (split, split, wide, split, split, wide, line, line, split)
    )
    return jax.shard_map(
        functools.partial(body, mesh.shape["dp"]),
        mesh=mesh,
        in_specs=in_specs,
        out_specs=out_specs,
        check_vma=False,
    )
```
